32 devices in a mesh: dp: 16 (over z, y, x), fsdp: 2 (over core).
Axes of the slice: x: 2, y: 2, z: 4, core: 2. Of those that a mesh axis runs over, the one named last changes fastest.
Arguments:
- points: float32 [3, 524288], P(None, ('dp', 'fsdp')), may hold values from -6 to 6
- point_count: int32 [16384], P(('dp', 'fsdp')), may hold values from 1 to 32, as said below
- centre_slot: int32 [16384], P(('dp', 'fsdp')), may hold values from 0 to 31, as said below
- cloud_length: int32 [256], P(('dp', 'fsdp')), may hold values from 32 to 64
- cotangent: float32 [16384, 384], P(('dp', 'fsdp')), may hold values from -6 to 6
- point_master: float32 [493824], P(('dp', 'fsdp')), may hold values from -2 to 2
- block_master: float32 [1773312], P(('dp', 'fsdp')), may hold values from -2 to 2
- point_first: float32 [493824], P(('dp', 'fsdp')), may hold values from -362.03867 to 362.03867
- block_first: float32 [1773312], P(('dp', 'fsdp')), may hold values from -64 to 64
- point_second: float32 [493824], P(('dp', 'fsdp')), may hold values from 104.8576 to 524288
- block_second: float32 [1773312], P(('dp', 'fsdp')), may hold values from 3.2768 to 16384
Outputs:
- tokens_out: float32 [16384, 384], P(('dp', 'fsdp'))
- point_grad: float32 [3, 524288], P(None, ('dp', 'fsdp'))
- point_master_new: float32 [493824], P(('dp', 'fsdp'))
- block_master_new: float32 [1773312], P(('dp', 'fsdp'))
- point_first_new: float32 [493824], P(('dp', 'fsdp'))
- block_first_new: float32 [1773312], P(('dp', 'fsdp'))
- point_second_new: float32 [493824], P(('dp', 'fsdp'))
- block_second_new: float32 [1773312], P(('dp', 'fsdp'))
- point_copy: bfloat16 [493824], P(('dp', 'fsdp'))
- block_copy: bfloat16 [1773312], P(('dp', 'fsdp'))
- block_small_grad: float32 [3840], P(('dp', 'fsdp'))
The draws below stay inside these ranges and needn't reach their ends.
Inputs may be any that keep to these rules, and one draw needn't show every extreme that they name: Patch t holds its points in slots 0 to point_count[t] - 1; its other slots are padding. `centre_slot`: the centre slot of a patch is one of its points, below its point_count.
All inputs are finite; a program needn't handle non-finite values.
Results may differ from the reference program's by a relative error of at most 0.025.
Values may be sent and summed in bfloat16 or wider, within the bound.
A program may use at most 256 MiB of HBM per device.

```python
import math
import jax
import jax.numpy as jnp
from jax import lax

C1 = 128
C2 = 256
C3 = 512
D = 384
HEADS = 6
HEAD_DIM = 64
FF = 1536
GROUP = 32
PATCHES = 64
STEP = 10
CLOUDS = 256
TOKENS = 16384
POINTS_ALL = 524288
N_DP = 16
N_FSDP = 2


def point_layout_drawn():
    return [[('w1', (3, C1), 3.0 ** (-0.5), 0.1), ('bn1_gain', (C1,), 0.0, 0.2), ('bn1_shift', (C1,), -1.0, 0.2), ('b2', (C2,), -1.0, 0.2), ('bn3_gain', (C3,), 0.0, 0.3), ('bn3_shift', (C3,), -1.0, 0.3), ('b4', (D,), -1.0, 1.5)], [('w2', (C1, C2), C1 ** (-0.5), 0.1)], [('w3', (2 * C2, C3), (2 * C2) ** (-0.5), 0.15)], [('w4', (C3, D), C3 ** (-0.5), 0.5)]]


def block_layout_drawn():
    return [[('ln1_gain', (D,), 0.0, 0.5), ('ln1_shift', (D,), -1.0, 0.5), ('bo', (D,), -1.0, 1.2), ('ln2_gain', (D,), 0.0, 0.7), ('ln2_shift', (D,), -1.0, 0.7), ('bf1', (FF,), -1.0, 0.3), ('bf2', (D,), -1.0, 1.0)], [('wqkv', (D, 3 * D), D ** (-0.5), 0.3)], [('wo', (D, D), 3.0 * D ** (-0.5), 0.4)], [('wf1', (D, FF), D ** (-0.5), 0.3)], [('wf2', (FF, D), FF ** (-0.5), 0.65)]]


def fill_segments(key, layout, fill_fn, rows_summed):
    devices_all = N_DP * N_FSDP
    seg_list = []
    for seg_index, segment in enumerate(layout):
        piece_list = []
        used_len = 0
        for entry_index, entry_item in enumerate(segment):
            extent = math.prod(entry_item[1])
            piece_list.append(fill_fn(jax.random.fold_in(key, 100 * seg_index + entry_index), extent, entry_item[2], entry_item[3], rows_summed))
            used_len += extent
        seg_len = -(-used_len // devices_all) * devices_all
        piece_list.append(fill_fn(jax.random.fold_in(key, 100 * seg_index + 99), seg_len - used_len, -1.0, 1.0, rows_summed))
        seg_list.append(jnp.concatenate(piece_list).reshape(devices_all, -1))
    return jnp.concatenate(seg_list, axis=1).reshape(-1)


def master_fill(sub_key, extent, spread, factor, rows_summed):
    if spread > 0.0:
        return spread * jax.random.truncated_normal(sub_key, -3.0, 3.0, (extent,), jnp.float32)
    if spread == 0.0:
        return jax.random.uniform(sub_key, (extent,), jnp.float32, 0.5, 1.5)
    return 0.3 * jax.random.truncated_normal(sub_key, -3.0, 3.0, (extent,), jnp.float32)


def first_fill(sub_key, extent, spread, factor, rows_summed):
    return factor * rows_summed ** 0.5 * (0.1 / 0.9) * jax.random.truncated_normal(sub_key, -3.0, 3.0, (extent,), jnp.float32)


def second_fill(sub_key, extent, spread, factor, rows_summed):
    size_sq = factor * factor * rows_summed * (0.05 / 0.95)
    return size_sq * jnp.exp(jax.random.uniform(sub_key, (extent,), jnp.float32, math.log(0.5), math.log(8.0)))


def count_table(key):
    index_all = jnp.arange(TOKENS, dtype=jnp.int32)
    lowest = max(GROUP // 3, 1)
    ceiling = lowest + (GROUP - lowest) * index_all // max(TOKENS - 1, 1)
    counts = jax.random.randint(key, (TOKENS,), 1, ceiling + 1, dtype=jnp.int32)
    return (jnp.where(index_all == TOKENS - 1, GROUP, counts), index_all)


def draw_point_count(key, part):
    counts, index_all = count_table(key)
    return counts


def draw_centre_slot(key, part):
    counts, index_all = count_table(key)
    key = jax.random.fold_in(key, 2)
    slot_draw = jax.random.randint(key, (TOKENS,), 0, counts, dtype=jnp.int32)
    return jnp.where(index_all == TOKENS - 1, GROUP - 1, slot_draw)


def draw_cloud_length(key, part):
    key = jax.random.fold_in(key, 3)
    lengths_drawn = jax.random.randint(key, (CLOUDS,), PATCHES // 2, PATCHES + 1, dtype=jnp.int32)
    return lengths_drawn.at[0].set(PATCHES).at[1].set(PATCHES // 2)


def draw_point_master(key, part):
    key = jax.random.fold_in(key, 11)
    return fill_segments(key, point_layout_drawn(), master_fill, 1.0)


def draw_block_master(key, part):
    key = jax.random.fold_in(key, 12)
    return fill_segments(key, block_layout_drawn(), master_fill, 1.0)


def draw_point_first(key, part):
    key = jax.random.fold_in(key, 13)
    return fill_segments(key, point_layout_drawn(), first_fill, float(TOKENS * GROUP))


def draw_block_first(key, part):
    key = jax.random.fold_in(key, 14)
    return fill_segments(key, block_layout_drawn(), first_fill, float(TOKENS))


def draw_point_second(key, part):
    key = jax.random.fold_in(key, 15)
    return fill_segments(key, point_layout_drawn(), second_fill, float(TOKENS * GROUP))


def draw_block_second(key, part):
    key = jax.random.fold_in(key, 16)
    return fill_segments(key, block_layout_drawn(), second_fill, float(TOKENS))


def steps_of(key, shape, pieces, least, largest):
    factor_of = 1.0
    for axis_at, shards_of in pieces:
        heights = jax.random.uniform(jax.random.fold_in(jax.random.fold_in(key, 6), axis_at), (shards_of,), jnp.float32, least / len(pieces), largest / len(pieces))
        factor_of = factor_of * jnp.repeat(jnp.exp(heights), shape[axis_at] // shards_of).reshape((-1,) + (1,) * (len(shape) - 1 - axis_at))
    return factor_of


def bell_draw(stream_key, shape, width, reach, shards=(), held_as=jnp.bfloat16):
    array = jax.random.normal(stream_key, shape, jnp.float32) * width
    if len(shards) > 0:
        array = steps_of(stream_key, shape, shards, -0.22, 0.18) * array
    return jnp.clip(array, min=-reach, max=reach).astype(held_as)


def setup_inputs(seed: int = 0) -> dict:
    seeds = jax.random.split(jax.random.key(seed), 12)
    return {
        "points": bell_draw(seeds[0], (3, POINTS_ALL), 1.0, 6.0, ((1, 32),), jnp.float32),
        "point_count": draw_point_count(jax.random.fold_in(seeds[11], 71), 0),
        "centre_slot": draw_centre_slot(jax.random.fold_in(seeds[11], 71), 0),
        "cloud_length": draw_cloud_length(jax.random.fold_in(seeds[11], 71), 0),
        "cotangent": bell_draw(seeds[4], (TOKENS, D), 1.0, 6.0, ((0, 32),), jnp.float32),
        "point_master": draw_point_master(jax.random.fold_in(seeds[11], 71), 0),
        "block_master": draw_block_master(jax.random.fold_in(seeds[11], 71), 0),
        "point_first": draw_point_first(jax.random.fold_in(seeds[11], 71), 0),
        "block_first": draw_block_first(jax.random.fold_in(seeds[11], 71), 0),
        "point_second": draw_point_second(jax.random.fold_in(seeds[11], 71), 0),
        "block_second": draw_block_second(jax.random.fold_in(seeds[11], 71), 0),
    }


EPS_NORM = 1e-05
BETA_ONE = 0.9
BETA_TWO = 0.95
ADAM_EPS = 1e-08
DECAY_RATE = 0.05
NEG_FILL = -1e+30
HIGH = lax.Precision.HIGHEST

@jax.custom_vjp
def low(v):
    return lax.optimization_barrier(v.astype(jnp.bfloat16)).astype(jnp.float32)

@jax.custom_vjp
def low_back(v):
    return v

def low_keep(v):
    return (low(v), None)

def low_pass(kept, grad):
    return (grad,)

def back_keep(v):
    return (v, None)

def back_low(kept, grad):
    return (low(grad),)
low.defvjp(low_keep, low_pass)
low_back.defvjp(back_keep, back_low)

def point_layout():
    return [[('w1', (3, C1), 3.0 ** (-0.5), 0.1), ('bn1_gain', (C1,), 0.0, 0.2), ('bn1_shift', (C1,), -1.0, 0.2), ('b2', (C2,), -1.0, 0.2), ('bn3_gain', (C3,), 0.0, 0.3), ('bn3_shift', (C3,), -1.0, 0.3), ('b4', (D,), -1.0, 1.5)], [('w2', (C1, C2), C1 ** (-0.5), 0.1)], [('w3', (2 * C2, C3), (2 * C2) ** (-0.5), 0.15)], [('w4', (C3, D), C3 ** (-0.5), 0.5)]]

def block_layout():
    return [[('ln1_gain', (D,), 0.0, 0.5), ('ln1_shift', (D,), -1.0, 0.5), ('bo', (D,), -1.0, 1.2), ('ln2_gain', (D,), 0.0, 0.7), ('ln2_shift', (D,), -1.0, 0.7), ('bf1', (FF,), -1.0, 0.3), ('bf2', (D,), -1.0, 1.0)], [('wqkv', (D, 3 * D), D ** (-0.5), 0.3)], [('wo', (D, D), 3.0 * D ** (-0.5), 0.4)], [('wf1', (D, FF), D ** (-0.5), 0.3)], [('wf2', (FF, D), FF ** (-0.5), 0.65)]]

def rate_for(spread):
    return 2.0 * spread if spread > 0.0 else 0.5 if spread == 0.0 else 0.6

def decay_for(spread):
    return DECAY_RATE if spread > 0.0 else 0.0

def segment_lengths(layout, devices):
    lengths_out = []
    for segment in layout:
        used_len = sum((math.prod(entry_item[1]) for entry_item in segment))
        lengths_out.append(-(-used_len // devices) * devices)
    return lengths_out

def to_segments(flat_vector, layout):
    devices_all = N_DP * N_FSDP
    table_rows = flat_vector.reshape(devices_all, -1)
    seg_list = []
    offset = 0
    for seg_len in segment_lengths(layout, devices_all):
        piece_len = seg_len // devices_all
        seg_list.append(table_rows[:, offset:offset + piece_len].reshape(-1))
        offset += piece_len
    return seg_list

def from_segments(seg_list):
    devices_all = N_DP * N_FSDP
    return jnp.concatenate([seg_values.reshape(devices_all, -1) for seg_values in seg_list], axis=1).reshape(-1)

def unpack(seg_list, layout):
    weight_table = {}
    for seg_values, segment in zip(seg_list, layout):
        offset = 0
        for entry_label, entry_dims, spread, factor in segment:
            extent = math.prod(entry_dims)
            weight_table[entry_label] = seg_values[offset:offset + extent].reshape(entry_dims)
            offset += extent
    return weight_table

def full_rates(layout):
    devices_all = N_DP * N_FSDP
    rate_segs = []
    decay_segs = []
    for segment, seg_len in zip(layout, segment_lengths(layout, devices_all)):
        rate_parts = []
        decay_parts = []
        used_len = 0
        for entry_label, entry_dims, spread, factor in segment:
            extent = math.prod(entry_dims)
            rate_parts.append(jnp.full((extent,), rate_for(spread), jnp.float32))
            decay_parts.append(jnp.full((extent,), decay_for(spread), jnp.float32))
            used_len += extent
        rate_parts.append(jnp.zeros((seg_len - used_len,), jnp.float32))
        decay_parts.append(jnp.zeros((seg_len - used_len,), jnp.float32))
        rate_segs.append(jnp.concatenate(rate_parts))
        decay_segs.append(jnp.concatenate(decay_parts))
    return (from_segments(rate_segs), from_segments(decay_segs))

def cloud_geometry(cloud_points, cloud_counts, cloud_centres):
    grid_points = cloud_points.reshape(3, -1, GROUP)
    slot_ids = jnp.arange(GROUP, dtype=jnp.int32)
    picker = (slot_ids[None, :] == cloud_centres[:, None]).astype(jnp.float32)
    centre = lax.optimization_barrier(jnp.sum(grid_points * picker[None], axis=2))
    relative = (grid_points - centre[:, :, None]).reshape(3, -1)
    valid_mask = (slot_ids[None, :] < cloud_counts[:, None]).astype(jnp.float32).reshape(-1)
    return (relative, valid_mask, picker)

def pool_mean(values, valid_mask, cloud_counts):
    grid_vals = values.reshape(-1, GROUP, values.shape[-1])
    return lax.optimization_barrier(jnp.sum(grid_vals * valid_mask.reshape(-1, GROUP, 1), 1)) / cloud_counts[:, None].astype(jnp.float32)

def batch_terms(values, valid_mask):
    masked = values * valid_mask[:, None]
    return (jnp.sum(valid_mask), lax.optimization_barrier(jnp.sum(masked, 0)), lax.optimization_barrier(jnp.sum(masked * values, 0)))

def zero_totals(width_len):
    return (jnp.zeros((), jnp.float32), jnp.zeros((width_len,), jnp.float32), jnp.zeros((width_len,), jnp.float32))

def normalize(values, totals, gain_vec, shift_vec):
    tally_all, sum_all, squares = totals
    centre_value = sum_all / tally_all
    spread_sq = squares / tally_all - centre_value * centre_value
    inverse = lax.rsqrt(spread_sq + EPS_NORM)
    unit_vals = (values - centre_value) * inverse
    return (unit_vals, inverse, unit_vals * gain_vec + shift_vec)

def layer_norm(values, gain_vec, shift_vec):
    centred = values - lax.optimization_barrier(jnp.mean(values, -1, keepdims=True))
    inverse = lax.rsqrt(lax.optimization_barrier(jnp.mean(centred * centred, -1, keepdims=True)) + EPS_NORM)
    unit_vals = centred * inverse
    return (unit_vals, inverse, unit_vals * gain_vec + shift_vec)

def first_layer(point_w, relative):
    return low_back(jnp.dot(low(relative).T, point_w['w1'], precision=HIGH))

def lower_net(point_w, relative, valid_mask, cloud_counts, first_totals):
    pre_one = first_layer(point_w, relative)
    unit_one, inv_one, norm_one = normalize(pre_one, first_totals, point_w['bn1_gain'], point_w['bn1_shift'])
    act_one = low(jax.nn.gelu(norm_one))
    pre_two = low_back(jnp.dot(act_one, point_w['w2'], precision=HIGH)) + point_w['b2']
    feat_two = low(pre_two)
    pooled_low = low(pool_mean(feat_two, valid_mask, cloud_counts))
    global_part = jnp.dot(pooled_low, point_w['w3'][:C2], precision=HIGH)
    local_part = jnp.dot(feat_two, point_w['w3'][C2:], precision=HIGH)
    return low_back((local_part.reshape(-1, GROUP, C3) + global_part[:, None, :]).reshape(-1, C3))

def encoder(block_w, x_zero, slab_lengths):
    unit_a, inv_a, normed_a = layer_norm(x_zero, block_w['ln1_gain'], block_w['ln1_shift'])
    qkv_low = low(low_back(jnp.dot(low(normed_a), block_w['wqkv'], precision=HIGH)))
    qkv_low = qkv_low.reshape(-1, PATCHES, 3, HEADS, HEAD_DIM)
    queries = qkv_low[:, :, 0]
    key_rows = qkv_low[:, :, 1]
    values = qkv_low[:, :, 2]
    scores = low_back(jnp.einsum('nqhe,nkhe->nhqk', queries, key_rows, precision=HIGH) * HEAD_DIM ** (-0.5))
    key_valid = jnp.arange(PATCHES, dtype=jnp.int32)[None, :] < slab_lengths[:, None]
    scores = jnp.where(key_valid[:, None, None, :], scores, NEG_FILL)
    row_top = lax.optimization_barrier(jnp.max(scores, -1, keepdims=True))
    raised = jnp.exp(scores - row_top)
    soft_probs = low(raised / lax.optimization_barrier(jnp.sum(raised, -1, keepdims=True)))
    mixed_out = low(low_back(jnp.einsum('nhqk,nkhe->nqhe', soft_probs, values, precision=HIGH))).reshape(-1, D)
    x_one = x_zero + low_back(jnp.dot(mixed_out, block_w['wo'], precision=HIGH)) + block_w['bo']
    unit_b, inv_b, normed_b = layer_norm(x_one, block_w['ln2_gain'], block_w['ln2_shift'])
    hidden_pre = low_back(jnp.dot(low(normed_b), block_w['wf1'], precision=HIGH)) + block_w['bf1']
    hidden_low = low(jax.nn.gelu(hidden_pre))
    return x_one + low_back(jnp.dot(hidden_low, block_w['wf2'], precision=HIGH)) + block_w['bf2']

def forward(point_vec, block_vec, points, point_count, centre_slot, cloud_length):
    point_w = unpack(to_segments(low(point_vec), point_layout()), point_layout())
    block_w = unpack(to_segments(low(block_vec), block_layout()), block_layout())
    slab_total = N_DP * N_FSDP
    slabs = (points.reshape(3, slab_total, -1).transpose(1, 0, 2), point_count.reshape(slab_total, -1), centre_slot.reshape(slab_total, -1))

    def first_step(running, slab_in):
        relative, valid_mask, picker = cloud_geometry(*slab_in)
        pre_one = first_layer(point_w, relative)
        return (jax.tree.map(jnp.add, running, batch_terms(pre_one, valid_mask)), None)
    first_totals, _ = lax.scan(jax.checkpoint(first_step), zero_totals(C1), slabs)

    def third_step(running, slab_in):
        relative, valid_mask, picker = cloud_geometry(*slab_in)
        pre_three = lower_net(point_w, relative, valid_mask, slab_in[1], first_totals)
        return (jax.tree.map(jnp.add, running, batch_terms(pre_three, valid_mask)), None)
    third_totals, _ = lax.scan(jax.checkpoint(third_step), zero_totals(C3), slabs)

    def final_step(slab_in):
        relative, valid_mask, picker = cloud_geometry(slab_in[0], slab_in[1], slab_in[2])
        pre_three = lower_net(point_w, relative, valid_mask, slab_in[1], first_totals)
        unit_three, inv_three, norm_three = normalize(pre_three, third_totals, point_w['bn3_gain'], point_w['bn3_shift'])
        act_three = low(jax.nn.gelu(norm_three))
        pre_four = low_back(jnp.dot(act_three, point_w['w4'], precision=HIGH)) + point_w['b4']
        x_zero = pool_mean(pre_four, valid_mask, slab_in[1])
        return encoder(block_w, x_zero, slab_in[3])
    outputs = lax.map(jax.checkpoint(final_step), slabs + (cloud_length.reshape(slab_total, -1),))
    return outputs.reshape(TOKENS, D)

def adam_update(master, moment_one, moment_two, gradient, step_rates, decays):
    one_new = BETA_ONE * moment_one + (1.0 - BETA_ONE) * gradient
    two_new = BETA_TWO * moment_two + (1.0 - BETA_TWO) * gradient * gradient
    fix_one = 1.0 - BETA_ONE ** STEP
    fix_two = 1.0 - BETA_TWO ** STEP
    direction = one_new / fix_one / (jnp.sqrt(two_new / fix_two) + ADAM_EPS)
    master_new = master - step_rates * (direction + decays * master)
    return (master_new, one_new, two_new)

def reference(points, point_count, centre_slot, cloud_length, cotangent, point_master, block_master, point_first, block_first, point_second, block_second):

    def forward_of(point_arg, block_arg, points_arg):
        return forward(point_arg, block_arg, points_arg, point_count, centre_slot, cloud_length)
    tokens_out, pull_back = jax.vjp(forward_of, point_master, block_master, points)
    grad_point, grad_block, grad_points = pull_back(cotangent)
    point_rates, point_decays = full_rates(point_layout())
    block_rates, block_decays = full_rates(block_layout())
    point_new, point_one, point_two = adam_update(point_master, point_first, point_second, grad_point, point_rates, point_decays)
    block_new, block_one, block_two = adam_update(block_master, block_first, block_second, grad_block, block_rates, block_decays)
    block_small_grad = to_segments(grad_block, block_layout())[0]
    return (tokens_out, grad_points, point_new, block_new, point_one, block_one, point_two, block_two, point_new.astype(jnp.bfloat16), block_new.astype(jnp.bfloat16), block_small_grad)
```

```python
import functools
import math

import jax
import jax.numpy as jnp
from jax import lax
from jax.experimental import pallas as pl
from jax.experimental.pallas import tpu as pltpu
from jax.sharding import PartitionSpec as P

C1 = 128
C2 = 256
C3 = 512
D = 384
HEADS = 6
HEAD_DIM = 64
FF = 1536
GROUP = 32
PATCHES = 64
STEP = 10

EPS_NORM = 1e-05
BETA_ONE = 0.9
BETA_TWO = 0.95
ADAM_EPS = 1e-08
DECAY_RATE = 0.05
NEG_FILL = -1e30

F32 = jnp.float32
BF16 = jnp.bfloat16
AXES = ("dp", "fsdp")
MESH = pl.DeviceIdType.MESH
VMEM_LIMIT = 60 * 2**20
TILE = 2048
TOK = TILE // GROUP
SUB = 512
TB = 256
PAIR = 128

NZ, NY, NX, NC = 4, 2, 2, 2
W3_AT, W4_AT, QKV_AT, WO_AT, WF1_AT, WF2_AT, WIDTH = 0, 512, 896, 2048, 2432, 3968, 5120
W2_AT, PSMALL_AT, BSMALL_AT = 896, 1152, 1280
HALF = WIDTH // 2
PROWS, BROWS = 128, 440


def point_layout():
    return [
        [
            ("w1", (3, C1), 3.0 ** (-0.5)),
            ("bn1_gain", (C1,), 0.0),
            ("bn1_shift", (C1,), -1.0),
            ("b2", (C2,), -1.0),
            ("bn3_gain", (C3,), 0.0),
            ("bn3_shift", (C3,), -1.0),
            ("b4", (D,), -1.0),
        ],
        [("w2", (C1, C2), C1 ** (-0.5))],
        [("w3", (2 * C2, C3), (2 * C2) ** (-0.5))],
        [("w4", (C3, D), C3 ** (-0.5))],
    ]


def block_layout():
    return [
        [
            ("ln1_gain", (D,), 0.0),
            ("ln1_shift", (D,), -1.0),
            ("bo", (D,), -1.0),
            ("ln2_gain", (D,), 0.0),
            ("ln2_shift", (D,), -1.0),
            ("bf1", (FF,), -1.0),
            ("bf2", (D,), -1.0),
        ],
        [("wqkv", (D, 3 * D), D ** (-0.5))],
        [("wo", (D, D), 3.0 * D ** (-0.5))],
        [("wf1", (D, FF), D ** (-0.5))],
        [("wf2", (FF, D), FF ** (-0.5))],
    ]


def rate_for(spread):
    return 2.0 * spread if spread > 0.0 else 0.5 if spread == 0.0 else 0.6


def decay_for(spread):
    return DECAY_RATE if spread > 0.0 else 0.0


def segment_lengths(layout, devices):
    lengths_out = []
    for segment in layout:
        used_len = sum((math.prod(entry[1]) for entry in segment))
        lengths_out.append(-(-used_len // devices) * devices)
    return lengths_out


def shard_rates(layout, devices, own_rank):
    rate_parts = []
    decay_parts = []
    for segment, seg_len in zip(layout, segment_lengths(layout, devices)):
        piece_len = seg_len // devices
        position = own_rank * piece_len + jnp.arange(piece_len, dtype=jnp.int32)
        seg_rates = jnp.zeros((piece_len,), F32)
        seg_decays = jnp.zeros((piece_len,), F32)
        offset = 0
        for entry_label, entry_dims, spread in segment:
            extent = math.prod(entry_dims)
            inside = (position >= offset) & (position < offset + extent)
            seg_rates = jnp.where(inside, rate_for(spread), seg_rates)
            seg_decays = jnp.where(inside, decay_for(spread), seg_decays)
            offset += extent
        rate_parts.append(seg_rates)
        decay_parts.append(seg_decays)
    return (jnp.concatenate(rate_parts), jnp.concatenate(decay_parts))


def mm(a, b):
    return jnp.dot(a, b, preferred_element_type=F32)


def mm_tn(a, b):
    return lax.dot_general(a, b, (((0,), (0,)), ((), ())), preferred_element_type=F32)


def mm_nt(a, b):
    return lax.dot_general(a, b, (((1,), (1,)), ((), ())), preferred_element_type=F32)


def low(v):
    return v.astype(BF16)


def split_three(v):
    hi = low(v)
    rest = v - hi.astype(F32)
    mid = low(rest)
    return hi, mid, low(rest - mid.astype(F32))


def mm_exact(a, b):
    hi, mid, lo = split_three(a)
    return mm(hi, b) + (mm(mid, b) + mm(lo, b))


GELU_A = math.sqrt(2.0 / math.pi)
GELU_B = GELU_A * 0.044715


def gelu_pair(v):
    square = v * v
    t = jnp.tanh(v * (GELU_A + GELU_B * square))
    h = 0.5 + 0.5 * t
    g = v * h
    return g, h + (g - g * h) * (2.0 * GELU_A + 6.0 * GELU_B * square)


def patch_ones():
    i = lax.broadcasted_iota(jnp.int32, (256, 256), 0) // GROUP
    j = lax.broadcasted_iota(jnp.int32, (256, 256), 1) // GROUP
    return (i == j).astype(F32).astype(BF16)


def token_ones():
    t = lax.broadcasted_iota(jnp.int32, (TOK, TILE), 0)
    p = lax.broadcasted_iota(jnp.int32, (TOK, TILE), 1) // GROUP
    return (t == p).astype(F32).astype(BF16)


def patch_sum(rows, ones):
    return mm_exact(rows, ones)


def groups(dp):
    lower = math.gcd(dp, 4)
    return lower, dp // lower


def ring_peers(dp, upper_stage):
    lower, upper = groups(dp)
    at, core = lax.axis_index("dp"), lax.axis_index("fsdp")
    up, down = at // lower, lax.rem(at, lower)
    peers = []
    if upper_stage:
        for k in range(1, upper):
            peers.append((lax.rem(up + k, upper) * lower + down, core))
    else:
        for k in range(1, lower * NC):
            p = lax.rem(down * NC + core + k, lower * NC)
            peers.append((up * lower + p // NC, lax.rem(p, NC)))
    return peers


def greet(peers):
    barrier = pltpu.get_barrier_semaphore()
    for peer in peers:
        pl.semaphore_signal(barrier, inc=1, device_id=peer, device_id_type=MESH)
    return len(peers)


def greeted(count):
    pl.semaphore_wait(pltpu.get_barrier_semaphore(), count)


def sum_start(dp, upper_stage, acc, slots, send, recv):
    lower, upper = groups(dp)
    first = lower * NC - 1 if upper_stage else 0
    copies = []
    for k, peer in enumerate(ring_peers(dp, upper_stage)):
        copy = pltpu.make_async_remote_copy(
            src_ref=acc,
            dst_ref=slots.at[first + k],
            send_sem=send.at[first + k],
            recv_sem=recv.at[first + k],
            device_id=peer,
            device_id_type=MESH,
        )
        copy.start()
        copies.append(copy)
    return copies


def sum_finish(dp, upper_stage, acc, slots, copies):
    lower, upper = groups(dp)
    first = lower * NC - 1 if upper_stage else 0
    for copy in copies:
        copy.wait()
    total = acc[...]
    for k in range(len(copies)):
        total = total + slots[first + k]
    acc[...] = total


def sum_over_devices(dp, acc, slots, send, recv):
    for upper_stage in (False, True):
        copies = sum_start(dp, upper_stage, acc, slots, send, recv)
        sum_finish(dp, upper_stage, acc, slots, copies)


def sum_scratch(dp, shape):
    lower, upper = groups(dp)
    count = lower * NC - 1 + upper - 1
    return [
        pltpu.VMEM(shape, F32),
        pltpu.VMEM((count,) + shape, F32),
        pltpu.SemaphoreType.DMA((count,)),
        pltpu.SemaphoreType.DMA((count,)),
    ]


def all_peers(dp):
    return ring_peers(dp, False) + ring_peers(dp, True)


def vmem(count):
    return [pl.BlockSpec(memory_space=pltpu.VMEM)] * count


def shaped(*items):
    return [jax.ShapeDtypeStruct(s, t) for s, t in items]


def params(**more):
    return pltpu.CompilerParams(vmem_limit_bytes=VMEM_LIMIT, **more)


def geometry(points_ref, slots_ref, rel_ref, moment_ref):
    ones = patch_ones()
    moment_ref[...] = jnp.zeros_like(moment_ref)
    lane = lax.rem(lax.broadcasted_iota(jnp.int32, (1, 256), 1), GROUP)

    def piece(i, carry):
        at = pl.ds(pl.multiple_of(i * 256, 256), 256)
        pts = points_ref[:, at]
        valid = (lane < slots_ref[0:1, at]).astype(F32)
        pick = (lane == slots_ref[1:2, at]).astype(F32)
        relative = (pts - patch_sum(pts * pick, ones)) * valid
        rows = low(jnp.concatenate([relative, valid, relative, valid], axis=0))
        rel_ref[:, at] = rows
        moment_ref[:, 0:8] += mm_nt(rows, rows)
        return carry

    lax.fori_loop(0, points_ref.shape[1] // 256, piece, 0, unroll=8)


def prepare_one(moments, small):
    n = moments[3:4, 3:4]
    w = [small[k : k + 1, :] for k in range(3)]
    gain, shift = small[3:4, :], small[4:5, :]
    mean = sum(w[k] * moments[k : k + 1, 3:4] for k in range(3)) / n
    square = jnp.zeros_like(mean)
    for j in range(3):
        for k in range(3):
            square = square + w[j] * w[k] * moments[j : j + 1, k : k + 1]
    inverse = lax.rsqrt(square / n - mean * mean + EPS_NORM)
    scale = inverse * gain
    scaled = [wk * scale for wk in w]
    offset = shift - mean * scale
    high = [low(v) for v in scaled + [offset]]
    rest = [low(v - h.astype(F32)) for v, h in zip(scaled + [offset], high)]
    forward = jnp.concatenate(high + rest, axis=0)
    zero = jnp.zeros((1, C1), BF16)
    backward = jnp.concatenate(high[:3] + [zero] + rest[:3] + [zero], axis=0)
    stats = jnp.concatenate(
        [mean, inverse, jnp.broadcast_to(n, (1, C1)), scale, jnp.zeros((4, C1), F32)], axis=0
    )
    return forward, backward, stats


def flat_rows(pieces, length, rows):
    lane = lax.broadcasted_iota(jnp.int32, (1, 128), 1)
    out = [jnp.zeros((1, 128), F32) for _ in range(rows)]
    for r in range(pieces.shape[0]):
        row = jnp.where(lane < length, pieces[r : r + 1, :], 0.0)
        at = length * r
        row = pltpu.roll(row, at % 128, 1) if at % 128 else row
        first = at // 128
        out[first] = out[first] + jnp.where(lane >= at % 128, row, 0.0)
        if at % 128 + length > 128:
            out[first + 1] = out[first + 1] + jnp.where(lane < at % 128, row, 0.0)
    return jnp.concatenate(out, axis=0)


def piece_of(rows, at, length):
    lane = lax.broadcasted_iota(jnp.int32, (1, 128), 1)
    first, shift = at // 128, at % 128
    row = rows[first : first + 1, :]
    if shift:
        row = pltpu.roll(row, 128 - shift, 1)
        if shift + length > 128:
            other = pltpu.roll(rows[first + 1 : first + 2, :], 128 - shift, 1)
            row = jnp.where(lane < 128 - shift, row, other)
    return jnp.where(lane < length, row, 0.0)


def where_am_i():
    at = lax.axis_index("dp")
    return at // (NY * NX), lax.rem(at // NX, NY), lax.rem(at, NX), lax.axis_index("fsdp")


def chip(z, y, x):
    return (z * NY + y) * NX + x


def rows_twelve():
    return [(QKV_AT, 3 * D), (WO_AT, D), (WF1_AT, FF)]


def gather_kernel(
    points_ref, slots_ref, pflat, bflat,
    rel_ref, moment_ref, psmall_o, bsmall_o, w2_o, w3_o, w4_o, wqkv_o, wo_o, wf1_o, wf2_o,
    blocks, stage, wide, acc, sums, ssend, srecv, gsend, grecv,
):
    z, y, x, core = where_am_i()
    dp = NZ * NY * NX
    near = [(chip(lax.rem(z + k, NZ), y, x), core) for k in range(1, NZ)]
    over_y, over_x, twin = (chip(z, 1 - y, x), core), (chip(z, y, 1 - x), core), (chip(z, y, x), 1 - core)
    count = greet(all_peers(dp) + near + [over_y, over_x, twin])

    stage[...] = jnp.zeros_like(stage)
    for at, start, rows, cols, under in (
        (W3_AT, 9, 16, C3, 0), (W4_AT, 73, 16, D, 0), (W2_AT, 1, 4, C2, 12),
    ):
        for j in range(cols // 128):
            stage[under : under + rows, at + 128 * j : at + 128 * j + 128] = pflat[
                pl.ds(start + j, rows, stride=cols // 128), :
            ]
    stage[12:13, PSMALL_AT : PSMALL_AT + 128] = pflat[0:1, :]
    stage[12:13, BSMALL_AT : BSMALL_AT + 128] = bflat[0:1, :]
    start = 1
    for at, cols in rows_twelve():
        for j in range(cols // 128):
            stage[0:12, at + 128 * j : at + 128 * j + 128] = bflat[
                pl.ds(start + j, 12, stride=cols // 128), :
            ]
        start += 12 * cols // 128
    for b in range(3):
        for j in range(D // 128):
            to = WF2_AT + D * b + 128 * j
            stage[:, to : to + 128] = bflat[pl.ds(start + 48 * b + j, 16, stride=3), :]
    blocks[z, y, x, core] = low(stage[...])

    greeted(count)
    used = [0]

    def send(view, peer):
        k = used[0]
        used[0] += 1
        copy = pltpu.make_async_remote_copy(
            src_ref=view, dst_ref=view, send_sem=gsend.at[k], recv_sem=grecv.at[k],
            device_id=peer, device_id_type=MESH,
        )
        copy.start()
        return copy

    one, two = pl.ds(0, HALF), pl.ds(HALF, HALF)
    live = [send(blocks.at[z, y, x, core], peer) for peer in near]
    geometry(points_ref, slots_ref, rel_ref, acc)
    small = sum_start(dp, False, acc, sums, ssend, srecv)
    for copy in live:
        copy.wait()
    live = [
        send(blocks.at[:, y, x, core, :, one], over_y),
        send(blocks.at[:, y, x, core, :, two], over_x),
    ]
    inner = [send(blocks.at[:, y, x, core], twin)]
    sum_finish(dp, False, acc, sums, small)
    small = sum_start(dp, True, acc, sums, ssend, srecv)
    for copy in live:
        copy.wait()
    live = [
        send(blocks.at[:, :, x, core, :, one], over_x),
        send(blocks.at[:, y, :, core, :, two], over_y),
    ]
    inner += [
        send(blocks.at[:, 1 - y, x, core, :, one], twin),
        send(blocks.at[:, y, 1 - x, core, :, two], twin),
    ]
    sum_finish(dp, True, acc, sums, small)
    moment_ref[...] = acc[...]
    for copy in live:
        copy.wait()
    inner += [
        send(blocks.at[:, :, 1 - x, core, :, one], twin),
        send(blocks.at[:, 1 - y, :, core, :, two], twin),
    ]
    for copy in inner:
        copy.wait()

    for d in range(dp * NC):
        cz, cy, cx, cc = d // 8, d // 4 % 2, d // 2 % 2, d % 2
        block = blocks.at[cz, cy, cx, cc]
        w3_o[16 * d : 16 * d + 16, :] = block[:, W3_AT : W3_AT + C3]
        w4_o[16 * d : 16 * d + 16, :] = block[:, W4_AT : W4_AT + D]
        for b in range(3):
            at = 48 * d + 16 * b
            wf2_o[at : at + 16, :] = block[:, WF2_AT + D * b : WF2_AT + D * b + D]
        under = block[:, QKV_AT:WF2_AT].astype(F32)
        wide[12 * d : 12 * d + 12, :] = under[0:12, :]
        tail = under[12:16, 0 : BSMALL_AT + 128 - QKV_AT]
        wide[384 + 4 * d : 384 + 4 * d + 4, 0 : BSMALL_AT + 128 - QKV_AT] = tail
    for at, cols, out in ((QKV_AT, 3 * D, wqkv_o), (WO_AT, D, wo_o), (WF1_AT, FF, wf1_o)):
        out[...] = low(wide[0:384, at - QKV_AT : at - QKV_AT + cols])
    w2_o[...] = low(wide[384:512, 0:C2])
    tails = wide[pl.ds(384, 32, stride=4), :] if False else None
    psmall = jnp.concatenate(
        [wide[384 + 4 * d : 385 + 4 * d, PSMALL_AT - QKV_AT : PSMALL_AT - QKV_AT + 128] for d in range(32)], 0
    )
    bsmall = jnp.concatenate(
        [wide[384 + 4 * d : 385 + 4 * d, BSMALL_AT - QKV_AT : BSMALL_AT - QKV_AT + 128] for d in range(32)], 0
    )
    psmall_o[0:18, :] = flat_rows(psmall, 72, 18)
    bsmall_o[0:30, :] = flat_rows(bsmall, 120, 30)


def gather_call(points, slots, pflat, bflat):
    dp = NZ * NY * NX
    count = points.shape[1]
    outs = shaped(
        ((8, count), BF16), ((8, 128), F32), ((24, 128), F32), ((32, 128), F32),
        ((C1, C2), BF16), ((2 * C2, C3), BF16), ((C3, D), BF16),
        ((D, 3 * D), BF16), ((D, D), BF16), ((D, FF), BF16), ((FF, D), BF16),
    )
    return pl.pallas_call(
        gather_kernel,
        out_shape=outs,
        in_specs=vmem(4),
        out_specs=vmem(len(outs)),
        scratch_shapes=[
            pltpu.VMEM((NZ, NY, NX, NC, 16, WIDTH), BF16),
            pltpu.VMEM((16, WIDTH), F32),
            pltpu.VMEM((512, WF2_AT - QKV_AT), F32),
        ]
        + sum_scratch(dp, (8, 128))
        + [pltpu.SemaphoreType.DMA((16,)), pltpu.SemaphoreType.DMA((16,))],
        compiler_params=params(collective_id=0, has_side_effects=True),
        name="gather",
    )(points, slots, pflat, bflat)


def first_kernel(
    rel_ref, moment_ref, psmall_ref, w2_ref, w3_ref,
    ext_o, gp_o, f_o, ft_o, gram_o, fs_o, cnt_o, g_o, fw_o, pooled_o, sums_o, stats_o, wd_o,
    e_s, wn_s, w2_s,
):
    step = pl.program_id(0)

    @pl.when(step == 0)
    def _():
        gram_o[...] = jnp.zeros_like(gram_o)
        e_s[...] = token_ones()
        small = psmall_ref[...]
        forward, backward, stats = prepare_one(moment_ref[:, 0:8], small)
        wn_s[...] = forward
        wd_o[...] = backward
        stats_o[...] = stats
        w2_s[0:C1, :] = w2_ref[...]
        b2 = jnp.concatenate([small[5:6, :], small[6:7, :]], axis=1)
        w2_s[C1:, :] = low(jnp.concatenate([b2, jnp.zeros((15, C2), F32)], axis=0))

    rel = rel_ref[...]
    valid = rel[3:4, :].astype(F32)
    for j in range(TILE // 256):
        at = slice(256 * j, 256 * j + 256)
        g, gp = gelu_pair(mm_tn(wn_s[...], rel[:, at]))
        ext_o[0:C1, at] = low(g * valid[:, at])
        gp_o[:, at] = low(gp * valid[:, at])
    ext_o[C1:, :] = jnp.concatenate([rel[3:4], jnp.zeros((15, TILE), BF16)], axis=0)
    ext = ext_o[...]
    ft = low(mm_tn(w2_s[...], ext))
    f = low(mm_tn(ext, w2_s[...]))
    ft_o[...] = ft
    f_o[...] = f
    gram_o[...] += mm(ft, f)
    at = pl.ds(pl.multiple_of(step * TOK, TOK), TOK)
    fs_o[at, :] = mm(e_s[...], f)
    cnt_o[at, :] = jnp.broadcast_to(mm_nt(e_s[...], rel)[:, 3:4], (TOK, 128))

    @pl.when(step == pl.num_programs(0) - 1)
    def _():
        count = cnt_o[:, 0:1]
        fs = fs_o[...]
        pooled = low(fs / count)
        pooled_o[...] = pooled
        g = mm(pooled, w3_ref[0:C2, :])
        g_o[...] = g
        lower = w3_ref[C2:, :]
        fw = mm_exact(fs, lower)
        fw_o[...] = fw
        one = jnp.sum(fw + count * g, axis=0, keepdims=True)
        two = jnp.sum(mm_exact(gram_o[...], lower) * lower.astype(F32), axis=0, keepdims=True)
        two = two + jnp.sum(g * (2.0 * fw + count * g), axis=0, keepdims=True)
        sums_o[...] = jnp.concatenate([one, two, jnp.zeros((6, C3), F32)], axis=0)


def first_call(rel, moments, psmall, w2, w3):
    count = rel.shape[1]
    tokens = count // GROUP
    full = lambda *s: pl.BlockSpec(s, lambda i: (0, 0))
    cols = lambda r: pl.BlockSpec((r, TILE), lambda i: (0, i))
    return pl.pallas_call(
        first_kernel,
        grid=(count // TILE,),
        in_specs=[cols(8), full(8, 128), full(24, 128), full(C1, C2), full(2 * C2, C3)],
        out_specs=[
            cols(C1 + 16), cols(C1), pl.BlockSpec((TILE, C2), lambda i: (i, 0)), cols(C2),
            full(C2, C2), full(tokens, C2), full(tokens, 128), full(tokens, C3), full(tokens, C3),
            full(tokens, C2), full(8, C3), full(8, C1), full(8, C1),
        ],
        out_shape=shaped(
            ((C1 + 16, count), BF16), ((C1, count), BF16), ((count, C2), BF16), ((C2, count), BF16),
            ((C2, C2), F32), ((tokens, C2), F32), ((tokens, 128), F32), ((tokens, C3), F32),
            ((tokens, C3), F32), ((tokens, C2), BF16), ((8, C3), F32), ((8, C1), F32), ((8, C1), BF16),
        ),
        scratch_shapes=[pltpu.VMEM((TOK, TILE), BF16), pltpu.VMEM((8, C1), BF16), pltpu.VMEM((C1 + 16, C2), BF16)],
        compiler_params=params(),
        name="first",
    )(rel, moments, psmall, w2, w3)


def third_kernel(dp, sums_ref, g_ref, stats_ref, psmall_ref, gm_o, sv_o, acc, slots, send, recv):
    count = greet(all_peers(dp))
    acc[...] = sums_ref[...]
    greeted(count)
    sum_over_devices(dp, acc, slots, send, recv)
    n = stats_ref[2:3, 0:1]
    mean = acc[0:1, :] / n
    inverse = lax.rsqrt(acc[1:2, :] / n - mean * mean + EPS_NORM)
    gain = jnp.concatenate([psmall_ref[k : k + 1, :] for k in range(7, 11)], axis=1)
    shift = jnp.concatenate([psmall_ref[k : k + 1, :] for k in range(11, 15)], axis=1)
    gm_o[...] = g_ref[...] - mean
    sv_o[...] = jnp.concatenate(
        [inverse * gain, shift, mean, inverse, jnp.zeros((4, C3), F32)], axis=0
    )


def third_call(dp, sums, g, stats, psmall):
    return pl.pallas_call(
        functools.partial(third_kernel, dp),
        out_shape=shaped((g.shape, F32), ((8, C3), F32)),
        in_specs=vmem(4),
        out_specs=vmem(2),
        scratch_shapes=sum_scratch(dp, (8, C3)),
        compiler_params=params(collective_id=1, has_side_effects=True),
        name="third",
    )(sums, g, stats, psmall)


def second_kernel(f_ref, rel_ref, w3_ref, gm_ref, sv_ref, gp_o, pa_o, pg_o, pc_o, e_s):
    @pl.when(pl.program_id(0) == 0)
    def _():
        e_s[...] = token_ones()

    mask = e_s[...] * rel_ref[3:4, :]
    lower = w3_ref[C2:, :]
    scale, shift = low(sv_ref[0:1, :]), low(sv_ref[1:2, :])
    tokens = SUB // GROUP
    for j in range(TILE // SUB):
        at, ts = slice(SUB * j, SUB * j + SUB), slice(tokens * j, tokens * j + tokens)
        c = mm(f_ref[at, :], lower).reshape(tokens, GROUP, C3) + gm_ref[ts, :][:, None, :]
        c = low(c)
        g, gp = gelu_pair(c * scale[None] + shift[None])
        gc = (gp * c).reshape(SUB, C3)
        gp = gp.reshape(SUB, C3)
        gp_o[at, :] = gp
        m = mask[ts, at]
        pa_o[ts, :] = mm(m, g.reshape(SUB, C3))
        pg_o[ts, :] = mm(m, gp)
        pc_o[ts, :] = mm(m, gc)


def second_call(f, rel, w3, gm, sv):
    count = f.shape[0]
    tokens = count // GROUP
    full = lambda *s: pl.BlockSpec(s, lambda i: (0, 0))
    rows = lambda r, c: pl.BlockSpec((r, c), lambda i: (i, 0))
    return pl.pallas_call(
        second_kernel,
        grid=(count // TILE,),
        in_specs=[rows(TILE, C2), pl.BlockSpec((8, TILE), lambda i: (0, i)), full(2 * C2, C3), rows(TOK, C3), full(8, C3)],
        out_specs=[rows(TILE, C3), rows(TOK, C3), rows(TOK, C3), rows(TOK, C3)],
        out_shape=shaped(((count, C3), BF16), ((tokens, C3), F32), ((tokens, C3), F32), ((tokens, C3), F32)),
        scratch_shapes=[pltpu.VMEM((TOK, TILE), BF16)],
        compiler_params=params(),
        name="second",
    )(f, rel, w3, gm, sv)


def wide_row(ref, first, rows):
    return jnp.concatenate([ref[k : k + 1, :] for k in range(first, first + rows)], axis=1)


def layer_norm(v, gain, shift):
    centred = v - jnp.mean(v, -1, keepdims=True)
    inverse = lax.rsqrt(jnp.mean(centred * centred, -1, keepdims=True) + EPS_NORM)
    unit = centred * inverse
    return unit, inverse, low(unit * gain + shift)


def norm_back(d_unit, unit, inverse):
    return inverse * (
        d_unit - jnp.mean(d_unit, -1, keepdims=True) - unit * jnp.mean(d_unit * unit, -1, keepdims=True)
    )


def col_sum(v):
    return jnp.sum(v, axis=0, keepdims=True)


def block_kernel(
    pa_ref, pg_ref, pc_ref, cnt_ref, len_ref, cot_ref, psmall_ref, bsmall_ref, sv_ref,
    w4_ref, wqkv_ref, wo_ref, wf1_ref, wf2_ref,
    out_o, gw4_o, gwqkv_o, gwo_o, gwf1_o, gwf2_o, small_o, tok_o, tg_o, back_o,
    qkv_s, mixed_s, soft_s, dmix_s, dqkv_s,
):
    step = pl.program_id(0)

    @pl.when(step == 0)
    def _():
        for ref in (gw4_o, gwqkv_o, gwo_o, gwf1_o, gwf2_o, small_o, back_o):
            ref[...] = jnp.zeros_like(ref)

    count = cnt_ref[:, 0:1]
    scale = HEAD_DIM ** (-0.5)
    b4 = wide_row(psmall_ref, 15, 3)
    ln1_gain, ln1_shift, bo = wide_row(bsmall_ref, 0, 3), wide_row(bsmall_ref, 3, 3), wide_row(bsmall_ref, 6, 3)
    ln2_gain, ln2_shift = wide_row(bsmall_ref, 9, 3), wide_row(bsmall_ref, 12, 3)
    bf1, bf2 = wide_row(bsmall_ref, 15, 12), wide_row(bsmall_ref, 27, 3)

    act = low(pa_ref[...] / count)
    x_zero = mm(act, w4_ref[...]) + b4
    unit_a, inv_a, normed_a = layer_norm(x_zero, ln1_gain, ln1_shift)
    qkv_s[...] = low(mm(normed_a, wqkv_ref[...]))

    row_cloud = lax.broadcasted_iota(jnp.int32, (PAIR, PAIR), 0) // PATCHES
    col = lax.broadcasted_iota(jnp.int32, (PAIR, PAIR), 1)
    left = lax.broadcasted_iota(jnp.int32, (1, 128), 1) < HEAD_DIM
    zero = jnp.zeros((1, 1), BF16)

    def halves(v):
        return jnp.where(left, v, zero), jnp.where(left, zero, v)

    tiles = TB // PAIR
    for s in range(tiles):
        first = (step * tiles + s) * 2
        visible = (row_cloud == col // PATCHES) & (
            lax.rem(col, PATCHES) < jnp.where(col < PATCHES, len_ref[first], len_ref[first + 1])
        )
        rows = slice(PAIR * s, PAIR * s + PAIR)
        for p in range(HEADS // 2):
            at = 128 * p
            q = qkv_s[rows, at : at + 128]
            k = qkv_s[rows, D + at : D + at + 128]
            v = qkv_s[rows, 2 * D + at : 2 * D + at + 128]
            mixed = []
            for a, q_half in enumerate(halves(q)):
                score = jnp.where(visible, mm_nt(q_half, k) * scale, NEG_FILL)
                raised = jnp.exp(score - jnp.max(score, -1, keepdims=True))
                soft = raised / jnp.sum(raised, -1, keepdims=True)
                soft_s[(s * (HEADS // 2) + p) * 2 + a] = soft
                mixed.append(mm(low(soft), v))
            mixed_s[rows, at : at + 128] = low(jnp.where(left, mixed[0], mixed[1]))

    mixed_low = mixed_s[...]
    x_one = x_zero + mm(mixed_low, wo_ref[...]) + bo
    unit_b, inv_b, normed_b = layer_norm(x_one, ln2_gain, ln2_shift)
    hidden, d_hidden = gelu_pair(mm(normed_b, wf1_ref[...]) + bf1)
    hidden = low(hidden)
    out_o[...] = x_one + mm(hidden, wf2_ref[...]) + bf2

    cot = cot_ref[...]
    grad = low(cot)
    gwf2_o[...] += mm_tn(hidden, grad)
    d_pre = mm_nt(grad, wf2_ref[...]) * d_hidden
    d_pre_low = low(d_pre)
    gwf1_o[...] += mm_tn(normed_b, d_pre_low)
    d_normed_b = mm_nt(d_pre_low, wf1_ref[...])
    d_x_one = cot + norm_back(d_normed_b * ln2_gain, unit_b, inv_b)
    d_x_low = low(d_x_one)
    gwo_o[...] += mm_tn(mixed_low, d_x_low)
    dmix_s[...] = low(mm_nt(d_x_low, wo_ref[...]))

    for s in range(tiles):
        rows = slice(PAIR * s, PAIR * s + PAIR)
        for p in range(HEADS // 2):
            at = 128 * p
            q = qkv_s[rows, at : at + 128]
            k = qkv_s[rows, D + at : D + at + 128]
            v = qkv_s[rows, 2 * D + at : 2 * D + at + 128]
            dm = dmix_s[rows, at : at + 128]
            d_q, d_k, d_v = [], [], []
            for a, dm_half in enumerate(halves(dm)):
                soft = soft_s[(s * (HEADS // 2) + p) * 2 + a]
                d_soft = mm_nt(dm_half, v)
                d_v.append(mm_tn(low(soft), dm))
                d_score = low(soft * (d_soft - jnp.sum(soft * d_soft, -1, keepdims=True)))
                d_q.append(mm(d_score, k))
                d_k.append(mm_tn(d_score, q))
            dqkv_s[rows, at : at + 128] = low(jnp.where(left, d_q[0], d_q[1]) * scale)
            dqkv_s[rows, D + at : D + at + 128] = low(jnp.where(left, d_k[0], d_k[1]) * scale)
            dqkv_s[rows, 2 * D + at : 2 * D + at + 128] = low(jnp.where(left, d_v[0], d_v[1]))

    d_qkv = dqkv_s[...]
    gwqkv_o[...] += mm_tn(normed_a, d_qkv)
    d_normed_a = mm_nt(d_qkv, wqkv_ref[...])
    d_x_zero = d_x_one + norm_back(d_normed_a * ln1_gain, unit_a, inv_a)
    d_x_low = low(d_x_zero)
    gw4_o[...] += mm_tn(act, d_x_low)
    token = mm_nt(d_x_low, w4_ref[...]) / count
    tok_o[...] = token
    grouped = token * pg_ref[...]
    tg_o[...] = grouped
    back_o[0:1, :] += col_sum(grouped)
    back_o[1:2, :] += col_sum(token * pc_ref[...]) * sv_ref[3:4, :]
    narrow = [
        col_sum(d_normed_a * unit_a), col_sum(d_normed_a), col_sum(d_x_one),
        col_sum(d_normed_b * unit_b), col_sum(d_normed_b), col_sum(cot), col_sum(d_x_zero),
    ]
    for k, row in enumerate(narrow):
        small_o[k : k + 1, 0:D] += row
    small_o[7:8, :] += col_sum(d_pre)


def block_call(pa, pg, pc, cnt, length, cot, psmall, bsmall, sv, w4, wqkv, wo, wf1, wf2):
    tokens = pa.shape[0]
    full = lambda *s: pl.BlockSpec(s, lambda i: (0, 0))
    rows = lambda c: pl.BlockSpec((TB, c), lambda i: (i, 0))
    return pl.pallas_call(
        block_kernel,
        grid=(tokens // TB,),
        in_specs=[
            rows(C3), rows(C3), rows(C3), rows(128), pl.BlockSpec(memory_space=pltpu.SMEM), rows(D),
            full(24, 128), full(32, 128), full(8, C3),
            full(C3, D), full(D, 3 * D), full(D, D), full(D, FF), full(FF, D),
        ],
        out_specs=[
            rows(D), full(C3, D), full(D, 3 * D), full(D, D), full(D, FF), full(FF, D), full(8, FF),
            rows(C3), rows(C3), full(8, C3),
        ],
        out_shape=shaped(
            ((tokens, D), F32), ((C3, D), F32), ((D, 3 * D), F32), ((D, D), F32), ((D, FF), F32),
            ((FF, D), F32), ((8, FF), F32), ((tokens, C3), F32), ((tokens, C3), F32), ((8, C3), F32),
        ),
        scratch_shapes=[
            pltpu.VMEM((TB, 3 * D), BF16), pltpu.VMEM((TB, D), BF16),
            pltpu.VMEM((TB // PAIR * HEADS, PAIR, PAIR), F32), pltpu.VMEM((TB, D), BF16),
            pltpu.VMEM((TB, 3 * D), BF16),
        ],
        compiler_params=params(),
        name="block",
    )(pa, pg, pc, cnt, length, cot, psmall, bsmall, sv, w4, wqkv, wo, wf1, wf2)


def third_back_kernel(
    dp, back_ref, tok_ref, tg_ref, fs_ref, fw_ref, gm_ref, cnt_ref, pooled_ref, gram_ref, w3_ref, sv_ref, stats_ref,
    tot_o, tok_o, kap_o, k_o, ws_o, top_o, corr_o, acc, slots, send, recv,
):
    greeting = greet(all_peers(dp))
    acc[...] = back_ref[...]
    tok_o[...] = low(tok_ref[...])
    lower = w3_ref[C2:, :].astype(F32)
    gain = sv_ref[0:1, :]
    ws_o[...] = low(lower * gain)
    greeted(greeting)
    sum_over_devices(dp, acc, slots, send, recv)
    tot_o[...] = acc[...]
    n = stats_ref[2:3, 0:1]
    alpha = gain * acc[0:1, :] / n
    beta = gain * acc[1:2, :] * sv_ref[3:4, :] / n
    count = cnt_ref[:, 0:1]
    gm = gm_ref[...]
    per_token = low(gain * tg_ref[...] - (count * alpha + beta * (fw_ref[...] + count * gm)))
    d_pooled = mm_nt(per_token, w3_ref[0:C2, :])
    shifted = low(alpha + beta * gm)
    kap_o[...] = d_pooled / count - mm_nt(shifted, w3_ref[C2:, :])
    k_o[...] = low(-mm_nt(low(lower * beta), w3_ref[C2:, :]))
    top_o[...] = mm_tn(pooled_ref[...], per_token)
    corr_o[...] = mm_tn(low(fs_ref[...]), shifted) + beta * mm(low(gram_ref[...]), w3_ref[C2:, :])


def third_back_call(dp, back, tok, tg, fs, fw, gm, cnt, pooled, gram, w3, sv, stats):
    tokens = tok.shape[0]
    outs = shaped(
        ((8, C3), F32), ((tokens, C3), BF16), ((tokens, C2), F32), ((C2, C2), BF16), ((C2, C3), BF16),
        ((C2, C3), F32), ((C2, C3), F32),
    )
    return pl.pallas_call(
        functools.partial(third_back_kernel, dp),
        out_shape=outs,
        in_specs=vmem(12),
        out_specs=vmem(len(outs)),
        scratch_shapes=sum_scratch(dp, (8, C3)),
        compiler_params=params(collective_id=2, has_side_effects=True),
        name="third_back",
    )(back, tok, tg, fs, fw, gm, cnt, pooled, gram, w3, sv, stats)


def last_kernel(
    gp_ref, f_ref, ft_ref, ext_ref, gp1_ref, rel_ref, tok_ref, kap_ref, k_ref, ws_ref, w2_ref, wd_ref,
    h_o, gw2_o, q_o, d_o, dn_s,
):
    @pl.when(pl.program_id(0) == 0)
    def _():
        for ref in (h_o, gw2_o, q_o):
            ref[...] = jnp.zeros_like(ref)

    tokens = SUB // GROUP
    for j in range(TILE // SUB):
        at, ts = slice(SUB * j, SUB * j + SUB), slice(tokens * j, tokens * j + tokens)
        gp = gp_ref[at, :].reshape(tokens, GROUP, C3)
        dn_s[at, :] = (gp * tok_ref[ts, :][:, None, :]).reshape(SUB, C3)
    dn = dn_s[...]
    h_o[...] += mm(ft_ref[...], dn)
    d_feat = mm_nt(dn, ws_ref[...]) + mm(f_ref[...], k_ref[...])
    d_feat = (d_feat.reshape(TOK, GROUP, C2) + kap_ref[...][:, None, :]).reshape(TILE, C2)
    d_feat = low(d_feat)
    gw2_o[...] += mm(ext_ref[...], d_feat)
    d_one = low(mm_nt(w2_ref[...], d_feat) * gp1_ref[...].astype(F32))
    d_o[...] = mm(wd_ref[...], d_one)
    q_o[...] += mm_nt(rel_ref[...], d_one)


def last_call(gp, f, ft, ext, gp1, rel, tok, kap, k, ws, w2, wd):
    count = f.shape[0]
    full = lambda *s: pl.BlockSpec(s, lambda i: (0, 0))
    rows = lambda r, c: pl.BlockSpec((r, c), lambda i: (i, 0))
    cols = lambda r: pl.BlockSpec((r, TILE), lambda i: (0, i))
    return pl.pallas_call(
        last_kernel,
        grid=(count // TILE,),
        in_specs=[
            rows(TILE, C3), rows(TILE, C2), cols(C2), cols(C1 + 16), cols(C1), cols(8), rows(TOK, C3), rows(TOK, C2),
            full(C2, C2), full(C2, C3), full(C1, C2), full(8, C1),
        ],
        out_specs=[full(C2, C3), full(C1 + 16, C2), full(8, C1), cols(8)],
        out_shape=shaped(((C2, C3), F32), ((C1 + 16, C2), F32), ((8, C1), F32), ((8, count), F32)),
        scratch_shapes=[pltpu.VMEM((TILE, C3), BF16)],
        compiler_params=params(),
        name="last",
    )(gp, f, ft, ext, gp1, rel, tok, kap, k, ws, w2, wd)


def first_grads(q, moments, psmall, stats):
    mean, inverse, n, scale = stats[0:1], stats[1:2], stats[2:3], stats[3:4]
    w = [psmall[k : k + 1, :] for k in range(3)]
    one = q[3:4, :]
    two = inverse * (sum(w[k] * q[k : k + 1, :] for k in range(3)) - mean * one)
    grad_w = []
    for k in range(3):
        along = sum(w[j] * moments[k : k + 1, j : j + 1] for j in range(3)) - mean * moments[k : k + 1, 3:4]
        grad_w.append(scale * (q[k : k + 1, :] - (one * moments[k : k + 1, 3:4] + two * inverse * along) / n))
    flat = [
        jnp.sum(scale * w[k] * (one - two * inverse * mean) / n, axis=1, keepdims=True) for k in range(3)
    ]
    slope = [
        [jnp.sum(scale * w[k] * two * inverse * w[j] / n, axis=1, keepdims=True) for j in range(3)]
        for k in range(3)
    ]
    return grad_w, two, one, flat, slope


def point_gradient(d_ref, rel_ref, slots_ref, flat, slope, out_ref):
    ones = patch_ones()
    lane = lax.rem(lax.broadcasted_iota(jnp.int32, (1, 256), 1), GROUP)
    base = jnp.concatenate(flat, axis=0)
    columns = [jnp.concatenate([slope[k][j] for k in range(3)], axis=0) for j in range(3)]

    def piece(i, carry):
        at = pl.ds(pl.multiple_of(i * 256, 256), 256)
        rel = rel_ref[:, at].astype(F32)
        d = d_ref[:, at]
        out = d[0:3] + d[4:7] - rel[3:4] * base
        for j in range(3):
            out = out - columns[j] * rel[j : j + 1]
        pick = (lane == slots_ref[1:2, at]).astype(F32)
        out_ref[:, at] = out - pick * patch_sum(out, ones)
        return carry

    lax.fori_loop(0, d_ref.shape[1] // 256, piece, 0, unroll=8)


def point_small_rows(grad_w, gain1, shift1, b2, tot, b4):
    rows = list(grad_w) + [gain1, shift1]
    rows += [b2[:, 128 * k : 128 * k + 128] for k in range(2)]
    rows += [tot[1:2, 128 * k : 128 * k + 128] for k in range(4)]
    rows += [tot[0:1, 128 * k : 128 * k + 128] for k in range(4)]
    rows += [b4[:, 128 * k : 128 * k + 128] for k in range(3)]
    return jnp.concatenate(rows, axis=0)


def block_small_rows(small_ref):
    rows = [small_ref[k : k + 1, 128 * j : 128 * j + 128] for k in range(5) for j in range(3)]
    rows += [small_ref[7:8, 128 * j : 128 * j + 128] for j in range(12)]
    rows += [small_ref[5:6, 128 * j : 128 * j + 128] for j in range(3)]
    return jnp.concatenate(rows, axis=0)


def scatter_kernel(
    q_ref, moment_ref, psmall_ref, stats_ref, tot_ref, small_ref, d_ref, rel_ref, slots_ref,
    gw2_ref, top_ref, h_ref, corr_ref, sv_ref, gw4_ref, gwqkv_ref, gwo_ref, gwf1_ref, gwf2_ref,
    pg_o, pflat_o, bflat_o,
    blocks, stage, land1, land2, land3, land4, acc, slots, ssend, srecv, gsend, grecv,
):
    z, y, x, core = where_am_i()
    dp = NZ * NY * NX
    near = [(chip(lax.rem(z + k, NZ), y, x), core) for k in range(1, NZ)]
    over_y, over_x, twin = (chip(z, 1 - y, x), core), (chip(z, y, 1 - x), core), (chip(z, y, x), 1 - core)
    count = greet(all_peers(dp) + near + [over_y, over_x, twin])
    acc[...] = q_ref[...]
    greeted(count)
    small = sum_start(dp, False, acc, slots, ssend, srecv)

    none = jnp.zeros((1, 128), F32)
    prow = point_small_rows(
        [none] * 3, none, none, gw2_ref[C1 : C1 + 1, :], jnp.zeros((8, C3), F32), small_ref[6:7, 0:D]
    )
    brow = block_small_rows(small_ref)
    stage[...] = jnp.zeros_like(stage)
    gain = sv_ref[0:1, :]
    for d in range(dp * NC):
        cz, cy, cx, cc = d // 8, d // 4 % 2, d // 2 % 2, d % 2
        if d < 16:
            stage[:, W3_AT : W3_AT + C3] = top_ref[16 * d : 16 * d + 16, :]
        else:
            rows = slice(16 * (d - 16), 16 * (d - 16) + 16)
            stage[:, W3_AT : W3_AT + C3] = h_ref[rows, :] * gain - corr_ref[rows, :]
        stage[:, W4_AT : W4_AT + D] = gw4_ref[16 * d : 16 * d + 16, :]
        stage[0:12, QKV_AT : QKV_AT + 3 * D] = gwqkv_ref[12 * d : 12 * d + 12, :]
        stage[0:12, WO_AT : WO_AT + D] = gwo_ref[12 * d : 12 * d + 12, :]
        stage[0:12, WF1_AT : WF1_AT + FF] = gwf1_ref[12 * d : 12 * d + 12, :]
        stage[12:16, W2_AT : W2_AT + C2] = gw2_ref[4 * d : 4 * d + 4, :]
        stage[12:13, PSMALL_AT : PSMALL_AT + 128] = piece_of(prow, 72 * d, 72)
        stage[12:13, BSMALL_AT : BSMALL_AT + 128] = piece_of(brow, 120 * d, 120)
        for b in range(3):
            at = 48 * d + 16 * b
            stage[:, WF2_AT + D * b : WF2_AT + D * b + D] = gwf2_ref[at : at + 16, :]
        blocks[cc, cz, cy, cx] = low(stage[...])

    used = [0]

    def send(src, dst, peer):
        k = used[0]
        used[0] += 1
        copy = pltpu.make_async_remote_copy(
            src_ref=src, dst_ref=dst, send_sem=gsend.at[k], recv_sem=grecv.at[k],
            device_id=peer, device_id_type=MESH,
        )
        copy.start()
        return copy

    one, two = pl.ds(0, HALF), pl.ds(HALF, HALF)
    mine = blocks.at[core]
    live = [send(blocks.at[1 - core], land1, twin)]
    sum_finish(dp, False, acc, slots, small)
    small = sum_start(dp, True, acc, slots, ssend, srecv)
    for copy in live:
        copy.wait()

    def add(dst, index, landed):
        dst[index] = low(dst[index].astype(F32) + landed.astype(F32))

    for cz in range(NZ):
        for cy in range(NY):
            for cx in range(NX):
                add(mine, (cz, cy, cx), land1[cz, cy, cx])
    live = [
        send(mine.at[:, :, 1 - x, :, one], land2.at[0], over_x),
        send(mine.at[:, 1 - y, :, :, two], land2.at[1], over_y),
    ]
    sum_finish(dp, True, acc, slots, small)
    totals = acc[...]
    moments = moment_ref[...]
    grad_w, gain1, shift1, flat, slope = first_grads(totals, moments, psmall_ref[...], stats_ref[...])
    for copy in live:
        copy.wait()
    for cz in range(NZ):
        for k in range(2):
            add(mine, (cz, k, x, slice(None), one), land2[0, cz, k])
            add(mine, (cz, y, k, slice(None), two), land2[1, cz, k])
    live = [
        send(mine.at[:, 1 - y, x, :, one], land3.at[0], over_y),
        send(mine.at[:, y, 1 - x, :, two], land3.at[1], over_x),
    ]
    point_gradient(d_ref, rel_ref, slots_ref, flat, slope, pg_o)
    for copy in live:
        copy.wait()
    for cz in range(NZ):
        add(mine, (cz, y, x, slice(None), one), land3[0, cz])
        add(mine, (cz, y, x, slice(None), two), land3[1, cz])
    live = [
        send(mine.at[lax.rem(z + k, NZ), y, x], land4.at[k - 1], near[k - 1]) for k in range(1, NZ)
    ]
    for copy in live:
        copy.wait()
    total = mine[z, y, x].astype(F32)
    for k in range(NZ - 1):
        total = total + land4[k].astype(F32)
    stage[...] = total

    full_rows = point_small_rows(grad_w, gain1, shift1, jnp.zeros((1, C2), F32), tot_ref[...], jnp.zeros((1, D), F32))
    rank = chip(z, y, x) * NC + core
    lane = lax.broadcasted_iota(jnp.int32, (1, 128), 1)
    own = jnp.zeros((1, 128), F32)
    for d in range(dp * NC):
        own = own + jnp.where(rank == d, piece_of(full_rows, 72 * d, 72), 0.0)
    pflat_o[0:1, :] = stage[12:13, PSMALL_AT : PSMALL_AT + 128] + own
    bflat_o[0:1, :] = stage[12:13, BSMALL_AT : BSMALL_AT + 128]
    for at, start, rows, cols, under in (
        (W3_AT, 9, 16, C3, 0), (W4_AT, 73, 16, D, 0), (W2_AT, 1, 4, C2, 12),
    ):
        for j in range(cols // 128):
            pflat_o[pl.ds(start + j, rows, stride=cols // 128), :] = stage[
                under : under + rows, at + 128 * j : at + 128 * j + 128
            ]
    start = 1
    for at, cols in rows_twelve():
        for j in range(cols // 128):
            bflat_o[pl.ds(start + j, 12, stride=cols // 128), :] = stage[
                0:12, at + 128 * j : at + 128 * j + 128
            ]
        start += 12 * cols // 128
    for b in range(3):
        for j in range(D // 128):
            at = WF2_AT + D * b + 128 * j
            bflat_o[pl.ds(start + 48 * b + j, 16, stride=3), :] = stage[:, at : at + 128]


def scatter_call(*args):
    dp = NZ * NY * NX
    count = args[7].shape[1]
    outs = shaped(((3, count), F32), ((PROWS, 128), F32), ((BROWS, 128), F32))
    return pl.pallas_call(
        scatter_kernel,
        out_shape=outs,
        in_specs=vmem(len(args)),
        out_specs=vmem(len(outs)),
        scratch_shapes=[
            pltpu.VMEM((NC, NZ, NY, NX, 16, WIDTH), BF16),
            pltpu.VMEM((16, WIDTH), F32),
            pltpu.VMEM((NZ, NY, NX, 16, WIDTH), BF16),
            pltpu.VMEM((2, NZ, 2, 16, HALF), BF16),
            pltpu.VMEM((2, NZ, 16, HALF), BF16),
            pltpu.VMEM((NZ - 1, 16, WIDTH), BF16),
        ]
        + sum_scratch(dp, (8, 128))
        + [pltpu.SemaphoreType.DMA((16,)), pltpu.SemaphoreType.DMA((16,))],
        compiler_params=params(collective_id=3, has_side_effects=True),
        name="scatter",
    )(*args)


def geometry_call(points, slots):
    outs = shaped(((8, points.shape[1]), BF16), ((8, 128), F32))
    return pl.pallas_call(
        geometry, out_shape=outs, in_specs=vmem(2), out_specs=vmem(2),
        compiler_params=params(), name="geometry",
    )(points, slots)


def gather_plain(points, slots, point_master, block_master, devices):
    rel, moments = geometry_call(points, slots)
    moments = lax.psum(moments, AXES)
    tables = []
    for master, layout in ((point_master, point_layout()), (block_master, block_layout())):
        offset = 0
        parts = []
        for segment, seg_len in zip(layout, segment_lengths(layout, devices)):
            piece = master[offset : offset + seg_len // devices].astype(BF16)
            offset += seg_len // devices
            parts.append(lax.all_gather(piece, AXES, axis=0, tiled=True))
        tables.append(parts)
    (ps, w2, w3, w4), (bs, wqkv, wo, wf1, wf2) = tables

    def rows_of(v, rows, used):
        v = v[:used].astype(F32).reshape(-1, 128)
        return jnp.concatenate([v, jnp.zeros((rows - v.shape[0], 128), F32)], axis=0)

    return (
        rel, moments, rows_of(ps, 24, 18 * 128), rows_of(bs, 32, 30 * 128),
        w2.reshape(C1, C2), w3.reshape(2 * C2, C3), w4.reshape(C3, D),
        wqkv.reshape(D, 3 * D), wo.reshape(D, D), wf1.reshape(D, FF), wf2.reshape(FF, D),
    )


def point_gradient_kernel(d_ref, rel_ref, slots_ref, table_ref, out_ref):
    flat = [table_ref[k : k + 1, 3:4] for k in range(3)]
    slope = [[table_ref[k : k + 1, j : j + 1] for j in range(3)] for k in range(3)]
    point_gradient(d_ref, rel_ref, slots_ref, flat, slope, out_ref)


def scatter_plain(
    devices, q, moments, psmall, stats, tot, small, d, rel, slots,
    gw2, top, h, corr, sv, gw4, gwqkv, gwo, gwf1, gwf2,
):
    q = lax.psum(q, AXES)
    grad_w, gain1, shift1, flat, slope = first_grads(q, moments, psmall, stats)
    table = jnp.concatenate([jnp.concatenate(slope[k] + [flat[k]], axis=1) for k in range(3)], axis=0)
    table = jnp.pad(table, ((0, 5), (0, 124)))
    point_grad = pl.pallas_call(
        point_gradient_kernel, out_shape=jax.ShapeDtypeStruct((3, d.shape[1]), F32),
        in_specs=vmem(4), out_specs=vmem(1)[0], compiler_params=params(), name="point_gradient",
    )(d, rel, slots, table)
    none = jnp.zeros((1, 128), F32)
    local = point_small_rows(
        [none] * 3, none, none, gw2[C1 : C1 + 1, :], jnp.zeros((8, C3), F32), small[6:7, 0:D]
    )
    known = point_small_rows(grad_w, gain1, shift1, jnp.zeros((1, C2), F32), tot, jnp.zeros((1, D), F32))
    w3 = jnp.concatenate([top, h * sv[0:1, :] - corr], axis=0)
    pieces = []
    for layout, tables in (
        (point_layout(), (local + known / devices, gw2[:C1], w3, gw4)),
        (block_layout(), (block_small_rows(small), gwqkv, gwo, gwf1, gwf2)),
    ):
        parts = []
        for values, seg_len in zip(tables, segment_lengths(layout, devices)):
            values = values.reshape(-1)
            values = jnp.concatenate([values, jnp.zeros((seg_len - values.shape[0],), F32)])
            parts.append(lax.psum_scatter(values, AXES, scatter_dimension=0, tiled=True))
        pieces.append(parts)
    return point_grad, pieces[0], pieces[1]


def adam_update(master, moment_one, moment_two, gradient, step_rates, decays):
    one_new = BETA_ONE * moment_one + (1.0 - BETA_ONE) * gradient
    two_new = BETA_TWO * moment_two + (1.0 - BETA_TWO) * gradient * gradient
    fix_one = 1.0 - BETA_ONE**STEP
    fix_two = 1.0 - BETA_TWO**STEP
    direction = one_new / fix_one / (jnp.sqrt(two_new / fix_two) + ADAM_EPS)
    master_new = master - step_rates * (direction + decays * master)
    return (master_new, one_new, two_new)


def flat_of(vector, small, rows):
    pad = jnp.zeros((128 - small,), F32)
    tail = jnp.zeros((rows * 128 - 128 - (vector.shape[0] - small),), F32)
    return jnp.concatenate([vector[:small], pad, vector[small:], tail]).reshape(rows, 128)


def on_device(
    points, point_count, centre_slot, cloud_length, cotangent, point_master, block_master,
    point_first, block_first, point_second, block_second,
):
    dp, fsdp = lax.axis_size("dp"), lax.axis_size("fsdp")
    devices = dp * fsdp
    own_rank = lax.axis_index(AXES)
    known = dp == NZ * NY * NX and fsdp == NC
    slots = jnp.repeat(jnp.stack([point_count, centre_slot]), GROUP, axis=1)
    if known:
        gathered = gather_call(
            points, slots, flat_of(point_master, 72, PROWS), flat_of(block_master, 120, BROWS)
        )
    else:
        gathered = gather_plain(points, slots, point_master, block_master, devices)
    rel, moments, psmall, bsmall, w2, w3, w4, wqkv, wo, wf1, wf2 = gathered
    ext, gp1, f, ft, gram, fs, cnt, g, fw, pooled, sums, stats, wd = first_call(rel, moments, psmall, w2, w3)
    gm, sv = third_call(dp, sums, g, stats, psmall)
    gp, pa, pg, pc = second_call(f, rel, w3, gm, sv)
    tokens_out, gw4, gwqkv, gwo, gwf1, gwf2, small, tok, tg, back = block_call(
        pa, pg, pc, cnt, cloud_length, cotangent, psmall, bsmall, sv, w4, wqkv, wo, wf1, wf2
    )
    tot, tok_low, kap, k, ws, top, corr = third_back_call(
        dp, back, tok, tg, fs, fw, gm, cnt, pooled, gram, w3, sv, stats
    )
    h, gw2, q, d = last_call(gp, f, ft, ext, gp1, rel, tok_low, kap, k, ws, w2, wd)
    grads = (
        q, moments, psmall, stats, tot, small, d, rel, slots,
        gw2, top, h, corr, sv, gw4, gwqkv, gwo, gwf1, gwf2,
    )
    if known:
        point_grad, pflat, bflat = scatter_call(*grads)
        pflat, bflat = pflat.reshape(-1), bflat.reshape(-1)
        block_small = bflat[:120]
        point_gradient_vec = jnp.concatenate([pflat[:72], pflat[128 : 128 + point_master.shape[0] - 72]])
        block_gradient = jnp.concatenate([block_small, bflat[128 : 128 + block_master.shape[0] - 120]])
    else:
        point_grad, point_parts, block_parts = scatter_plain(devices, *grads)
        block_small = block_parts[0]
        point_gradient_vec = jnp.concatenate(point_parts)
        block_gradient = jnp.concatenate(block_parts)
    point_rates, point_decays = shard_rates(point_layout(), devices, own_rank)
    block_rates, block_decays = shard_rates(block_layout(), devices, own_rank)
    point_new, point_one, point_two = adam_update(
        point_master, point_first, point_second, point_gradient_vec, point_rates, point_decays
    )
    block_new, block_one, block_two = adam_update(
        block_master, block_first, block_second, block_gradient, block_rates, block_decays
    )
    return (
        tokens_out, point_grad, point_new, block_new, point_one, block_one, point_two, block_two,
        point_new.astype(BF16), block_new.astype(BF16), block_small,
    )


def solution(mesh):
    split = P(AXES)
    return jax.shard_map(
        on_device,
        mesh=mesh,
        in_specs=(P(None, AXES), split, split, split, P(AXES, None)) + (split,) * 6,
        out_specs=(P(AXES, None), P(None, AXES)) + (split,) * 9,
        check_vma=False,
    )
```

```python
import functools
import math

import jax
import jax.numpy as jnp
from jax import lax
from jax.experimental import pallas as pl
from jax.experimental.pallas import tpu as pltpu
from jax.sharding import PartitionSpec as P

C1 = 128
C2 = 256
C3 = 512
D = 384
HEADS = 6
HEAD_DIM = 64
FF = 1536
GROUP = 32
PATCHES = 64
STEP = 10

EPS_NORM = 1e-05
BETA_ONE = 0.9
BETA_TWO = 0.95
ADAM_EPS = 1e-08
DECAY_RATE = 0.05
NEG_FILL = -1e30

F32 = jnp.float32
BF16 = jnp.bfloat16
AXES = ("dp", "fsdp")
MESH = pl.DeviceIdType.MESH
VMEM_LIMIT = 60 * 2**20
TILE = 2048
TOK = TILE // GROUP
SUB = 512
TB = 256
PAIR = 128

NZ, NY, NX, NC = 4, 2, 2, 2
W3_AT, W4_AT, QKV_AT, WO_AT, WF1_AT, WF2_AT, WIDTH = 0, 512, 896, 2048, 2432, 3968, 5120
W2_AT, PSMALL_AT, BSMALL_AT = 896, 1152, 1280
HALF = WIDTH // 2
PROWS, BROWS = 128, 440


def point_layout():
    return [
        [
            ("w1", (3, C1), 3.0 ** (-0.5)),
            ("bn1_gain", (C1,), 0.0),
            ("bn1_shift", (C1,), -1.0),
            ("b2", (C2,), -1.0),
            ("bn3_gain", (C3,), 0.0),
            ("bn3_shift", (C3,), -1.0),
            ("b4", (D,), -1.0),
        ],
        [("w2", (C1, C2), C1 ** (-0.5))],
        [("w3", (2 * C2, C3), (2 * C2) ** (-0.5))],
        [("w4", (C3, D), C3 ** (-0.5))],
    ]


def block_layout():
    return [
        [
            ("ln1_gain", (D,), 0.0),
            ("ln1_shift", (D,), -1.0),
            ("bo", (D,), -1.0),
            ("ln2_gain", (D,), 0.0),
            ("ln2_shift", (D,), -1.0),
            ("bf1", (FF,), -1.0),
            ("bf2", (D,), -1.0),
        ],
        [("wqkv", (D, 3 * D), D ** (-0.5))],
        [("wo", (D, D), 3.0 * D ** (-0.5))],
        [("wf1", (D, FF), D ** (-0.5))],
        [("wf2", (FF, D), FF ** (-0.5))],
    ]


def rate_for(spread):
    return 2.0 * spread if spread > 0.0 else 0.5 if spread == 0.0 else 0.6


def decay_for(spread):
    return DECAY_RATE if spread > 0.0 else 0.0


def segment_lengths(layout, devices):
    lengths_out = []
    for segment in layout:
        used_len = sum((math.prod(entry[1]) for entry in segment))
        lengths_out.append(-(-used_len // devices) * devices)
    return lengths_out


def shard_rates(layout, devices, own_rank):
    rate_parts = []
    decay_parts = []
    for segment, seg_len in zip(layout, segment_lengths(layout, devices)):
        piece_len = seg_len // devices
        position = own_rank * piece_len + jnp.arange(piece_len, dtype=jnp.int32)
        seg_rates = jnp.zeros((piece_len,), F32)
        seg_decays = jnp.zeros((piece_len,), F32)
        offset = 0
        for entry_label, entry_dims, spread in segment:
            extent = math.prod(entry_dims)
            inside = (position >= offset) & (position < offset + extent)
            seg_rates = jnp.where(inside, rate_for(spread), seg_rates)
            seg_decays = jnp.where(inside, decay_for(spread), seg_decays)
            offset += extent
        rate_parts.append(seg_rates)
        decay_parts.append(seg_decays)
    return (jnp.concatenate(rate_parts), jnp.concatenate(decay_parts))


def mm(a, b):
    return jnp.dot(a, b, preferred_element_type=F32)


def mm_tn(a, b):
    return lax.dot_general(a, b, (((0,), (0,)), ((), ())), preferred_element_type=F32)


def mm_nt(a, b):
    return lax.dot_general(a, b, (((1,), (1,)), ((), ())), preferred_element_type=F32)


def low(v):
    return v.astype(BF16)


def split_three(v):
    hi = low(v)
    rest = v - hi.astype(F32)
    mid = low(rest)
    return hi, mid, low(rest - mid.astype(F32))


def mm_exact(a, b):
    hi, mid, lo = split_three(a)
    return mm(hi, b) + (mm(mid, b) + mm(lo, b))


GELU_A = math.sqrt(2.0 / math.pi)
GELU_B = GELU_A * 0.044715


def gelu_pair(v):
    square = v * v
    t = jnp.tanh(v * (GELU_A + GELU_B * square))
    h = 0.5 + 0.5 * t
    g = v * h
    return g, h + (g - g * h) * (2.0 * GELU_A + 6.0 * GELU_B * square)


def patch_ones():
    i = lax.broadcasted_iota(jnp.int32, (256, 256), 0) // GROUP
    j = lax.broadcasted_iota(jnp.int32, (256, 256), 1) // GROUP
    return (i == j).astype(F32).astype(BF16)


def token_ones():
    t = lax.broadcasted_iota(jnp.int32, (TOK, TILE), 0)
    p = lax.broadcasted_iota(jnp.int32, (TOK, TILE), 1) // GROUP
    return (t == p).astype(F32).astype(BF16)


def patch_sum(rows, ones):
    return mm_exact(rows, ones)


def groups(dp):
    lower = math.gcd(dp, 4)
    return lower, dp // lower


def ring_peers(dp, upper_stage):
    lower, upper = groups(dp)
    at, core = lax.axis_index("dp"), lax.axis_index("fsdp")
    up, down = at // lower, lax.rem(at, lower)
    peers = []
    if upper_stage:
        for k in range(1, upper):
            peers.append((lax.rem(up + k, upper) * lower + down, core))
    else:
        for k in range(1, lower * NC):
            p = lax.rem(down * NC + core + k, lower * NC)
            peers.append((up * lower + p // NC, lax.rem(p, NC)))
    return peers


def greet(peers):
    barrier = pltpu.get_barrier_semaphore()
    for peer in peers:
        pl.semaphore_signal(barrier, inc=1, device_id=peer, device_id_type=MESH)
    return len(peers)


def greeted(count):
    pl.semaphore_wait(pltpu.get_barrier_semaphore(), count)


def sum_start(dp, upper_stage, acc, slots, send, recv):
    lower, upper = groups(dp)
    first = lower * NC - 1 if upper_stage else 0
    copies = []
    for k, peer in enumerate(ring_peers(dp, upper_stage)):
        copy = pltpu.make_async_remote_copy(
            src_ref=acc,
            dst_ref=slots.at[first + k],
            send_sem=send.at[first + k],
            recv_sem=recv.at[first + k],
            device_id=peer,
            device_id_type=MESH,
        )
        copy.start()
        copies.append(copy)
    return copies


def sum_finish(dp, upper_stage, acc, slots, copies):
    lower, upper = groups(dp)
    first = lower * NC - 1 if upper_stage else 0
    for copy in copies:
        copy.wait()
    total = acc[...]
    for k in range(len(copies)):
        total = total + slots[first + k]
    acc[...] = total


def sum_over_devices(dp, acc, slots, send, recv):
    for upper_stage in (False, True):
        copies = sum_start(dp, upper_stage, acc, slots, send, recv)
        sum_finish(dp, upper_stage, acc, slots, copies)


def sum_scratch(dp, shape):
    lower, upper = groups(dp)
    count = lower * NC - 1 + upper - 1
    return [
        pltpu.VMEM(shape, F32),
        pltpu.VMEM((count,) + shape, F32),
        pltpu.SemaphoreType.DMA((count,)),
        pltpu.SemaphoreType.DMA((count,)),
    ]


def all_peers(dp):
    return ring_peers(dp, False) + ring_peers(dp, True)


def vmem(count):
    return [pl.BlockSpec(memory_space=pltpu.VMEM)] * count


def shaped(*items):
    return [jax.ShapeDtypeStruct(s, t) for s, t in items]


def params(**more):
    return pltpu.CompilerParams(vmem_limit_bytes=VMEM_LIMIT, **more)


def geometry(points_ref, slots_ref, rel_ref, moment_ref):
    ones = patch_ones()
    moment_ref[...] = jnp.zeros_like(moment_ref)
    lane = lax.rem(lax.broadcasted_iota(jnp.int32, (1, 256), 1), GROUP)

    def piece(i, carry):
        at = pl.ds(pl.multiple_of(i * 256, 256), 256)
        pts = points_ref[:, at]
        valid = (lane < slots_ref[0:1, at]).astype(F32)
        pick = (lane == slots_ref[1:2, at]).astype(F32)
        relative = (pts - patch_sum(pts * pick, ones)) * valid
        rows = low(jnp.concatenate([relative, valid, relative, valid], axis=0))
        rel_ref[:, at] = rows
        moment_ref[:, 0:8] += mm_nt(rows, rows)
        return carry

    lax.fori_loop(0, points_ref.shape[1] // 256, piece, 0, unroll=8)


def prepare_one(moments, small):
    n = moments[3:4, 3:4]
    w = [small[k : k + 1, :] for k in range(3)]
    gain, shift = small[3:4, :], small[4:5, :]
    mean = sum(w[k] * moments[k : k + 1, 3:4] for k in range(3)) / n
    square = jnp.zeros_like(mean)
    for j in range(3):
        for k in range(3):
            square = square + w[j] * w[k] * moments[j : j + 1, k : k + 1]
    inverse = lax.rsqrt(square / n - mean * mean + EPS_NORM)
    scale = inverse * gain
    scaled = [wk * scale for wk in w]
    offset = shift - mean * scale
    high = [low(v) for v in scaled + [offset]]
    rest = [low(v - h.astype(F32)) for v, h in zip(scaled + [offset], high)]
    forward = jnp.concatenate(high + rest, axis=0)
    zero = jnp.zeros((1, C1), BF16)
    backward = jnp.concatenate(high[:3] + [zero] + rest[:3] + [zero], axis=0)
    stats = jnp.concatenate(
        [mean, inverse, jnp.broadcast_to(n, (1, C1)), scale, jnp.zeros((4, C1), F32)], axis=0
    )
    return forward, backward, stats


def flat_rows(pieces, length, rows):
    lane = lax.broadcasted_iota(jnp.int32, (1, 128), 1)
    out = [jnp.zeros((1, 128), F32) for _ in range(rows)]
    for r in range(pieces.shape[0]):
        row = jnp.where(lane < length, pieces[r : r + 1, :], 0.0)
        at = length * r
        row = pltpu.roll(row, at % 128, 1) if at % 128 else row
        first = at // 128
        out[first] = out[first] + jnp.where(lane >= at % 128, row, 0.0)
        if at % 128 + length > 128:
            out[first + 1] = out[first + 1] + jnp.where(lane < at % 128, row, 0.0)
    return jnp.concatenate(out, axis=0)


def piece_of(rows, at, length):
    lane = lax.broadcasted_iota(jnp.int32, (1, 128), 1)
    first, shift = at // 128, at % 128
    row = rows[first : first + 1, :]
    if shift:
        row = pltpu.roll(row, 128 - shift, 1)
        if shift + length > 128:
            other = pltpu.roll(rows[first + 1 : first + 2, :], 128 - shift, 1)
            row = jnp.where(lane < 128 - shift, row, other)
    return jnp.where(lane < length, row, 0.0)


def where_am_i():
    at = lax.axis_index("dp")
    return at // (NY * NX), lax.rem(at // NX, NY), lax.rem(at, NX), lax.axis_index("fsdp")


def chip(z, y, x):
    return (z * NY + y) * NX + x


def rows_twelve():
    return [(QKV_AT, 3 * D), (WO_AT, D), (WF1_AT, FF)]


def first_kernel(
    rel_ref, moment_ref, psmall_ref, w2_ref, w3_ref,
    ext_o, gp_o, f_o, ft_o, gram_o, fs_o, cnt_o, g_o, fw_o, pooled_o, sums_o, stats_o, wd_o,
    e_s, wn_s, w2_s,
):
    step = pl.program_id(0)

    @pl.when(step == 0)
    def _():
        gram_o[...] = jnp.zeros_like(gram_o)
        e_s[...] = token_ones()
        small = psmall_ref[...]
        forward, backward, stats = prepare_one(moment_ref[:, 0:8], small)
        wn_s[...] = forward
        wd_o[...] = backward
        stats_o[...] = stats
        w2_s[0:C1, :] = w2_ref[...]
        b2 = jnp.concatenate([small[5:6, :], small[6:7, :]], axis=1)
        w2_s[C1:, :] = low(jnp.concatenate([b2, jnp.zeros((15, C2), F32)], axis=0))

    rel = rel_ref[...]
    valid = rel[3:4, :].astype(F32)
    for j in range(TILE // 256):
        at = slice(256 * j, 256 * j + 256)
        g, gp = gelu_pair(mm_tn(wn_s[...], rel[:, at]))
        ext_o[0:C1, at] = low(g * valid[:, at])
        gp_o[:, at] = low(gp * valid[:, at])
    ext_o[C1:, :] = jnp.concatenate([rel[3:4], jnp.zeros((15, TILE), BF16)], axis=0)
    ext = ext_o[...]
    ft = low(mm_tn(w2_s[...], ext))
    f = low(mm_tn(ext, w2_s[...]))
    ft_o[...] = ft
    f_o[...] = f
    gram_o[...] += mm(ft, f)
    at = pl.ds(pl.multiple_of(step * TOK, TOK), TOK)
    fs_o[at, :] = mm(e_s[...], f)
    cnt_o[at, :] = jnp.broadcast_to(mm_nt(e_s[...], rel)[:, 3:4], (TOK, 128))

    @pl.when(step == pl.num_programs(0) - 1)
    def _():
        count = cnt_o[:, 0:1]
        fs = fs_o[...]
        pooled = low(fs / count)
        pooled_o[...] = pooled
        g = mm(pooled, w3_ref[0:C2, :])
        g_o[...] = g
        lower = w3_ref[C2:, :]
        fw = mm_exact(fs, lower)
        fw_o[...] = fw
        one = jnp.sum(fw + count * g, axis=0, keepdims=True)
        two = jnp.sum(mm_exact(gram_o[...], lower) * lower.astype(F32), axis=0, keepdims=True)
        two = two + jnp.sum(g * (2.0 * fw + count * g), axis=0, keepdims=True)
        sums_o[...] = jnp.concatenate([one, two, jnp.zeros((6, C3), F32)], axis=0)


def first_call(rel, moments, psmall, w2, w3):
    count = rel.shape[1]
    tokens = count // GROUP
    full = lambda *s: pl.BlockSpec(s, lambda i: (0, 0))
    cols = lambda r: pl.BlockSpec((r, TILE), lambda i: (0, i))
    return pl.pallas_call(
        first_kernel,
        grid=(count // TILE,),
        in_specs=[cols(8), full(8, 128), full(24, 128), full(C1, C2), full(2 * C2, C3)],
        out_specs=[
            cols(C1 + 16), cols(C1), pl.BlockSpec((TILE, C2), lambda i: (i, 0)), cols(C2),
            full(C2, C2), full(tokens, C2), full(tokens, 128), full(tokens, C3), full(tokens, C3),
            full(tokens, C2), full(8, C3), full(8, C1), full(8, C1),
        ],
        out_shape=shaped(
            ((C1 + 16, count), BF16), ((C1, count), BF16), ((count, C2), BF16), ((C2, count), BF16),
            ((C2, C2), F32), ((tokens, C2), F32), ((tokens, 128), F32), ((tokens, C3), F32),
            ((tokens, C3), F32), ((tokens, C2), BF16), ((8, C3), F32), ((8, C1), F32), ((8, C1), BF16),
        ),
        scratch_shapes=[pltpu.VMEM((TOK, TILE), BF16), pltpu.VMEM((8, C1), BF16), pltpu.VMEM((C1 + 16, C2), BF16)],
        compiler_params=params(),
        name="first",
    )(rel, moments, psmall, w2, w3)


def third_kernel(dp, sums_ref, g_ref, stats_ref, psmall_ref, gm_o, sv_o, acc, slots, send, recv):
    count = greet(all_peers(dp))
    acc[...] = sums_ref[...]
    greeted(count)
    sum_over_devices(dp, acc, slots, send, recv)
    n = stats_ref[2:3, 0:1]
    mean = acc[0:1, :] / n
    inverse = lax.rsqrt(acc[1:2, :] / n - mean * mean + EPS_NORM)
    gain = jnp.concatenate([psmall_ref[k : k + 1, :] for k in range(7, 11)], axis=1)
    shift = jnp.concatenate([psmall_ref[k : k + 1, :] for k in range(11, 15)], axis=1)
    gm_o[...] = g_ref[...] - mean
    sv_o[...] = jnp.concatenate(
        [inverse * gain, shift, mean, inverse, jnp.zeros((4, C3), F32)], axis=0
    )


def third_call(dp, sums, g, stats, psmall):
    return pl.pallas_call(
        functools.partial(third_kernel, dp),
        out_shape=shaped((g.shape, F32), ((8, C3), F32)),
        in_specs=vmem(4),
        out_specs=vmem(2),
        scratch_shapes=sum_scratch(dp, (8, C3)),
        compiler_params=params(collective_id=1, has_side_effects=True),
        name="third",
    )(sums, g, stats, psmall)


def second_kernel(f_ref, rel_ref, w3_ref, gm_ref, sv_ref, gp_o, pa_o, pg_o, pc_o, e_s):
    @pl.when(pl.program_id(0) == 0)
    def _():
        e_s[...] = token_ones()

    mask = e_s[...] * rel_ref[3:4, :]
    lower = w3_ref[C2:, :]
    scale, shift = low(sv_ref[0:1, :]), low(sv_ref[1:2, :])
    tokens = SUB // GROUP
    for j in range(TILE // SUB):
        at, ts = slice(SUB * j, SUB * j + SUB), slice(tokens * j, tokens * j + tokens)
        c = mm(f_ref[at, :], lower).reshape(tokens, GROUP, C3) + gm_ref[ts, :][:, None, :]
        c = low(c)
        g, gp = gelu_pair(c * scale[None] + shift[None])
        gc = (gp * c).reshape(SUB, C3)
        gp = gp.reshape(SUB, C3)
        gp_o[at, :] = gp
        m = mask[ts, at]
        pa_o[ts, :] = mm(m, g.reshape(SUB, C3))
        pg_o[ts, :] = mm(m, gp)
        pc_o[ts, :] = mm(m, gc)


def second_call(f, rel, w3, gm, sv):
    count = f.shape[0]
    tokens = count // GROUP
    full = lambda *s: pl.BlockSpec(s, lambda i: (0, 0))
    rows = lambda r, c: pl.BlockSpec((r, c), lambda i: (i, 0))
    return pl.pallas_call(
        second_kernel,
        grid=(count // TILE,),
        in_specs=[rows(TILE, C2), pl.BlockSpec((8, TILE), lambda i: (0, i)), full(2 * C2, C3), rows(TOK, C3), full(8, C3)],
        out_specs=[rows(TILE, C3), rows(TOK, C3), rows(TOK, C3), rows(TOK, C3)],
        out_shape=shaped(((count, C3), BF16), ((tokens, C3), F32), ((tokens, C3), F32), ((tokens, C3), F32)),
        scratch_shapes=[pltpu.VMEM((TOK, TILE), BF16)],
        compiler_params=params(),
        name="second",
    )(f, rel, w3, gm, sv)


def first_tile(rel, wn, w2, ext_ref, gp_ref):
    valid = rel[3:4, :].astype(F32)
    for j in range(TILE // 256):
        at = slice(256 * j, 256 * j + 256)
        g, gp = gelu_pair(mm_tn(wn, rel[:, at]))
        ext_ref[0:C1, at] = low(g * valid[:, at])
        gp_ref[:, at] = low(gp * valid[:, at])
    ext_ref[C1:, :] = jnp.concatenate([rel[3:4], jnp.zeros((15, TILE), BF16)], axis=0)
    ext = ext_ref[...]
    return low(mm_tn(ext, w2)), low(mm_tn(w2, ext))


def first_tokens(cnt_ref, fs_ref, gram_ref, w3_ref, pooled_o, g_o, fw_o):
    count = cnt_ref[:, 0:1]
    fs = fs_ref[...]
    pooled = low(fs / count)
    pooled_o[...] = pooled
    g = mm(pooled, w3_ref[0:C2, :])
    g_o[...] = g
    lower = w3_ref[C2:, :]
    fw = mm_exact(fs, lower)
    fw_o[...] = fw
    one = jnp.sum(fw + count * g, axis=0, keepdims=True)
    two = jnp.sum(mm_exact(gram_ref[...], lower) * lower.astype(F32), axis=0, keepdims=True)
    two = two + jnp.sum(g * (2.0 * fw + count * g), axis=0, keepdims=True)
    return jnp.concatenate([one, two, jnp.zeros((6, C3), F32)], axis=0)


def third_vectors(totals, n, psmall_ref):
    mean = totals[0:1, :] / n
    inverse = lax.rsqrt(totals[1:2, :] / n - mean * mean + EPS_NORM)
    gain = jnp.concatenate([psmall_ref[k : k + 1, :] for k in range(7, 11)], axis=1)
    shift = jnp.concatenate([psmall_ref[k : k + 1, :] for k in range(11, 15)], axis=1)
    return jnp.concatenate([inverse * gain, shift, mean, inverse, jnp.zeros((4, C3), F32)], axis=0)


def second_tile(f_at, mask, lower, gm_at, sv_ref, gp_o, pa_o, pg_o, pc_o, first):
    scale, shift = low(sv_ref[0:1, :]), low(sv_ref[1:2, :])
    tokens = SUB // GROUP
    for j in range(TILE // SUB):
        at, ts = slice(SUB * j, SUB * j + SUB), slice(tokens * j, tokens * j + tokens)
        to = pl.ds(pl.multiple_of(first + tokens * j, tokens), tokens)
        c = mm(f_at(SUB * j, SUB), lower).reshape(tokens, GROUP, C3) + gm_at(to)[:, None, :]
        c = low(c)
        g, gp = gelu_pair(c * scale[None] + shift[None])
        gc = (gp * c).reshape(SUB, C3)
        gp = gp.reshape(SUB, C3)
        gp_o[at, :] = gp
        m = mask[ts, at]
        pa_o[to, :] = mm(m, g.reshape(SUB, C3))
        pg_o[to, :] = mm(m, gp)
        pc_o[to, :] = mm(m, gc)


class Gather:
    def __init__(self, blocks, send, recv, base):
        self.blocks, self.sems, self.base = blocks, (send, recv), base
        z, y, x, core = where_am_i()
        half = blocks.shape[-1] // 2
        one, two = pl.ds(0, half), pl.ds(half, half)
        every = slice(None)
        near = [(chip(lax.rem(z + k, NZ), y, x), core) for k in range(1, NZ)]
        over_y, over_x, twin = (chip(z, 1 - y, x), core), (chip(z, y, 1 - x), core), (chip(z, y, x), 1 - core)
        self.stages = [
            [((z, y, x, core), peer) for peer in near],
            [((every, y, x, core, every, one), over_y), ((every, y, x, core, every, two), over_x)],
            [((every, every, x, core, every, one), over_x), ((every, y, every, core, every, two), over_y)],
            [],
        ]
        self.inner = [
            [],
            [((every, y, x, core), twin)],
            [((every, 1 - y, x, core, every, one), twin), ((every, y, 1 - x, core, every, two), twin)],
            [((every, every, 1 - x, core, every, one), twin), ((every, 1 - y, every, core, every, two), twin)],
        ]

    def copies(self, stage, inner):
        table = self.inner if inner else self.stages
        k = self.base + (7 if inner else 0) + sum(len(s) for s in table[:stage])
        out = []
        for i, (index, peer) in enumerate(table[stage]):
            view = self.blocks.at[index]
            out.append(
                pltpu.make_async_remote_copy(
                    src_ref=view, dst_ref=view, send_sem=self.sems[0].at[k + i], recv_sem=self.sems[1].at[k + i],
                    device_id=peer, device_id_type=MESH,
                )
            )
        return out

    def advance(self, stage):
        if stage > 0:
            for copy in self.copies(stage - 1, False):
                copy.wait()
        if stage < 4:
            for copy in self.copies(stage, False) + self.copies(stage, True):
                copy.start()
        else:
            for inner_stage in range(4):
                for copy in self.copies(inner_stage, True):
                    copy.wait()


GATHER_SEMS = 12
REST = [("w4", 0, D), ("wqkv", 384, 3 * D), ("wo", 1536, D), ("wf1", 1920, FF), ("wf2", 3456, 3 * D)]
REST_WIDTH = 4608


def forward_kernel(
    points_ref, slots_ref, pflat, bflat,
    rel_o, moment_o, psmall_o, bsmall_o, w2_o, w3_o, w4_o, wqkv_o, wo_o, wf1_o, wf2_o,
    ext_o, gp1_o, f_o, ft_o, gram_o, fs_o, cnt_o, gm_o, fw_o, pooled_o, sv_o, stats_o, wd_o,
    gp_o, pa_o, pg_o, pc_o,
    tiny, rest, stage, wide, f_s, e_s, wn_s, w2_s,
    acc, sums, ssend, srecv, acc3, sums3, ssend3, srecv3, tsend, trecv, gsend, grecv, fsem, three, flat2,
):
    step = pl.program_id(0)
    tiles = pl.num_programs(0) // 2
    z, y, x, core = where_am_i()
    dp = NZ * NY * NX
    plane = (y * NX + x) * NC + core
    gather_w3 = Gather(three, gsend, grecv, 0)
    gather_rest = Gather(rest, gsend, grecv, GATHER_SEMS)
    f_copy = pltpu.make_async_copy(f_s, f_o, fsem)

    @pl.when(step == 0)
    def _():
        count = greet(all_peers(dp) + [(chip(z, 1 - y, x), core), (chip(z, y, 1 - x), core), (chip(z, y, x), 1 - core)])
        rows = [pflat[1:9, :], pflat[0:1, :], bflat[0:1, :], jnp.zeros((6, 128), F32)]
        tiny[z, plane] = low(jnp.concatenate(rows, axis=0))
        for j in range(C3 // 128):
            three[z, y, x, core, :, 128 * j : 128 * j + 128] = low(pflat[pl.ds(9 + j, 16, stride=C3 // 128), :])
        stage[...] = jnp.zeros_like(stage)
        for j in range(D // 128):
            stage[:, 128 * j : 128 * j + 128] = pflat[pl.ds(73 + j, 16, stride=D // 128), :]
        start = 1
        for name, at, cols in REST[1:4]:
            for j in range(cols // 128):
                stage[0:12, at + 128 * j : at + 128 * j + 128] = bflat[pl.ds(start + j, 12, stride=cols // 128), :]
            start += 12 * cols // 128
        for b in range(3):
            for j in range(D // 128):
                to = REST[4][1] + D * b + 128 * j
                stage[:, to : to + 128] = bflat[pl.ds(start + 48 * b + j, 16, stride=3), :]
        rest[z, y, x, core] = low(stage[...])
        geometry(points_ref, slots_ref, rel_o, acc)
        e_s[...] = token_ones()
        gram_o[...] = jnp.zeros_like(gram_o)
        greeted(count)

        def tiny_copies(upper_stage):
            view = tiny.at[z] if upper_stage else tiny.at[z, plane]
            first = 7 if upper_stage else 0
            return [
                pltpu.make_async_remote_copy(
                    src_ref=view, dst_ref=view, send_sem=tsend.at[first + k], recv_sem=trecv.at[first + k],
                    device_id=peer, device_id_type=MESH,
                )
                for k, peer in enumerate(ring_peers(dp, upper_stage))
            ]

        for upper_stage in (False, True):
            copies = tiny_copies(upper_stage)
            small = sum_start(dp, upper_stage, acc, sums, ssend, srecv)
            for copy in copies:
                copy.start()
            sum_finish(dp, upper_stage, acc, sums, small)
            for copy in copies:
                copy.wait()
        gather_w3.advance(0)
        moment_o[...] = acc[...]
        psmall, bsmall = [], []
        for d in range(dp * NC):
            rows = tiny[d // 8, d % 8].astype(F32)
            flat2[8 * d : 8 * d + 8, :] = rows[0:8, :]
            psmall.append(rows[8:9, :])
            bsmall.append(rows[9:10, :])
        psmall_o[0:18, :] = flat_rows(jnp.concatenate(psmall, axis=0), 72, 18)
        bsmall_o[0:30, :] = flat_rows(jnp.concatenate(bsmall, axis=0), 120, 30)
        for j in range(2):
            w2_o[:, 128 * j : 128 * j + 128] = low(flat2[pl.ds(j, C1, stride=2), :])
        small = psmall_o[...]
        forward, backward, stats = prepare_one(acc[:, 0:8], small)
        wn_s[...] = forward
        wd_o[...] = backward
        stats_o[...] = stats
        w2_s[0:C1, :] = w2_o[...]
        b2 = jnp.concatenate([small[5:6, :], small[6:7, :]], axis=1)
        w2_s[C1:, :] = low(jnp.concatenate([b2, jnp.zeros((15, C2), F32)], axis=0))

    for at_step, work in (
        (1, lambda: gather_rest.advance(0)),
        (2, lambda: gather_w3.advance(1)),
        (3, lambda: gather_w3.advance(2)),
        (5, lambda: gather_w3.advance(3)),
        (6, lambda: gather_rest.advance(1)),
        (7, lambda: gather_w3.advance(4)),
        (9, lambda: gather_rest.advance(2)),
        (12, lambda: gather_rest.advance(3)),
    ):
        pl.when(step == at_step)(work)

    at_points = pl.multiple_of(lax.rem(step, tiles) * TILE, TILE)
    rel = rel_o[:, pl.ds(at_points, TILE)]
    first = pl.multiple_of(lax.rem(step, tiles) * TOK, TOK)

    @pl.when(step < tiles)
    def _():
        f, ft = first_tile(rel, wn_s[...], w2_s[...], ext_o, gp1_o)
        ft_o[...] = ft
        f_s[pl.ds(at_points, TILE), :] = f
        gram_o[...] += mm(ft, f)
        fs_o[pl.ds(first, TOK), :] = mm(e_s[...], f)
        cnt_o[pl.ds(first, TOK), :] = jnp.broadcast_to(mm_nt(e_s[...], rel)[:, 3:4], (TOK, 128))

    @pl.when(step == tiles)
    def _():
        f_copy.start()
        for d in range(dp * NC):
            w3_o[16 * d : 16 * d + 16, :] = three[d // 8, d // 4 % 2, d // 2 % 2, d % 2]
        acc3[...] = first_tokens(cnt_o, fs_o, gram_o, w3_o, pooled_o, gm_o, fw_o)
        sum_over_devices(dp, acc3, sums3, ssend3, srecv3)
        sv_o[...] = third_vectors(acc3[...], stats_o[2:3, 0:1], psmall_o)
        gm_o[...] = gm_o[...] - sv_o[2:3, :]

    @pl.when(step >= tiles)
    def _():
        mask = e_s[...] * rel[3:4, :]
        second_tile(
            lambda start, size: f_s[pl.ds(pl.multiple_of(at_points + start, SUB), size), :],
            mask, w3_o[C2:, :], lambda to: gm_o[to, :], sv_o, gp_o, pa_o, pg_o, pc_o, first,
        )

    @pl.when(step == 2 * tiles - 1)
    def _():
        f_copy.wait()
        gather_rest.advance(4)
        for d in range(dp * NC):
            block = rest.at[d // 8, d // 4 % 2, d // 2 % 2, d % 2]
            w4_o[16 * d : 16 * d + 16, :] = block[:, 0:D]
            for b in range(3):
                at = 48 * d + 16 * b
                wf2_o[at : at + 16, :] = block[:, 3456 + D * b : 3456 + D * b + D]
            wide[12 * d : 12 * d + 12, :] = block[:, 384:3456].astype(F32)[0:12, :]
        for out, at, cols in ((wqkv_o, 0, 3 * D), (wo_o, 1152, D), (wf1_o, 1536, FF)):
            out[...] = low(wide[:, at : at + cols])


def forward_call(points, slots, pflat, bflat):
    dp = NZ * NY * NX
    count = points.shape[1]
    tokens, tiles = count // GROUP, count // TILE
    single = dict(pipeline_mode=pl.Buffered(1))
    full = lambda *s: pl.BlockSpec(s, lambda i: (0, 0), **single)
    early = lambda r: pl.BlockSpec((r, TILE), lambda i: (0, jnp.minimum(i, tiles - 1)))
    outs = [
        (full(8, count), (8, count), BF16), (full(8, 128), (8, 128), F32), (full(24, 128), (24, 128), F32),
        (full(32, 128), (32, 128), F32), (full(C1, C2), (C1, C2), BF16), (full(2 * C2, C3), (2 * C2, C3), BF16),
        (full(C3, D), (C3, D), BF16), (full(D, 3 * D), (D, 3 * D), BF16), (full(D, D), (D, D), BF16),
        (full(D, FF), (D, FF), BF16), (full(FF, D), (FF, D), BF16),
        (early(C1 + 16), (C1 + 16, count), BF16), (early(C1), (C1, count), BF16),
        (pl.BlockSpec(memory_space=pl.ANY), (count, C2), BF16), (early(C2), (C2, count), BF16),
        (full(C2, C2), (C2, C2), F32), (full(tokens, C2), (tokens, C2), F32), (full(tokens, 128), (tokens, 128), F32),
        (full(tokens, C3), (tokens, C3), F32), (full(tokens, C3), (tokens, C3), F32),
        (full(tokens, C2), (tokens, C2), BF16), (full(8, C3), (8, C3), F32), (full(8, C1), (8, C1), F32),
        (full(8, C1), (8, C1), BF16),
        (pl.BlockSpec((TILE, C3), lambda i: (jnp.maximum(i - tiles, 0), 0)), (count, C3), BF16),
        (full(tokens, C3), (tokens, C3), F32), (full(tokens, C3), (tokens, C3), F32), (full(tokens, C3), (tokens, C3), F32),
    ]
    return pl.pallas_call(
        forward_kernel,
        grid=(2 * tiles,),
        in_specs=[full(3, count), full(2, count), full(PROWS, 128), full(BROWS, 128)],
        out_specs=[o[0] for o in outs],
        out_shape=shaped(*[o[1:] for o in outs]),
        scratch_shapes=[
            pltpu.VMEM((NZ, 2 * NY * NX, 16, 128), BF16),
            pltpu.VMEM((NZ, NY, NX, NC, 16, REST_WIDTH), BF16),
            pltpu.VMEM((16, REST_WIDTH), F32),
            pltpu.VMEM((384, 3456 - 384), F32),
            pltpu.VMEM((count, C2), BF16),
            pltpu.VMEM((TOK, TILE), BF16), pltpu.VMEM((8, C1), BF16), pltpu.VMEM((C1 + 16, C2), BF16),
        ]
        + sum_scratch(dp, (8, 128))
        + sum_scratch(dp, (8, C3))
        + [pltpu.SemaphoreType.DMA((10,)), pltpu.SemaphoreType.DMA((10,))]
        + [pltpu.SemaphoreType.DMA((2 * GATHER_SEMS,)), pltpu.SemaphoreType.DMA((2 * GATHER_SEMS,))]
        + [pltpu.SemaphoreType.DMA, pltpu.VMEM((NZ, NY, NX, NC, 16, C3), BF16), pltpu.VMEM((256, 128), F32)],
        compiler_params=params(collective_id=0, has_side_effects=True),
        name="forward",
    )(points, slots, pflat, bflat)


def wide_row(ref, first, rows):
    return jnp.concatenate([ref[k : k + 1, :] for k in range(first, first + rows)], axis=1)


def layer_norm(v, gain, shift):
    centred = v - jnp.mean(v, -1, keepdims=True)
    inverse = lax.rsqrt(jnp.mean(centred * centred, -1, keepdims=True) + EPS_NORM)
    unit = centred * inverse
    return unit, inverse, low(unit * gain + shift)


def norm_back(d_unit, unit, inverse):
    return inverse * (
        d_unit - jnp.mean(d_unit, -1, keepdims=True) - unit * jnp.mean(d_unit * unit, -1, keepdims=True)
    )


def col_sum(v):
    return jnp.sum(v, axis=0, keepdims=True)


def block_kernel(
    pa_ref, pg_ref, pc_ref, cnt_ref, len_ref, cot_ref, psmall_ref, bsmall_ref, sv_ref,
    w4_ref, wqkv_ref, wo_ref, wf1_ref, wf2_ref,
    out_o, gw4_o, gwqkv_o, gwo_o, gwf1_o, gwf2_o, small_o, tok_o, tg_o, back_o,
    qkv_s, mixed_s, soft_s, dmix_s, dqkv_s,
):
    step = pl.program_id(0)

    @pl.when(step == 0)
    def _():
        for ref in (gw4_o, gwqkv_o, gwo_o, gwf1_o, gwf2_o, small_o, back_o):
            ref[...] = jnp.zeros_like(ref)

    count = cnt_ref[:, 0:1]
    scale = HEAD_DIM ** (-0.5)
    b4 = wide_row(psmall_ref, 15, 3)
    ln1_gain, ln1_shift, bo = wide_row(bsmall_ref, 0, 3), wide_row(bsmall_ref, 3, 3), wide_row(bsmall_ref, 6, 3)
    ln2_gain, ln2_shift = wide_row(bsmall_ref, 9, 3), wide_row(bsmall_ref, 12, 3)
    bf1, bf2 = wide_row(bsmall_ref, 15, 12), wide_row(bsmall_ref, 27, 3)

    act = low(pa_ref[...] / count)
    x_zero = mm(act, w4_ref[...]) + b4
    unit_a, inv_a, normed_a = layer_norm(x_zero, ln1_gain, ln1_shift)
    qkv_s[...] = low(mm(normed_a, wqkv_ref[...]))

    row_cloud = lax.broadcasted_iota(jnp.int32, (PAIR, PAIR), 0) // PATCHES
    col = lax.broadcasted_iota(jnp.int32, (PAIR, PAIR), 1)
    left = lax.broadcasted_iota(jnp.int32, (1, 128), 1) < HEAD_DIM
    zero = jnp.zeros((1, 1), BF16)

    def halves(v):
        return jnp.where(left, v, zero), jnp.where(left, zero, v)

    tiles = TB // PAIR
    for s in range(tiles):
        first = (step * tiles + s) * 2
        visible = (row_cloud == col // PATCHES) & (
            lax.rem(col, PATCHES) < jnp.where(col < PATCHES, len_ref[first], len_ref[first + 1])
        )
        rows = slice(PAIR * s, PAIR * s + PAIR)
        for p in range(HEADS // 2):
            at = 128 * p
            q = qkv_s[rows, at : at + 128]
            k = qkv_s[rows, D + at : D + at + 128]
            v = qkv_s[rows, 2 * D + at : 2 * D + at + 128]
            mixed = []
            for a, q_half in enumerate(halves(q)):
                score = jnp.where(visible, mm_nt(q_half, k) * scale, NEG_FILL)
                raised = jnp.exp(score - jnp.max(score, -1, keepdims=True))
                soft = raised / jnp.sum(raised, -1, keepdims=True)
                soft_s[(s * (HEADS // 2) + p) * 2 + a] = soft
                mixed.append(mm(low(soft), v))
            mixed_s[rows, at : at + 128] = low(jnp.where(left, mixed[0], mixed[1]))

    mixed_low = mixed_s[...]
    x_one = x_zero + mm(mixed_low, wo_ref[...]) + bo
    unit_b, inv_b, normed_b = layer_norm(x_one, ln2_gain, ln2_shift)
    hidden, d_hidden = gelu_pair(mm(normed_b, wf1_ref[...]) + bf1)
    hidden = low(hidden)
    out_o[...] = x_one + mm(hidden, wf2_ref[...]) + bf2

    cot = cot_ref[...]
    grad = low(cot)
    gwf2_o[...] += mm_tn(hidden, grad)
    d_pre = mm_nt(grad, wf2_ref[...]) * d_hidden
    d_pre_low = low(d_pre)
    gwf1_o[...] += mm_tn(normed_b, d_pre_low)
    d_normed_b = mm_nt(d_pre_low, wf1_ref[...])
    d_x_one = cot + norm_back(d_normed_b * ln2_gain, unit_b, inv_b)
    d_x_low = low(d_x_one)
    gwo_o[...] += mm_tn(mixed_low, d_x_low)
    dmix_s[...] = low(mm_nt(d_x_low, wo_ref[...]))

    for s in range(tiles):
        rows = slice(PAIR * s, PAIR * s + PAIR)
        for p in range(HEADS // 2):
            at = 128 * p
            q = qkv_s[rows, at : at + 128]
            k = qkv_s[rows, D + at : D + at + 128]
            v = qkv_s[rows, 2 * D + at : 2 * D + at + 128]
            dm = dmix_s[rows, at : at + 128]
            d_q, d_k, d_v = [], [], []
            for a, dm_half in enumerate(halves(dm)):
                soft = soft_s[(s * (HEADS // 2) + p) * 2 + a]
                d_soft = mm_nt(dm_half, v)
                d_v.append(mm_tn(low(soft), dm))
                d_score = low(soft * (d_soft - jnp.sum(soft * d_soft, -1, keepdims=True)))
                d_q.append(mm(d_score, k))
                d_k.append(mm_tn(d_score, q))
            dqkv_s[rows, at : at + 128] = low(jnp.where(left, d_q[0], d_q[1]) * scale)
            dqkv_s[rows, D + at : D + at + 128] = low(jnp.where(left, d_k[0], d_k[1]) * scale)
            dqkv_s[rows, 2 * D + at : 2 * D + at + 128] = low(jnp.where(left, d_v[0], d_v[1]))

    d_qkv = dqkv_s[...]
    gwqkv_o[...] += mm_tn(normed_a, d_qkv)
    d_normed_a = mm_nt(d_qkv, wqkv_ref[...])
    d_x_zero = d_x_one + norm_back(d_normed_a * ln1_gain, unit_a, inv_a)
    d_x_low = low(d_x_zero)
    gw4_o[...] += mm_tn(act, d_x_low)
    token = mm_nt(d_x_low, w4_ref[...]) / count
    tok_o[...] = token
    grouped = token * pg_ref[...]
    tg_o[...] = grouped
    back_o[0:1, :] += col_sum(grouped)
    back_o[1:2, :] += col_sum(token * pc_ref[...]) * sv_ref[3:4, :]
    narrow = [
        col_sum(d_normed_a * unit_a), col_sum(d_normed_a), col_sum(d_x_one),
        col_sum(d_normed_b * unit_b), col_sum(d_normed_b), col_sum(cot), col_sum(d_x_zero),
    ]
    for k, row in enumerate(narrow):
        small_o[k : k + 1, 0:D] += row
    small_o[7:8, :] += col_sum(d_pre)


def block_call(pa, pg, pc, cnt, length, cot, psmall, bsmall, sv, w4, wqkv, wo, wf1, wf2):
    tokens = pa.shape[0]
    full = lambda *s: pl.BlockSpec(s, lambda i: (0, 0))
    rows = lambda c: pl.BlockSpec((TB, c), lambda i: (i, 0))
    return pl.pallas_call(
        block_kernel,
        grid=(tokens // TB,),
        in_specs=[
            rows(C3), rows(C3), rows(C3), rows(128), pl.BlockSpec(memory_space=pltpu.SMEM), rows(D),
            full(24, 128), full(32, 128), full(8, C3),
            full(C3, D), full(D, 3 * D), full(D, D), full(D, FF), full(FF, D),
        ],
        out_specs=[
            rows(D), full(C3, D), full(D, 3 * D), full(D, D), full(D, FF), full(FF, D), full(8, FF),
            rows(C3), rows(C3), full(8, C3),
        ],
        out_shape=shaped(
            ((tokens, D), F32), ((C3, D), F32), ((D, 3 * D), F32), ((D, D), F32), ((D, FF), F32),
            ((FF, D), F32), ((8, FF), F32), ((tokens, C3), F32), ((tokens, C3), F32), ((8, C3), F32),
        ),
        scratch_shapes=[
            pltpu.VMEM((TB, 3 * D), BF16), pltpu.VMEM((TB, D), BF16),
            pltpu.VMEM((TB // PAIR * HEADS, PAIR, PAIR), F32), pltpu.VMEM((TB, D), BF16),
            pltpu.VMEM((TB, 3 * D), BF16),
        ],
        compiler_params=params(),
        name="block",
    )(pa, pg, pc, cnt, length, cot, psmall, bsmall, sv, w4, wqkv, wo, wf1, wf2)


def third_back_kernel(
    dp, back_ref, tok_ref, tg_ref, fs_ref, fw_ref, gm_ref, cnt_ref, pooled_ref, gram_ref, w3_ref, sv_ref, stats_ref,
    tot_o, tok_o, kap_o, k_o, ws_o, top_o, corr_o, acc, slots, send, recv,
):
    greeting = greet(all_peers(dp))
    acc[...] = back_ref[...]
    tok_o[...] = low(tok_ref[...])
    lower = w3_ref[C2:, :].astype(F32)
    gain = sv_ref[0:1, :]
    ws_o[...] = low(lower * gain)
    greeted(greeting)
    sum_over_devices(dp, acc, slots, send, recv)
    tot_o[...] = acc[...]
    n = stats_ref[2:3, 0:1]
    alpha = gain * acc[0:1, :] / n
    beta = gain * acc[1:2, :] * sv_ref[3:4, :] / n
    count = cnt_ref[:, 0:1]
    gm = gm_ref[...]
    per_token = low(gain * tg_ref[...] - (count * alpha + beta * (fw_ref[...] + count * gm)))
    d_pooled = mm_nt(per_token, w3_ref[0:C2, :])
    shifted = low(alpha + beta * gm)
    kap_o[...] = d_pooled / count - mm_nt(shifted, w3_ref[C2:, :])
    k_o[...] = low(-mm_nt(low(lower * beta), w3_ref[C2:, :]))
    top_o[...] = mm_tn(pooled_ref[...], per_token)
    corr_o[...] = mm_tn(low(fs_ref[...]), shifted) + beta * mm(low(gram_ref[...]), w3_ref[C2:, :])


def third_back_call(dp, back, tok, tg, fs, fw, gm, cnt, pooled, gram, w3, sv, stats):
    tokens = tok.shape[0]
    outs = shaped(
        ((8, C3), F32), ((tokens, C3), BF16), ((tokens, C2), F32), ((C2, C2), BF16), ((C2, C3), BF16),
        ((C2, C3), F32), ((C2, C3), F32),
    )
    return pl.pallas_call(
        functools.partial(third_back_kernel, dp),
        out_shape=outs,
        in_specs=vmem(12),
        out_specs=vmem(len(outs)),
        scratch_shapes=sum_scratch(dp, (8, C3)),
        compiler_params=params(collective_id=2, has_side_effects=True),
        name="third_back",
    )(back, tok, tg, fs, fw, gm, cnt, pooled, gram, w3, sv, stats)


def last_kernel(
    gp_ref, f_ref, ft_ref, ext_ref, gp1_ref, rel_ref, tok_ref, kap_ref, k_ref, ws_ref, w2_ref, wd_ref,
    h_o, gw2_o, q_o, d_o, dn_s,
):
    @pl.when(pl.program_id(0) == 0)
    def _():
        for ref in (h_o, gw2_o, q_o):
            ref[...] = jnp.zeros_like(ref)

    tokens = SUB // GROUP
    for j in range(TILE // SUB):
        at, ts = slice(SUB * j, SUB * j + SUB), slice(tokens * j, tokens * j + tokens)
        gp = gp_ref[at, :].reshape(tokens, GROUP, C3)
        dn_s[at, :] = (gp * tok_ref[ts, :][:, None, :]).reshape(SUB, C3)
    dn = dn_s[...]
    h_o[...] += mm(ft_ref[...], dn)
    d_feat = mm_nt(dn, ws_ref[...]) + mm(f_ref[...], k_ref[...])
    d_feat = (d_feat.reshape(TOK, GROUP, C2) + kap_ref[...][:, None, :]).reshape(TILE, C2)
    d_feat = low(d_feat)
    gw2_o[...] += mm(ext_ref[...], d_feat)
    d_one = low(mm_nt(w2_ref[...], d_feat) * gp1_ref[...].astype(F32))
    d_o[...] = mm(wd_ref[...], d_one)
    q_o[...] += mm_nt(rel_ref[...], d_one)


def last_call(gp, f, ft, ext, gp1, rel, tok, kap, k, ws, w2, wd):
    count = f.shape[0]
    full = lambda *s: pl.BlockSpec(s, lambda i: (0, 0))
    rows = lambda r, c: pl.BlockSpec((r, c), lambda i: (i, 0))
    cols = lambda r: pl.BlockSpec((r, TILE), lambda i: (0, i))
    return pl.pallas_call(
        last_kernel,
        grid=(count // TILE,),
        in_specs=[
            rows(TILE, C3), rows(TILE, C2), cols(C2), cols(C1 + 16), cols(C1), cols(8), rows(TOK, C3), rows(TOK, C2),
            full(C2, C2), full(C2, C3), full(C1, C2), full(8, C1),
        ],
        out_specs=[full(C2, C3), full(C1 + 16, C2), full(8, C1), cols(8)],
        out_shape=shaped(((C2, C3), F32), ((C1 + 16, C2), F32), ((8, C1), F32), ((8, count), F32)),
        scratch_shapes=[pltpu.VMEM((TILE, C3), BF16)],
        compiler_params=params(),
        name="last",
    )(gp, f, ft, ext, gp1, rel, tok, kap, k, ws, w2, wd)


def first_grads(q, moments, psmall, stats):
    mean, inverse, n, scale = stats[0:1], stats[1:2], stats[2:3], stats[3:4]
    w = [psmall[k : k + 1, :] for k in range(3)]
    one = q[3:4, :]
    two = inverse * (sum(w[k] * q[k : k + 1, :] for k in range(3)) - mean * one)
    grad_w = []
    for k in range(3):
        along = sum(w[j] * moments[k : k + 1, j : j + 1] for j in range(3)) - mean * moments[k : k + 1, 3:4]
        grad_w.append(scale * (q[k : k + 1, :] - (one * moments[k : k + 1, 3:4] + two * inverse * along) / n))
    flat = [
        jnp.sum(scale * w[k] * (one - two * inverse * mean) / n, axis=1, keepdims=True) for k in range(3)
    ]
    slope = [
        [jnp.sum(scale * w[k] * two * inverse * w[j] / n, axis=1, keepdims=True) for j in range(3)]
        for k in range(3)
    ]
    return grad_w, two, one, flat, slope


def point_gradient(d_ref, rel_ref, slots_ref, flat, slope, out_ref):
    ones = patch_ones()
    lane = lax.rem(lax.broadcasted_iota(jnp.int32, (1, 256), 1), GROUP)
    base = jnp.concatenate(flat, axis=0)
    columns = [jnp.concatenate([slope[k][j] for k in range(3)], axis=0) for j in range(3)]

    def piece(i, carry):
        at = pl.ds(pl.multiple_of(i * 256, 256), 256)
        rel = rel_ref[:, at].astype(F32)
        d = d_ref[:, at]
        out = d[0:3] + d[4:7] - rel[3:4] * base
        for j in range(3):
            out = out - columns[j] * rel[j : j + 1]
        pick = (lane == slots_ref[1:2, at]).astype(F32)
        out_ref[:, at] = out - pick * patch_sum(out, ones)
        return carry

    lax.fori_loop(0, d_ref.shape[1] // 256, piece, 0, unroll=8)


def point_small_rows(grad_w, gain1, shift1, b2, tot, b4):
    rows = list(grad_w) + [gain1, shift1]
    rows += [b2[:, 128 * k : 128 * k + 128] for k in range(2)]
    rows += [tot[1:2, 128 * k : 128 * k + 128] for k in range(4)]
    rows += [tot[0:1, 128 * k : 128 * k + 128] for k in range(4)]
    rows += [b4[:, 128 * k : 128 * k + 128] for k in range(3)]
    return jnp.concatenate(rows, axis=0)


def block_small_rows(small_ref):
    rows = [small_ref[k : k + 1, 128 * j : 128 * j + 128] for k in range(5) for j in range(3)]
    rows += [small_ref[7:8, 128 * j : 128 * j + 128] for j in range(12)]
    rows += [small_ref[5:6, 128 * j : 128 * j + 128] for j in range(3)]
    return jnp.concatenate(rows, axis=0)


def scatter_kernel(
    q_ref, moment_ref, psmall_ref, stats_ref, tot_ref, small_ref, d_ref, rel_ref, slots_ref,
    gw2_ref, top_ref, h_ref, corr_ref, sv_ref, gw4_ref, gwqkv_ref, gwo_ref, gwf1_ref, gwf2_ref,
    pg_o, pflat_o, bflat_o,
    blocks, stage, land1, land2, land3, land4, acc, slots, ssend, srecv, gsend, grecv,
):
    z, y, x, core = where_am_i()
    dp = NZ * NY * NX
    near = [(chip(lax.rem(z + k, NZ), y, x), core) for k in range(1, NZ)]
    over_y, over_x, twin = (chip(z, 1 - y, x), core), (chip(z, y, 1 - x), core), (chip(z, y, x), 1 - core)
    count = greet(all_peers(dp) + near + [over_y, over_x, twin])
    acc[...] = q_ref[...]
    greeted(count)
    small = sum_start(dp, False, acc, slots, ssend, srecv)

    none = jnp.zeros((1, 128), F32)
    prow = point_small_rows(
        [none] * 3, none, none, gw2_ref[C1 : C1 + 1, :], jnp.zeros((8, C3), F32), small_ref[6:7, 0:D]
    )
    brow = block_small_rows(small_ref)
    stage[...] = jnp.zeros_like(stage)
    gain = sv_ref[0:1, :]
    for d in range(dp * NC):
        cz, cy, cx, cc = d // 8, d // 4 % 2, d // 2 % 2, d % 2
        if d < 16:
            stage[:, W3_AT : W3_AT + C3] = top_ref[16 * d : 16 * d + 16, :]
        else:
            rows = slice(16 * (d - 16), 16 * (d - 16) + 16)
            stage[:, W3_AT : W3_AT + C3] = h_ref[rows, :] * gain - corr_ref[rows, :]
        stage[:, W4_AT : W4_AT + D] = gw4_ref[16 * d : 16 * d + 16, :]
        stage[0:12, QKV_AT : QKV_AT + 3 * D] = gwqkv_ref[12 * d : 12 * d + 12, :]
        stage[0:12, WO_AT : WO_AT + D] = gwo_ref[12 * d : 12 * d + 12, :]
        stage[0:12, WF1_AT : WF1_AT + FF] = gwf1_ref[12 * d : 12 * d + 12, :]
        stage[12:16, W2_AT : W2_AT + C2] = gw2_ref[4 * d : 4 * d + 4, :]
        stage[12:13, PSMALL_AT : PSMALL_AT + 128] = piece_of(prow, 72 * d, 72)
        stage[12:13, BSMALL_AT : BSMALL_AT + 128] = piece_of(brow, 120 * d, 120)
        for b in range(3):
            at = 48 * d + 16 * b
            stage[:, WF2_AT + D * b : WF2_AT + D * b + D] = gwf2_ref[at : at + 16, :]
        blocks[cc, cz, cy, cx] = low(stage[...])

    used = [0]

    def send(src, dst, peer):
        k = used[0]
        used[0] += 1
        copy = pltpu.make_async_remote_copy(
            src_ref=src, dst_ref=dst, send_sem=gsend.at[k], recv_sem=grecv.at[k],
            device_id=peer, device_id_type=MESH,
        )
        copy.start()
        return copy

    one, two = pl.ds(0, HALF), pl.ds(HALF, HALF)
    mine = blocks.at[core]
    live = [send(blocks.at[1 - core], land1, twin)]
    sum_finish(dp, False, acc, slots, small)
    small = sum_start(dp, True, acc, slots, ssend, srecv)
    for copy in live:
        copy.wait()

    def add(dst, index, landed):
        dst[index] = low(dst[index].astype(F32) + landed.astype(F32))

    for cz in range(NZ):
        for cy in range(NY):
            for cx in range(NX):
                add(mine, (cz, cy, cx), land1[cz, cy, cx])
    live = [
        send(mine.at[:, :, 1 - x, :, one], land2.at[0], over_x),
        send(mine.at[:, 1 - y, :, :, two], land2.at[1], over_y),
    ]
    sum_finish(dp, True, acc, slots, small)
    totals = acc[...]
    moments = moment_ref[...]
    grad_w, gain1, shift1, flat, slope = first_grads(totals, moments, psmall_ref[...], stats_ref[...])
    for copy in live:
        copy.wait()
    for cz in range(NZ):
        for k in range(2):
            add(mine, (cz, k, x, slice(None), one), land2[0, cz, k])
            add(mine, (cz, y, k, slice(None), two), land2[1, cz, k])
    live = [
        send(mine.at[:, 1 - y, x, :, one], land3.at[0], over_y),
        send(mine.at[:, y, 1 - x, :, two], land3.at[1], over_x),
    ]
    point_gradient(d_ref, rel_ref, slots_ref, flat, slope, pg_o)
    for copy in live:
        copy.wait()
    for cz in range(NZ):
        add(mine, (cz, y, x, slice(None), one), land3[0, cz])
        add(mine, (cz, y, x, slice(None), two), land3[1, cz])
    live = [
        send(mine.at[lax.rem(z + k, NZ), y, x], land4.at[k - 1], near[k - 1]) for k in range(1, NZ)
    ]
    for copy in live:
        copy.wait()
    total = mine[z, y, x].astype(F32)
    for k in range(NZ - 1):
        total = total + land4[k].astype(F32)
    stage[...] = total

    full_rows = point_small_rows(grad_w, gain1, shift1, jnp.zeros((1, C2), F32), tot_ref[...], jnp.zeros((1, D), F32))
    rank = chip(z, y, x) * NC + core
    lane = lax.broadcasted_iota(jnp.int32, (1, 128), 1)
    own = jnp.zeros((1, 128), F32)
    for d in range(dp * NC):
        own = own + jnp.where(rank == d, piece_of(full_rows, 72 * d, 72), 0.0)
    pflat_o[0:1, :] = stage[12:13, PSMALL_AT : PSMALL_AT + 128] + own
    bflat_o[0:1, :] = stage[12:13, BSMALL_AT : BSMALL_AT + 128]
    for at, start, rows, cols, under in (
        (W3_AT, 9, 16, C3, 0), (W4_AT, 73, 16, D, 0), (W2_AT, 1, 4, C2, 12),
    ):
        for j in range(cols // 128):
            pflat_o[pl.ds(start + j, rows, stride=cols // 128), :] = stage[
                under : under + rows, at + 128 * j : at + 128 * j + 128
            ]
    start = 1
    for at, cols in rows_twelve():
        for j in range(cols // 128):
            bflat_o[pl.ds(start + j, 12, stride=cols // 128), :] = stage[
                0:12, at + 128 * j : at + 128 * j + 128
            ]
        start += 12 * cols // 128
    for b in range(3):
        for j in range(D // 128):
            at = WF2_AT + D * b + 128 * j
            bflat_o[pl.ds(start + 48 * b + j, 16, stride=3), :] = stage[:, at : at + 128]


def scatter_call(*args):
    dp = NZ * NY * NX
    count = args[7].shape[1]
    outs = shaped(((3, count), F32), ((PROWS, 128), F32), ((BROWS, 128), F32))
    return pl.pallas_call(
        scatter_kernel,
        out_shape=outs,
        in_specs=vmem(len(args)),
        out_specs=vmem(len(outs)),
        scratch_shapes=[
            pltpu.VMEM((NC, NZ, NY, NX, 16, WIDTH), BF16),
            pltpu.VMEM((16, WIDTH), F32),
            pltpu.VMEM((NZ, NY, NX, 16, WIDTH), BF16),
            pltpu.VMEM((2, NZ, 2, 16, HALF), BF16),
            pltpu.VMEM((2, NZ, 16, HALF), BF16),
            pltpu.VMEM((NZ - 1, 16, WIDTH), BF16),
        ]
        + sum_scratch(dp, (8, 128))
        + [pltpu.SemaphoreType.DMA((16,)), pltpu.SemaphoreType.DMA((16,))],
        compiler_params=params(collective_id=3, has_side_effects=True),
        name="scatter",
    )(*args)


def geometry_call(points, slots):
    outs = shaped(((8, points.shape[1]), BF16), ((8, 128), F32))
    return pl.pallas_call(
        geometry, out_shape=outs, in_specs=vmem(2), out_specs=vmem(2),
        compiler_params=params(), name="geometry",
    )(points, slots)


def gather_plain(points, slots, point_master, block_master, devices):
    rel, moments = geometry_call(points, slots)
    moments = lax.psum(moments, AXES)
    tables = []
    for master, layout in ((point_master, point_layout()), (block_master, block_layout())):
        offset = 0
        parts = []
        for segment, seg_len in zip(layout, segment_lengths(layout, devices)):
            piece = master[offset : offset + seg_len // devices].astype(BF16)
            offset += seg_len // devices
            parts.append(lax.all_gather(piece, AXES, axis=0, tiled=True))
        tables.append(parts)
    (ps, w2, w3, w4), (bs, wqkv, wo, wf1, wf2) = tables

    def rows_of(v, rows, used):
        v = v[:used].astype(F32).reshape(-1, 128)
        return jnp.concatenate([v, jnp.zeros((rows - v.shape[0], 128), F32)], axis=0)

    return (
        rel, moments, rows_of(ps, 24, 18 * 128), rows_of(bs, 32, 30 * 128),
        w2.reshape(C1, C2), w3.reshape(2 * C2, C3), w4.reshape(C3, D),
        wqkv.reshape(D, 3 * D), wo.reshape(D, D), wf1.reshape(D, FF), wf2.reshape(FF, D),
    )


def point_gradient_kernel(d_ref, rel_ref, slots_ref, table_ref, out_ref):
    flat = [table_ref[k : k + 1, 3:4] for k in range(3)]
    slope = [[table_ref[k : k + 1, j : j + 1] for j in range(3)] for k in range(3)]
    point_gradient(d_ref, rel_ref, slots_ref, flat, slope, out_ref)


def scatter_plain(
    devices, q, moments, psmall, stats, tot, small, d, rel, slots,
    gw2, top, h, corr, sv, gw4, gwqkv, gwo, gwf1, gwf2,
):
    q = lax.psum(q, AXES)
    grad_w, gain1, shift1, flat, slope = first_grads(q, moments, psmall, stats)
    table = jnp.concatenate([jnp.concatenate(slope[k] + [flat[k]], axis=1) for k in range(3)], axis=0)
    table = jnp.pad(table, ((0, 5), (0, 124)))
    point_grad = pl.pallas_call(
        point_gradient_kernel, out_shape=jax.ShapeDtypeStruct((3, d.shape[1]), F32),
        in_specs=vmem(4), out_specs=vmem(1)[0], compiler_params=params(), name="point_gradient",
    )(d, rel, slots, table)
    none = jnp.zeros((1, 128), F32)
    local = point_small_rows(
        [none] * 3, none, none, gw2[C1 : C1 + 1, :], jnp.zeros((8, C3), F32), small[6:7, 0:D]
    )
    known = point_small_rows(grad_w, gain1, shift1, jnp.zeros((1, C2), F32), tot, jnp.zeros((1, D), F32))
    w3 = jnp.concatenate([top, h * sv[0:1, :] - corr], axis=0)
    pieces = []
    for layout, tables in (
        (point_layout(), (local + known / devices, gw2[:C1], w3, gw4)),
        (block_layout(), (block_small_rows(small), gwqkv, gwo, gwf1, gwf2)),
    ):
        parts = []
        for values, seg_len in zip(tables, segment_lengths(layout, devices)):
            values = values.reshape(-1)
            values = jnp.concatenate([values, jnp.zeros((seg_len - values.shape[0],), F32)])
            parts.append(lax.psum_scatter(values, AXES, scatter_dimension=0, tiled=True))
        pieces.append(parts)
    return point_grad, pieces[0], pieces[1]


def adam_update(master, moment_one, moment_two, gradient, step_rates, decays):
    one_new = BETA_ONE * moment_one + (1.0 - BETA_ONE) * gradient
    two_new = BETA_TWO * moment_two + (1.0 - BETA_TWO) * gradient * gradient
    fix_one = 1.0 - BETA_ONE**STEP
    fix_two = 1.0 - BETA_TWO**STEP
    direction = one_new / fix_one / (jnp.sqrt(two_new / fix_two) + ADAM_EPS)
    master_new = master - step_rates * (direction + decays * master)
    return (master_new, one_new, two_new)


def flat_of(vector, small, rows):
    pad = jnp.zeros((128 - small,), F32)
    tail = jnp.zeros((rows * 128 - 128 - (vector.shape[0] - small),), F32)
    return jnp.concatenate([vector[:small], pad, vector[small:], tail]).reshape(rows, 128)


def on_device(
    points, point_count, centre_slot, cloud_length, cotangent, point_master, block_master,
    point_first, block_first, point_second, block_second,
):
    dp, fsdp = lax.axis_size("dp"), lax.axis_size("fsdp")
    devices = dp * fsdp
    own_rank = lax.axis_index(AXES)
    known = dp == NZ * NY * NX and fsdp == NC
    slots = jnp.repeat(jnp.stack([point_count, centre_slot]), GROUP, axis=1)
    if known:
        (
            rel, moments, psmall, bsmall, w2, w3, w4, wqkv, wo, wf1, wf2, ext, gp1, f, ft,
            gram, fs, cnt, gm, fw, pooled, sv, stats, wd, gp, pa, pg, pc,
        ) = forward_call(points, slots, flat_of(point_master, 72, PROWS), flat_of(block_master, 120, BROWS))
    else:
        rel, moments, psmall, bsmall, w2, w3, w4, wqkv, wo, wf1, wf2 = gather_plain(
            points, slots, point_master, block_master, devices
        )
        ext, gp1, f, ft, gram, fs, cnt, g, fw, pooled, sums, stats, wd = first_call(rel, moments, psmall, w2, w3)
        gm, sv = third_call(dp, sums, g, stats, psmall)
        gp, pa, pg, pc = second_call(f, rel, w3, gm, sv)
    tokens_out, gw4, gwqkv, gwo, gwf1, gwf2, small, tok, tg, back = block_call(
        pa, pg, pc, cnt, cloud_length, cotangent, psmall, bsmall, sv, w4, wqkv, wo, wf1, wf2
    )
    tot, tok_low, kap, k, ws, top, corr = third_back_call(
        dp, back, tok, tg, fs, fw, gm, cnt, pooled, gram, w3, sv, stats
    )
    h, gw2, q, d = last_call(gp, f, ft, ext, gp1, rel, tok_low, kap, k, ws, w2, wd)
    grads = (
        q, moments, psmall, stats, tot, small, d, rel, slots,
        gw2, top, h, corr, sv, gw4, gwqkv, gwo, gwf1, gwf2,
    )
    if known:
        point_grad, pflat, bflat = scatter_call(*grads)
        pflat, bflat = pflat.reshape(-1), bflat.reshape(-1)
        block_small = bflat[:120]
        point_gradient_vec = jnp.concatenate([pflat[:72], pflat[128 : 128 + point_master.shape[0] - 72]])
        block_gradient = jnp.concatenate([block_small, bflat[128 : 128 + block_master.shape[0] - 120]])
    else:
        point_grad, point_parts, block_parts = scatter_plain(devices, *grads)
        block_small = block_parts[0]
        point_gradient_vec = jnp.concatenate(point_parts)
        block_gradient = jnp.concatenate(block_parts)
    point_rates, point_decays = shard_rates(point_layout(), devices, own_rank)
    block_rates, block_decays = shard_rates(block_layout(), devices, own_rank)
    point_new, point_one, point_two = adam_update(
        point_master, point_first, point_second, point_gradient_vec, point_rates, point_decays
    )
    block_new, block_one, block_two = adam_update(
        block_master, block_first, block_second, block_gradient, block_rates, block_decays
    )
    return (
        tokens_out, point_grad, point_new, block_new, point_one, block_one, point_two, block_two,
        point_new.astype(BF16), block_new.astype(BF16), block_small,
    )


def solution(mesh):
    split = P(AXES)
    return jax.shard_map(
        on_device,
        mesh=mesh,
        in_specs=(P(None, AXES), split, split, split, P(AXES, None)) + (split,) * 6,
        out_specs=(P(AXES, None), P(None, AXES)) + (split,) * 9,
        check_vma=False,
    )
```

```python
import functools
import math

import jax
import jax.numpy as jnp
from jax import lax
from jax.experimental import pallas as pl
from jax.experimental.pallas import tpu as pltpu
from jax.sharding import PartitionSpec as P

C1 = 128
C2 = 256
C3 = 512
D = 384
HEADS = 6
HEAD_DIM = 64
FF = 1536
GROUP = 32
PATCHES = 64
STEP = 10

EPS_NORM = 1e-05
BETA_ONE = 0.9
BETA_TWO = 0.95
ADAM_EPS = 1e-08
DECAY_RATE = 0.05
NEG_FILL = -1e30

F32 = jnp.float32
BF16 = jnp.bfloat16
AXES = ("dp", "fsdp")
MESH = pl.DeviceIdType.MESH
VMEM_LIMIT = 60 * 2**20
TILE = 2048
TOK = TILE // GROUP
SUB = 512
TB = 256
PAIR = 128

NZ, NY, NX, NC = 4, 2, 2, 2
W3_AT, W4_AT, QKV_AT, WO_AT, WF1_AT, WF2_AT, WIDTH = 0, 512, 896, 2048, 2432, 3968, 5120
W2_AT, PSMALL_AT, BSMALL_AT = 896, 1152, 1280
HALF = WIDTH // 2
PROWS, BROWS = 128, 440


def point_layout():
    return [
        [
            ("w1", (3, C1), 3.0 ** (-0.5)),
            ("bn1_gain", (C1,), 0.0),
            ("bn1_shift", (C1,), -1.0),
            ("b2", (C2,), -1.0),
            ("bn3_gain", (C3,), 0.0),
            ("bn3_shift", (C3,), -1.0),
            ("b4", (D,), -1.0),
        ],
        [("w2", (C1, C2), C1 ** (-0.5))],
        [("w3", (2 * C2, C3), (2 * C2) ** (-0.5))],
        [("w4", (C3, D), C3 ** (-0.5))],
    ]


def block_layout():
    return [
        [
            ("ln1_gain", (D,), 0.0),
            ("ln1_shift", (D,), -1.0),
            ("bo", (D,), -1.0),
            ("ln2_gain", (D,), 0.0),
            ("ln2_shift", (D,), -1.0),
            ("bf1", (FF,), -1.0),
            ("bf2", (D,), -1.0),
        ],
        [("wqkv", (D, 3 * D), D ** (-0.5))],
        [("wo", (D, D), 3.0 * D ** (-0.5))],
        [("wf1", (D, FF), D ** (-0.5))],
        [("wf2", (FF, D), FF ** (-0.5))],
    ]


def rate_for(spread):
    return 2.0 * spread if spread > 0.0 else 0.5 if spread == 0.0 else 0.6


def decay_for(spread):
    return DECAY_RATE if spread > 0.0 else 0.0


def segment_lengths(layout, devices):
    lengths_out = []
    for segment in layout:
        used_len = sum((math.prod(entry[1]) for entry in segment))
        lengths_out.append(-(-used_len // devices) * devices)
    return lengths_out


def shard_rates(layout, devices, own_rank):
    rate_parts = []
    decay_parts = []
    for segment, seg_len in zip(layout, segment_lengths(layout, devices)):
        piece_len = seg_len // devices
        position = own_rank * piece_len + jnp.arange(piece_len, dtype=jnp.int32)
        seg_rates = jnp.zeros((piece_len,), F32)
        seg_decays = jnp.zeros((piece_len,), F32)
        offset = 0
        for entry_label, entry_dims, spread in segment:
            extent = math.prod(entry_dims)
            inside = (position >= offset) & (position < offset + extent)
            seg_rates = jnp.where(inside, rate_for(spread), seg_rates)
            seg_decays = jnp.where(inside, decay_for(spread), seg_decays)
            offset += extent
        rate_parts.append(seg_rates)
        decay_parts.append(seg_decays)
    return (jnp.concatenate(rate_parts), jnp.concatenate(decay_parts))


def mm(a, b):
    return jnp.dot(a, b, preferred_element_type=F32)


def mm_tn(a, b):
    return lax.dot_general(a, b, (((0,), (0,)), ((), ())), preferred_element_type=F32)


def mm_nt(a, b):
    return lax.dot_general(a, b, (((1,), (1,)), ((), ())), preferred_element_type=F32)


def low(v):
    return v.astype(BF16)


def split_three(v):
    hi = low(v)
    rest = v - hi.astype(F32)
    mid = low(rest)
    return hi, mid, low(rest - mid.astype(F32))


def mm_exact(a, b):
    hi, mid, lo = split_three(a)
    return mm(hi, b) + (mm(mid, b) + mm(lo, b))


GELU_A = math.sqrt(2.0 / math.pi)
GELU_B = GELU_A * 0.044715


def gelu_pair(v):
    square = v * v
    t = jnp.tanh(v * (GELU_A + GELU_B * square))
    h = 0.5 + 0.5 * t
    g = v * h
    return g, h + (g - g * h) * (2.0 * GELU_A + 6.0 * GELU_B * square)


def patch_ones():
    i = lax.broadcasted_iota(jnp.int32, (256, 256), 0) // GROUP
    j = lax.broadcasted_iota(jnp.int32, (256, 256), 1) // GROUP
    return (i == j).astype(F32).astype(BF16)


def token_ones():
    t = lax.broadcasted_iota(jnp.int32, (TOK, TILE), 0)
    p = lax.broadcasted_iota(jnp.int32, (TOK, TILE), 1) // GROUP
    return (t == p).astype(F32).astype(BF16)


def patch_sum(rows, ones):
    return mm_exact(rows, ones)


def groups(dp):
    lower = math.gcd(dp, 4)
    return lower, dp // lower


def ring_peers(dp, upper_stage):
    lower, upper = groups(dp)
    at, core = lax.axis_index("dp"), lax.axis_index("fsdp")
    up, down = at // lower, lax.rem(at, lower)
    peers = []
    if upper_stage:
        for k in range(1, upper):
            peers.append((lax.rem(up + k, upper) * lower + down, core))
    else:
        for k in range(1, lower * NC):
            p = lax.rem(down * NC + core + k, lower * NC)
            peers.append((up * lower + p // NC, lax.rem(p, NC)))
    return peers


def greet(peers):
    barrier = pltpu.get_barrier_semaphore()
    for peer in peers:
        pl.semaphore_signal(barrier, inc=1, device_id=peer, device_id_type=MESH)
    return len(peers)


def greeted(count):
    pl.semaphore_wait(pltpu.get_barrier_semaphore(), count)


def sum_start(dp, upper_stage, acc, slots, send, recv):
    lower, upper = groups(dp)
    first = lower * NC - 1 if upper_stage else 0
    copies = []
    for k, peer in enumerate(ring_peers(dp, upper_stage)):
        copy = pltpu.make_async_remote_copy(
            src_ref=acc,
            dst_ref=slots.at[first + k],
            send_sem=send.at[first + k],
            recv_sem=recv.at[first + k],
            device_id=peer,
            device_id_type=MESH,
        )
        copy.start()
        copies.append(copy)
    return copies


def sum_finish(dp, upper_stage, acc, slots, copies):
    lower, upper = groups(dp)
    first = lower * NC - 1 if upper_stage else 0
    for copy in copies:
        copy.wait()
    total = acc[...]
    for k in range(len(copies)):
        total = total + slots[first + k]
    acc[...] = total


def sum_over_devices(dp, acc, slots, send, recv):
    for upper_stage in (False, True):
        copies = sum_start(dp, upper_stage, acc, slots, send, recv)
        sum_finish(dp, upper_stage, acc, slots, copies)


def sum_scratch(dp, shape):
    lower, upper = groups(dp)
    count = lower * NC - 1 + upper - 1
    return [
        pltpu.VMEM(shape, F32),
        pltpu.VMEM((count,) + shape, F32),
        pltpu.SemaphoreType.DMA((count,)),
        pltpu.SemaphoreType.DMA((count,)),
    ]


def as_rows(*vectors):
    return jnp.concatenate(
        [v[:, 128 * k : 128 * k + 128] for v in vectors for k in range(v.shape[1] // 128)], axis=0
    )


def as_vector(rows, first, count):
    return jnp.concatenate([rows[k : k + 1, :] for k in range(first, first + count)], axis=1)


def all_peers(dp):
    return ring_peers(dp, False) + ring_peers(dp, True)


def vmem(count):
    return [pl.BlockSpec(memory_space=pltpu.VMEM)] * count


def shaped(*items):
    return [jax.ShapeDtypeStruct(s, t) for s, t in items]


def params(**more):
    return pltpu.CompilerParams(vmem_limit_bytes=VMEM_LIMIT, **more)


def geometry(points_ref, slots_ref, rel_ref, moment_ref):
    ones = patch_ones()
    moment_ref[...] = jnp.zeros_like(moment_ref)
    lane = lax.rem(lax.broadcasted_iota(jnp.int32, (1, 256), 1), GROUP)

    def piece(i, carry):
        at = pl.ds(pl.multiple_of(i * 256, 256), 256)
        pts = points_ref[:, at]
        valid = (lane < slots_ref[0:1, at]).astype(F32)
        pick = (lane == slots_ref[1:2, at]).astype(F32)
        relative = (pts - patch_sum(pts * pick, ones)) * valid
        rows = low(jnp.concatenate([relative, valid, relative, valid], axis=0))
        rel_ref[:, at] = rows
        moment_ref[:, 0:8] += mm_nt(rows, rows)
        return carry

    lax.fori_loop(0, points_ref.shape[1] // 256, piece, 0, unroll=8)


def prepare_one(moments, small):
    n = moments[3:4, 3:4]
    w = [small[k : k + 1, :] for k in range(3)]
    gain, shift = small[3:4, :], small[4:5, :]
    mean = sum(w[k] * moments[k : k + 1, 3:4] for k in range(3)) / n
    square = jnp.zeros_like(mean)
    for j in range(3):
        for k in range(3):
            square = square + w[j] * w[k] * moments[j : j + 1, k : k + 1]
    inverse = lax.rsqrt(square / n - mean * mean + EPS_NORM)
    scale = inverse * gain
    scaled = [wk * scale for wk in w]
    offset = shift - mean * scale
    high = [low(v) for v in scaled + [offset]]
    rest = [low(v - h.astype(F32)) for v, h in zip(scaled + [offset], high)]
    forward = jnp.concatenate(high + rest, axis=0)
    zero = jnp.zeros((1, C1), BF16)
    backward = jnp.concatenate(high[:3] + [zero] + rest[:3] + [zero], axis=0)
    stats = jnp.concatenate(
        [mean, inverse, jnp.broadcast_to(n, (1, C1)), scale, jnp.zeros((4, C1), F32)], axis=0
    )
    return forward, backward, stats


def flat_rows(pieces, length, rows):
    lane = lax.broadcasted_iota(jnp.int32, (1, 128), 1)
    out = [jnp.zeros((1, 128), F32) for _ in range(rows)]
    for r in range(pieces.shape[0]):
        row = jnp.where(lane < length, pieces[r : r + 1, :], 0.0)
        at = length * r
        row = pltpu.roll(row, at % 128, 1) if at % 128 else row
        first = at // 128
        out[first] = out[first] + jnp.where(lane >= at % 128, row, 0.0)
        if at % 128 + length > 128:
            out[first + 1] = out[first + 1] + jnp.where(lane < at % 128, row, 0.0)
    return jnp.concatenate(out, axis=0)


def piece_of(rows, at, length):
    lane = lax.broadcasted_iota(jnp.int32, (1, 128), 1)
    first, shift = at // 128, at % 128
    row = rows[first : first + 1, :]
    if shift:
        row = pltpu.roll(row, 128 - shift, 1)
        if shift + length > 128:
            other = pltpu.roll(rows[first + 1 : first + 2, :], 128 - shift, 1)
            row = jnp.where(lane < 128 - shift, row, other)
    return jnp.where(lane < length, row, 0.0)


def where_am_i():
    at = lax.axis_index("dp")
    return at // (NY * NX), lax.rem(at // NX, NY), lax.rem(at, NX), lax.axis_index("fsdp")


def chip(z, y, x):
    return (z * NY + y) * NX + x


def rows_twelve():
    return [(QKV_AT, 3 * D), (WO_AT, D), (WF1_AT, FF)]


def first_kernel(
    rel_ref, moment_ref, psmall_ref, w2_ref, w3_ref,
    ext_o, gp_o, f_o, ft_o, gram_o, fs_o, cnt_o, g_o, fw_o, pooled_o, sums_o, stats_o, wd_o,
    e_s, wn_s, w2_s,
):
    step = pl.program_id(0)

    @pl.when(step == 0)
    def _():
        gram_o[...] = jnp.zeros_like(gram_o)
        e_s[...] = token_ones()
        small = psmall_ref[...]
        forward, backward, stats = prepare_one(moment_ref[:, 0:8], small)
        wn_s[...] = forward
        wd_o[...] = backward
        stats_o[...] = stats
        w2_s[0:C1, :] = w2_ref[...]
        b2 = jnp.concatenate([small[5:6, :], small[6:7, :]], axis=1)
        w2_s[C1:, :] = low(jnp.concatenate([b2, jnp.zeros((15, C2), F32)], axis=0))

    rel = rel_ref[...]
    f, ft = first_tile(rel, wn_s[...], w2_s[...], ext_o, gp_o)
    ft_o[...] = ft
    f_o[...] = f
    gram_o[...] += mm(ft, f)
    at = pl.ds(pl.multiple_of(step * TOK, TOK), TOK)
    fs_o[at, :] = mm(e_s[...], f)
    cnt_o[at, :] = jnp.broadcast_to(mm_nt(e_s[...], rel)[:, 3:4], (TOK, 128))

    @pl.when(step == pl.num_programs(0) - 1)
    def _():
        sums_o[...] = first_tokens(cnt_o, fs_o, gram_o, w3_ref, pooled_o, g_o, fw_o)


def first_call(rel, moments, psmall, w2, w3):
    count = rel.shape[1]
    tokens = count // GROUP
    full = lambda *s: pl.BlockSpec(s, lambda i: (0, 0))
    cols = lambda r: pl.BlockSpec((r, TILE), lambda i: (0, i))
    return pl.pallas_call(
        first_kernel,
        grid=(count // TILE,),
        in_specs=[cols(8), full(8, 128), full(24, 128), full(C1, C2), full(2 * C2, C3)],
        out_specs=[
            cols(C1 + 16), cols(C1), pl.BlockSpec((TILE, C2), lambda i: (i, 0)), cols(C2),
            full(C2, C2), full(tokens, C2), full(tokens, 128), full(tokens, C3), full(tokens, C3),
            full(tokens, C2), full(8, 128), full(8, C1), full(8, C1),
        ],
        out_shape=shaped(
            ((C1 + 16, count), BF16), ((C1, count), BF16), ((count, C2), BF16), ((C2, count), BF16),
            ((C2, C2), F32), ((tokens, C2), F32), ((tokens, 128), F32), ((tokens, C3), F32),
            ((tokens, C3), F32), ((tokens, C2), BF16), ((8, 128), F32), ((8, C1), F32), ((8, C1), BF16),
        ),
        scratch_shapes=[pltpu.VMEM((TOK, TILE), BF16), pltpu.VMEM((8, C1), BF16), pltpu.VMEM((C1 + 16, C2), BF16)],
        compiler_params=params(),
        name="first",
    )(rel, moments, psmall, w2, w3)


def third_kernel(dp, sums_ref, g_ref, stats_ref, psmall_ref, gm_o, sv_o, acc, slots, send, recv):
    count = greet(all_peers(dp))
    acc[...] = sums_ref[...]
    greeted(count)
    sum_over_devices(dp, acc, slots, send, recv)
    sv_o[...] = third_vectors(acc[...], stats_ref[2:3, 0:1], psmall_ref)
    gm_o[...] = g_ref[...] - sv_o[2:3, :]


def third_call(dp, sums, g, stats, psmall):
    return pl.pallas_call(
        functools.partial(third_kernel, dp),
        out_shape=shaped((g.shape, F32), ((8, C3), F32)),
        in_specs=vmem(4),
        out_specs=vmem(2),
        scratch_shapes=sum_scratch(dp, (8, 128)),
        compiler_params=params(collective_id=1, has_side_effects=True),
        name="third",
    )(sums, g, stats, psmall)


def second_kernel(f_ref, rel_ref, w3_ref, gm_ref, sv_ref, gp_o, pa_o, pg_o, pc_o, e_s):
    @pl.when(pl.program_id(0) == 0)
    def _():
        e_s[...] = token_ones()

    second_tile(
        lambda start, size: f_ref[start : start + size, :], e_s[...] * rel_ref[3:4, :], w3_ref[C2:, :],
        lambda to: gm_ref[to, :], sv_ref, gp_o, pa_o, pg_o, pc_o, 0,
    )


def second_call(f, rel, w3, gm, sv):
    count = f.shape[0]
    tokens = count // GROUP
    full = lambda *s: pl.BlockSpec(s, lambda i: (0, 0))
    rows = lambda r, c: pl.BlockSpec((r, c), lambda i: (i, 0))
    return pl.pallas_call(
        second_kernel,
        grid=(count // TILE,),
        in_specs=[rows(TILE, C2), pl.BlockSpec((8, TILE), lambda i: (0, i)), full(2 * C2, C3), rows(TOK, C3), full(8, C3)],
        out_specs=[rows(TILE, C3), rows(TOK, C3), rows(TOK, C3), rows(TOK, C3)],
        out_shape=shaped(((count, C3), BF16), ((tokens, C3), F32), ((tokens, C3), F32), ((tokens, C3), F32)),
        scratch_shapes=[pltpu.VMEM((TOK, TILE), BF16)],
        compiler_params=params(),
        name="second",
    )(f, rel, w3, gm, sv)


def first_tile(rel, wn, w2, ext_ref, gp_ref):
    valid = rel[3:4, :].astype(F32)
    for j in range(TILE // 256):
        at = slice(256 * j, 256 * j + 256)
        g, gp = gelu_pair(mm_tn(wn, rel[:, at]))
        ext_ref[0:C1, at] = low(g * valid[:, at])
        gp_ref[:, at] = low(gp * valid[:, at])
    ext_ref[C1:, :] = jnp.concatenate([rel[3:4], jnp.zeros((15, TILE), BF16)], axis=0)
    ext = ext_ref[...]
    return low(mm_tn(ext, w2)), low(mm_tn(w2, ext))


def first_tokens(cnt_ref, fs_ref, gram_ref, w3_ref, pooled_o, g_o, fw_o):
    count = cnt_ref[:, 0:1]
    fs = fs_ref[...]
    pooled = low(fs / count)
    pooled_o[...] = pooled
    g = mm(pooled, w3_ref[0:C2, :])
    g_o[...] = g
    lower = w3_ref[C2:, :]
    fw = mm_exact(fs, lower)
    fw_o[...] = fw
    one = jnp.sum(fw + count * g, axis=0, keepdims=True)
    two = jnp.sum(mm_exact(gram_ref[...], lower) * lower.astype(F32), axis=0, keepdims=True)
    two = two + jnp.sum(g * (2.0 * fw + count * g), axis=0, keepdims=True)
    return as_rows(one, two)


def third_vectors(totals, n, psmall_ref):
    mean = as_vector(totals, 0, 4) / n
    inverse = lax.rsqrt(as_vector(totals, 4, 4) / n - mean * mean + EPS_NORM)
    gain = jnp.concatenate([psmall_ref[k : k + 1, :] for k in range(7, 11)], axis=1)
    shift = jnp.concatenate([psmall_ref[k : k + 1, :] for k in range(11, 15)], axis=1)
    return jnp.concatenate([inverse * gain, shift, mean, inverse, jnp.zeros((4, C3), F32)], axis=0)


def second_tile(f_at, mask, lower, gm_at, sv_ref, gp_o, pa_o, pg_o, pc_o, first):
    scale, shift = low(sv_ref[0:1, :]), low(sv_ref[1:2, :])
    tokens = SUB // GROUP
    for j in range(TILE // SUB):
        at, ts = slice(SUB * j, SUB * j + SUB), slice(tokens * j, tokens * j + tokens)
        to = pl.ds(first + tokens * j, tokens)
        c = mm(f_at(SUB * j, SUB), lower).reshape(tokens, GROUP, C3) + gm_at(to)[:, None, :]
        c = low(c)
        g, gp = gelu_pair(c * scale[None] + shift[None])
        gc = (gp * c).reshape(SUB, C3)
        gp = gp.reshape(SUB, C3)
        gp_o[at, :] = gp
        m = mask[ts, at]
        pa_o[to, :] = mm(m, g.reshape(SUB, C3))
        pg_o[to, :] = mm(m, gp)
        pc_o[to, :] = mm(m, gc)


class Gather:
    def __init__(self, blocks, send, recv, base):
        self.blocks, self.sems, self.base = blocks, (send, recv), base
        z, y, x, core = where_am_i()
        half = blocks.shape[-1] // 2
        one, two = pl.ds(0, half), pl.ds(half, half)
        every = slice(None)
        near = [(chip(lax.rem(z + k, NZ), y, x), core) for k in range(1, NZ)]
        over_y, over_x, twin = (chip(z, 1 - y, x), core), (chip(z, y, 1 - x), core), (chip(z, y, x), 1 - core)
        self.stages = [
            [((z, y, x, core), peer) for peer in near],
            [((every, y, x, core, every, one), over_y), ((every, y, x, core, every, two), over_x)],
            [((every, every, x, core, every, one), over_x), ((every, y, every, core, every, two), over_y)],
            [],
        ]
        self.inner = [
            [],
            [((every, y, x, core), twin)],
            [((every, 1 - y, x, core, every, one), twin), ((every, y, 1 - x, core, every, two), twin)],
            [((every, every, 1 - x, core, every, one), twin), ((every, 1 - y, every, core, every, two), twin)],
        ]

    def copies(self, stage, inner):
        table = self.inner if inner else self.stages
        k = self.base + (7 if inner else 0) + sum(len(s) for s in table[:stage])
        out = []
        for i, (index, peer) in enumerate(table[stage]):
            view = self.blocks.at[index]
            out.append(
                pltpu.make_async_remote_copy(
                    src_ref=view, dst_ref=view, send_sem=self.sems[0].at[k + i], recv_sem=self.sems[1].at[k + i],
                    device_id=peer, device_id_type=MESH,
                )
            )
        return out

    def advance(self, stage):
        if stage > 0:
            for copy in self.copies(stage - 1, False):
                copy.wait()
        if stage < 4:
            for copy in self.copies(stage, False) + self.copies(stage, True):
                copy.start()
        else:
            for inner_stage in range(4):
                for copy in self.copies(inner_stage, True):
                    copy.wait()


GATHER_SEMS = 12
REST = [("w4", 0, D), ("wqkv", 384, 3 * D), ("wo", 1536, D), ("wf1", 1920, FF), ("wf2", 3456, 3 * D)]
REST_WIDTH = 4608


def forward_kernel(
    points_ref, slots_ref, pflat, bflat,
    rel_o, moment_o, psmall_o, bsmall_o, w2_o, w3_o, w4_o, wqkv_o, wo_o, wf1_o, wf2_o,
    ext_o, gp1_o, f_o, ft_o, gram_o, fs_o, cnt_o, gm_o, fw_o, pooled_o, sv_o, stats_o, wd_o,
    gp_o, pa_o, pg_o, pc_o,
    tiny, rest, stage, wide, f_s, e_s, wn_s, w2_s,
    acc, sums, ssend, srecv, acc3, sums3, ssend3, srecv3, tsend, trecv, gsend, grecv, fsem, three, flat2,
):
    step = pl.program_id(0)
    tiles = pl.num_programs(0) // 2
    z, y, x, core = where_am_i()
    dp = NZ * NY * NX
    plane = (y * NX + x) * NC + core
    gather_w3 = Gather(three, gsend, grecv, 0)
    gather_rest = Gather(rest, gsend, grecv, GATHER_SEMS)
    f_copy = pltpu.make_async_copy(f_s, f_o, fsem)

    @pl.when(step == 0)
    def _():
        count = greet(all_peers(dp) + [(chip(z, 1 - y, x), core), (chip(z, y, 1 - x), core), (chip(z, y, x), 1 - core)])
        rows = [pflat[1:9, :], pflat[0:1, :], bflat[0:1, :], jnp.zeros((6, 128), F32)]
        tiny[z, plane] = low(jnp.concatenate(rows, axis=0))
        for j in range(C3 // 128):
            three[z, y, x, core, :, 128 * j : 128 * j + 128] = low(pflat[pl.ds(9 + j, 16, stride=C3 // 128), :])
        stage[...] = jnp.zeros_like(stage)
        for j in range(D // 128):
            stage[:, 128 * j : 128 * j + 128] = pflat[pl.ds(73 + j, 16, stride=D // 128), :]
        start = 1
        for name, at, cols in REST[1:4]:
            for j in range(cols // 128):
                stage[0:12, at + 128 * j : at + 128 * j + 128] = bflat[pl.ds(start + j, 12, stride=cols // 128), :]
            start += 12 * cols // 128
        for b in range(3):
            for j in range(D // 128):
                to = REST[4][1] + D * b + 128 * j
                stage[:, to : to + 128] = bflat[pl.ds(start + 48 * b + j, 16, stride=3), :]
        rest[z, y, x, core] = low(stage[...])
        geometry(points_ref, slots_ref, rel_o, acc)
        e_s[...] = token_ones()
        gram_o[...] = jnp.zeros_like(gram_o)
        greeted(count)

        def tiny_copies(upper_stage):
            view = tiny.at[z] if upper_stage else tiny.at[z, plane]
            first = 7 if upper_stage else 0
            return [
                pltpu.make_async_remote_copy(
                    src_ref=view, dst_ref=view, send_sem=tsend.at[first + k], recv_sem=trecv.at[first + k],
                    device_id=peer, device_id_type=MESH,
                )
                for k, peer in enumerate(ring_peers(dp, upper_stage))
            ]

        for upper_stage in (False, True):
            copies = tiny_copies(upper_stage)
            small = sum_start(dp, upper_stage, acc, sums, ssend, srecv)
            for copy in copies:
                copy.start()
            sum_finish(dp, upper_stage, acc, sums, small)
            for copy in copies:
                copy.wait()
        gather_w3.advance(0)
        moment_o[...] = acc[...]
        psmall, bsmall = [], []
        for d in range(dp * NC):
            rows = tiny[d // 8, d % 8].astype(F32)
            flat2[8 * d : 8 * d + 8, :] = rows[0:8, :]
            psmall.append(rows[8:9, :])
            bsmall.append(rows[9:10, :])
        psmall_o[0:18, :] = flat_rows(jnp.concatenate(psmall, axis=0), 72, 18)
        bsmall_o[0:30, :] = flat_rows(jnp.concatenate(bsmall, axis=0), 120, 30)
        for j in range(2):
            w2_o[:, 128 * j : 128 * j + 128] = low(flat2[pl.ds(j, C1, stride=2), :])
        small = psmall_o[...]
        forward, backward, stats = prepare_one(acc[:, 0:8], small)
        wn_s[...] = forward
        wd_o[...] = backward
        stats_o[...] = stats
        w2_s[0:C1, :] = w2_o[...]
        b2 = jnp.concatenate([small[5:6, :], small[6:7, :]], axis=1)
        w2_s[C1:, :] = low(jnp.concatenate([b2, jnp.zeros((15, C2), F32)], axis=0))

    for at_step, work in (
        (1, lambda: gather_rest.advance(0)),
        (2, lambda: gather_w3.advance(1)),
        (3, lambda: gather_w3.advance(2)),
        (5, lambda: gather_w3.advance(3)),
        (6, lambda: gather_rest.advance(1)),
        (7, lambda: gather_w3.advance(4)),
        (9, lambda: gather_rest.advance(2)),
        (12, lambda: gather_rest.advance(3)),
    ):
        pl.when(step == at_step)(work)

    at_points = pl.multiple_of(lax.rem(step, tiles) * TILE, TILE)
    rel = rel_o[:, pl.ds(at_points, TILE)]
    first = pl.multiple_of(lax.rem(step, tiles) * TOK, TOK)

    @pl.when(step < tiles)
    def _():
        f, ft = first_tile(rel, wn_s[...], w2_s[...], ext_o, gp1_o)
        ft_o[...] = ft
        f_s[pl.ds(at_points, TILE), :] = f
        gram_o[...] += mm(ft, f)
        fs_o[pl.ds(first, TOK), :] = mm(e_s[...], f)
        cnt_o[pl.ds(first, TOK), :] = jnp.broadcast_to(mm_nt(e_s[...], rel)[:, 3:4], (TOK, 128))

    @pl.when(step == tiles)
    def _():
        f_copy.start()
        for d in range(dp * NC):
            w3_o[16 * d : 16 * d + 16, :] = three[d // 8, d // 4 % 2, d // 2 % 2, d % 2]
        acc3[...] = first_tokens(cnt_o, fs_o, gram_o, w3_o, pooled_o, gm_o, fw_o)
        sum_over_devices(dp, acc3, sums3, ssend3, srecv3)
        sv_o[...] = third_vectors(acc3[...], stats_o[2:3, 0:1], psmall_o)
        gm_o[...] = gm_o[...] - sv_o[2:3, :]

    @pl.when(step >= tiles)
    def _():
        mask = e_s[...] * rel[3:4, :]
        second_tile(
            lambda start, size: f_s[pl.ds(pl.multiple_of(at_points + start, SUB), size), :],
            mask, w3_o[C2:, :], lambda to: gm_o[to, :], sv_o, gp_o, pa_o, pg_o, pc_o, first,
        )

    @pl.when(step == 2 * tiles - 1)
    def _():
        f_copy.wait()
        gather_rest.advance(4)
        for d in range(dp * NC):
            block = rest.at[d // 8, d // 4 % 2, d // 2 % 2, d % 2]
            w4_o[16 * d : 16 * d + 16, :] = block[:, 0:D]
            for b in range(3):
                at = 48 * d + 16 * b
                wf2_o[at : at + 16, :] = block[:, 3456 + D * b : 3456 + D * b + D]
            wide[12 * d : 12 * d + 12, :] = block[:, 384:3456].astype(F32)[0:12, :]
        for out, at, cols in ((wqkv_o, 0, 3 * D), (wo_o, 1152, D), (wf1_o, 1536, FF)):
            out[...] = low(wide[:, at : at + cols])


def forward_call(points, slots, pflat, bflat):
    dp = NZ * NY * NX
    count = points.shape[1]
    tokens, tiles = count // GROUP, count // TILE
    single = dict(pipeline_mode=pl.Buffered(1))
    full = lambda *s: pl.BlockSpec(s, lambda i: (0, 0), **single)
    early = lambda r: pl.BlockSpec((r, TILE), lambda i: (0, jnp.minimum(i, tiles - 1)))
    outs = [
        (full(8, count), (8, count), BF16), (full(8, 128), (8, 128), F32), (full(24, 128), (24, 128), F32),
        (full(32, 128), (32, 128), F32), (full(C1, C2), (C1, C2), BF16), (full(2 * C2, C3), (2 * C2, C3), BF16),
        (full(C3, D), (C3, D), BF16), (full(D, 3 * D), (D, 3 * D), BF16), (full(D, D), (D, D), BF16),
        (full(D, FF), (D, FF), BF16), (full(FF, D), (FF, D), BF16),
        (early(C1 + 16), (C1 + 16, count), BF16), (early(C1), (C1, count), BF16),
        (pl.BlockSpec(memory_space=pl.ANY), (count, C2), BF16), (early(C2), (C2, count), BF16),
        (full(C2, C2), (C2, C2), F32), (full(tokens, C2), (tokens, C2), F32), (full(tokens, 128), (tokens, 128), F32),
        (full(tokens, C3), (tokens, C3), F32), (full(tokens, C3), (tokens, C3), F32),
        (full(tokens, C2), (tokens, C2), BF16), (full(8, C3), (8, C3), F32), (full(8, C1), (8, C1), F32),
        (full(8, C1), (8, C1), BF16),
        (pl.BlockSpec((TILE, C3), lambda i: (jnp.maximum(i - tiles, 0), 0)), (count, C3), BF16),
        (full(tokens, C3), (tokens, C3), F32), (full(tokens, C3), (tokens, C3), F32), (full(tokens, C3), (tokens, C3), F32),
    ]
    return pl.pallas_call(
        forward_kernel,
        grid=(2 * tiles,),
        in_specs=[full(3, count), full(2, count), full(PROWS, 128), full(BROWS, 128)],
        out_specs=[o[0] for o in outs],
        out_shape=shaped(*[o[1:] for o in outs]),
        scratch_shapes=[
            pltpu.VMEM((NZ, 2 * NY * NX, 16, 128), BF16),
            pltpu.VMEM((NZ, NY, NX, NC, 16, REST_WIDTH), BF16),
            pltpu.VMEM((16, REST_WIDTH), F32),
            pltpu.VMEM((384, 3456 - 384), F32),
            pltpu.VMEM((count, C2), BF16),
            pltpu.VMEM((TOK, TILE), BF16), pltpu.VMEM((8, C1), BF16), pltpu.VMEM((C1 + 16, C2), BF16),
        ]
        + sum_scratch(dp, (8, 128))
        + sum_scratch(dp, (8, 128))
        + [pltpu.SemaphoreType.DMA((10,)), pltpu.SemaphoreType.DMA((10,))]
        + [pltpu.SemaphoreType.DMA((2 * GATHER_SEMS,)), pltpu.SemaphoreType.DMA((2 * GATHER_SEMS,))]
        + [pltpu.SemaphoreType.DMA, pltpu.VMEM((NZ, NY, NX, NC, 16, C3), BF16), pltpu.VMEM((256, 128), F32)],
        compiler_params=params(collective_id=0, has_side_effects=True),
        name="forward",
    )(points, slots, pflat, bflat)


def wide_row(ref, first, rows):
    return jnp.concatenate([ref[k : k + 1, :] for k in range(first, first + rows)], axis=1)


def layer_norm(v, gain, shift):
    centred = v - jnp.mean(v, -1, keepdims=True)
    inverse = lax.rsqrt(jnp.mean(centred * centred, -1, keepdims=True) + EPS_NORM)
    unit = centred * inverse
    return unit, inverse, low(unit * gain + shift)


def norm_back(d_unit, unit, inverse):
    return inverse * (
        d_unit - jnp.mean(d_unit, -1, keepdims=True) - unit * jnp.mean(d_unit * unit, -1, keepdims=True)
    )


def col_sum(v):
    return jnp.sum(v, axis=0, keepdims=True)


def block_kernel(
    pa_ref, pg_ref, pc_ref, cnt_ref, len_ref, cot_ref, psmall_ref, bsmall_ref, sv_ref,
    w4_ref, wqkv_ref, wo_ref, wf1_ref, wf2_ref,
    out_o, gw4_o, gwqkv_o, gwo_o, gwf1_o, gwf2_o, small_o, tok_o, tg_o, back_o,
    qkv_s, mixed_s, soft_s, dmix_s, dqkv_s,
):
    step = pl.program_id(0)

    @pl.when(step == 0)
    def _():
        for ref in (gw4_o, gwqkv_o, gwo_o, gwf1_o, gwf2_o, small_o, back_o):
            ref[...] = jnp.zeros_like(ref)

    count = cnt_ref[:, 0:1]
    scale = HEAD_DIM ** (-0.5)
    b4 = wide_row(psmall_ref, 15, 3)
    ln1_gain, ln1_shift, bo = wide_row(bsmall_ref, 0, 3), wide_row(bsmall_ref, 3, 3), wide_row(bsmall_ref, 6, 3)
    ln2_gain, ln2_shift = wide_row(bsmall_ref, 9, 3), wide_row(bsmall_ref, 12, 3)
    bf1, bf2 = wide_row(bsmall_ref, 15, 12), wide_row(bsmall_ref, 27, 3)

    act = low(pa_ref[...] / count)
    x_zero = mm(act, w4_ref[...]) + b4
    unit_a, inv_a, normed_a = layer_norm(x_zero, ln1_gain, ln1_shift)
    qkv_s[...] = low(mm(normed_a, wqkv_ref[...]))

    row_cloud = lax.broadcasted_iota(jnp.int32, (PAIR, PAIR), 0) // PATCHES
    col = lax.broadcasted_iota(jnp.int32, (PAIR, PAIR), 1)
    left = lax.broadcasted_iota(jnp.int32, (1, 128), 1) < HEAD_DIM
    zero = jnp.zeros((1, 1), BF16)

    def halves(v):
        return jnp.where(left, v, zero), jnp.where(left, zero, v)

    tiles = TB // PAIR
    for s in range(tiles):
        first = (step * tiles + s) * 2
        visible = (row_cloud == col // PATCHES) & (
            lax.rem(col, PATCHES) < jnp.where(col < PATCHES, len_ref[first], len_ref[first + 1])
        )
        rows = slice(PAIR * s, PAIR * s + PAIR)
        for p in range(HEADS // 2):
            at = 128 * p
            q = qkv_s[rows, at : at + 128]
            k = qkv_s[rows, D + at : D + at + 128]
            v = qkv_s[rows, 2 * D + at : 2 * D + at + 128]
            mixed = []
            for a, q_half in enumerate(halves(q)):
                score = jnp.where(visible, mm_nt(q_half, k) * scale, NEG_FILL)
                raised = jnp.exp(score - jnp.max(score, -1, keepdims=True))
                soft = raised / jnp.sum(raised, -1, keepdims=True)
                soft_s[(s * (HEADS // 2) + p) * 2 + a] = soft
                mixed.append(mm(low(soft), v))
            mixed_s[rows, at : at + 128] = low(jnp.where(left, mixed[0], mixed[1]))

    mixed_low = mixed_s[...]
    x_one = x_zero + mm(mixed_low, wo_ref[...]) + bo
    unit_b, inv_b, normed_b = layer_norm(x_one, ln2_gain, ln2_shift)
    hidden, d_hidden = gelu_pair(mm(normed_b, wf1_ref[...]) + bf1)
    hidden = low(hidden)
    out_o[...] = x_one + mm(hidden, wf2_ref[...]) + bf2

    cot = cot_ref[...]
    grad = low(cot)
    gwf2_o[...] += mm_tn(hidden, grad)
    d_pre = mm_nt(grad, wf2_ref[...]) * d_hidden
    d_pre_low = low(d_pre)
    gwf1_o[...] += mm_tn(normed_b, d_pre_low)
    d_normed_b = mm_nt(d_pre_low, wf1_ref[...])
    d_x_one = cot + norm_back(d_normed_b * ln2_gain, unit_b, inv_b)
    d_x_low = low(d_x_one)
    gwo_o[...] += mm_tn(mixed_low, d_x_low)
    dmix_s[...] = low(mm_nt(d_x_low, wo_ref[...]))

    for s in range(tiles):
        rows = slice(PAIR * s, PAIR * s + PAIR)
        for p in range(HEADS // 2):
            at = 128 * p
            q = qkv_s[rows, at : at + 128]
            k = qkv_s[rows, D + at : D + at + 128]
            v = qkv_s[rows, 2 * D + at : 2 * D + at + 128]
            dm = dmix_s[rows, at : at + 128]
            d_q, d_k, d_v = [], [], []
            for a, dm_half in enumerate(halves(dm)):
                soft = soft_s[(s * (HEADS // 2) + p) * 2 + a]
                d_soft = mm_nt(dm_half, v)
                d_v.append(mm_tn(low(soft), dm))
                d_score = low(soft * (d_soft - jnp.sum(soft * d_soft, -1, keepdims=True)))
                d_q.append(mm(d_score, k))
                d_k.append(mm_tn(d_score, q))
            dqkv_s[rows, at : at + 128] = low(jnp.where(left, d_q[0], d_q[1]) * scale)
            dqkv_s[rows, D + at : D + at + 128] = low(jnp.where(left, d_k[0], d_k[1]) * scale)
            dqkv_s[rows, 2 * D + at : 2 * D + at + 128] = low(jnp.where(left, d_v[0], d_v[1]))

    d_qkv = dqkv_s[...]
    gwqkv_o[...] += mm_tn(normed_a, d_qkv)
    d_normed_a = mm_nt(d_qkv, wqkv_ref[...])
    d_x_zero = d_x_one + norm_back(d_normed_a * ln1_gain, unit_a, inv_a)
    d_x_low = low(d_x_zero)
    gw4_o[...] += mm_tn(act, d_x_low)
    token = mm_nt(d_x_low, w4_ref[...]) / count
    tok_o[...] = token
    grouped = token * pg_ref[...]
    tg_o[...] = grouped
    back_o[0:1, :] += col_sum(grouped)
    back_o[1:2, :] += col_sum(token * pc_ref[...]) * sv_ref[3:4, :]
    narrow = [
        col_sum(d_normed_a * unit_a), col_sum(d_normed_a), col_sum(d_x_one),
        col_sum(d_normed_b * unit_b), col_sum(d_normed_b), col_sum(cot), col_sum(d_x_zero),
    ]
    for k, row in enumerate(narrow):
        small_o[k : k + 1, 0:D] += row
    small_o[7:8, :] += col_sum(d_pre)


def block_call(pa, pg, pc, cnt, length, cot, psmall, bsmall, sv, w4, wqkv, wo, wf1, wf2):
    tokens = pa.shape[0]
    full = lambda *s: pl.BlockSpec(s, lambda i: (0, 0))
    rows = lambda c: pl.BlockSpec((TB, c), lambda i: (i, 0))
    return pl.pallas_call(
        block_kernel,
        grid=(tokens // TB,),
        in_specs=[
            rows(C3), rows(C3), rows(C3), rows(128), pl.BlockSpec(memory_space=pltpu.SMEM), rows(D),
            full(24, 128), full(32, 128), full(8, C3),
            full(C3, D), full(D, 3 * D), full(D, D), full(D, FF), full(FF, D),
        ],
        out_specs=[
            rows(D), full(C3, D), full(D, 3 * D), full(D, D), full(D, FF), full(FF, D), full(8, FF),
            rows(C3), rows(C3), full(8, C3),
        ],
        out_shape=shaped(
            ((tokens, D), F32), ((C3, D), F32), ((D, 3 * D), F32), ((D, D), F32), ((D, FF), F32),
            ((FF, D), F32), ((8, FF), F32), ((tokens, C3), F32), ((tokens, C3), F32), ((8, C3), F32),
        ),
        scratch_shapes=[
            pltpu.VMEM((TB, 3 * D), BF16), pltpu.VMEM((TB, D), BF16),
            pltpu.VMEM((TB // PAIR * HEADS, PAIR, PAIR), F32), pltpu.VMEM((TB, D), BF16),
            pltpu.VMEM((TB, 3 * D), BF16),
        ],
        compiler_params=params(),
        name="block",
    )(pa, pg, pc, cnt, length, cot, psmall, bsmall, sv, w4, wqkv, wo, wf1, wf2)


def third_back_tokens(
    totals, tg_ref, fs_ref, fw_ref, gm_ref, cnt_ref, pooled_ref, gram_ref, w3_ref, sv_ref, stats_ref,
    kap_o, k_o, top_o, corr_o,
):
    lower = w3_ref[C2:, :].astype(F32)
    gain = sv_ref[0:1, :]
    n = stats_ref[2:3, 0:1]
    alpha = gain * as_vector(totals, 0, 4) / n
    beta = gain * as_vector(totals, 4, 4) * sv_ref[3:4, :] / n
    count = cnt_ref[:, 0:1]
    gm = gm_ref[...]
    per_token = low(gain * tg_ref[...] - (count * alpha + beta * (fw_ref[...] + count * gm)))
    d_pooled = mm_nt(per_token, w3_ref[0:C2, :])
    shifted = low(alpha + beta * gm)
    kap_o[...] = d_pooled / count - mm_nt(shifted, w3_ref[C2:, :])
    k_o[...] = low(-mm_nt(low(lower * beta), w3_ref[C2:, :]))
    top_o[...] = mm_tn(pooled_ref[...], per_token)
    corr_o[...] = mm_tn(low(fs_ref[...]), shifted) + beta * mm(low(gram_ref[...]), w3_ref[C2:, :])


def third_back_kernel(
    dp, back_ref, tok_ref, tg_ref, fs_ref, fw_ref, gm_ref, cnt_ref, pooled_ref, gram_ref, w3_ref, sv_ref, stats_ref,
    tot_o, tok_o, kap_o, k_o, ws_o, top_o, corr_o, acc, slots, send, recv,
):
    greeting = greet(all_peers(dp))
    acc[...] = as_rows(back_ref[0:1, :], back_ref[1:2, :])
    tok_o[...] = low(tok_ref[...])
    ws_o[...] = low(w3_ref[C2:, :].astype(F32) * sv_ref[0:1, :])
    greeted(greeting)
    sum_over_devices(dp, acc, slots, send, recv)
    tot_o[...] = acc[...]
    third_back_tokens(
        acc[...], tg_ref, fs_ref, fw_ref, gm_ref, cnt_ref, pooled_ref, gram_ref, w3_ref, sv_ref, stats_ref,
        kap_o, k_o, top_o, corr_o,
    )


def third_back_call(dp, back, tok, tg, fs, fw, gm, cnt, pooled, gram, w3, sv, stats):
    tokens = tok.shape[0]
    outs = shaped(
        ((8, 128), F32), ((tokens, C3), BF16), ((tokens, C2), F32), ((C2, C2), BF16), ((C2, C3), BF16),
        ((C2, C3), F32), ((C2, C3), F32),
    )
    return pl.pallas_call(
        functools.partial(third_back_kernel, dp),
        out_shape=outs,
        in_specs=vmem(12),
        out_specs=vmem(len(outs)),
        scratch_shapes=sum_scratch(dp, (8, 128)),
        compiler_params=params(collective_id=2, has_side_effects=True),
        name="third_back",
    )(back, tok, tg, fs, fw, gm, cnt, pooled, gram, w3, sv, stats)


def last_tile(
    gp_ref, f_ref, ft_ref, ext_ref, gp1_ref, rel, tok, kap, k_ref, ws_ref, w2_ref, wd_ref, h_o, gw2_o, q_o, d_at, dn_s
):
    tokens = SUB // GROUP
    for j in range(TILE // SUB):
        at, ts = slice(SUB * j, SUB * j + SUB), slice(tokens * j, tokens * j + tokens)
        gp = gp_ref[at, :].reshape(tokens, GROUP, C3)
        dn_s[at, :] = (gp * tok[ts, :][:, None, :]).reshape(SUB, C3)
    dn = dn_s[...]
    h_o[...] += mm(ft_ref[...], dn)
    d_feat = mm_nt(dn, ws_ref[...]) + mm(f_ref[...], k_ref[...])
    d_feat = low((d_feat.reshape(TOK, GROUP, C2) + kap[:, None, :]).reshape(TILE, C2))
    gw2_o[...] += mm(ext_ref[...], d_feat)
    d_one = low(mm_nt(w2_ref[...], d_feat) * gp1_ref[...].astype(F32))
    d_at(mm(wd_ref[...], d_one))
    q_o[...] += mm_nt(rel, d_one)


def last_kernel(
    gp_ref, f_ref, ft_ref, ext_ref, gp1_ref, rel_ref, tok_ref, kap_ref, k_ref, ws_ref, w2_ref, wd_ref,
    h_o, gw2_o, q_o, d_o, dn_s,
):
    @pl.when(pl.program_id(0) == 0)
    def _():
        for ref in (h_o, gw2_o, q_o):
            ref[...] = jnp.zeros_like(ref)

    def put(d):
        d_o[...] = d

    last_tile(
        gp_ref, f_ref, ft_ref, ext_ref, gp1_ref, rel_ref[...], tok_ref[...], kap_ref[...], k_ref, ws_ref, w2_ref,
        wd_ref, h_o, gw2_o, q_o, put, dn_s,
    )


def last_call(gp, f, ft, ext, gp1, rel, tok, kap, k, ws, w2, wd):
    count = f.shape[0]
    full = lambda *s: pl.BlockSpec(s, lambda i: (0, 0))
    rows = lambda r, c: pl.BlockSpec((r, c), lambda i: (i, 0))
    cols = lambda r: pl.BlockSpec((r, TILE), lambda i: (0, i))
    return pl.pallas_call(
        last_kernel,
        grid=(count // TILE,),
        in_specs=[
            rows(TILE, C3), rows(TILE, C2), cols(C2), cols(C1 + 16), cols(C1), cols(8), rows(TOK, C3), rows(TOK, C2),
            full(C2, C2), full(C2, C3), full(C1, C2), full(8, C1),
        ],
        out_specs=[full(C2, C3), full(C1 + 16, C2), full(8, C1), cols(8)],
        out_shape=shaped(((C2, C3), F32), ((C1 + 16, C2), F32), ((8, C1), F32), ((8, count), F32)),
        scratch_shapes=[pltpu.VMEM((TILE, C3), BF16)],
        compiler_params=params(),
        name="last",
    )(gp, f, ft, ext, gp1, rel, tok, kap, k, ws, w2, wd)


def first_grads(q, moments, psmall, stats):
    mean, inverse, n, scale = stats[0:1], stats[1:2], stats[2:3], stats[3:4]
    w = [psmall[k : k + 1, :] for k in range(3)]
    one = q[3:4, :]
    two = inverse * (sum(w[k] * q[k : k + 1, :] for k in range(3)) - mean * one)
    grad_w = []
    for k in range(3):
        along = sum(w[j] * moments[k : k + 1, j : j + 1] for j in range(3)) - mean * moments[k : k + 1, 3:4]
        grad_w.append(scale * (q[k : k + 1, :] - (one * moments[k : k + 1, 3:4] + two * inverse * along) / n))
    flat = [
        jnp.sum(scale * w[k] * (one - two * inverse * mean) / n, axis=1, keepdims=True) for k in range(3)
    ]
    slope = [
        [jnp.sum(scale * w[k] * two * inverse * w[j] / n, axis=1, keepdims=True) for j in range(3)]
        for k in range(3)
    ]
    return grad_w, two, one, flat, slope


def point_gradient(d_ref, rel_ref, slots_ref, flat, slope, out_ref):
    ones = patch_ones()
    lane = lax.rem(lax.broadcasted_iota(jnp.int32, (1, 256), 1), GROUP)
    base = jnp.concatenate(flat, axis=0)
    columns = [jnp.concatenate([slope[k][j] for k in range(3)], axis=0) for j in range(3)]

    def piece(i, carry):
        at = pl.ds(pl.multiple_of(i * 256, 256), 256)
        rel = rel_ref[:, at].astype(F32)
        d = d_ref[:, at]
        out = d[0:3] + d[4:7] - rel[3:4] * base
        for j in range(3):
            out = out - columns[j] * rel[j : j + 1]
        pick = (lane == slots_ref[1:2, at]).astype(F32)
        out_ref[:, at] = out - pick * patch_sum(out, ones)
        return carry

    lax.fori_loop(0, d_ref.shape[1] // 256, piece, 0, unroll=8)


def point_small_rows(grad_w, gain1, shift1, b2, tot, b4):
    rows = list(grad_w) + [gain1, shift1]
    rows += [b2[:, 128 * k : 128 * k + 128] for k in range(2)]
    rows += [tot[4:8, :], tot[0:4, :]]
    rows += [b4[:, 128 * k : 128 * k + 128] for k in range(3)]
    return jnp.concatenate(rows, axis=0)


def block_small_rows(small_ref):
    rows = [small_ref[k : k + 1, 128 * j : 128 * j + 128] for k in range(5) for j in range(3)]
    rows += [small_ref[7:8, 128 * j : 128 * j + 128] for j in range(12)]
    rows += [small_ref[5:6, 128 * j : 128 * j + 128] for j in range(3)]
    return jnp.concatenate(rows, axis=0)


class Scatter:
    def __init__(self, blocks, lands, send, recv, base):
        self.blocks, self.lands, self.sems, self.base = blocks, lands, (send, recv), base
        z, y, x, core = self.at = where_am_i()
        half = blocks.shape[-1] // 2
        self.one, self.two = pl.ds(0, half), pl.ds(half, half)
        every = slice(None)
        mine = blocks.at[core]
        near = [(chip(lax.rem(z + k, NZ), y, x), core) for k in range(1, NZ)]
        over_y, over_x, twin = (chip(z, 1 - y, x), core), (chip(z, y, 1 - x), core), (chip(z, y, x), 1 - core)
        land1, land2, land3, land4 = lands
        self.stages = [
            [(blocks.at[1 - core], land1, twin)],
            [
                (mine.at[:, :, 1 - x, :, self.one], land2.at[0], over_x),
                (mine.at[:, 1 - y, :, :, self.two], land2.at[1], over_y),
            ],
            [
                (mine.at[:, 1 - y, x, :, self.one], land3.at[0], over_y),
                (mine.at[:, y, 1 - x, :, self.two], land3.at[1], over_x),
            ],
            [(mine.at[lax.rem(z + k, NZ), y, x], land4.at[k - 1], near[k - 1]) for k in range(1, NZ)],
        ]

    def copies(self, stage):
        k = self.base + sum(len(s) for s in self.stages[:stage])
        return [
            pltpu.make_async_remote_copy(
                src_ref=src, dst_ref=dst, send_sem=self.sems[0].at[k + i], recv_sem=self.sems[1].at[k + i],
                device_id=peer, device_id_type=MESH,
            )
            for i, (src, dst, peer) in enumerate(self.stages[stage])
        ]

    def advance(self, stage):
        z, y, x, core = self.at
        mine = self.blocks.at[core]
        land1, land2, land3, land4 = self.lands
        if stage > 0:
            for copy in self.copies(stage - 1):
                copy.wait()
        if stage == 1:
            for cz in range(NZ):
                for cy in range(NY):
                    for cx in range(NX):
                        mine[cz, cy, cx] = mine[cz, cy, cx] + land1[cz, cy, cx]
        if stage == 2:
            for cz in range(NZ):
                for k in range(2):
                    mine[cz, k, x, :, self.one] = mine[cz, k, x, :, self.one] + land2[0, cz, k]
                    mine[cz, y, k, :, self.two] = mine[cz, y, k, :, self.two] + land2[1, cz, k]
        if stage == 3:
            for cz in range(NZ):
                mine[cz, y, x, :, self.one] = mine[cz, y, x, :, self.one] + land3[0, cz]
                mine[cz, y, x, :, self.two] = mine[cz, y, x, :, self.two] + land3[1, cz]
        if stage < 4:
            for copy in self.copies(stage):
                copy.start()
            return None
        total = mine[z, y, x].astype(F32)
        for k in range(NZ - 1):
            total = total + land4[k].astype(F32)
        return total


SCATTER_SEMS = 8
POINT_WIDTH = 1024


def scatter_scratch(width):
    return [
        pltpu.VMEM((NC, NZ, NY, NX, 16, width), BF16),
        pltpu.VMEM((NZ, NY, NX, 16, width), BF16),
        pltpu.VMEM((2, NZ, 2, 16, width // 2), BF16),
        pltpu.VMEM((2, NZ, 16, width // 2), BF16),
        pltpu.VMEM((NZ - 1, 16, width), BF16),
    ]


def backward_kernel(
    pa_ref, pg_ref, pc_ref, cnt_ref, len_ref, cot_ref, psmall_ref, bsmall_ref, sv_ref, stats_ref, moment_ref,
    w2_ref, w3_ref, w4_ref, wqkv_ref, wo_ref, wf1_ref, wf2_ref,
    fs_ref, fw_ref, gm_ref, pooled_ref, gram_ref, wd_ref, rel_ref, slots_ref,
    gp_ref, f_ref, ft_ref, ext_ref, gp1_ref,
    out_o, pg_o, pflat_o, bflat_o,
    gw4_s, gwqkv_s, gwo_s, gwf1_s, gwf2_s, small_s, tok_s, tg_s, back_s,
    qkv_s, mixed_s, soft_s, dmix_s, dqkv_s,
    tot_s, kap_s, k_s, ws_s, top_s, corr_s, h_s, gw2_s, q_s, d_s, dn_s,
    rest0, rest1, rest2, rest3, rest4, point0, point1, point2, point3, point4, stage, pstage,
    acc, slots, ssend, srecv, acc3, slots3, ssend3, srecv3, gsend, grecv,
):
    step = pl.program_id(0)
    steps = pl.num_programs(0)
    z, y, x, core = where_am_i()
    dp = NZ * NY * NX
    rest = Scatter(rest0, (rest1, rest2, rest3, rest4), gsend, grecv, 0)
    point = Scatter(point0, (point1, point2, point3, point4), gsend, grecv, SCATTER_SEMS)
    peers = all_peers(dp) + [(chip(z, 1 - y, x), core), (chip(z, y, 1 - x), core), (chip(z, y, x), 1 - core)]
    blocks = cnt_ref.shape[0] // TB

    @pl.when(step == 0)
    def _():
        greet(peers)

    @pl.when(step < blocks)
    def _():
        rows = pl.ds(pl.multiple_of(step * TB, TB), TB)
        block_kernel(
            pa_ref, pg_ref, pc_ref, cnt_ref.at[rows], len_ref, cot_ref, psmall_ref, bsmall_ref, sv_ref,
            w4_ref, wqkv_ref, wo_ref, wf1_ref, wf2_ref,
            out_o, gw4_s, gwqkv_s, gwo_s, gwf1_s, gwf2_s, small_s, tok_s.at[rows], tg_s.at[rows], back_s,
            qkv_s, mixed_s, soft_s, dmix_s, dqkv_s,
        )

    @pl.when(step == blocks - 1)
    def _():
        greeted(len(peers))
        acc3[...] = as_rows(back_s[0:1, :], back_s[1:2, :])
        copies = sum_start(dp, False, acc3, slots3, ssend3, srecv3)
        brow = block_small_rows(small_s)
        stage[...] = jnp.zeros_like(stage)
        for d in range(dp * NC):
            stage[:, 0:D] = gw4_s[16 * d : 16 * d + 16, :]
            for ref, at, cols in ((gwqkv_s, 384, 3 * D), (gwo_s, 1536, D), (gwf1_s, 1920, FF)):
                stage[0:12, at : at + cols] = ref[12 * d : 12 * d + 12, :]
            for b in range(3):
                at = 48 * d + 16 * b
                stage[:, 3456 + D * b : 3456 + D * b + D] = gwf2_s[at : at + 16, :]
            stage[12:13, 384:512] = piece_of(brow, 120 * d, 120)
            rest0[d % 2, d // 8, d // 4 % 2, d // 2 % 2] = low(stage[...])
        rest.advance(0)
        sum_finish(dp, False, acc3, slots3, copies)
        copies = sum_start(dp, True, acc3, slots3, ssend3, srecv3)
        ws_s[...] = low(w3_ref[C2:, :].astype(F32) * sv_ref[0:1, :])
        for ref in (h_s, gw2_s, q_s):
            ref[...] = jnp.zeros_like(ref)
        sum_finish(dp, True, acc3, slots3, copies)
        tot_s[...] = acc3[...]
        third_back_tokens(
            acc3[...], tg_s, fs_ref, fw_ref, gm_ref, cnt_ref, pooled_ref, gram_ref, w3_ref, sv_ref, stats_ref,
            kap_s, k_s, top_s, corr_s,
        )
        rest.advance(1)

    for at_step, number in ((5, 2), (7, 3)):
        pl.when(step == at_step)(functools.partial(rest.advance, number))

    @pl.when(step >= blocks)
    def _():
        tile = step - blocks
        at = pl.ds(pl.multiple_of(tile * TILE, TILE), TILE)
        ts = pl.ds(pl.multiple_of(tile * TOK, TOK), TOK)

        def put(d):
            d_s[:, at] = d

        last_tile(
            gp_ref, f_ref, ft_ref, ext_ref, gp1_ref, rel_ref[:, at], low(tok_s[ts, :]), kap_s[ts, :], k_s, ws_s,
            w2_ref, wd_ref, h_s, gw2_s, q_s, put, dn_s,
        )

    @pl.when(step == steps - 1)
    def _():
        acc[...] = q_s[...]
        copies = sum_start(dp, False, acc, slots, ssend, srecv)
        none = jnp.zeros((1, 128), F32)
        prow = point_small_rows(
            [none] * 3, none, none, gw2_s[C1 : C1 + 1, :], jnp.zeros((8, 128), F32), small_s[6:7, 0:D]
        )
        pstage[...] = jnp.zeros_like(pstage)
        for d in range(dp * NC):
            if d < 16:
                pstage[:, 0:C3] = top_s[16 * d : 16 * d + 16, :]
            else:
                rows = slice(16 * (d - 16), 16 * (d - 16) + 16)
                pstage[:, 0:C3] = h_s[rows, :] * sv_ref[0:1, :] - corr_s[rows, :]
            pstage[0:4, C3 : C3 + C2] = gw2_s[4 * d : 4 * d + 4, :]
            pstage[0:1, 768:896] = piece_of(prow, 72 * d, 72)
            point0[d % 2, d // 8, d // 4 % 2, d // 2 % 2] = low(pstage[...])
        point.advance(0)
        sum_finish(dp, False, acc, slots, copies)
        copies = sum_start(dp, True, acc, slots, ssend, srecv)
        point.advance(1)
        sum_finish(dp, True, acc, slots, copies)
        grad_w, gain1, shift1, flat, slope = first_grads(acc[...], moment_ref[...], psmall_ref[...], stats_ref[...])
        point.advance(2)
        stage[...] = rest.advance(4)
        point.advance(3)
        point_gradient(d_s, rel_ref, slots_ref, flat, slope, pg_o)
        pstage[...] = point.advance(4)

        full_rows = point_small_rows(grad_w, gain1, shift1, jnp.zeros((1, C2), F32), tot_s[...], jnp.zeros((1, D), F32))
        rank = chip(z, y, x) * NC + core
        own = jnp.zeros((1, 128), F32)
        for d in range(dp * NC):
            own = own + jnp.where(rank == d, piece_of(full_rows, 72 * d, 72), 0.0)
        pflat_o[0:1, :] = pstage[0:1, 768:896] + own
        bflat_o[0:1, :] = stage[12:13, 384:512]
        for j in range(C2 // 128):
            pflat_o[pl.ds(1 + j, 4, stride=2), :] = pstage[0:4, C3 + 128 * j : C3 + 128 * j + 128]
        for j in range(C3 // 128):
            pflat_o[pl.ds(9 + j, 16, stride=4), :] = pstage[:, 128 * j : 128 * j + 128]
        for j in range(D // 128):
            pflat_o[pl.ds(73 + j, 16, stride=3), :] = stage[:, 128 * j : 128 * j + 128]
        start = 1
        for name, at, cols in REST[1:4]:
            for j in range(cols // 128):
                bflat_o[pl.ds(start + j, 12, stride=cols // 128), :] = stage[0:12, at + 128 * j : at + 128 * j + 128]
            start += 12 * cols // 128
        for b in range(3):
            for j in range(D // 128):
                at = 3456 + D * b + 128 * j
                bflat_o[pl.ds(start + 48 * b + j, 16, stride=3), :] = stage[:, at : at + 128]


def backward_call(*args):
    dp = NZ * NY * NX
    count = args[24].shape[1]
    tokens, blocks, tiles = count // GROUP, count // GROUP // TB, count // TILE
    single = dict(pipeline_mode=pl.Buffered(1))
    full = lambda *s: pl.BlockSpec(s, lambda i: (0, 0), **single)
    chunk = lambda c: pl.BlockSpec((TB, c), lambda i: (jnp.minimum(i, blocks - 1), 0))
    rows = lambda c: pl.BlockSpec((TILE, c), lambda i: (jnp.maximum(i - blocks, 0), 0))
    cols = lambda r: pl.BlockSpec((r, TILE), lambda i: (0, jnp.maximum(i - blocks, 0)))
    specs = [chunk(C3), chunk(C3), chunk(C3), full(tokens, 128), pl.BlockSpec(memory_space=pltpu.SMEM), chunk(D)]
    specs += [full(*a.shape) for a in args[6:26]]
    specs += [rows(C3), rows(C2), cols(C2), cols(C1 + 16), cols(C1)]
    return pl.pallas_call(
        backward_kernel,
        grid=(blocks + tiles,),
        in_specs=specs,
        out_specs=[chunk(D), full(3, count), full(PROWS, 128), full(BROWS, 128)],
        out_shape=shaped(((tokens, D), F32), ((3, count), F32), ((PROWS, 128), F32), ((BROWS, 128), F32)),
        scratch_shapes=[
            pltpu.VMEM((C3, D), F32), pltpu.VMEM((D, 3 * D), F32), pltpu.VMEM((D, D), F32), pltpu.VMEM((D, FF), F32),
            pltpu.VMEM((FF, D), F32), pltpu.VMEM((8, FF), F32), pltpu.VMEM((tokens, C3), F32),
            pltpu.VMEM((tokens, C3), F32), pltpu.VMEM((8, C3), F32),
            pltpu.VMEM((TB, 3 * D), BF16), pltpu.VMEM((TB, D), BF16),
            pltpu.VMEM((TB // PAIR * HEADS, PAIR, PAIR), F32), pltpu.VMEM((TB, D), BF16), pltpu.VMEM((TB, 3 * D), BF16),
            pltpu.VMEM((8, 128), F32), pltpu.VMEM((tokens, C2), F32), pltpu.VMEM((C2, C2), BF16),
            pltpu.VMEM((C2, C3), BF16), pltpu.VMEM((C2, C3), F32), pltpu.VMEM((C2, C3), F32), pltpu.VMEM((C2, C3), F32),
            pltpu.VMEM((C1 + 16, C2), F32), pltpu.VMEM((8, C1), F32), pltpu.VMEM((8, count), F32),
            pltpu.VMEM((TILE, C3), BF16),
        ]
        + scatter_scratch(REST_WIDTH)
        + scatter_scratch(POINT_WIDTH)
        + [pltpu.VMEM((16, REST_WIDTH), F32), pltpu.VMEM((16, POINT_WIDTH), F32)]
        + sum_scratch(dp, (8, 128))
        + sum_scratch(dp, (8, 128))
        + [pltpu.SemaphoreType.DMA((2 * SCATTER_SEMS,)), pltpu.SemaphoreType.DMA((2 * SCATTER_SEMS,))],
        compiler_params=params(collective_id=3, has_side_effects=True),
        name="backward",
    )(*args)


def geometry_call(points, slots):
    outs = shaped(((8, points.shape[1]), BF16), ((8, 128), F32))
    return pl.pallas_call(
        geometry, out_shape=outs, in_specs=vmem(2), out_specs=vmem(2),
        compiler_params=params(), name="geometry",
    )(points, slots)


def gather_plain(points, slots, point_master, block_master, devices):
    rel, moments = geometry_call(points, slots)
    moments = lax.psum(moments, AXES)
    tables = []
    for master, layout in ((point_master, point_layout()), (block_master, block_layout())):
        offset = 0
        parts = []
        for segment, seg_len in zip(layout, segment_lengths(layout, devices)):
            piece = master[offset : offset + seg_len // devices].astype(BF16)
            offset += seg_len // devices
            parts.append(lax.all_gather(piece, AXES, axis=0, tiled=True))
        tables.append(parts)
    (ps, w2, w3, w4), (bs, wqkv, wo, wf1, wf2) = tables

    def rows_of(v, rows, used):
        v = v[:used].astype(F32).reshape(-1, 128)
        return jnp.concatenate([v, jnp.zeros((rows - v.shape[0], 128), F32)], axis=0)

    return (
        rel, moments, rows_of(ps, 24, 18 * 128), rows_of(bs, 32, 30 * 128),
        w2.reshape(C1, C2), w3.reshape(2 * C2, C3), w4.reshape(C3, D),
        wqkv.reshape(D, 3 * D), wo.reshape(D, D), wf1.reshape(D, FF), wf2.reshape(FF, D),
    )


def point_gradient_kernel(d_ref, rel_ref, slots_ref, table_ref, out_ref):
    flat = [table_ref[k : k + 1, 3:4] for k in range(3)]
    slope = [[table_ref[k : k + 1, j : j + 1] for j in range(3)] for k in range(3)]
    point_gradient(d_ref, rel_ref, slots_ref, flat, slope, out_ref)


def scatter_plain(
    devices, q, moments, psmall, stats, tot, small, d, rel, slots,
    gw2, top, h, corr, sv, gw4, gwqkv, gwo, gwf1, gwf2,
):
    q = lax.psum(q, AXES)
    grad_w, gain1, shift1, flat, slope = first_grads(q, moments, psmall, stats)
    table = jnp.concatenate([jnp.concatenate(slope[k] + [flat[k]], axis=1) for k in range(3)], axis=0)
    table = jnp.pad(table, ((0, 5), (0, 124)))
    point_grad = pl.pallas_call(
        point_gradient_kernel, out_shape=jax.ShapeDtypeStruct((3, d.shape[1]), F32),
        in_specs=vmem(4), out_specs=vmem(1)[0], compiler_params=params(), name="point_gradient",
    )(d, rel, slots, table)
    none = jnp.zeros((1, 128), F32)
    local = point_small_rows(
        [none] * 3, none, none, gw2[C1 : C1 + 1, :], jnp.zeros((8, 128), F32), small[6:7, 0:D]
    )
    known = point_small_rows(grad_w, gain1, shift1, jnp.zeros((1, C2), F32), tot, jnp.zeros((1, D), F32))
    w3 = jnp.concatenate([top, h * sv[0:1, :] - corr], axis=0)
    pieces = []
    for layout, tables in (
        (point_layout(), (local + known / devices, gw2[:C1], w3, gw4)),
        (block_layout(), (block_small_rows(small), gwqkv, gwo, gwf1, gwf2)),
    ):
        parts = []
        for values, seg_len in zip(tables, segment_lengths(layout, devices)):
            values = values.reshape(-1)
            values = jnp.concatenate([values, jnp.zeros((seg_len - values.shape[0],), F32)])
            parts.append(lax.psum_scatter(values, AXES, scatter_dimension=0, tiled=True))
        pieces.append(parts)
    return point_grad, pieces[0], pieces[1]


def adam_update(master, moment_one, moment_two, gradient, step_rates, decays):
    one_new = BETA_ONE * moment_one + (1.0 - BETA_ONE) * gradient
    two_new = BETA_TWO * moment_two + (1.0 - BETA_TWO) * gradient * gradient
    fix_one = 1.0 - BETA_ONE**STEP
    fix_two = 1.0 - BETA_TWO**STEP
    direction = one_new / fix_one / (jnp.sqrt(two_new / fix_two) + ADAM_EPS)
    master_new = master - step_rates * (direction + decays * master)
    return (master_new, one_new, two_new)


def flat_of(vector, small, rows):
    pad = jnp.zeros((128 - small,), F32)
    tail = jnp.zeros((rows * 128 - 128 - (vector.shape[0] - small),), F32)
    return jnp.concatenate([vector[:small], pad, vector[small:], tail]).reshape(rows, 128)


def on_device(
    points, point_count, centre_slot, cloud_length, cotangent, point_master, block_master,
    point_first, block_first, point_second, block_second,
):
    dp, fsdp = lax.axis_size("dp"), lax.axis_size("fsdp")
    devices = dp * fsdp
    own_rank = lax.axis_index(AXES)
    known = dp == NZ * NY * NX and fsdp == NC
    slots = jnp.repeat(jnp.stack([point_count, centre_slot]), GROUP, axis=1)
    if known:
        (
            rel, moments, psmall, bsmall, w2, w3, w4, wqkv, wo, wf1, wf2, ext, gp1, f, ft,
            gram, fs, cnt, gm, fw, pooled, sv, stats, wd, gp, pa, pg, pc,
        ) = forward_call(points, slots, flat_of(point_master, 72, PROWS), flat_of(block_master, 120, BROWS))
    else:
        rel, moments, psmall, bsmall, w2, w3, w4, wqkv, wo, wf1, wf2 = gather_plain(
            points, slots, point_master, block_master, devices
        )
        ext, gp1, f, ft, gram, fs, cnt, g, fw, pooled, sums, stats, wd = first_call(rel, moments, psmall, w2, w3)
        gm, sv = third_call(dp, sums, g, stats, psmall)
        gp, pa, pg, pc = second_call(f, rel, w3, gm, sv)
    if known:
        tokens_out, point_grad, pflat, bflat = backward_call(
            pa, pg, pc, cnt, cloud_length, cotangent, psmall, bsmall, sv, stats, moments,
            w2, w3, w4, wqkv, wo, wf1, wf2, fs, fw, gm, pooled, gram, wd, rel, slots, gp, f, ft, ext, gp1,
        )
        pflat, bflat = pflat.reshape(-1), bflat.reshape(-1)
        block_small = bflat[:120]
        point_gradient_vec = jnp.concatenate([pflat[:72], pflat[128 : 128 + point_master.shape[0] - 72]])
        block_gradient = jnp.concatenate([block_small, bflat[128 : 128 + block_master.shape[0] - 120]])
    else:
        tokens_out, gw4, gwqkv, gwo, gwf1, gwf2, small, tok, tg, back = block_call(
            pa, pg, pc, cnt, cloud_length, cotangent, psmall, bsmall, sv, w4, wqkv, wo, wf1, wf2
        )
        tot, tok_low, kap, k, ws, top, corr = third_back_call(
            dp, back, tok, tg, fs, fw, gm, cnt, pooled, gram, w3, sv, stats
        )
        h, gw2, q, d = last_call(gp, f, ft, ext, gp1, rel, tok_low, kap, k, ws, w2, wd)
        point_grad, point_parts, block_parts = scatter_plain(
            devices, q, moments, psmall, stats, tot, small, d, rel, slots,
            gw2, top, h, corr, sv, gw4, gwqkv, gwo, gwf1, gwf2,
        )
        block_small = block_parts[0]
        point_gradient_vec = jnp.concatenate(point_parts)
        block_gradient = jnp.concatenate(block_parts)
    point_rates, point_decays = shard_rates(point_layout(), devices, own_rank)
    block_rates, block_decays = shard_rates(block_layout(), devices, own_rank)
    point_new, point_one, point_two = adam_update(
        point_master, point_first, point_second, point_gradient_vec, point_rates, point_decays
    )
    block_new, block_one, block_two = adam_update(
        block_master, block_first, block_second, block_gradient, block_rates, block_decays
    )
    return (
        tokens_out, point_grad, point_new, block_new, point_one, block_one, point_two, block_two,
        point_new.astype(BF16), block_new.astype(BF16), block_small,
    )


def solution(mesh):
    split = P(AXES)
    return jax.shard_map(
        on_device,
        mesh=mesh,
        in_specs=(P(None, AXES), split, split, split, P(AXES, None)) + (split,) * 6,
        out_specs=(P(AXES, None), P(None, AXES)) + (split,) * 9,
        check_vma=False,
    )
```

```python
import functools
import math

import jax
import jax.numpy as jnp
from jax import lax
from jax.experimental import pallas as pl
from jax.experimental.pallas import tpu as pltpu
from jax.sharding import PartitionSpec as P

C1 = 128
C2 = 256
C3 = 512
D = 384
HEADS = 6
HEAD_DIM = 64
FF = 1536
GROUP = 32
PATCHES = 64
STEP = 10

EPS_NORM = 1e-05
BETA_ONE = 0.9
BETA_TWO = 0.95
ADAM_EPS = 1e-08
DECAY_RATE = 0.05
NEG_FILL = -1e30

F32 = jnp.float32
BF16 = jnp.bfloat16
AXES = ("dp", "fsdp")
MESH = pl.DeviceIdType.MESH
VMEM_LIMIT = 60 * 2**20
TILE = 2048
TOK = TILE // GROUP
TB = 256
PAIR = 128

NZ, NY, NX, NC = 4, 2, 2, 2
PROWS, BROWS = 128, 440
PSMALL, BSMALL = 72, 120


def point_layout():
    return [
        [
            ("w1", (3, C1), 3.0 ** (-0.5)),
            ("bn1_gain", (C1,), 0.0),
            ("bn1_shift", (C1,), -1.0),
            ("b2", (C2,), -1.0),
            ("bn3_gain", (C3,), 0.0),
            ("bn3_shift", (C3,), -1.0),
            ("b4", (D,), -1.0),
        ],
        [("w2", (C1, C2), C1 ** (-0.5))],
        [("w3", (2 * C2, C3), (2 * C2) ** (-0.5))],
        [("w4", (C3, D), C3 ** (-0.5))],
    ]


def block_layout():
    return [
        [
            ("ln1_gain", (D,), 0.0),
            ("ln1_shift", (D,), -1.0),
            ("bo", (D,), -1.0),
            ("ln2_gain", (D,), 0.0),
            ("ln2_shift", (D,), -1.0),
            ("bf1", (FF,), -1.0),
            ("bf2", (D,), -1.0),
        ],
        [("wqkv", (D, 3 * D), D ** (-0.5))],
        [("wo", (D, D), 3.0 * D ** (-0.5))],
        [("wf1", (D, FF), D ** (-0.5))],
        [("wf2", (FF, D), FF ** (-0.5))],
    ]


def rate_for(spread):
    return 2.0 * spread if spread > 0.0 else 0.5 if spread == 0.0 else 0.6


def decay_for(spread):
    return DECAY_RATE if spread > 0.0 else 0.0


def segment_lengths(layout, devices):
    lengths_out = []
    for segment in layout:
        used_len = sum((math.prod(entry[1]) for entry in segment))
        lengths_out.append(-(-used_len // devices) * devices)
    return lengths_out


def shard_rates(layout, devices, own_rank):
    rate_parts = []
    decay_parts = []
    for segment, seg_len in zip(layout, segment_lengths(layout, devices)):
        piece_len = seg_len // devices
        position = own_rank * piece_len + jnp.arange(piece_len, dtype=jnp.int32)
        seg_rates = jnp.zeros((piece_len,), F32)
        seg_decays = jnp.zeros((piece_len,), F32)
        offset = 0
        for entry_label, entry_dims, spread in segment:
            extent = math.prod(entry_dims)
            inside = (position >= offset) & (position < offset + extent)
            seg_rates = jnp.where(inside, rate_for(spread), seg_rates)
            seg_decays = jnp.where(inside, decay_for(spread), seg_decays)
            offset += extent
        rate_parts.append(seg_rates)
        decay_parts.append(seg_decays)
    return (jnp.concatenate(rate_parts), jnp.concatenate(decay_parts))


def mm(a, b):
    return jnp.dot(a, b, preferred_element_type=F32)


def mm_tn(a, b):
    return lax.dot_general(a, b, (((0,), (0,)), ((), ())), preferred_element_type=F32)


def mm_nt(a, b):
    return lax.dot_general(a, b, (((1,), (1,)), ((), ())), preferred_element_type=F32)


def low(v):
    return v.astype(BF16)


def split_three(v):
    hi = low(v)
    rest = v - hi.astype(F32)
    mid = low(rest)
    return hi, mid, low(rest - mid.astype(F32))


def mm_exact(a, b):
    hi, mid, lo = split_three(a)
    return mm(hi, b) + (mm(mid, b) + mm(lo, b))


LAM = (math.sqrt(2.0 / math.pi) * 0.044715) ** (-1.0 / 3.0)
ARG = math.sqrt(2.0 / math.pi) * LAM


def gelu_twice(y):
    square = y * y
    near = square + ARG
    t = jnp.tanh(y * near)
    up = 1.0 + t
    g = y * up
    return g, up + g * (1.0 - t) * (near + (square + square))


def gelu_pair(v):
    g, d = gelu_twice(v * (1.0 / LAM))
    return (0.5 * LAM) * g, 0.5 * d


def patch_ones():
    i = lax.broadcasted_iota(jnp.int32, (256, 256), 0) // GROUP
    j = lax.broadcasted_iota(jnp.int32, (256, 256), 1) // GROUP
    return (i == j).astype(F32).astype(BF16)


def token_ones():
    t = lax.broadcasted_iota(jnp.int32, (TOK, TILE), 0)
    p = lax.broadcasted_iota(jnp.int32, (TOK, TILE), 1) // GROUP
    return (t == p).astype(F32).astype(BF16)


def patch_sum(rows, ones):
    return mm_exact(rows, ones)


def rank_of(peer_dp, peer_core):
    return peer_dp * NC + peer_core


def me():
    return rank_of(lax.axis_index("dp"), lax.axis_index("fsdp"))


def all_peers(dp):
    n = dp * NC
    peers = []
    for k in range(1, n):
        p = lax.rem(me() + k, n)
        peers.append((p // NC, lax.rem(p, NC)))
    return peers


def greet(peers):
    barrier = pltpu.get_barrier_semaphore()
    for peer in peers:
        pl.semaphore_signal(barrier, inc=1, device_id=peer, device_id_type=MESH)


def greeted(peers):
    pl.semaphore_wait(pltpu.get_barrier_semaphore(), len(peers))


def send_to_all(dp, src, dst_of, send, recv):
    copies = []
    for k, peer in enumerate(all_peers(dp)):
        copy = pltpu.make_async_remote_copy(
            src_ref=src, dst_ref=dst_of(k), send_sem=send.at[k], recv_sem=recv.at[k],
            device_id=peer, device_id_type=MESH,
        )
        copy.start()
        copies.append(copy)
    return copies


def sum_start(dp, acc, slots, send, recv):
    return send_to_all(dp, acc, lambda k: slots.at[k], send, recv)


def sum_finish(acc, slots, copies):
    for copy in copies:
        copy.wait()
    return acc[...] + jnp.sum(slots[...], axis=0)


def sum_scratch(dp):
    n = dp * NC - 1
    return [
        pltpu.VMEM((8, 128), F32), pltpu.VMEM((n, 8, 128), F32),
        pltpu.SemaphoreType.DMA((n,)), pltpu.SemaphoreType.DMA((n,)),
    ]


def as_rows(*vectors):
    return jnp.concatenate(
        [v[:, 128 * k : 128 * k + 128] for v in vectors for k in range(v.shape[1] // 128)], axis=0
    )


def as_vector(rows, first, count):
    return jnp.concatenate([rows[k : k + 1, :] for k in range(first, first + count)], axis=1)


def vmem(count):
    return [pl.BlockSpec(memory_space=pltpu.VMEM)] * count


def shaped(*items):
    return [jax.ShapeDtypeStruct(s, t) for s, t in items]


def params(**more):
    return pltpu.CompilerParams(vmem_limit_bytes=VMEM_LIMIT, **more)


def where_am_i():
    at = lax.axis_index("dp")
    return at // (NY * NX), lax.rem(at // NX, NY), lax.rem(at, NX), lax.axis_index("fsdp")


def chip(z, y, x):
    return (z * NY + y) * NX + x


def spread_tokens(values):
    t = lax.broadcasted_iota(jnp.int32, (8, 256), 0)
    p = lax.broadcasted_iota(jnp.int32, (8, 256), 1) // GROUP
    return mm(low(values.astype(F32)), low((t == p).astype(F32)))


def geometry(points_ref, tokens_ref, rel_ref, counts_s, picked_s):
    pieces = points_ref.shape[1] // 256
    lane = lax.rem(lax.broadcasted_iota(jnp.int32, (1, 256), 1), GROUP).astype(F32)
    counts_s[...] = spread_tokens(tokens_ref[...])
    for i in range(pieces):
        at = slice(256 * i, 256 * i + 256)
        pick = (lane == counts_s[pieces + i : pieces + i + 1, :]).astype(F32)
        rows = points_ref[:, at] * pick
        picked_s[8 * i : 8 * i + 8, :] = jnp.concatenate([rows, jnp.zeros((5, 256), F32)], axis=0)
    picked_s[...] = patch_sum(picked_s[...], patch_ones())
    for i in range(pieces):
        at = slice(256 * i, 256 * i + 256)
        valid = (lane < counts_s[i : i + 1, :]).astype(F32)
        relative = (points_ref[:, at] - picked_s[8 * i : 8 * i + 3, :]) * valid
        rel_ref[:, at] = low(jnp.concatenate([relative, valid, relative, valid], axis=0))
    rel = rel_ref[...]
    return mm_nt(rel, rel)


def prepare_one(moments, small):
    n = moments[3:4, 3:4]
    w = [small[k : k + 1, :] for k in range(3)]
    gain, shift = small[3:4, :], small[4:5, :]
    mean = sum(w[k] * moments[k : k + 1, 3:4] for k in range(3)) / n
    square = jnp.zeros_like(mean)
    for j in range(3):
        for k in range(3):
            square = square + w[j] * w[k] * moments[j : j + 1, k : k + 1]
    inverse = lax.rsqrt(square / n - mean * mean + EPS_NORM)
    scale = inverse * gain
    scaled = [wk * scale for wk in w]
    parts = [v * (1.0 / LAM) for v in scaled + [shift - mean * scale]]
    high = [low(v) for v in parts]
    rest = [low(v - h.astype(F32)) for v, h in zip(parts, high)]
    forward = jnp.concatenate(high + rest, axis=0)
    high = [low(v) for v in scaled]
    rest = [low(v - h.astype(F32)) for v, h in zip(scaled, high)]
    zero = jnp.zeros((1, C1), BF16)
    backward = jnp.concatenate(high + [zero] + rest + [zero], axis=0)
    stats = jnp.concatenate(
        [mean, inverse, jnp.broadcast_to(n, (1, C1)), scale, jnp.zeros((4, C1), F32)], axis=0
    )
    return forward, backward, stats


def flat_rows(pieces, length, rows):
    lane = lax.broadcasted_iota(jnp.int32, (1, 128), 1)
    out = [jnp.zeros((1, 128), F32) for _ in range(rows)]
    for r in range(pieces.shape[0]):
        row = jnp.where(lane < length, pieces[r : r + 1, :], 0.0)
        at = length * r
        row = pltpu.roll(row, at % 128, 1) if at % 128 else row
        first = at // 128
        out[first] = out[first] + jnp.where(lane >= at % 128, row, 0.0)
        if at % 128 + length > 128:
            out[first + 1] = out[first + 1] + jnp.where(lane < at % 128, row, 0.0)
    return jnp.concatenate(out, axis=0)


def piece_of(rows, at, length):
    lane = lax.broadcasted_iota(jnp.int32, (1, 128), 1)
    first, shift = at // 128, at % 128
    row = rows[first : first + 1, :]
    if shift:
        row = pltpu.roll(row, 128 - shift, 1)
        if shift + length > 128:
            other = pltpu.roll(rows[first + 1 : first + 2, :], 128 - shift, 1)
            row = jnp.where(lane < 128 - shift, row, other)
    return jnp.where(lane < length, row, 0.0)


def segments_apart(flat, small):
    lane = lax.broadcasted_iota(jnp.int32, (1, 128), 1)
    turned = pltpu.roll(flat, 128 - small, 1)
    return jnp.where(lane < 128 - small, pltpu.roll(turned, 1, 0), turned)


def segments_joined(rows, first, small):
    lane = lax.broadcasted_iota(jnp.int32, (1, 128), 1)
    turned = pltpu.roll(rows, small, 1)
    row = lax.broadcasted_iota(jnp.int32, (rows.shape[0], 1), 0)
    joined = jnp.where(lane < small, turned, pltpu.roll(turned, rows.shape[0] - 1, 0))
    return jnp.where((lane < small) & (row == 0), first, joined)


def first_tile(rel, wn, ext_ref, gp_ref):
    valid = rel[3:4, :].astype(F32)
    for j in range(TILE // 256):
        at = slice(256 * j, 256 * j + 256)
        g, d = gelu_twice(mm_tn(wn, rel[:, at]))
        ext_ref[0:C1, at] = low(g * (valid[:, at] * (0.5 * LAM)))
        gp_ref[:, at] = low(d * (valid[:, at] * 0.5))
    ext_ref[C1:, :] = jnp.concatenate([rel[3:4], jnp.zeros((15, TILE), BF16)], axis=0)


def first_tokens(gext, ps_ref, w2e, w3_ref, pooled_o, gm_o, fw_o):
    lower = w3_ref[C2:, :]
    count = ps_ref[:, C1 : C1 + 1]
    fs = mm_exact(ps_ref[:, 0 : C1 + 16], w2e)
    pooled = low(fs / count)
    pooled_o[...] = pooled
    g = mm(pooled, w3_ref[0:C2, :])
    gm_o[...] = g
    fw = mm_exact(fs, lower)
    fw_o[...] = fw
    gram = sum(mm_tn(w2e, part) for part in split_three(mm_exact(gext, w2e)))
    one = jnp.sum(fw + count * g, axis=0, keepdims=True)
    two = jnp.sum(mm_exact(gram, lower) * lower.astype(F32), axis=0, keepdims=True)
    two = two + jnp.sum(g * (2.0 * fw + count * g), axis=0, keepdims=True)
    return as_rows(one, two)


def third_vectors(totals, n, psmall_ref):
    mean = as_vector(totals, 0, 4) / n
    inverse = lax.rsqrt(as_vector(totals, 4, 4) / n - mean * mean + EPS_NORM)
    gain, shift = as_vector(psmall_ref, 7, 4), as_vector(psmall_ref, 11, 4)
    return jnp.concatenate([inverse * gain, shift, mean, inverse, jnp.zeros((4, C3), F32)], axis=0)


def second_tile(act, mask, w23, gm, sv_ref, gp_o, pa_o, pg_o, pc_o, first):
    scale, shift = low(sv_ref[0:1, :] * (1.0 / LAM)), low(sv_ref[1:2, :] * (1.0 / LAM))
    turned = act.T
    c = mm(jnp.concatenate([turned, turned], axis=1), w23).reshape(TOK, GROUP, C3) + gm[:, None, :]
    c = low(c)
    g, gp = gelu_twice(c * scale[None] + shift[None])
    gc = (gp * c).reshape(TILE, C3)
    gp = gp.reshape(TILE, C3)
    gp_o[...] = gp
    g = g.reshape(TILE, C3)
    for q in range(TILE // 256):
        to = pl.ds(pl.multiple_of(first + 8 * q, 8), 8)
        at = slice(256 * q, 256 * q + 256)
        m = mask[8 * q : 8 * q + 8, at]
        pa_o[to, :] = mm(m, g[at]) * (0.5 * LAM)
        pg_o[to, :] = mm(m, gp[at]) * 0.5
        pc_o[to, :] = mm(m, gc[at]) * 0.5


class Gather:
    def __init__(self, blocks, send, recv, base):
        self.blocks, self.sems, self.base = blocks, (send, recv), base
        z, y, x, core = where_am_i()
        half = blocks.shape[-1] // 2
        one, two = pl.ds(0, half), pl.ds(half, half)
        every = slice(None)
        near = [(chip(lax.rem(z + k, NZ), y, x), core) for k in range(1, NZ)]
        over_y, over_x, twin = (chip(z, 1 - y, x), core), (chip(z, y, 1 - x), core), (chip(z, y, x), 1 - core)
        self.stages = [
            [((z, y, x, core), peer) for peer in near],
            [((every, y, x, core, every, one), over_y), ((every, y, x, core, every, two), over_x)],
            [((every, every, x, core, every, one), over_x), ((every, y, every, core, every, two), over_y)],
            [],
        ]
        self.inner = [
            [],
            [((every, y, x, core), twin)],
            [((every, 1 - y, x, core, every, one), twin), ((every, y, 1 - x, core, every, two), twin)],
            [((every, every, 1 - x, core, every, one), twin), ((every, 1 - y, every, core, every, two), twin)],
        ]

    def copies(self, stage, inner):
        table = self.inner if inner else self.stages
        k = self.base + (7 if inner else 0) + sum(len(s) for s in table[:stage])
        out = []
        for i, (index, peer) in enumerate(table[stage]):
            view = self.blocks.at[index]
            out.append(
                pltpu.make_async_remote_copy(
                    src_ref=view, dst_ref=view, send_sem=self.sems[0].at[k + i], recv_sem=self.sems[1].at[k + i],
                    device_id=peer, device_id_type=MESH,
                )
            )
        return out

    def advance(self, stage):
        if stage > 0:
            for copy in self.copies(stage - 1, False):
                copy.wait()
        if stage < 4:
            for copy in self.copies(stage, False) + self.copies(stage, True):
                copy.start()
        else:
            for inner_stage in range(4):
                for copy in self.copies(inner_stage, True):
                    copy.wait()


GATHER_SEMS = 12
W4_AT, QKV_AT, WO_AT, WF1_AT, WF2_AT, REST_WIDTH = 0, 384, 1536, 1920, 3456, 3840
UNDER = [("wqkv", QKV_AT, 3 * D), ("wo", WO_AT, D), ("wf1", WF1_AT, FF)]


def rest_wf2(d):
    out = [(48 * d, 16, 0, WF2_AT)]
    out += [(48 * d + 16 + 4 * j, 4, 12, QKV_AT + D * j) for j in range(8)]
    return out


def place(d):
    return d // 8, d // 4 % 2, d // 2 % 2, d % 2


def forward_kernel(known, dp, *refs):
    refs = list(refs)
    take = lambda count: [refs.pop(0) for _ in range(count)]
    points_ref, tokens_ref, pflat, bflat = take(4) if known else [None] * 4
    rel_o, moment_o, psmall_o, bsmall_o, w2_o, w3_o = take(6)
    w4_o, wqkv_o, wo_o, wf1_o, wf2_o = take(5) if known else [None] * 5
    ext_o, gp1_o, g_o, ps_o, gm_o, fw_o, pooled_o, sv_o, stats_o, wd_o, w23_o, gp_o, pa_o, pg_o, pc_o = take(15)
    ext_s, e_s, wn_s, w2_s, w23_s, acc3, sums3, ssend3, srecv3 = take(9)
    step = pl.program_id(0)
    tiles = pl.num_programs(0) // 2
    peers = all_peers(dp)
    if known:
        (
            tiny, rest, three, stage, wide, flat2, pal, bal, counts_s, picked_s,
            tsend, trecv, gsend, grecv,
        ) = take(14)
        z, y, x, core = where_am_i()
        gather_w3 = Gather(three, gsend, grecv, 0)
        gather_rest = Gather(rest, gsend, grecv, GATHER_SEMS)

    @pl.when(step == 0)
    def _():
        greet(peers)
        g_o[...] = jnp.zeros_like(g_o)
        e_s[...] = token_ones()
        if known:
            pal[...] = segments_apart(pflat[...], PSMALL)
            bal[...] = segments_apart(bflat[...], BSMALL)
            for j in range(C3 // 128):
                three[z, y, x, core, :, 128 * j : 128 * j + 128] = low(pal[pl.ds(9 + j, 16, stride=C3 // 128), :])
            for j in range(D // 128):
                stage[:, 128 * j : 128 * j + 128] = pal[pl.ds(73 + j, 16, stride=D // 128), :]
            start = 1
            for name, at, cols in UNDER:
                for j in range(cols // 128):
                    stage[0:12, at + 128 * j : at + 128 * j + 128] = bal[pl.ds(start + j, 12, stride=cols // 128), :]
                start += 12 * cols // 128
            for row, rows, under, at in rest_wf2(0):
                for j in range(D // 128):
                    stage[under : under + rows, at + 128 * j : at + 128 * j + 128] = bal[
                        pl.ds(start + 3 * row + j, rows, stride=3), :
                    ]
            rest[z, y, x, core] = low(stage[...])
            moments = geometry(points_ref, tokens_ref, rel_o, counts_s, picked_s)[0:4, :]
            moments = jnp.concatenate([moments, jnp.zeros((4, 120), F32)], axis=1)
            hi, mid, lo = [part.astype(F32) for part in split_three(moments)]
            packed = hi + pltpu.roll(mid, 8, 1) + pltpu.roll(lo, 16, 1)
            rows = [pal[1:9, :], pflat[0:1, :], bflat[0:1, :], packed, jnp.zeros((2, 128), F32)]
            own = tiny.at[me()]
            own[...] = low(jnp.concatenate(rows, axis=0))
            greeted(peers)
            for copy in send_to_all(dp, own, lambda k: own, tsend, trecv):
                copy.wait()
            gather_w3.advance(0)
            gather_rest.advance(0)
            psmall, bsmall = [], []
            packed = jnp.zeros((4, 128), F32)
            for d in range(dp * NC):
                rows = tiny[d].astype(F32)
                flat2[8 * d : 8 * d + 8, :] = rows[0:8, :]
                psmall.append(rows[8:9, :])
                bsmall.append(rows[9:10, :])
                packed = packed + rows[10:14, :]
            total = packed + pltpu.roll(packed, 120, 1) + pltpu.roll(packed, 112, 1)
            moment_o[...] = jnp.concatenate([total, jnp.zeros((4, 128), F32)], axis=0)
            psmall_o[0:18, :] = flat_rows(jnp.concatenate(psmall, axis=0), PSMALL, 18)
            bsmall_o[0:30, :] = flat_rows(jnp.concatenate(bsmall, axis=0), BSMALL, 30)
            for j in range(2):
                w2_o[:, 128 * j : 128 * j + 128] = low(flat2[pl.ds(j, C1, stride=2), :])
        else:
            greeted(peers)
        small = psmall_o[...]
        forward, backward, stats = prepare_one(moment_o[:, 0:8], small)
        wn_s[...] = forward
        wd_o[...] = backward
        stats_o[...] = stats
        w2_s[0:C1, :] = w2_o[...]
        b2 = as_vector(small, 5, 2)
        w2_s[C1:, :] = low(jnp.concatenate([b2, jnp.zeros((15, C2), F32)], axis=0))

    if known:
        for at_step, gather, number in (
            (2, gather_w3, 1), (3, gather_w3, 2), (5, gather_w3, 3), (6, gather_rest, 1), (7, gather_w3, 4),
            (8, gather_rest, 2), (12, gather_rest, 3),
        ):
            pl.when(step == at_step)(functools.partial(gather.advance, number))

    at = pl.ds(pl.multiple_of(lax.rem(step, tiles) * TILE, TILE), TILE)
    rel = rel_o[:, at]
    first = pl.multiple_of(lax.rem(step, tiles) * TOK, TOK)

    @pl.when(step < tiles)
    def _():
        first_tile(rel, wn_s[...], ext_o, gp1_o)
        ext = ext_o[...]
        ext_s[:, at] = ext[0:C1]
        both = mm_nt(jnp.concatenate([ext, e_s[...]], axis=0), ext)
        g_o[:, 0 : C1 + 16] += both[0 : C1 + 16]
        ps_o[pl.ds(first, TOK), 0 : C1 + 16] = both[C1 + 16 :]

    @pl.when(step == tiles)
    def _():
        if known:
            for d in range(dp * NC):
                w3_o[16 * d : 16 * d + 16, :] = three[place(d)]
        acc3[...] = first_tokens(g_o[:, 0 : C1 + 16], ps_o, w2_s[...], w3_o, pooled_o, gm_o, fw_o)
        copies = sum_start(dp, acc3, sums3, ssend3, srecv3)
        w23 = mm(w2_s[...], w3_o[C2:, :])
        w23_o[...] = w23
        high = low(w23[0:C1])
        w23_s[0:C1, :] = high
        w23_s[C1:, :] = low(w23[0:C1] - high.astype(F32))
        sv_o[...] = third_vectors(sum_finish(acc3, sums3, copies), stats_o[2:3, 0:1], psmall_o)
        mean = sv_o[2:3, :]
        gm = gm_o[...] - mean
        fw_o[...] = fw_o[...] + ps_o[:, C1 : C1 + 1] * gm
        gm_o[...] = gm + w23[C1 : C1 + 1, :]

    @pl.when(step >= tiles)
    def _():
        second_tile(
            ext_s[:, at], e_s[...] * rel[3:4, :], w23_s[...], gm_o[pl.ds(first, TOK), :], sv_o,
            gp_o, pa_o, pg_o, pc_o, first,
        )

    if known:

        @pl.when(step == 2 * tiles - 1)
        def _():
            gather_rest.advance(4)
            for d in range(dp * NC):
                block = rest.at[place(d)]
                w4_o[16 * d : 16 * d + 16, :] = block[:, W4_AT : W4_AT + D]
                wf2_o[48 * d : 48 * d + 16, :] = block[:, WF2_AT : WF2_AT + D]
                under = block[:, QKV_AT:WF2_AT].astype(F32)
                wide[12 * d : 12 * d + 12, :] = under[0:12, :]
                tail = [under[12:16, D * j : D * j + D] for j in range(8)]
                wf2_o[48 * d + 16 : 48 * d + 48, :] = low(jnp.concatenate(tail, axis=0))
            for (name, at_col, cols), out in zip(UNDER, (wqkv_o, wo_o, wf1_o)):
                out[...] = low(wide[:, at_col - QKV_AT : at_col - QKV_AT + cols])


def forward_call(known, dp, count, *args):
    tokens, tiles = count // GROUP, count // TILE
    single = dict(pipeline_mode=pl.Buffered(1))
    full = lambda *s: pl.BlockSpec(s, lambda i: (0, 0), **single)
    early = lambda r: pl.BlockSpec((r, TILE), lambda i: (0, jnp.minimum(i, tiles - 1)))
    given = [
        ((8, count), BF16), ((8, 128), F32), ((24, 128), F32), ((32, 128), F32), ((C1, C2), BF16), ((2 * C2, C3), BF16),
    ]
    gathered = [((C3, D), BF16), ((D, 3 * D), BF16), ((D, D), BF16), ((D, FF), BF16), ((FF, D), BF16)]
    outs = [(full(*s), s, t) for s, t in given + gathered] if known else []
    outs += [(early(C1 + 16), (C1 + 16, count), BF16), (early(C1), (C1, count), BF16)]
    outs += [
        (full(*s), s, t)
        for s, t in (
            ((C1 + 16, 256), F32), ((tokens, 256), F32), ((tokens, C3), F32), ((tokens, C3), F32),
            ((tokens, C2), BF16), ((8, C3), F32), ((8, C1), F32), ((8, C1), BF16), ((C1 + 16, C3), F32),
        )
    ]
    outs += [(pl.BlockSpec((TILE, C3), lambda i: (jnp.maximum(i - tiles, 0), 0)), (count, C3), BF16)]
    outs += [(full(tokens, C3), (tokens, C3), F32)] * 3
    scratch = [
        pltpu.VMEM((C1, count), BF16), pltpu.VMEM((TOK, TILE), BF16), pltpu.VMEM((8, C1), BF16),
        pltpu.VMEM((C1 + 16, C2), BF16), pltpu.VMEM((2 * C1, C3), BF16),
    ] + sum_scratch(dp)
    if known:
        n = dp * NC
        scratch += [
            pltpu.VMEM((n, 16, 128), BF16),
            pltpu.VMEM((NZ, NY, NX, NC, 16, REST_WIDTH), BF16),
            pltpu.VMEM((NZ, NY, NX, NC, 16, C3), BF16),
            pltpu.VMEM((16, REST_WIDTH), F32),
            pltpu.VMEM((D, WF2_AT - QKV_AT), F32),
            pltpu.VMEM((8 * n, 128), F32),
            pltpu.VMEM((PROWS, 128), F32), pltpu.VMEM((BROWS, 128), F32),
            pltpu.VMEM((count // 128, 256), F32), pltpu.VMEM((count // 32, 256), F32),
            pltpu.SemaphoreType.DMA((n - 1,)), pltpu.SemaphoreType.DMA((n - 1,)),
            pltpu.SemaphoreType.DMA((2 * GATHER_SEMS,)), pltpu.SemaphoreType.DMA((2 * GATHER_SEMS,)),
        ]
    return pl.pallas_call(
        functools.partial(forward_kernel, known, dp),
        grid=(2 * tiles,),
        in_specs=[full(*a.shape) for a in args],
        out_specs=[o[0] for o in outs],
        out_shape=shaped(*[o[1:] for o in outs]),
        scratch_shapes=scratch,
        compiler_params=params(collective_id=0, has_side_effects=True),
        name="forward",
    )(*args)


def wide_row(ref, first, rows):
    return jnp.concatenate([ref[k : k + 1, :] for k in range(first, first + rows)], axis=1)


def layer_norm(v, gain, shift):
    centred = v - jnp.mean(v, -1, keepdims=True)
    inverse = lax.rsqrt(jnp.mean(centred * centred, -1, keepdims=True) + EPS_NORM)
    unit = centred * inverse
    return unit, inverse, low(unit * gain + shift)


def norm_back(d_unit, unit, inverse):
    return inverse * (
        d_unit - jnp.mean(d_unit, -1, keepdims=True) - unit * jnp.mean(d_unit * unit, -1, keepdims=True)
    )


def col_sum(v):
    return jnp.sum(v, axis=0, keepdims=True)


def block_kernel(
    pa_ref, pg_ref, pc_ref, cnt_ref, len_ref, cot_ref, psmall_ref, bsmall_ref, sv_ref,
    w4_ref, wqkv_ref, wo_ref, wf1_ref, wf2_ref,
    out_o, gw4_o, gwqkv_o, gwo_o, gwf1_o, gwf2_o, small_o, tok_o, tg_o, back_o,
    qkv_s, mixed_s, soft_s, dmix_s, dqkv_s,
):
    step = pl.program_id(0)

    @pl.when(step == 0)
    def _():
        for ref in (gw4_o, gwqkv_o, gwo_o, gwf1_o, gwf2_o, small_o, back_o):
            ref[...] = jnp.zeros_like(ref)

    count = cnt_ref[:, C1 : C1 + 1]
    scale = HEAD_DIM ** (-0.5)
    b4 = wide_row(psmall_ref, 15, 3)
    ln1_gain, ln1_shift, bo = wide_row(bsmall_ref, 0, 3), wide_row(bsmall_ref, 3, 3), wide_row(bsmall_ref, 6, 3)
    ln2_gain, ln2_shift = wide_row(bsmall_ref, 9, 3), wide_row(bsmall_ref, 12, 3)
    bf1, bf2 = wide_row(bsmall_ref, 15, 12), wide_row(bsmall_ref, 27, 3)

    act = low(pa_ref[...] / count)
    x_zero = mm(act, w4_ref[...]) + b4
    unit_a, inv_a, normed_a = layer_norm(x_zero, ln1_gain, ln1_shift)
    qkv_s[...] = low(mm(normed_a, wqkv_ref[...]))

    row_cloud = lax.broadcasted_iota(jnp.int32, (PAIR, PAIR), 0) // PATCHES
    col = lax.broadcasted_iota(jnp.int32, (PAIR, PAIR), 1)
    left = lax.broadcasted_iota(jnp.int32, (1, 128), 1) < HEAD_DIM
    zero = jnp.zeros((1, 1), BF16)

    def halves(v):
        return jnp.where(left, v, zero), jnp.where(left, zero, v)

    tiles = TB // PAIR
    for s in range(tiles):
        first = (step * tiles + s) * 2
        visible = (row_cloud == col // PATCHES) & (
            lax.rem(col, PATCHES) < jnp.where(col < PATCHES, len_ref[first], len_ref[first + 1])
        )
        rows = slice(PAIR * s, PAIR * s + PAIR)
        for p in range(HEADS // 2):
            at = 128 * p
            q = qkv_s[rows, at : at + 128]
            k = qkv_s[rows, D + at : D + at + 128]
            v = qkv_s[rows, 2 * D + at : 2 * D + at + 128]
            mixed = []
            for a, q_half in enumerate(halves(q)):
                score = jnp.where(visible, mm_nt(q_half, k) * scale, NEG_FILL)
                raised = jnp.exp(score - jnp.max(score, -1, keepdims=True))
                soft = raised / jnp.sum(raised, -1, keepdims=True)
                soft_s[(s * (HEADS // 2) + p) * 2 + a] = soft
                mixed.append(mm(low(soft), v))
            mixed_s[rows, at : at + 128] = low(jnp.where(left, mixed[0], mixed[1]))

    mixed_low = mixed_s[...]
    x_one = x_zero + mm(mixed_low, wo_ref[...]) + bo
    unit_b, inv_b, normed_b = layer_norm(x_one, ln2_gain, ln2_shift)
    hidden, d_hidden = gelu_pair(mm(normed_b, wf1_ref[...]) + bf1)
    hidden = low(hidden)
    out_o[...] = x_one + mm(hidden, wf2_ref[...]) + bf2

    cot = cot_ref[...]
    grad = low(cot)
    gwf2_o[...] += mm_tn(hidden, grad)
    d_pre = mm_nt(grad, wf2_ref[...]) * d_hidden
    d_pre_low = low(d_pre)
    gwf1_o[...] += mm_tn(normed_b, d_pre_low)
    d_normed_b = mm_nt(d_pre_low, wf1_ref[...])
    d_x_one = cot + norm_back(d_normed_b * ln2_gain, unit_b, inv_b)
    d_x_low = low(d_x_one)
    gwo_o[...] += mm_tn(mixed_low, d_x_low)
    dmix_s[...] = low(mm_nt(d_x_low, wo_ref[...]))

    for s in range(tiles):
        rows = slice(PAIR * s, PAIR * s + PAIR)
        for p in range(HEADS // 2):
            at = 128 * p
            q = qkv_s[rows, at : at + 128]
            k = qkv_s[rows, D + at : D + at + 128]
            v = qkv_s[rows, 2 * D + at : 2 * D + at + 128]
            dm = dmix_s[rows, at : at + 128]
            d_q, d_k, d_v = [], [], []
            for a, dm_half in enumerate(halves(dm)):
                soft = soft_s[(s * (HEADS // 2) + p) * 2 + a]
                d_soft = mm_nt(dm_half, v)
                d_v.append(mm_tn(low(soft), dm))
                d_score = low(soft * (d_soft - jnp.sum(soft * d_soft, -1, keepdims=True)))
                d_q.append(mm(d_score, k))
                d_k.append(mm_tn(d_score, q))
            dqkv_s[rows, at : at + 128] = low(jnp.where(left, d_q[0], d_q[1]) * scale)
            dqkv_s[rows, D + at : D + at + 128] = low(jnp.where(left, d_k[0], d_k[1]) * scale)
            dqkv_s[rows, 2 * D + at : 2 * D + at + 128] = low(jnp.where(left, d_v[0], d_v[1]))

    d_qkv = dqkv_s[...]
    gwqkv_o[...] += mm_tn(normed_a, d_qkv)
    d_normed_a = mm_nt(d_qkv, wqkv_ref[...])
    d_x_zero = d_x_one + norm_back(d_normed_a * ln1_gain, unit_a, inv_a)
    d_x_low = low(d_x_zero)
    gw4_o[...] += mm_tn(act, d_x_low)
    token = mm_nt(d_x_low, w4_ref[...]) / count
    tok_o[...] = token
    grouped = token * pg_ref[...]
    tg_o[...] = grouped
    back_o[0:1, :] += col_sum(grouped)
    back_o[1:2, :] += col_sum(token * pc_ref[...]) * sv_ref[3:4, :]
    narrow = [
        col_sum(d_normed_a * unit_a), col_sum(d_normed_a), col_sum(d_x_one),
        col_sum(d_normed_b * unit_b), col_sum(d_normed_b), col_sum(cot), col_sum(d_x_zero),
    ]
    for k, row in enumerate(narrow):
        small_o[k : k + 1, 0:D] += row
    small_o[7:8, :] += col_sum(d_pre)


def third_back_tokens(
    totals, tg_ref, sc_ref, gm_ref, ps_ref, pooled_ref, gext_ref, w2_ref, w3_ref, w23_ref, sv_ref, stats_ref,
    kap_o, k_o, wb_o, top_o, corr_o, base_o,
):
    gain = sv_ref[0:1, :]
    n = stats_ref[2:3, 0:1]
    alpha = gain * as_vector(totals, 0, 4) / n
    beta = gain * as_vector(totals, 4, 4) * sv_ref[3:4, :] / n
    count = ps_ref[:, C1 : C1 + 1]
    w23 = w23_ref[...]
    act = low(w23[0:C1])
    per_token = low(gain * tg_ref[...] - (count * alpha + beta * sc_ref[...]))
    pooled = low(mm_nt(per_token, w3_ref[0:C2, :]) / count)
    shifted = low(alpha + beta * gm_ref[...])
    kap_o[...] = low(mm_nt(pooled, w2_ref[...]) - mm_nt(shifted, act))
    k_o[:, 0:C1] = low(-mm_nt(low(w23[0:C1] * beta), act))
    wb_o[...] = low(w23[0:C1] * gain)
    top_o[...] = mm_tn(pooled_ref[...], per_token)
    sums = low(ps_ref[:, 0 : C1 + 16])
    corr_o[...] = mm_tn(sums, shifted) + beta * mm(low(gext_ref[:, 0:C1]), act)
    base_o[...] = mm_tn(sums, pooled)


def last_tile(gp_ref, ext_ref, gp1_ref, rel, tok, kap, k_s, xe_s, wb_ref, wd_ref, h_o, q_o, d_at):
    dn = (gp_ref[...].reshape(TOK, GROUP, C3) * tok[:, None, :]).reshape(TILE, C3)
    xe_s[0:C1, :] = ext_ref[0:C1, :]
    k_s[:, C1 : C1 + TOK] = kap.T
    h_o[...] += mm(ext_ref[...], dn)
    d_act = mm_nt(wb_ref[...], dn) + mm(k_s[...], xe_s[...])
    d_one = low(d_act * gp1_ref[...].astype(F32))
    d_at(mm(wd_ref[...], d_one))
    q_o[...] += mm_nt(rel, d_one)


def last_weights(h, gain, corr, base, w2e, w3_ref):
    m = h * gain - corr
    parts = split_three(m)[0:2]
    grad_w3 = sum(mm_tn(w2e, part) for part in parts)
    return grad_w3, sum(mm_nt(part, w3_ref[C2:, :]) for part in parts) + base


def first_grads(q, moments, psmall, stats):
    mean, inverse, n, scale = stats[0:1], stats[1:2], stats[2:3], stats[3:4]
    w = [psmall[k : k + 1, :] for k in range(3)]
    one = q[3:4, :]
    two = inverse * (sum(w[k] * q[k : k + 1, :] for k in range(3)) - mean * one)
    grad_w = []
    for k in range(3):
        along = sum(w[j] * moments[k : k + 1, j : j + 1] for j in range(3)) - mean * moments[k : k + 1, 3:4]
        grad_w.append(scale * (q[k : k + 1, :] - (one * moments[k : k + 1, 3:4] + two * inverse * along) / n))
    flat = [
        jnp.sum(scale * w[k] * (one - two * inverse * mean) / n, axis=1, keepdims=True) for k in range(3)
    ]
    slope = [
        [jnp.sum(scale * w[k] * two * inverse * w[j] / n, axis=1, keepdims=True) for j in range(3)]
        for k in range(3)
    ]
    return grad_w, two, one, flat, slope


def point_gradient(d_ref, rel_ref, tokens_ref, flat, slope, out_ref, spread_s, sums_s):
    pieces = d_ref.shape[1] // 256
    lane = lax.rem(lax.broadcasted_iota(jnp.int32, (1, 256), 1), GROUP).astype(F32)
    base = jnp.concatenate(flat, axis=0)
    columns = [jnp.concatenate([slope[k][j] for k in range(3)], axis=0) for j in range(3)]
    spread_s[...] = spread_tokens(tokens_ref[pieces : 2 * pieces, :])
    for i in range(pieces):
        at = slice(256 * i, 256 * i + 256)
        rel = rel_ref[:, at].astype(F32)
        d = d_ref[:, at]
        out = d[0:3] + d[4:7] - rel[3:4] * base
        for j in range(3):
            out = out - columns[j] * rel[j : j + 1]
        out_ref[:, at] = out
        sums_s[8 * i : 8 * i + 8, :] = jnp.concatenate([out, jnp.zeros((5, 256), F32)], axis=0)
    sums_s[...] = patch_sum(sums_s[...], patch_ones())
    for i in range(pieces):
        at = slice(256 * i, 256 * i + 256)
        pick = (lane == spread_s[i : i + 1, :]).astype(F32)
        out_ref[:, at] = out_ref[:, at] - pick * sums_s[8 * i : 8 * i + 3, :]


def point_small_rows(grad_w, gain1, shift1, b2, tot, b4):
    rows = list(grad_w) + [gain1, shift1]
    rows += [b2[:, 128 * k : 128 * k + 128] for k in range(2)]
    rows += [tot[4:8, :], tot[0:4, :]]
    rows += [b4[:, 128 * k : 128 * k + 128] for k in range(3)]
    return jnp.concatenate(rows, axis=0)


def block_small_rows(small_ref):
    rows = [small_ref[k : k + 1, 128 * j : 128 * j + 128] for k in range(5) for j in range(3)]
    rows += [small_ref[7:8, 128 * j : 128 * j + 128] for j in range(12)]
    rows += [small_ref[5:6, 128 * j : 128 * j + 128] for j in range(3)]
    return jnp.concatenate(rows, axis=0)


class Scatter:
    def __init__(self, blocks, lands, send, recv, base):
        self.blocks, self.lands, self.sems, self.base = blocks, lands, (send, recv), base
        z, y, x, core = self.at = where_am_i()
        half = blocks.shape[-1] // 2
        self.one, self.two = pl.ds(0, half), pl.ds(half, half)
        every = slice(None)
        mine = blocks.at[core]
        near = [(chip(lax.rem(z + k, NZ), y, x), core) for k in range(1, NZ)]
        over_y, over_x, twin = (chip(z, 1 - y, x), core), (chip(z, y, 1 - x), core), (chip(z, y, x), 1 - core)
        land1, land2, land3, land4 = lands
        self.stages = [
            [(blocks.at[1 - core], land1, twin)],
            [
                (mine.at[:, :, 1 - x, :, self.one], land2.at[0], over_x),
                (mine.at[:, 1 - y, :, :, self.two], land2.at[1], over_y),
            ],
            [
                (mine.at[:, 1 - y, x, :, self.one], land3.at[0], over_y),
                (mine.at[:, y, 1 - x, :, self.two], land3.at[1], over_x),
            ],
            [(mine.at[lax.rem(z + k, NZ), y, x], land4.at[k - 1], near[k - 1]) for k in range(1, NZ)],
        ]

    def copies(self, stage):
        k = self.base + sum(len(s) for s in self.stages[:stage])
        return [
            pltpu.make_async_remote_copy(
                src_ref=src, dst_ref=dst, send_sem=self.sems[0].at[k + i], recv_sem=self.sems[1].at[k + i],
                device_id=peer, device_id_type=MESH,
            )
            for i, (src, dst, peer) in enumerate(self.stages[stage])
        ]

    def advance(self, stage):
        z, y, x, core = self.at
        mine = self.blocks.at[core]
        land1, land2, land3, land4 = self.lands
        if stage > 0:
            for copy in self.copies(stage - 1):
                copy.wait()
        if stage == 1:
            for cz in range(NZ):
                for cy in range(NY):
                    for cx in range(NX):
                        mine[cz, cy, cx] = mine[cz, cy, cx] + land1[cz, cy, cx]
        if stage == 2:
            for cz in range(NZ):
                for k in range(2):
                    mine[cz, k, x, :, self.one] = mine[cz, k, x, :, self.one] + land2[0, cz, k]
                    mine[cz, y, k, :, self.two] = mine[cz, y, k, :, self.two] + land2[1, cz, k]
        if stage == 3:
            for cz in range(NZ):
                mine[cz, y, x, :, self.one] = mine[cz, y, x, :, self.one] + land3[0, cz]
                mine[cz, y, x, :, self.two] = mine[cz, y, x, :, self.two] + land3[1, cz]
        if stage < 4:
            for copy in self.copies(stage):
                copy.start()
            return None
        total = mine[z, y, x].astype(F32)
        for k in range(NZ - 1):
            total = total + land4[k].astype(F32)
        return total


SCATTER_SEMS = 8
POINT_WIDTH = 768


def scatter_scratch(width):
    return [
        pltpu.VMEM((NC, NZ, NY, NX, 16, width), BF16),
        pltpu.VMEM((NZ, NY, NX, 16, width), BF16),
        pltpu.VMEM((2, NZ, 2, 16, width // 2), BF16),
        pltpu.VMEM((2, NZ, 16, width // 2), BF16),
        pltpu.VMEM((NZ - 1, 16, width), BF16),
    ]


def backward_kernel(known, dp, *refs):
    refs = list(refs)
    take = lambda count: [refs.pop(0) for _ in range(count)]
    pa_ref, pg_ref, pc_ref, ps_ref, len_ref, cot_ref, psmall_ref, bsmall_ref, sv_ref, stats_ref, moment_ref = take(11)
    w2_ref, w3_ref, w4_ref, wqkv_ref, wo_ref, wf1_ref, wf2_ref, w23_ref = take(8)
    sc_ref, gm_ref, pooled_ref, gext_ref, wd_ref, rel_ref, tokens_ref, gp_ref, ext_ref, gp1_ref = take(10)
    out_o, pg_o = take(2)
    if known:
        pflat_o, bflat_o = take(2)
        gw4_s, gwqkv_s, gwo_s, gwf1_s, gwf2_s = None, None, None, None, None
    else:
        prow_o, brow_o, gw2_o, gw3_o = take(4)
        gw4_s, gwqkv_s, gwo_s, gwf1_s, gwf2_s = take(5)
    small_s, tok_s, tg_s, back_s, qkv_s, mixed_s, soft_s, dmix_s, dqkv_s = take(9)
    tot_s, kap_s, k_s, wb_s, top_s, corr_s, base_s, h_s, q_s, d_s, xe_s, spread_s, sums_s = take(13)
    acc, slots, ssend, srecv, acc3, slots3, ssend3, srecv3 = take(8)
    step = pl.program_id(0)
    steps = pl.num_programs(0)
    peers = all_peers(dp)
    if known:
        gw4_s, gwqkv_s, gwo_s, gwf1_s, gwf2_s = take(5)
        rest0, rest1, rest2, rest3, rest4, point0, point1, point2, point3, point4 = take(10)
        stage, pstage, pal, bal, gsend, grecv = take(6)
        z, y, x, core = where_am_i()
        rest = Scatter(rest0, (rest1, rest2, rest3, rest4), gsend, grecv, 0)
        point = Scatter(point0, (point1, point2, point3, point4), gsend, grecv, SCATTER_SEMS)
    blocks = ps_ref.shape[0] // TB

    @pl.when(step == 0)
    def _():
        greet(peers)

    @pl.when(step < blocks)
    def _():
        rows = pl.ds(pl.multiple_of(step * TB, TB), TB)
        block_kernel(
            pa_ref, pg_ref, pc_ref, ps_ref.at[rows], len_ref, cot_ref, psmall_ref, bsmall_ref, sv_ref,
            w4_ref, wqkv_ref, wo_ref, wf1_ref, wf2_ref,
            out_o, gw4_s, gwqkv_s, gwo_s, gwf1_s, gwf2_s, small_s, tok_s.at[rows], tg_s.at[rows], back_s,
            qkv_s, mixed_s, soft_s, dmix_s, dqkv_s,
        )

    @pl.when(step == blocks - 1)
    def _():
        greeted(peers)
        acc3[...] = as_rows(back_s[0:1, :], back_s[1:2, :])
        copies = sum_start(dp, acc3, slots3, ssend3, srecv3)
        if known:
            for d in range(dp * NC):
                stage[:, W4_AT : W4_AT + D] = gw4_s[16 * d : 16 * d + 16, :]
                for (name, at, cols), ref in zip(UNDER, (gwqkv_s, gwo_s, gwf1_s)):
                    stage[0:12, at : at + cols] = ref[12 * d : 12 * d + 12, :]
                for row, rows, under, at in rest_wf2(d):
                    stage[under : under + rows, at : at + D] = gwf2_s[row : row + rows, :]
                cz, cy, cx, cc = place(d)
                rest0[cc, cz, cy, cx] = low(stage[...])
            rest.advance(0)
        for ref in (h_s, q_s):
            ref[...] = jnp.zeros_like(ref)
        xe_s[C1:, :] = token_ones()
        if known:
            rest.advance(1)
        tot_s[...] = sum_finish(acc3, slots3, copies)
        third_back_tokens(
            tot_s[...], tg_s, sc_ref, gm_ref, ps_ref, pooled_ref, gext_ref, w2_ref, w3_ref, w23_ref, sv_ref, stats_ref,
            kap_s, k_s, wb_s, top_s, corr_s, base_s,
        )

    if known:
        for at_step, number in ((5, 2), (7, 3)):
            pl.when(step == at_step)(functools.partial(rest.advance, number))

    @pl.when(step >= blocks)
    def _():
        tile = step - blocks
        at = pl.ds(pl.multiple_of(tile * TILE, TILE), TILE)
        ts = pl.ds(pl.multiple_of(tile * TOK, TOK), TOK)

        def put(d):
            d_s[:, at] = d

        last_tile(
            gp_ref, ext_ref, gp1_ref, rel_ref[:, at], low(tok_s[ts, :] * 0.5), kap_s[ts, :], k_s, xe_s, wb_s, wd_ref,
            h_s, q_s, put,
        )

    @pl.when(step == steps - 1)
    def _():
        acc[...] = q_s[...]
        copies = sum_start(dp, acc, slots, ssend, srecv)
        b2 = as_vector(psmall_ref, 5, 2)
        w2e = jnp.concatenate([w2_ref[...], low(jnp.concatenate([b2, jnp.zeros((15, C2), F32)], axis=0))], axis=0)
        gw3, gw2 = last_weights(h_s[...], sv_ref[0:1, :], corr_s[...], base_s[...], w2e, w3_ref)
        none = jnp.zeros((1, 128), F32)
        prow = point_small_rows([none] * 3, none, none, gw2[C1 : C1 + 1, :], jnp.zeros((8, 128), F32), small_s[6:7, 0:D])
        brow = block_small_rows(small_s)
        if known:
            pstage[...] = jnp.zeros_like(pstage)
            for d in range(dp * NC):
                if d < 16:
                    pstage[:, 0:C3] = top_s[16 * d : 16 * d + 16, :]
                else:
                    pstage[:, 0:C3] = gw3[16 * (d - 16) : 16 * (d - 16) + 16, :]
                pstage[0:4, C3 : C3 + C2] = gw2[4 * d : 4 * d + 4, :]
                pstage[4:5, C3 : C3 + 128] = piece_of(prow, PSMALL * d, PSMALL)
                pstage[5:6, C3 : C3 + 128] = piece_of(brow, BSMALL * d, BSMALL)
                cz, cy, cx, cc = place(d)
                point0[cc, cz, cy, cx] = low(pstage[...])
            point.advance(0)
            point.advance(1)
        totals = sum_finish(acc, slots, copies)
        grad_w, gain1, shift1, flat, slope = first_grads(totals, moment_ref[...], psmall_ref[...], stats_ref[...])
        full_rows = point_small_rows(grad_w, gain1, shift1, jnp.zeros((1, C2), F32), tot_s[...], jnp.zeros((1, D), F32))
        if known:
            point.advance(2)
            stage[...] = rest.advance(4)
            point.advance(3)
        point_gradient(d_s, rel_ref, tokens_ref, flat, slope, pg_o, spread_s, sums_s)
        if not known:
            prow_o[0:18, :] = prow + full_rows * (1.0 / (dp * NC))
            brow_o[0:30, :] = brow
            gw2_o[...] = gw2[0:C1]
            gw3_o[0:C2, :] = top_s[...]
            gw3_o[C2:, :] = gw3
            return
        own = jnp.zeros((1, 128), F32)
        for d in range(dp * NC):
            own = own + jnp.where(me() == d, piece_of(full_rows, PSMALL * d, PSMALL), 0.0)
        for j in range(D // 128):
            pal[pl.ds(73 + j, 16, stride=3), :] = stage[:, 128 * j : 128 * j + 128]
        start = 1
        for name, at, cols in UNDER:
            for j in range(cols // 128):
                bal[pl.ds(start + j, 12, stride=cols // 128), :] = stage[0:12, at + 128 * j : at + 128 * j + 128]
            start += 12 * cols // 128
        for row, rows, under, at in rest_wf2(0):
            for j in range(D // 128):
                bal[pl.ds(start + 3 * row + j, rows, stride=3), :] = stage[
                    under : under + rows, at + 128 * j : at + 128 * j + 128
                ]
        pstage[...] = point.advance(4)
        for j in range(C2 // 128):
            pal[pl.ds(1 + j, 4, stride=2), :] = pstage[0:4, C3 + 128 * j : C3 + 128 * j + 128]
        for j in range(C3 // 128):
            pal[pl.ds(9 + j, 16, stride=4), :] = pstage[:, 128 * j : 128 * j + 128]
        pflat_o[...] = segments_joined(pal[...], pstage[4:5, C3 : C3 + 128] + own, PSMALL)
        bflat_o[...] = segments_joined(bal[...], pstage[5:6, C3 : C3 + 128], BSMALL)


def backward_call(known, dp, *args):
    count = args[24].shape[1]
    tokens, blocks, tiles = count // GROUP, count // GROUP // TB, count // TILE
    single = dict(pipeline_mode=pl.Buffered(1))
    full = lambda *s: pl.BlockSpec(s, lambda i: (0, 0), **single)
    chunk = lambda c: pl.BlockSpec((TB, c), lambda i: (jnp.minimum(i, blocks - 1), 0))
    cols = lambda r: pl.BlockSpec((r, TILE), lambda i: (0, jnp.maximum(i - blocks, 0)))
    specs = [chunk(C3), chunk(C3), chunk(C3), full(tokens, 256), pl.BlockSpec(memory_space=pltpu.SMEM), chunk(D)]
    specs += [full(*a.shape) for a in args[6:26]]
    specs += [pl.BlockSpec((TILE, C3), lambda i: (jnp.maximum(i - blocks, 0), 0)), cols(C1 + 16), cols(C1)]
    grads = [((C3, D), F32), ((D, 3 * D), F32), ((D, D), F32), ((D, FF), F32), ((FF, D), F32)]
    outs = [(chunk(D), (tokens, D), F32), (full(3, count), (3, count), F32)]
    if known:
        outs += [(full(*s), s, t) for s, t in (((PROWS, 128), F32), ((BROWS, 128), F32))]
    else:
        more = [((24, 128), F32), ((32, 128), F32), ((C1, C2), F32), ((2 * C2, C3), F32)] + grads
        outs += [(full(*s), s, t) for s, t in more]
    pieces = count // 256
    scratch = [
        pltpu.VMEM((8, FF), F32), pltpu.VMEM((tokens, C3), F32), pltpu.VMEM((tokens, C3), F32), pltpu.VMEM((8, C3), F32),
        pltpu.VMEM((TB, 3 * D), BF16), pltpu.VMEM((TB, D), BF16),
        pltpu.VMEM((TB // PAIR * HEADS, PAIR, PAIR), F32), pltpu.VMEM((TB, D), BF16), pltpu.VMEM((TB, 3 * D), BF16),
        pltpu.VMEM((8, 128), F32), pltpu.VMEM((tokens, C1), BF16), pltpu.VMEM((C1, C1 + TOK), BF16),
        pltpu.VMEM((C1, C3), BF16), pltpu.VMEM((C2, C3), F32), pltpu.VMEM((C1 + 16, C3), F32),
        pltpu.VMEM((C1 + 16, C2), F32), pltpu.VMEM((C1 + 16, C3), F32), pltpu.VMEM((8, C1), F32),
        pltpu.VMEM((8, count), F32), pltpu.VMEM((C1 + TOK, TILE), BF16),
        pltpu.VMEM((pieces, 256), F32), pltpu.VMEM((8 * pieces, 256), F32),
    ]
    scratch += sum_scratch(dp) + sum_scratch(dp)
    if known:
        scratch += [pltpu.VMEM(s, t) for s, t in grads]
        scratch += scatter_scratch(REST_WIDTH) + scatter_scratch(POINT_WIDTH)
        scratch += [
            pltpu.VMEM((16, REST_WIDTH), F32), pltpu.VMEM((16, POINT_WIDTH), F32),
            pltpu.VMEM((PROWS, 128), F32), pltpu.VMEM((BROWS, 128), F32),
            pltpu.SemaphoreType.DMA((2 * SCATTER_SEMS,)), pltpu.SemaphoreType.DMA((2 * SCATTER_SEMS,)),
        ]
    return pl.pallas_call(
        functools.partial(backward_kernel, known, dp),
        grid=(blocks + tiles,),
        in_specs=specs,
        out_specs=[o[0] for o in outs],
        out_shape=shaped(*[o[1:] for o in outs]),
        scratch_shapes=scratch,
        compiler_params=params(collective_id=1, has_side_effects=True),
        name="backward",
    )(*args)


def geometry_kernel(points_ref, tokens_ref, rel_o, moment_o, counts_s, picked_s):
    moment_o[...] = jnp.concatenate(
        [geometry(points_ref, tokens_ref, rel_o, counts_s, picked_s), jnp.zeros((8, 120), F32)], axis=1
    )


def geometry_call(points, tokens):
    count = points.shape[1]
    return pl.pallas_call(
        geometry_kernel,
        out_shape=shaped(((8, count), BF16), ((8, 128), F32)),
        in_specs=vmem(2),
        out_specs=vmem(2),
        scratch_shapes=[pltpu.VMEM((count // 128, 256), F32), pltpu.VMEM((count // 32, 256), F32)],
        compiler_params=params(),
        name="geometry",
    )(points, tokens)


def gather_plain(points, tokens, point_master, block_master, devices):
    rel, moments = geometry_call(points, tokens)
    moments = lax.psum(moments, AXES)
    tables = []
    for master, layout in ((point_master, point_layout()), (block_master, block_layout())):
        offset = 0
        parts = []
        for seg_len in segment_lengths(layout, devices):
            piece = master[offset : offset + seg_len // devices].astype(BF16)
            offset += seg_len // devices
            parts.append(lax.all_gather(piece, AXES, axis=0, tiled=True))
        tables.append(parts)
    (ps, w2, w3, w4), (bs, wqkv, wo, wf1, wf2) = tables

    def rows_of(v, rows, used):
        v = v[:used].astype(F32).reshape(-1, 128)
        return jnp.concatenate([v, jnp.zeros((rows - v.shape[0], 128), F32)], axis=0)

    small = (rel, moments, rows_of(ps, 24, 18 * 128), rows_of(bs, 32, 30 * 128))
    point = (w2.reshape(C1, C2), w3.reshape(2 * C2, C3))
    block = (w4.reshape(C3, D), wqkv.reshape(D, 3 * D), wo.reshape(D, D), wf1.reshape(D, FF), wf2.reshape(FF, D))
    return small + point, block


def scatter_plain(devices, prow, brow, gw2, gw3, gw4, gwqkv, gwo, gwf1, gwf2):
    pieces = []
    for layout, tables in (
        (point_layout(), (prow[:18], gw2, gw3, gw4)),
        (block_layout(), (brow[:30], gwqkv, gwo, gwf1, gwf2)),
    ):
        parts = []
        for values, seg_len in zip(tables, segment_lengths(layout, devices)):
            values = values.reshape(-1)
            values = jnp.concatenate([values, jnp.zeros((seg_len - values.shape[0],), F32)])
            parts.append(lax.psum_scatter(values, AXES, scatter_dimension=0, tiled=True))
        pieces.append(parts)
    return pieces


def adam_update(master, moment_one, moment_two, gradient, step_rates, decays):
    one_new = BETA_ONE * moment_one + (1.0 - BETA_ONE) * gradient
    two_new = BETA_TWO * moment_two + (1.0 - BETA_TWO) * gradient * gradient
    fix_one = 1.0 - BETA_ONE**STEP
    fix_two = 1.0 - BETA_TWO**STEP
    direction = one_new / fix_one / (jnp.sqrt(two_new / fix_two) + ADAM_EPS)
    master_new = master - step_rates * (direction + decays * master)
    return (master_new, one_new, two_new)


def flat_of(vector, rows):
    return jnp.pad(vector, (0, rows * 128 - vector.shape[0])).reshape(rows, 128)


def on_device(
    points, point_count, centre_slot, cloud_length, cotangent, point_master, block_master,
    point_first, block_first, point_second, block_second,
):
    dp, fsdp = lax.axis_size("dp"), lax.axis_size("fsdp")
    devices = dp * fsdp
    own_rank = lax.axis_index(AXES)
    known = dp == NZ * NY * NX and fsdp == NC
    count = points.shape[1]
    tokens = jnp.concatenate([point_count, centre_slot]).reshape(-1, 8)
    if known:
        outs = forward_call(
            True, dp, count, points, tokens, flat_of(point_master, PROWS), flat_of(block_master, BROWS)
        )
        given, block, outs = outs[:6], outs[6:11], outs[11:]
    else:
        given, block = gather_plain(points, tokens, point_master, block_master, devices)
        outs = forward_call(False, dp, count, *given)
    rel, moments, psmall, bsmall, w2, w3 = given
    ext, gp1, gext, ps, gm, sc, pooled, sv, stats, wd, w23, gp, pa, pg, pc = outs
    outs = backward_call(
        known, dp, pa, pg, pc, ps, cloud_length, cotangent, psmall, bsmall, sv, stats, moments,
        w2, w3, *block, w23, sc, gm, pooled, gext, wd, rel, tokens, gp, ext, gp1,
    )
    tokens_out, point_grad = outs[:2]
    if known:
        point_gradient_vec = outs[2].reshape(-1)[: point_master.shape[0]]
        block_gradient = outs[3].reshape(-1)[: block_master.shape[0]]
        block_small = block_gradient[:BSMALL]
    else:
        point_parts, block_parts = scatter_plain(devices, *outs[2:])
        block_small = block_parts[0]
        point_gradient_vec = jnp.concatenate(point_parts)
        block_gradient = jnp.concatenate(block_parts)
    point_rates, point_decays = shard_rates(point_layout(), devices, own_rank)
    block_rates, block_decays = shard_rates(block_layout(), devices, own_rank)
    point_new, point_one, point_two = adam_update(
        point_master, point_first, point_second, point_gradient_vec, point_rates, point_decays
    )
    block_new, block_one, block_two = adam_update(
        block_master, block_first, block_second, block_gradient, block_rates, block_decays
    )
    return (
        tokens_out, point_grad, point_new, block_new, point_one, block_one, point_two, block_two,
        point_new.astype(BF16), block_new.astype(BF16), block_small,
    )


def solution(mesh):
    split = P(AXES)
    return jax.shard_map(
        on_device,
        mesh=mesh,
        in_specs=(P(None, AXES), split, split, split, P(AXES, None)) + (split,) * 6,
        out_specs=(P(AXES, None), P(None, AXES)) + (split,) * 9,
        check_vma=False,
    )
```

```python
import functools
import math

import jax
import jax.numpy as jnp
from jax import lax
from jax.experimental import pallas as pl
from jax.experimental.pallas import tpu as pltpu
from jax.sharding import PartitionSpec as P

C1 = 128
C2 = 256
C3 = 512
D = 384
HEADS = 6
HEAD_DIM = 64
FF = 1536
GROUP = 32
PATCHES = 64
STEP = 10

EPS_NORM = 1e-05
BETA_ONE = 0.9
BETA_TWO = 0.95
ADAM_EPS = 1e-08
DECAY_RATE = 0.05
NEG_FILL = -1e30

F32 = jnp.float32
BF16 = jnp.bfloat16
AXES = ("dp", "fsdp")
MESH = pl.DeviceIdType.MESH
VMEM_LIMIT = 60 * 2**20
TILE = 2048
TOK = TILE // GROUP
PAIR = 128

NZ, NY, NX, NC = 4, 2, 2, 2
PROWS, BROWS = 128, 440
PSMALL, BSMALL = 72, 120


def point_layout():
    return [
        [
            ("w1", (3, C1), 3.0 ** (-0.5)),
            ("bn1_gain", (C1,), 0.0),
            ("bn1_shift", (C1,), -1.0),
            ("b2", (C2,), -1.0),
            ("bn3_gain", (C3,), 0.0),
            ("bn3_shift", (C3,), -1.0),
            ("b4", (D,), -1.0),
        ],
        [("w2", (C1, C2), C1 ** (-0.5))],
        [("w3", (2 * C2, C3), (2 * C2) ** (-0.5))],
        [("w4", (C3, D), C3 ** (-0.5))],
    ]


def block_layout():
    return [
        [
            ("ln1_gain", (D,), 0.0),
            ("ln1_shift", (D,), -1.0),
            ("bo", (D,), -1.0),
            ("ln2_gain", (D,), 0.0),
            ("ln2_shift", (D,), -1.0),
            ("bf1", (FF,), -1.0),
            ("bf2", (D,), -1.0),
        ],
        [("wqkv", (D, 3 * D), D ** (-0.5))],
        [("wo", (D, D), 3.0 * D ** (-0.5))],
        [("wf1", (D, FF), D ** (-0.5))],
        [("wf2", (FF, D), FF ** (-0.5))],
    ]


def rate_for(spread):
    return 2.0 * spread if spread > 0.0 else 0.5 if spread == 0.0 else 0.6


def decay_for(spread):
    return DECAY_RATE if spread > 0.0 else 0.0


def segment_lengths(layout, devices):
    lengths_out = []
    for segment in layout:
        used_len = sum((math.prod(entry[1]) for entry in segment))
        lengths_out.append(-(-used_len // devices) * devices)
    return lengths_out


def shard_rates(layout, devices, own_rank):
    lengths = segment_lengths(layout, devices)
    position = jnp.arange(sum(lengths) // devices, dtype=jnp.int32)
    rates = jnp.zeros(position.shape, F32)
    decays = jnp.zeros(position.shape, F32)
    start = 0
    for segment, seg_len in zip(layout, lengths):
        piece_len = seg_len // devices
        here = (position >= start) & (position < start + piece_len)
        inner = position + (own_rank * piece_len - start)
        offset = 0
        for entry_label, entry_dims, spread in segment:
            extent = math.prod(entry_dims)
            inside = here & (inner >= offset) & (inner < offset + extent)
            rates = jnp.where(inside, rate_for(spread), rates)
            decays = jnp.where(inside, decay_for(spread), decays)
            offset += extent
        start += piece_len
    return rates, decays


def mm(a, b):
    return jnp.dot(a, b, preferred_element_type=F32)


def mm_tn(a, b):
    return lax.dot_general(a, b, (((0,), (0,)), ((), ())), preferred_element_type=F32)


def mm_nt(a, b):
    return lax.dot_general(a, b, (((1,), (1,)), ((), ())), preferred_element_type=F32)


def low(v):
    return v.astype(BF16)


def split_three(v):
    hi = low(v)
    rest = v - hi.astype(F32)
    mid = low(rest)
    return hi, mid, low(rest - mid.astype(F32))


def mm_exact(a, b):
    hi, mid, lo = split_three(a)
    return mm(hi, b) + (mm(mid, b) + mm(lo, b))


LAM = (math.sqrt(2.0 / math.pi) * 0.044715) ** (-1.0 / 3.0)
ARG = math.sqrt(2.0 / math.pi) * LAM


def gelu_twice(y):
    square = y * y
    near = square + ARG
    t = jnp.tanh(y * near)
    up = 1.0 + t
    g = y * up
    return g, up + g * (1.0 - t) * (near + (square + square))


def gelu_pair(v):
    g, d = gelu_twice(v * (1.0 / LAM))
    return (0.5 * LAM) * g, 0.5 * d


def patch_ones():
    i = lax.broadcasted_iota(jnp.int32, (256, 256), 0) // GROUP
    j = lax.broadcasted_iota(jnp.int32, (256, 256), 1) // GROUP
    return (i == j).astype(F32).astype(BF16)


def token_ones():
    t = lax.broadcasted_iota(jnp.int32, (TOK, TILE), 0)
    p = lax.broadcasted_iota(jnp.int32, (TOK, TILE), 1) // GROUP
    return (t == p).astype(F32).astype(BF16)


def patch_sum(rows, ones):
    return mm_exact(rows, ones)


def rank_of(peer_dp, peer_core):
    return peer_dp * NC + peer_core


def me():
    return rank_of(lax.axis_index("dp"), lax.axis_index("fsdp"))


def all_peers(dp):
    n = dp * NC
    peers = []
    for k in range(1, n):
        p = lax.rem(me() + k, n)
        peers.append((p // NC, lax.rem(p, NC)))
    return peers


def greet(peers):
    barrier = pltpu.get_barrier_semaphore()
    for peer in peers:
        pl.semaphore_signal(barrier, inc=1, device_id=peer, device_id_type=MESH)


def greeted(peers):
    pl.semaphore_wait(pltpu.get_barrier_semaphore(), len(peers))


def sum_copies(dp, src, dst_of, send, recv):
    return [
        pltpu.make_async_remote_copy(
            src_ref=src, dst_ref=dst_of(k), send_sem=send.at[k], recv_sem=recv.at[k],
            device_id=peer, device_id_type=MESH,
        )
        for k, peer in enumerate(all_peers(dp))
    ]


def send_to_all(dp, src, dst_of, send, recv):
    copies = sum_copies(dp, src, dst_of, send, recv)
    for copy in copies:
        copy.start()
    return copies


def sum_start(dp, acc, slots, send, recv):
    return send_to_all(dp, acc, lambda k: slots.at[k], send, recv)


def sum_finish(acc, slots, copies):
    for copy in copies:
        copy.wait()
    return acc[...] + jnp.sum(slots[...], axis=0)


def sum_scratch(dp):
    n = dp * NC - 1
    return [
        pltpu.VMEM((8, 128), F32), pltpu.VMEM((n, 8, 128), F32),
        pltpu.SemaphoreType.DMA((n,)), pltpu.SemaphoreType.DMA((n,)),
    ]


def as_rows(*vectors):
    return jnp.concatenate(
        [v[:, 128 * k : 128 * k + 128] for v in vectors for k in range(v.shape[1] // 128)], axis=0
    )


def as_vector(rows, first, count):
    return jnp.concatenate([rows[k : k + 1, :] for k in range(first, first + count)], axis=1)


def vmem(count):
    return [pl.BlockSpec(memory_space=pltpu.VMEM)] * count


def shaped(*items):
    return [jax.ShapeDtypeStruct(s, t) for s, t in items]


def params(**more):
    return pltpu.CompilerParams(vmem_limit_bytes=VMEM_LIMIT, **more)


def where_am_i():
    at = lax.axis_index("dp")
    return at // (NY * NX), lax.rem(at // NX, NY), lax.rem(at, NX), lax.axis_index("fsdp")


def chip(z, y, x):
    return (z * NY + y) * NX + x


def spread_tokens(values):
    t = lax.broadcasted_iota(jnp.int32, (8, 256), 0)
    p = lax.broadcasted_iota(jnp.int32, (8, 256), 1) // GROUP
    return mm(low(values.astype(F32)), low((t == p).astype(F32)))


def geometry(points_ref, tokens_ref, rel_ref, counts_s, picked_s):
    pieces = points_ref.shape[1] // 256
    lane = lax.rem(lax.broadcasted_iota(jnp.int32, (1, 256), 1), GROUP).astype(F32)
    counts_s[...] = spread_tokens(tokens_ref[...])
    for i in range(pieces):
        at = slice(256 * i, 256 * i + 256)
        pick = (lane == counts_s[pieces + i : pieces + i + 1, :]).astype(F32)
        rows = points_ref[:, at] * pick
        picked_s[8 * i : 8 * i + 8, :] = jnp.concatenate([rows, jnp.zeros((5, 256), F32)], axis=0)
    picked_s[...] = patch_sum(picked_s[...], patch_ones())
    for i in range(pieces):
        at = slice(256 * i, 256 * i + 256)
        valid = (lane < counts_s[i : i + 1, :]).astype(F32)
        relative = (points_ref[:, at] - picked_s[8 * i : 8 * i + 3, :]) * valid
        rel_ref[:, at] = low(jnp.concatenate([relative, valid, relative, valid], axis=0))
    rel = rel_ref[...]
    return mm_nt(rel, rel)


def prepare_one(moments, small):
    n = moments[3:4, 3:4]
    w = [small[k : k + 1, :] for k in range(3)]
    gain, shift = small[3:4, :], small[4:5, :]
    mean = sum(w[k] * moments[k : k + 1, 3:4] for k in range(3)) / n
    square = jnp.zeros_like(mean)
    for j in range(3):
        for k in range(3):
            square = square + w[j] * w[k] * moments[j : j + 1, k : k + 1]
    inverse = lax.rsqrt(square / n - mean * mean + EPS_NORM)
    scale = inverse * gain
    scaled = [wk * scale for wk in w]
    parts = [v * (1.0 / LAM) for v in scaled + [shift - mean * scale]]
    high = [low(v) for v in parts]
    rest = [low(v - h.astype(F32)) for v, h in zip(parts, high)]
    forward = jnp.concatenate(high + rest, axis=0)
    high = [low(v) for v in scaled]
    rest = [low(v - h.astype(F32)) for v, h in zip(scaled, high)]
    zero = jnp.zeros((1, C1), BF16)
    backward = jnp.concatenate(high + [zero] + rest + [zero], axis=0)
    stats = jnp.concatenate(
        [mean, inverse, jnp.broadcast_to(n, (1, C1)), scale, jnp.zeros((4, C1), F32)], axis=0
    )
    return forward, backward, stats


def flat_rows(pieces, length, rows):
    lane = lax.broadcasted_iota(jnp.int32, (1, 128), 1)
    out = [jnp.zeros((1, 128), F32) for _ in range(rows)]
    for r in range(pieces.shape[0]):
        row = jnp.where(lane < length, pieces[r : r + 1, :], 0.0)
        at = length * r
        row = pltpu.roll(row, at % 128, 1) if at % 128 else row
        first = at // 128
        out[first] = out[first] + jnp.where(lane >= at % 128, row, 0.0)
        if at % 128 + length > 128:
            out[first + 1] = out[first + 1] + jnp.where(lane < at % 128, row, 0.0)
    return jnp.concatenate(out, axis=0)


def piece_of(rows, at, length):
    lane = lax.broadcasted_iota(jnp.int32, (1, 128), 1)
    first, shift = at // 128, at % 128
    row = rows[first : first + 1, :]
    if shift:
        row = pltpu.roll(row, 128 - shift, 1)
        if shift + length > 128:
            other = pltpu.roll(rows[first + 1 : first + 2, :], 128 - shift, 1)
            row = jnp.where(lane < 128 - shift, row, other)
    return jnp.where(lane < length, row, 0.0)


def segments_apart(flat, small):
    lane = lax.broadcasted_iota(jnp.int32, (1, 128), 1)
    turned = pltpu.roll(flat, 128 - small, 1)
    return jnp.where(lane < 128 - small, pltpu.roll(turned, 1, 0), turned)


def segments_joined(rows, first, small):
    lane = lax.broadcasted_iota(jnp.int32, (1, 128), 1)
    turned = pltpu.roll(rows, small, 1)
    row = lax.broadcasted_iota(jnp.int32, (rows.shape[0], 1), 0)
    joined = jnp.where(lane < small, turned, pltpu.roll(turned, rows.shape[0] - 1, 0))
    return jnp.where((lane < small) & (row == 0), first, joined)


def first_tile(rel, wn, ext_ref, gp_ref):
    valid = rel[3:4, :].astype(F32)
    for j in range(TILE // 256):
        at = slice(256 * j, 256 * j + 256)
        g, d = gelu_twice(mm_tn(wn, rel[:, at]))
        ext_ref[0:C1, at] = low(g * (valid[:, at] * (0.5 * LAM)))
        gp_ref[:, at] = low(d * (valid[:, at] * 0.5))
    ext_ref[C1:, :] = jnp.concatenate([rel[3:4], jnp.zeros((15, TILE), BF16)], axis=0)


def first_tokens(gext, ps_ref, w2e, w3_ref, pooled_o, gm_o, fw_o):
    lower = w3_ref[C2:, :]
    count = ps_ref[:, C1 : C1 + 1]
    fs = mm_exact(ps_ref[:, 0 : C1 + 16], w2e)
    pooled = low(fs / count)
    pooled_o[...] = pooled
    g = mm(pooled, w3_ref[0:C2, :])
    gm_o[...] = g
    fw = mm_exact(fs, lower)
    fw_o[...] = fw
    gram = sum(mm_tn(w2e, part) for part in split_three(mm_exact(gext, w2e)))
    one = jnp.sum(fw + count * g, axis=0, keepdims=True)
    two = jnp.sum(mm_exact(gram, lower) * lower.astype(F32), axis=0, keepdims=True)
    two = two + jnp.sum(g * (2.0 * fw + count * g), axis=0, keepdims=True)
    return as_rows(one, two)


def third_vectors(totals, n, psmall_ref):
    mean = as_vector(totals, 0, 4) / n
    inverse = lax.rsqrt(as_vector(totals, 4, 4) / n - mean * mean + EPS_NORM)
    gain, shift = as_vector(psmall_ref, 7, 4), as_vector(psmall_ref, 11, 4)
    return jnp.concatenate([inverse * gain, shift, mean, inverse, jnp.zeros((4, C3), F32)], axis=0)


def second_tile(act, mask, w23, gm, count, sv_ref, gp_o, pa_o, pg_o, pc_o, first):
    scale, shift = low(sv_ref[0:1, :] * (1.0 / LAM)), low(sv_ref[1:2, :] * (1.0 / LAM))
    turned = act.T
    c = mm(jnp.concatenate([turned, turned], axis=1), w23).reshape(TOK, GROUP, C3) + gm[:, None, :]
    c = low(c)
    g, gp = gelu_twice(c * scale[None] + shift[None])
    gc = (gp * c).reshape(TILE, C3)
    gp = gp.reshape(TILE, C3)
    gp_o[...] = gp
    g = g.reshape(TILE, C3)
    means, gps, gcs = [], [], []
    for q in range(TILE // 256):
        at = slice(256 * q, 256 * q + 256)
        m = mask[8 * q : 8 * q + 8, at]
        means.append(mm(m, g[at]) * (0.5 * LAM) / count[8 * q : 8 * q + 8, :])
        gps.append(mm(m, gp[at]) * 0.5)
        gcs.append(mm(m, gc[at]) * 0.5)
    to = pl.ds(first, TOK)
    for ref, parts in ((pa_o, means), (pg_o, gps), (pc_o, gcs)):
        ref[to, :] = low(jnp.concatenate(parts, axis=0))


class Gather:
    def __init__(self, blocks, send, recv, base):
        self.blocks, self.sems, self.base = blocks, (send, recv), base
        z, y, x, core = where_am_i()
        half = blocks.shape[-1] // 2
        one, two = pl.ds(0, half), pl.ds(half, half)
        every = slice(None)
        near = [(chip(lax.rem(z + k, NZ), y, x), core) for k in range(1, NZ)]
        over_y, over_x, twin = (chip(z, 1 - y, x), core), (chip(z, y, 1 - x), core), (chip(z, y, x), 1 - core)
        self.stages = [
            [((z, y, x, core), peer) for peer in near],
            [((every, y, x, core, every, one), over_y), ((every, y, x, core, every, two), over_x)],
            [((every, every, x, core, every, one), over_x), ((every, y, every, core, every, two), over_y)],
            [],
        ]
        self.inner = [
            [],
            [((every, y, x, core), twin)],
            [((every, 1 - y, x, core, every, one), twin), ((every, y, 1 - x, core, every, two), twin)],
            [((every, every, 1 - x, core, every, one), twin), ((every, 1 - y, every, core, every, two), twin)],
        ]

    def copies(self, stage, inner):
        table = self.inner if inner else self.stages
        k = self.base + (7 if inner else 0) + sum(len(s) for s in table[:stage])
        out = []
        for i, (index, peer) in enumerate(table[stage]):
            view = self.blocks.at[index]
            out.append(
                pltpu.make_async_remote_copy(
                    src_ref=view, dst_ref=view, send_sem=self.sems[0].at[k + i], recv_sem=self.sems[1].at[k + i],
                    device_id=peer, device_id_type=MESH,
                )
            )
        return out

    def advance(self, stage):
        if stage > 0:
            for copy in self.copies(stage - 1, False):
                copy.wait()
        if stage < 4:
            for copy in self.copies(stage, False) + self.copies(stage, True):
                copy.start()
        else:
            for inner_stage in range(4):
                for copy in self.copies(inner_stage, True):
                    copy.wait()


GATHER_SEMS = 12
ATT_WIDTH, FFN_WIDTH = 4 * D, 6 * D


def attention_rows(bal, pal, stage):
    start = 1
    for at, cols in ((0, 3 * D), (3 * D, D)):
        for j in range(cols // 128):
            stage[0:12, at + 128 * j : at + 128 * j + 128] = bal[pl.ds(start + j, 12, stride=cols // 128), :]
        start += 12 * cols // 128
    for k in range(4):
        for j in range(D // 128):
            to = D * k + 128 * j
            stage[12:16, to : to + 128] = pal[pl.ds(73 + 12 * k + j, 4, stride=3), :]


def attention_flat(stage, bal, pal):
    start = 1
    for at, cols in ((0, 3 * D), (3 * D, D)):
        for j in range(cols // 128):
            bal[pl.ds(start + j, 12, stride=cols // 128), :] = stage[0:12, at + 128 * j : at + 128 * j + 128]
        start += 12 * cols // 128
    for k in range(4):
        for j in range(D // 128):
            at = D * k + 128 * j
            pal[pl.ds(73 + 12 * k + j, 4, stride=3), :] = stage[12:16, at : at + 128]


FFN_PIECES = [(0, 16, 0, FF), (16, 16, 0, FF + D)] + [(32 + 4 * k, 4, 12, D * k) for k in range(4)]
FFN_START = 1 + 12 * 4 * D // 128


def ffn_rows(bal, stage):
    for j in range(FF // 128):
        stage[0:12, 128 * j : 128 * j + 128] = bal[pl.ds(FFN_START + j, 12, stride=FF // 128), :]
    start = FFN_START + 12 * FF // 128
    for row, rows, under, at in FFN_PIECES:
        for j in range(D // 128):
            to = at + 128 * j
            stage[under : under + rows, to : to + 128] = bal[pl.ds(start + 3 * row + j, rows, stride=3), :]


def ffn_flat(stage, bal):
    for j in range(FF // 128):
        bal[pl.ds(FFN_START + j, 12, stride=FF // 128), :] = stage[0:12, 128 * j : 128 * j + 128]
    start = FFN_START + 12 * FF // 128
    for row, rows, under, at in FFN_PIECES:
        for j in range(D // 128):
            bal[pl.ds(start + 3 * row + j, rows, stride=3), :] = stage[
                under : under + rows, at + 128 * j : at + 128 * j + 128
            ]


def place(d):
    return d // 8, d // 4 % 2, d // 2 % 2, d % 2


def forward_kernel(known, dp, *refs):
    refs = list(refs)
    take = lambda count: [refs.pop(0) for _ in range(count)]
    points_ref, tokens_ref, pflat, bflat = take(4) if known else [None] * 4
    rel_o, moment_o, psmall_o, bsmall_o, w2_o, w3_o = take(6)
    w4_o, wqkv_o, wo_o, wf1_o, wf2_o = take(5) if known else [None] * 5
    ext_o, gp1_o, g_o, ps_o, gm_o, fw_o, pooled_o, sv_o, stats_o, wd_o, w23_o, gp_o, pa_o, pg_o, pc_o = take(15)
    ext_s, gm_s, fw_s, e_s, wn_s, w2_s, w23_s, acc3, sums3, ssend3, srecv3 = take(11)
    step = pl.program_id(0)
    tiles = pl.num_programs(0) // 2
    peers = all_peers(dp)
    if known:
        (
            tiny, att, ffn, three, stage, wide, flat2, pal, bal, counts_s, picked_s,
            tsend, trecv, gsend, grecv,
        ) = take(15)
        z, y, x, core = where_am_i()
        gather_w3 = Gather(three, gsend, grecv, 0)
        gather_att = Gather(att, gsend, grecv, GATHER_SEMS)
        gather_ffn = Gather(ffn, gsend, grecv, 2 * GATHER_SEMS)

    @pl.when(step == 0)
    def _():
        greet(peers)
        g_o[...] = jnp.zeros_like(g_o)
        e_s[...] = token_ones()
        if known:
            pal[...] = segments_apart(pflat[...], PSMALL)
            bal[...] = segments_apart(bflat[...], BSMALL)
            for j in range(C3 // 128):
                three[z, y, x, core, :, 128 * j : 128 * j + 128] = low(pal[pl.ds(9 + j, 16, stride=C3 // 128), :])
            attention_rows(bal, pal, stage)
            att[z, y, x, core] = low(stage[:, 0:ATT_WIDTH])
            ffn_rows(bal, stage)
            ffn[z, y, x, core] = low(stage[...])
            moments = geometry(points_ref, tokens_ref, rel_o, counts_s, picked_s)[0:4, :]
            moments = jnp.concatenate([moments, jnp.zeros((4, 120), F32)], axis=1)
            hi, mid, lo = [part.astype(F32) for part in split_three(moments)]
            packed = hi + pltpu.roll(mid, 8, 1) + pltpu.roll(lo, 16, 1)
            rows = [pal[1:9, :], pflat[0:1, :], bflat[0:1, :], packed, jnp.zeros((2, 128), F32)]
            own = tiny.at[me()]
            own[...] = low(jnp.concatenate(rows, axis=0))
            greeted(peers)
            copies = send_to_all(dp, own, lambda k: own, tsend, trecv)
            gather_w3.advance(0)
            gather_att.advance(0)
            for copy in copies:
                copy.wait()
            gather_w3.advance(1)
            gather_att.advance(1)
            gather_ffn.advance(0)
            psmall, bsmall = [], []
            packed = jnp.zeros((4, 128), F32)
            for d in range(dp * NC):
                rows = tiny[d].astype(F32)
                flat2[8 * d : 8 * d + 8, :] = rows[0:8, :]
                psmall.append(rows[8:9, :])
                bsmall.append(rows[9:10, :])
                packed = packed + rows[10:14, :]
            total = packed + pltpu.roll(packed, 120, 1) + pltpu.roll(packed, 112, 1)
            moment_o[...] = jnp.concatenate([total, jnp.zeros((4, 128), F32)], axis=0)
            psmall_o[0:18, :] = flat_rows(jnp.concatenate(psmall, axis=0), PSMALL, 18)
            bsmall_o[0:30, :] = flat_rows(jnp.concatenate(bsmall, axis=0), BSMALL, 30)
            for j in range(2):
                w2_o[:, 128 * j : 128 * j + 128] = low(flat2[pl.ds(j, C1, stride=2), :])
        else:
            greeted(peers)
        small = psmall_o[...]
        forward, backward, stats = prepare_one(moment_o[:, 0:8], small)
        wn_s[...] = forward
        wd_o[...] = backward
        stats_o[...] = stats
        w2_s[0:C1, :] = w2_o[...]
        b2 = as_vector(small, 5, 2)
        w2_s[C1:, :] = low(jnp.concatenate([b2, jnp.zeros((15, C2), F32)], axis=0))

    if known:
        for at_step, gather, number in (
            (2, gather_w3, 2), (3, gather_att, 2), (4, gather_w3, 3), (5, gather_ffn, 1), (6, gather_att, 3),
            (7, gather_w3, 4), (8, gather_ffn, 2), (9, gather_att, 4), (11, gather_ffn, 3),
        ):
            pl.when(step == at_step)(functools.partial(gather.advance, number))

    at = pl.ds(pl.multiple_of(lax.rem(step, tiles) * TILE, TILE), TILE)
    rel = rel_o[:, at]
    first = pl.multiple_of(lax.rem(step, tiles) * TOK, TOK)

    @pl.when(step < tiles)
    def _():
        first_tile(rel, wn_s[...], ext_o, gp1_o)
        ext = ext_o[...]
        ext_s[:, at] = ext[0:C1]
        both = mm_nt(jnp.concatenate([ext, e_s[...]], axis=0), ext)
        g_o[:, 0 : C1 + 16] += both[0 : C1 + 16]
        ps_o[pl.ds(first, TOK), 0 : C1 + 16] = both[C1 + 16 :]

    @pl.when(step == tiles)
    def _():
        if known:
            for d in range(dp * NC):
                w3_o[16 * d : 16 * d + 16, :] = three[place(d)]
        acc3[...] = first_tokens(g_o[:, 0 : C1 + 16], ps_o, w2_s[...], w3_o, pooled_o, gm_s, fw_s)
        copies = sum_start(dp, acc3, sums3, ssend3, srecv3)
        w23 = mm(w2_s[...], w3_o[C2:, :])
        w23_o[...] = w23
        high = low(w23[0:C1])
        w23_s[0:C1, :] = high
        w23_s[C1:, :] = low(w23[0:C1] - high.astype(F32))
        sv_o[...] = third_vectors(sum_finish(acc3, sums3, copies), stats_o[2:3, 0:1], psmall_o)
        mean = sv_o[2:3, :]
        gm = gm_s[...] - mean
        fw_o[...] = low(fw_s[...] + ps_o[:, C1 : C1 + 1] * gm)
        gm = gm + w23[C1 : C1 + 1, :]
        gm_s[...] = gm
        gm_o[...] = low(gm)

    @pl.when(step >= tiles)
    def _():
        second_tile(
            ext_s[:, at], e_s[...] * rel[3:4, :], w23_s[...], gm_s[pl.ds(first, TOK), :],
            ps_o[pl.ds(first, TOK), C1 : C1 + 1], sv_o,
            gp_o, pa_o, pg_o, pc_o, first,
        )

    if known:

        @pl.when(step == tiles + 2)
        def _():
            for d in range(dp * NC):
                under = att[place(d)].astype(F32)
                wide[12 * d : 12 * d + 12, :] = under[0:12, :]
                tail = [under[12:16, D * k : D * k + D] for k in range(4)]
                w4_o[16 * d : 16 * d + 16, :] = low(jnp.concatenate(tail, axis=0))
            wqkv_o[...] = low(wide[:, 0 : 3 * D])
            wo_o[...] = low(wide[:, 3 * D : 4 * D])

        @pl.when(step == 2 * tiles - 1)
        def _():
            gather_ffn.advance(4)
            for d in range(dp * NC):
                block = ffn.at[place(d)]
                under = block[:, 0:FF].astype(F32)
                wide[12 * d : 12 * d + 12, :] = under[0:12, :]
                wf2_o[48 * d : 48 * d + 16, :] = block[:, FF : FF + D]
                wf2_o[48 * d + 16 : 48 * d + 32, :] = block[:, FF + D : FF + 2 * D]
                tail = [under[12:16, D * k : D * k + D] for k in range(4)]
                wf2_o[48 * d + 32 : 48 * d + 48, :] = low(jnp.concatenate(tail, axis=0))
            wf1_o[...] = low(wide[...])


def forward_call(known, dp, count, *args):
    tokens, tiles = count // GROUP, count // TILE
    single = dict(pipeline_mode=pl.Buffered(1))
    full = lambda *s: pl.BlockSpec(s, lambda i: (0, 0), **single)
    early = lambda r: pl.BlockSpec((r, TILE), lambda i: (0, jnp.minimum(i, tiles - 1)))
    given = [
        ((8, count), BF16), ((8, 128), F32), ((24, 128), F32), ((32, 128), F32), ((C1, C2), BF16), ((2 * C2, C3), BF16),
    ]
    gathered = [((C3, D), BF16), ((D, 3 * D), BF16), ((D, D), BF16), ((D, FF), BF16), ((FF, D), BF16)]
    outs = [(full(*s), s, t) for s, t in given + gathered] if known else []
    outs += [(early(C1 + 16), (C1 + 16, count), BF16), (early(C1), (C1, count), BF16)]
    outs += [
        (full(*s), s, t)
        for s, t in (
            ((C1 + 16, 256), F32), ((tokens, 256), F32), ((tokens, C3), BF16), ((tokens, C3), BF16),
            ((tokens, C2), BF16), ((8, C3), F32), ((8, C1), F32), ((8, C1), BF16), ((C1 + 16, C3), F32),
        )
    ]
    outs += [(pl.BlockSpec((TILE, C3), lambda i: (jnp.maximum(i - tiles, 0), 0)), (count, C3), BF16)]
    outs += [(full(tokens, C3), (tokens, C3), BF16)] * 3
    scratch = [
        pltpu.VMEM((C1, count), BF16), pltpu.VMEM((tokens, C3), F32), pltpu.VMEM((tokens, C3), F32),
        pltpu.VMEM((TOK, TILE), BF16), pltpu.VMEM((8, C1), BF16),
        pltpu.VMEM((C1 + 16, C2), BF16), pltpu.VMEM((2 * C1, C3), BF16),
    ] + sum_scratch(dp)
    if known:
        n = dp * NC
        scratch += [
            pltpu.VMEM((n, 16, 128), BF16),
            pltpu.VMEM((NZ, NY, NX, NC, 16, ATT_WIDTH), BF16),
            pltpu.VMEM((NZ, NY, NX, NC, 16, FFN_WIDTH), BF16),
            pltpu.VMEM((NZ, NY, NX, NC, 16, C3), BF16),
            pltpu.VMEM((16, FFN_WIDTH), F32),
            pltpu.VMEM((D, FF), F32),
            pltpu.VMEM((8 * n, 128), F32),
            pltpu.VMEM((PROWS, 128), F32), pltpu.VMEM((BROWS, 128), F32),
            pltpu.VMEM((count // 128, 256), F32), pltpu.VMEM((count // 32, 256), F32),
            pltpu.SemaphoreType.DMA((n - 1,)), pltpu.SemaphoreType.DMA((n - 1,)),
            pltpu.SemaphoreType.DMA((3 * GATHER_SEMS,)), pltpu.SemaphoreType.DMA((3 * GATHER_SEMS,)),
        ]
    return pl.pallas_call(
        functools.partial(forward_kernel, known, dp),
        grid=(2 * tiles,),
        in_specs=[full(*a.shape) for a in args],
        out_specs=[o[0] for o in outs],
        out_shape=shaped(*[o[1:] for o in outs]),
        scratch_shapes=scratch,
        compiler_params=params(collective_id=0, has_side_effects=True),
        name="forward",
    )(*args)


def wide_row(ref, first, rows):
    return jnp.concatenate([ref[k : k + 1, :] for k in range(first, first + rows)], axis=1)


def layer_norm(v, gain, shift):
    centred = v - jnp.mean(v, -1, keepdims=True)
    inverse = lax.rsqrt(jnp.mean(centred * centred, -1, keepdims=True) + EPS_NORM)
    unit = centred * inverse
    return unit, inverse, low(unit * gain + shift)


def norm_back(d_unit, unit, inverse):
    return inverse * (
        d_unit - jnp.mean(d_unit, -1, keepdims=True) - unit * jnp.mean(d_unit * unit, -1, keepdims=True)
    )


def col_sum(v):
    return jnp.sum(v, axis=0, keepdims=True)


def block_step(
    pa_ref, pg_ref, pc_ref, cnt_ref, len_ref, cot_ref, psmall_ref, bsmall_ref, sv_ref,
    w4_ref, wqkv_ref, wo_ref, wf1_ref, wf2_ref,
    out_o, small_o, tok_o, tg_o, back_o, qkv_s, mixed_s, soft_s, dmix_s, dqkv_s, dhid_s,
    ffn_grads, between, token_grads, attention_grads,
):
    count = cnt_ref[:, C1 : C1 + 1]
    scale = HEAD_DIM ** (-0.5)
    b4 = wide_row(psmall_ref, 15, 3)
    ln1_gain, ln1_shift, bo = wide_row(bsmall_ref, 0, 3), wide_row(bsmall_ref, 3, 3), wide_row(bsmall_ref, 6, 3)
    ln2_gain, ln2_shift = wide_row(bsmall_ref, 9, 3), wide_row(bsmall_ref, 12, 3)
    bf1, bf2 = wide_row(bsmall_ref, 15, 12), wide_row(bsmall_ref, 27, 3)

    act = pa_ref[...]
    x_zero = mm(act, w4_ref[...]) + b4
    unit_a, inv_a, normed_a = layer_norm(x_zero, ln1_gain, ln1_shift)
    qkv_s[...] = low(mm(normed_a, wqkv_ref[...]))

    row_cloud = lax.broadcasted_iota(jnp.int32, (PAIR, PAIR), 0) // PATCHES
    col = lax.broadcasted_iota(jnp.int32, (PAIR, PAIR), 1)
    left = lax.broadcasted_iota(jnp.int32, (1, 128), 1) < HEAD_DIM
    zero = jnp.zeros((1, 1), BF16)

    def halves(v):
        return jnp.where(left, v, zero), jnp.where(left, zero, v)

    tiles = pa_ref.shape[0] // PAIR
    for s in range(tiles):
        first = 2 * s
        visible = (row_cloud == col // PATCHES) & (
            lax.rem(col, PATCHES) < jnp.where(col < PATCHES, len_ref[first], len_ref[first + 1])
        )
        rows = slice(PAIR * s, PAIR * s + PAIR)
        for p in range(HEADS // 2):
            at = 128 * p
            q = qkv_s[rows, at : at + 128]
            k = qkv_s[rows, D + at : D + at + 128]
            v = qkv_s[rows, 2 * D + at : 2 * D + at + 128]
            mixed = []
            for a, q_half in enumerate(halves(q)):
                score = jnp.where(visible, mm_nt(q_half, k) * scale, NEG_FILL)
                raised = jnp.exp(score - jnp.max(score, -1, keepdims=True))
                soft = raised / jnp.sum(raised, -1, keepdims=True)
                soft_s[(s * (HEADS // 2) + p) * 2 + a] = soft
                mixed.append(mm(low(soft), v))
            mixed_s[rows, at : at + 128] = low(jnp.where(left, mixed[0], mixed[1]))

    mixed_low = mixed_s[...]
    x_one = x_zero + mm(mixed_low, wo_ref[...]) + bo
    unit_b, inv_b, normed_b = layer_norm(x_one, ln2_gain, ln2_shift)
    hidden, d_hidden = gelu_pair(mm(normed_b, wf1_ref[...]) + bf1)
    dhid_s[...] = low(d_hidden)
    hidden = low(hidden)
    out_o[...] = x_one + mm(hidden, wf2_ref[...]) + bf2

    cot = cot_ref[...]
    grad = low(cot)
    d_pre = mm_nt(grad, wf2_ref[...]) * dhid_s[...].astype(F32)
    d_pre_low = low(d_pre)
    small_o[7:8, :] = col_sum(d_pre)
    ffn_grads(mm_tn(normed_b, d_pre_low), mm_tn(hidden, grad))
    d_normed_b = mm_nt(d_pre_low, wf1_ref[...])
    d_x_one = cot + norm_back(d_normed_b * ln2_gain, unit_b, inv_b)
    d_x_low = low(d_x_one)
    d_x_one_low = d_x_low
    dmix_s[...] = low(mm_nt(d_x_low, wo_ref[...]))

    for s in range(tiles):
        rows = slice(PAIR * s, PAIR * s + PAIR)
        for p in range(HEADS // 2):
            at = 128 * p
            q = qkv_s[rows, at : at + 128]
            k = qkv_s[rows, D + at : D + at + 128]
            v = qkv_s[rows, 2 * D + at : 2 * D + at + 128]
            dm = dmix_s[rows, at : at + 128]
            d_q, d_k, d_v = [], [], []
            for a, dm_half in enumerate(halves(dm)):
                soft = soft_s[(s * (HEADS // 2) + p) * 2 + a]
                d_soft = mm_nt(dm_half, v)
                d_v.append(mm_tn(low(soft), dm))
                d_score = low(soft * (d_soft - jnp.sum(soft * d_soft, -1, keepdims=True)))
                d_q.append(mm(d_score, k))
                d_k.append(mm_tn(d_score, q))
            dqkv_s[rows, at : at + 128] = low(jnp.where(left, d_q[0], d_q[1]) * scale)
            dqkv_s[rows, D + at : D + at + 128] = low(jnp.where(left, d_k[0], d_k[1]) * scale)
            dqkv_s[rows, 2 * D + at : 2 * D + at + 128] = low(jnp.where(left, d_v[0], d_v[1]))

    between()
    d_qkv = dqkv_s[...]
    d_normed_a = mm_nt(d_qkv, wqkv_ref[...])
    d_x_zero = d_x_one + norm_back(d_normed_a * ln1_gain, unit_a, inv_a)
    d_x_low = low(d_x_zero)
    token = mm_nt(d_x_low, w4_ref[...]) / count
    tok_o[...] = token
    grouped = token * pg_ref[...].astype(F32)
    tg_o[...] = grouped
    back_o[...] = as_rows(col_sum(grouped), col_sum(token * pc_ref[...].astype(F32)) * sv_ref[3:4, :])
    token_grads()
    narrow = [
        col_sum(d_normed_a * unit_a), col_sum(d_normed_a), col_sum(d_x_one),
        col_sum(d_normed_b * unit_b), col_sum(d_normed_b), col_sum(cot), col_sum(d_x_zero),
    ]
    for k, row in enumerate(narrow):
        small_o[k : k + 1, 0:D] = row
    attention_grads(mm_tn(normed_a, d_qkv), mm_tn(mixed_low, d_x_one_low), mm_tn(act, d_x_low))


def third_back_tokens(
    totals, tg_ref, sc_ref, gm_ref, ps_ref, pooled_ref, gext_ref, w2_ref, w3_ref, w23_ref, sv_ref, stats_ref,
    kap_o, k_o, wb_o, top_o, corr_o, base_o,
):
    gain = sv_ref[0:1, :]
    n = stats_ref[2:3, 0:1]
    alpha = gain * as_vector(totals, 0, 4) / n
    beta = gain * as_vector(totals, 4, 4) * sv_ref[3:4, :] / n
    count = ps_ref[:, C1 : C1 + 1]
    w23 = w23_ref[...]
    act = low(w23[0:C1])
    per_token = low(gain * tg_ref[...] - (count * alpha + beta * sc_ref[...].astype(F32)))
    pooled = low(mm_nt(per_token, w3_ref[0:C2, :]) / count)
    shifted = low(alpha + beta * gm_ref[...].astype(F32))
    kap_o[...] = low(mm_nt(pooled, w2_ref[...]) - mm_nt(shifted, act))
    k_o[:, 0:C1] = low(-mm_nt(low(w23[0:C1] * beta), act))
    wb_o[...] = low(w23[0:C1] * gain)
    top_o[...] = mm_tn(pooled_ref[...], per_token)
    sums = low(ps_ref[:, 0 : C1 + 16])
    corr_o[...] = mm_tn(sums, shifted) + beta * mm(low(gext_ref[:, 0:C1]), act)
    base_o[...] = mm_tn(sums, pooled)


def last_tile(gp_ref, ext_ref, gp1_ref, rel, tok, kap, k_s, xe_s, wb_ref, wd_ref, h_o, q_o, d_at):
    dn = (gp_ref[...].reshape(TOK, GROUP, C3) * tok[:, None, :]).reshape(TILE, C3)
    xe_s[0:C1, :] = ext_ref[0:C1, :]
    k_s[:, C1 : C1 + TOK] = kap.T
    h_o[...] += mm(ext_ref[...], dn)
    d_act = mm_nt(wb_ref[...], dn) + mm(k_s[...], xe_s[...])
    d_one = low(d_act * gp1_ref[...].astype(F32))
    d_at(mm(wd_ref[...], d_one))
    q_o[...] += mm_nt(rel, d_one)


def last_weights(h, gain, corr, base, w2e, w3_ref):
    m = h * gain - corr
    parts = split_three(m)[0:2]
    grad_w3 = sum(mm_tn(w2e, part) for part in parts)
    return grad_w3, sum(mm_nt(part, w3_ref[C2:, :]) for part in parts) + base


def first_grads(q, moments, psmall, stats):
    mean, inverse, n, scale = stats[0:1], stats[1:2], stats[2:3], stats[3:4]
    w = [psmall[k : k + 1, :] for k in range(3)]
    one = q[3:4, :]
    two = inverse * (sum(w[k] * q[k : k + 1, :] for k in range(3)) - mean * one)
    grad_w = []
    for k in range(3):
        along = sum(w[j] * moments[k : k + 1, j : j + 1] for j in range(3)) - mean * moments[k : k + 1, 3:4]
        grad_w.append(scale * (q[k : k + 1, :] - (one * moments[k : k + 1, 3:4] + two * inverse * along) / n))
    flat = [
        jnp.sum(scale * w[k] * (one - two * inverse * mean) / n, axis=1, keepdims=True) for k in range(3)
    ]
    slope = [
        [jnp.sum(scale * w[k] * two * inverse * w[j] / n, axis=1, keepdims=True) for j in range(3)]
        for k in range(3)
    ]
    return grad_w, two, one, flat, slope


def point_gradient(d_ref, rel_ref, tokens_ref, flat, slope, out_ref, spread_s, sums_s):
    pieces = d_ref.shape[1] // 256
    lane = lax.rem(lax.broadcasted_iota(jnp.int32, (1, 256), 1), GROUP).astype(F32)
    base = jnp.concatenate(flat, axis=0)
    columns = [jnp.concatenate([slope[k][j] for k in range(3)], axis=0) for j in range(3)]
    spread_s[...] = spread_tokens(tokens_ref[pieces : 2 * pieces, :])
    for i in range(pieces):
        at = slice(256 * i, 256 * i + 256)
        rel = rel_ref[:, at].astype(F32)
        d = d_ref[:, at]
        out = d[0:3] + d[4:7] - rel[3:4] * base
        for j in range(3):
            out = out - columns[j] * rel[j : j + 1]
        out_ref[:, at] = out
        sums_s[8 * i : 8 * i + 8, :] = jnp.concatenate([out, jnp.zeros((5, 256), F32)], axis=0)
    sums_s[...] = patch_sum(sums_s[...], patch_ones())
    for i in range(pieces):
        at = slice(256 * i, 256 * i + 256)
        pick = (lane == spread_s[i : i + 1, :]).astype(F32)
        out_ref[:, at] = out_ref[:, at] - pick * sums_s[8 * i : 8 * i + 3, :]


def point_small_rows(grad_w, gain1, shift1, b2, tot, b4):
    rows = list(grad_w) + [gain1, shift1]
    rows += [b2[:, 128 * k : 128 * k + 128] for k in range(2)]
    rows += [tot[4:8, :], tot[0:4, :]]
    rows += [b4[:, 128 * k : 128 * k + 128] for k in range(3)]
    return jnp.concatenate(rows, axis=0)


def block_small_rows(small_ref):
    rows = [small_ref[k : k + 1, 128 * j : 128 * j + 128] for k in range(5) for j in range(3)]
    rows += [small_ref[7:8, 128 * j : 128 * j + 128] for j in range(12)]
    rows += [small_ref[5:6, 128 * j : 128 * j + 128] for j in range(3)]
    return jnp.concatenate(rows, axis=0)


class Scatter:
    def __init__(self, blocks, lands, send, recv, base):
        self.blocks, self.lands, self.sems, self.base = blocks, lands, (send, recv), base
        z, y, x, core = self.at = where_am_i()
        half = blocks.shape[-1] // 2
        self.one, self.two = pl.ds(0, half), pl.ds(half, half)
        every = slice(None)
        mine = blocks.at[core]
        near = [(chip(lax.rem(z + k, NZ), y, x), core) for k in range(1, NZ)]
        over_y, over_x, twin = (chip(z, 1 - y, x), core), (chip(z, y, 1 - x), core), (chip(z, y, x), 1 - core)
        land1, land2, land3, land4 = lands
        self.stages = [
            [(blocks.at[1 - core], land1, twin)],
            [
                (mine.at[:, :, 1 - x, :, self.one], land2.at[0], over_x),
                (mine.at[:, 1 - y, :, :, self.two], land2.at[1], over_y),
            ],
            [
                (mine.at[:, 1 - y, x, :, self.one], land3.at[0], over_y),
                (mine.at[:, y, 1 - x, :, self.two], land3.at[1], over_x),
            ],
            [(mine.at[lax.rem(z + k, NZ), y, x], land4.at[k - 1], near[k - 1]) for k in range(1, NZ)],
        ]

    def copies(self, stage):
        k = self.base + sum(len(s) for s in self.stages[:stage])
        return [
            pltpu.make_async_remote_copy(
                src_ref=src, dst_ref=dst, send_sem=self.sems[0].at[k + i], recv_sem=self.sems[1].at[k + i],
                device_id=peer, device_id_type=MESH,
            )
            for i, (src, dst, peer) in enumerate(self.stages[stage])
        ]

    def advance(self, stage):
        z, y, x, core = self.at
        mine = self.blocks.at[core]
        land1, land2, land3, land4 = self.lands
        if stage > 0:
            for copy in self.copies(stage - 1):
                copy.wait()
        if stage == 1:
            for cz in range(NZ):
                for cy in range(NY):
                    for cx in range(NX):
                        mine[cz, cy, cx] = mine[cz, cy, cx] + land1[cz, cy, cx]
        if stage == 2:
            for cz in range(NZ):
                for k in range(2):
                    mine[cz, k, x, :, self.one] = mine[cz, k, x, :, self.one] + land2[0, cz, k]
                    mine[cz, y, k, :, self.two] = mine[cz, y, k, :, self.two] + land2[1, cz, k]
        if stage == 3:
            for cz in range(NZ):
                mine[cz, y, x, :, self.one] = mine[cz, y, x, :, self.one] + land3[0, cz]
                mine[cz, y, x, :, self.two] = mine[cz, y, x, :, self.two] + land3[1, cz]
        if stage < 4:
            for copy in self.copies(stage):
                copy.start()
            return None
        total = mine[z, y, x].astype(F32)
        for k in range(NZ - 1):
            total = total + land4[k].astype(F32)
        return total


SCATTER_SEMS = 8
POINT_WIDTH = 768


def scatter_scratch(width):
    return [
        pltpu.VMEM((NC, NZ, NY, NX, 16, width), BF16),
        pltpu.VMEM((NZ, NY, NX, 16, width), BF16),
        pltpu.VMEM((2, NZ, 2, 16, width // 2), BF16),
        pltpu.VMEM((2, NZ, 16, width // 2), BF16),
        pltpu.VMEM((NZ - 1, 16, width), BF16),
    ]


def backward_kernel(known, dp, *refs):
    refs = list(refs)
    take = lambda count: [refs.pop(0) for _ in range(count)]
    pa_ref, pg_ref, pc_ref, ps_ref, len_ref, cot_ref, psmall_ref, bsmall_ref, sv_ref, stats_ref, moment_ref = take(11)
    w2_ref, w3_ref, w4_ref, wqkv_ref, wo_ref, wf1_ref, wf2_ref, w23_ref = take(8)
    sc_ref, gm_ref, pooled_ref, gext_ref, wd_ref, rel_ref, tokens_ref, gp_ref, ext_ref, gp1_ref = take(10)
    out_o, pg_o = take(2)
    if known:
        pflat_o, bflat_o = take(2)
    else:
        prow_o, brow_o, gw2_o, gw3_o, gw4_o, gwqkv_o, gwo_o, gwf1_o, gwf2_o = take(9)
    small_s, tok_s, tg_s, acc3, qkv_s, mixed_s, soft_s, dmix_s, dqkv_s, dhid_s = take(10)
    tot_s, kap_s, k_s, wb_s, top_s, corr_s, base_s, h_s, q_s, d_s, xe_s, spread_s, sums_s = take(13)
    acc, slots, ssend, srecv, unused, slots3, ssend3, srecv3 = take(8)
    step = pl.program_id(0)
    steps = pl.num_programs(0)
    peers = all_peers(dp)
    if known:
        ffn0, ffn1, ffn2, ffn3, ffn4, att0, att1, att2, att3, att4, point0, point1, point2, point3, point4 = take(15)
        wide, tall, stage, pstage, pal, bal, gsend, grecv = take(8)
        z, y, x, core = where_am_i()
        ffn = Scatter(ffn0, (ffn1, ffn2, ffn3, ffn4), gsend, grecv, 0)
        att = Scatter(att0, (att1, att2, att3, att4), gsend, grecv, SCATTER_SEMS)
        point = Scatter(point0, (point1, point2, point3, point4), gsend, grecv, 2 * SCATTER_SEMS)

    def ffn_grads(gwf1, gwf2):
        if not known:
            gwf1_o[...], gwf2_o[...] = gwf1, gwf2
            return
        wide[...] = gwf1
        tall[...] = gwf2
        for d in range(dp * NC):
            stage[0:12, 0:FF] = wide[12 * d : 12 * d + 12, :]
            for row, rows, under, at in FFN_PIECES:
                stage[under : under + rows, at : at + D] = tall[48 * d + row : 48 * d + row + rows, :]
            cz, cy, cx, cc = place(d)
            ffn0[cc, cz, cy, cx] = low(stage[...])
        greeted(peers)
        ffn.advance(0)

    def between():
        if known:
            ffn.advance(1)

    def token_grads():
        if not known:
            greeted(peers)
        sum_start(dp, acc3, slots3, ssend3, srecv3)

    def attention_grads(gwqkv, gwo, gw4):
        if not known:
            gwqkv_o[...], gwo_o[...], gw4_o[...] = gwqkv, gwo, gw4
            return
        wide[:, 0 : 3 * D] = gwqkv
        wide[:, 3 * D :] = gwo
        tall[0:C3, :] = gw4
        for d in range(dp * NC):
            stage[0:12, 0:ATT_WIDTH] = wide[12 * d : 12 * d + 12, :]
            for k in range(4):
                stage[12:16, D * k : D * k + D] = tall[16 * d + 4 * k : 16 * d + 4 * k + 4, :]
            cz, cy, cx, cc = place(d)
            att0[cc, cz, cy, cx] = low(stage[:, 0:ATT_WIDTH])
        att.advance(0)
        ffn.advance(2)
        att.advance(1)

    @pl.when(step == 0)
    def _():
        greet(peers)
        block_step(
            pa_ref, pg_ref, pc_ref, ps_ref, len_ref, cot_ref, psmall_ref, bsmall_ref, sv_ref,
            w4_ref, wqkv_ref, wo_ref, wf1_ref, wf2_ref,
            out_o, small_s, tok_s, tg_s, acc3, qkv_s, mixed_s, soft_s, dmix_s, dqkv_s, dhid_s,
            ffn_grads, between, token_grads, attention_grads,
        )
        for ref in (h_s, q_s):
            ref[...] = jnp.zeros_like(ref)
        xe_s[C1:, :] = token_ones()
        tot_s[...] = sum_finish(acc3, slots3, sum_copies(dp, acc3, lambda k: slots3.at[k], ssend3, srecv3))
        third_back_tokens(
            tot_s[...], tg_s, sc_ref, gm_ref, ps_ref, pooled_ref, gext_ref, w2_ref, w3_ref, w23_ref, sv_ref, stats_ref,
            kap_s, k_s, wb_s, top_s, corr_s, base_s,
        )

    if known:
        for at_step, group, number in ((3, ffn, 3), (4, att, 2), (6, att, 3)):
            pl.when(step == at_step)(functools.partial(group.advance, number))

    @pl.when(step >= 1)
    def _():
        tile = step - 1
        at = pl.ds(pl.multiple_of(tile * TILE, TILE), TILE)
        ts = pl.ds(pl.multiple_of(tile * TOK, TOK), TOK)

        def put(d):
            d_s[:, at] = d

        last_tile(
            gp_ref, ext_ref, gp1_ref, rel_ref[:, at], low(tok_s[ts, :] * 0.5), kap_s[ts, :], k_s, xe_s, wb_s, wd_ref,
            h_s, q_s, put,
        )

    @pl.when(step == steps - 1)
    def _():
        acc[...] = q_s[...]
        copies = sum_start(dp, acc, slots, ssend, srecv)
        b2 = as_vector(psmall_ref, 5, 2)
        w2e = jnp.concatenate([w2_ref[...], low(jnp.concatenate([b2, jnp.zeros((15, C2), F32)], axis=0))], axis=0)
        gw3, gw2 = last_weights(h_s[...], sv_ref[0:1, :], corr_s[...], base_s[...], w2e, w3_ref)
        none = jnp.zeros((1, 128), F32)
        prow = point_small_rows([none] * 3, none, none, gw2[C1 : C1 + 1, :], jnp.zeros((8, 128), F32), small_s[6:7, 0:D])
        brow = block_small_rows(small_s)
        if known:
            pstage[...] = jnp.zeros_like(pstage)
            for d in range(dp * NC):
                if d < 16:
                    pstage[:, 0:C3] = top_s[16 * d : 16 * d + 16, :]
                else:
                    pstage[:, 0:C3] = gw3[16 * (d - 16) : 16 * (d - 16) + 16, :]
                pstage[0:4, C3 : C3 + C2] = gw2[4 * d : 4 * d + 4, :]
                pstage[4:5, C3 : C3 + 128] = piece_of(prow, PSMALL * d, PSMALL)
                pstage[5:6, C3 : C3 + 128] = piece_of(brow, BSMALL * d, BSMALL)
                cz, cy, cx, cc = place(d)
                point0[cc, cz, cy, cx] = low(pstage[...])
            point.advance(0)
            point.advance(1)
        totals = sum_finish(acc, slots, copies)
        grad_w, gain1, shift1, flat, slope = first_grads(totals, moment_ref[...], psmall_ref[...], stats_ref[...])
        full_rows = point_small_rows(grad_w, gain1, shift1, jnp.zeros((1, C2), F32), tot_s[...], jnp.zeros((1, D), F32))
        if known:
            point.advance(2)
            stage[...] = ffn.advance(4)
            ffn_flat(stage, bal)
            stage[:, 0:ATT_WIDTH] = att.advance(4)
            attention_flat(stage, bal, pal)
            point.advance(3)
        point_gradient(d_s, rel_ref, tokens_ref, flat, slope, pg_o, spread_s, sums_s)
        if not known:
            prow_o[0:18, :] = prow + full_rows * (1.0 / (dp * NC))
            brow_o[0:30, :] = brow
            gw2_o[...] = gw2[0:C1]
            gw3_o[0:C2, :] = top_s[...]
            gw3_o[C2:, :] = gw3
            return
        own = jnp.zeros((1, 128), F32)
        for d in range(dp * NC):
            own = own + jnp.where(me() == d, piece_of(full_rows, PSMALL * d, PSMALL), 0.0)
        pstage[...] = point.advance(4)
        for j in range(C2 // 128):
            pal[pl.ds(1 + j, 4, stride=2), :] = pstage[0:4, C3 + 128 * j : C3 + 128 * j + 128]
        for j in range(C3 // 128):
            pal[pl.ds(9 + j, 16, stride=4), :] = pstage[:, 128 * j : 128 * j + 128]
        pflat_o[...] = segments_joined(pal[...], pstage[4:5, C3 : C3 + 128] + own, PSMALL)
        bflat_o[...] = segments_joined(bal[...], pstage[5:6, C3 : C3 + 128], BSMALL)


def backward_call(known, dp, *args):
    count = args[24].shape[1]
    tokens, tiles = count // GROUP, count // TILE
    single = dict(pipeline_mode=pl.Buffered(1))
    full = lambda *s: pl.BlockSpec(s, lambda i: (0, 0), **single)
    cols = lambda r: pl.BlockSpec((r, TILE), lambda i: (0, jnp.maximum(i - 1, 0)))
    specs = [full(*a.shape) for a in args[:26]]
    specs[4] = pl.BlockSpec(memory_space=pltpu.SMEM)
    specs += [pl.BlockSpec((TILE, C3), lambda i: (jnp.maximum(i - 1, 0), 0)), cols(C1 + 16), cols(C1)]
    outs = [((tokens, D), F32), ((3, count), F32)]
    if known:
        outs += [((PROWS, 128), F32), ((BROWS, 128), F32)]
    else:
        outs += [((24, 128), F32), ((32, 128), F32), ((C1, C2), F32), ((2 * C2, C3), F32), ((C3, D), F32)]
        outs += [((D, 3 * D), F32), ((D, D), F32), ((D, FF), F32), ((FF, D), F32)]
    pieces = count // 256
    scratch = [
        pltpu.VMEM((8, FF), F32), pltpu.VMEM((tokens, C3), F32), pltpu.VMEM((tokens, C3), F32), pltpu.VMEM((8, 128), F32),
        pltpu.VMEM((tokens, 3 * D), BF16), pltpu.VMEM((tokens, D), BF16),
        pltpu.VMEM((tokens // PAIR * HEADS, PAIR, PAIR), F32), pltpu.VMEM((tokens, D), BF16),
        pltpu.VMEM((tokens, 3 * D), BF16), pltpu.VMEM((tokens, FF), BF16),
        pltpu.VMEM((8, 128), F32), pltpu.VMEM((tokens, C1), BF16), pltpu.VMEM((C1, C1 + TOK), BF16),
        pltpu.VMEM((C1, C3), BF16), pltpu.VMEM((C2, C3), F32), pltpu.VMEM((C1 + 16, C3), F32),
        pltpu.VMEM((C1 + 16, C2), F32), pltpu.VMEM((C1 + 16, C3), F32), pltpu.VMEM((8, C1), F32),
        pltpu.VMEM((8, count), F32), pltpu.VMEM((C1 + TOK, TILE), BF16),
        pltpu.VMEM((pieces, 256), F32), pltpu.VMEM((8 * pieces, 256), F32),
    ]
    scratch += sum_scratch(dp) + sum_scratch(dp)
    if known:
        scratch += scatter_scratch(FFN_WIDTH) + scatter_scratch(ATT_WIDTH) + scatter_scratch(POINT_WIDTH)
        scratch += [
            pltpu.VMEM((D, FF), F32), pltpu.VMEM((FF, D), F32),
            pltpu.VMEM((16, FFN_WIDTH), F32), pltpu.VMEM((16, POINT_WIDTH), F32),
            pltpu.VMEM((PROWS, 128), F32), pltpu.VMEM((BROWS, 128), F32),
            pltpu.SemaphoreType.DMA((3 * SCATTER_SEMS,)), pltpu.SemaphoreType.DMA((3 * SCATTER_SEMS,)),
        ]
    return pl.pallas_call(
        functools.partial(backward_kernel, known, dp),
        grid=(1 + tiles,),
        in_specs=specs,
        out_specs=[full(*s) for s, t in outs],
        out_shape=shaped(*outs),
        scratch_shapes=scratch,
        compiler_params=params(collective_id=1, has_side_effects=True),
        name="backward",
    )(*args)


def geometry_kernel(points_ref, tokens_ref, rel_o, moment_o, counts_s, picked_s):
    moment_o[...] = jnp.concatenate(
        [geometry(points_ref, tokens_ref, rel_o, counts_s, picked_s), jnp.zeros((8, 120), F32)], axis=1
    )


def geometry_call(points, tokens):
    count = points.shape[1]
    return pl.pallas_call(
        geometry_kernel,
        out_shape=shaped(((8, count), BF16), ((8, 128), F32)),
        in_specs=vmem(2),
        out_specs=vmem(2),
        scratch_shapes=[pltpu.VMEM((count // 128, 256), F32), pltpu.VMEM((count // 32, 256), F32)],
        compiler_params=params(),
        name="geometry",
    )(points, tokens)


def gather_plain(points, tokens, point_master, block_master, devices):
    rel, moments = geometry_call(points, tokens)
    moments = lax.psum(moments, AXES)
    tables = []
    for master, layout in ((point_master, point_layout()), (block_master, block_layout())):
        offset = 0
        parts = []
        for seg_len in segment_lengths(layout, devices):
            piece = master[offset : offset + seg_len // devices].astype(BF16)
            offset += seg_len // devices
            parts.append(lax.all_gather(piece, AXES, axis=0, tiled=True))
        tables.append(parts)
    (ps, w2, w3, w4), (bs, wqkv, wo, wf1, wf2) = tables

    def rows_of(v, rows, used):
        v = v[:used].astype(F32).reshape(-1, 128)
        return jnp.concatenate([v, jnp.zeros((rows - v.shape[0], 128), F32)], axis=0)

    small = (rel, moments, rows_of(ps, 24, 18 * 128), rows_of(bs, 32, 30 * 128))
    point = (w2.reshape(C1, C2), w3.reshape(2 * C2, C3))
    block = (w4.reshape(C3, D), wqkv.reshape(D, 3 * D), wo.reshape(D, D), wf1.reshape(D, FF), wf2.reshape(FF, D))
    return small + point, block


def scatter_plain(devices, prow, brow, gw2, gw3, gw4, gwqkv, gwo, gwf1, gwf2):
    pieces = []
    for layout, tables in (
        (point_layout(), (prow[:18], gw2, gw3, gw4)),
        (block_layout(), (brow[:30], gwqkv, gwo, gwf1, gwf2)),
    ):
        parts = []
        for values, seg_len in zip(tables, segment_lengths(layout, devices)):
            values = values.reshape(-1)
            values = jnp.concatenate([values, jnp.zeros((seg_len - values.shape[0],), F32)])
            parts.append(lax.psum_scatter(values, AXES, scatter_dimension=0, tiled=True))
        pieces.append(parts)
    return pieces


def adam_update(master, moment_one, moment_two, gradient, step_rates, decays):
    one_new = BETA_ONE * moment_one + (1.0 - BETA_ONE) * gradient
    two_new = BETA_TWO * moment_two + (1.0 - BETA_TWO) * gradient * gradient
    fix_one = 1.0 - BETA_ONE**STEP
    fix_two = 1.0 - BETA_TWO**STEP
    direction = one_new / fix_one / (jnp.sqrt(two_new / fix_two) + ADAM_EPS)
    master_new = master - step_rates * (direction + decays * master)
    return (master_new, one_new, two_new)


def flat_of(vector, rows):
    return jnp.pad(vector, (0, rows * 128 - vector.shape[0])).reshape(rows, 128)


def on_device(
    points, point_count, centre_slot, cloud_length, cotangent, point_master, block_master,
    point_first, block_first, point_second, block_second,
):
    dp, fsdp = lax.axis_size("dp"), lax.axis_size("fsdp")
    devices = dp * fsdp
    own_rank = lax.axis_index(AXES)
    known = dp == NZ * NY * NX and fsdp == NC
    count = points.shape[1]
    tokens = jnp.concatenate([point_count, centre_slot]).reshape(-1, 8)
    if known:
        outs = forward_call(
            True, dp, count, points, tokens, flat_of(point_master, PROWS), flat_of(block_master, BROWS)
        )
        given, block, outs = outs[:6], outs[6:11], outs[11:]
    else:
        given, block = gather_plain(points, tokens, point_master, block_master, devices)
        outs = forward_call(False, dp, count, *given)
    rel, moments, psmall, bsmall, w2, w3 = given
    ext, gp1, gext, ps, gm, sc, pooled, sv, stats, wd, w23, gp, pa, pg, pc = outs
    outs = backward_call(
        known, dp, pa, pg, pc, ps, cloud_length, cotangent, psmall, bsmall, sv, stats, moments,
        w2, w3, *block, w23, sc, gm, pooled, gext, wd, rel, tokens, gp, ext, gp1,
    )
    tokens_out, point_grad = outs[:2]
    if known:
        point_gradient_vec = outs[2].reshape(-1)[: point_master.shape[0]]
        block_gradient = outs[3].reshape(-1)[: block_master.shape[0]]
        block_small = block_gradient[:BSMALL]
    else:
        point_parts, block_parts = scatter_plain(devices, *outs[2:])
        block_small = block_parts[0]
        point_gradient_vec = jnp.concatenate(point_parts)
        block_gradient = jnp.concatenate(block_parts)
    point_rates, point_decays = shard_rates(point_layout(), devices, own_rank)
    block_rates, block_decays = shard_rates(block_layout(), devices, own_rank)
    point_new, point_one, point_two = adam_update(
        point_master, point_first, point_second, point_gradient_vec, point_rates, point_decays
    )
    block_new, block_one, block_two = adam_update(
        block_master, block_first, block_second, block_gradient, block_rates, block_decays
    )
    return (
        tokens_out, point_grad, point_new, block_new, point_one, block_one, point_two, block_two,
        point_new.astype(BF16), block_new.astype(BF16), block_small,
    )


def solution(mesh):
    split = P(AXES)
    return jax.shard_map(
        on_device,
        mesh=mesh,
        in_specs=(P(None, AXES), split, split, split, P(AXES, None)) + (split,) * 6,
        out_specs=(P(AXES, None), P(None, AXES)) + (split,) * 9,
        check_vma=False,
    )
```

```python
import functools
import math

import jax
import jax.numpy as jnp
from jax import lax
from jax.experimental import pallas as pl
from jax.experimental.pallas import tpu as pltpu
from jax.sharding import PartitionSpec as P

C1 = 128
C2 = 256
C3 = 512
D = 384
HEADS = 6
HEAD_DIM = 64
FF = 1536
GROUP = 32
PATCHES = 64
STEP = 10

EPS_NORM = 1e-05
BETA_ONE = 0.9
BETA_TWO = 0.95
ADAM_EPS = 1e-08
DECAY_RATE = 0.05
NEG_FILL = -1e30

F32 = jnp.float32
BF16 = jnp.bfloat16
AXES = ("dp", "fsdp")
MESH = pl.DeviceIdType.MESH
VMEM_LIMIT = 60 * 2**20
TILE = 2048
TOK = TILE // GROUP
STEP_TILES = 2
AHEAD = 4
WIDE = TILE * STEP_TILES
PAIR = 256

NZ, NY, NX, NC = 4, 2, 2, 2
PROWS, BROWS = 128, 440
PSMALL, BSMALL = 72, 120


def point_layout():
    return [
        [
            ("w1", (3, C1), 3.0 ** (-0.5)),
            ("bn1_gain", (C1,), 0.0),
            ("bn1_shift", (C1,), -1.0),
            ("b2", (C2,), -1.0),
            ("bn3_gain", (C3,), 0.0),
            ("bn3_shift", (C3,), -1.0),
            ("b4", (D,), -1.0),
        ],
        [("w2", (C1, C2), C1 ** (-0.5))],
        [("w3", (2 * C2, C3), (2 * C2) ** (-0.5))],
        [("w4", (C3, D), C3 ** (-0.5))],
    ]


def block_layout():
    return [
        [
            ("ln1_gain", (D,), 0.0),
            ("ln1_shift", (D,), -1.0),
            ("bo", (D,), -1.0),
            ("ln2_gain", (D,), 0.0),
            ("ln2_shift", (D,), -1.0),
            ("bf1", (FF,), -1.0),
            ("bf2", (D,), -1.0),
        ],
        [("wqkv", (D, 3 * D), D ** (-0.5))],
        [("wo", (D, D), 3.0 * D ** (-0.5))],
        [("wf1", (D, FF), D ** (-0.5))],
        [("wf2", (FF, D), FF ** (-0.5))],
    ]


def rate_for(spread):
    return 2.0 * spread if spread > 0.0 else 0.5 if spread == 0.0 else 0.6


def decay_for(spread):
    return DECAY_RATE if spread > 0.0 else 0.0


def segment_lengths(layout, devices):
    lengths_out = []
    for segment in layout:
        used_len = sum((math.prod(entry[1]) for entry in segment))
        lengths_out.append(-(-used_len // devices) * devices)
    return lengths_out


def shard_rates(layout, devices, own_rank):
    lengths = segment_lengths(layout, devices)
    position = jnp.arange(sum(lengths) // devices, dtype=jnp.int32)
    rates = jnp.zeros(position.shape, F32)
    decays = jnp.zeros(position.shape, F32)
    start = 0
    for segment, seg_len in zip(layout, lengths):
        piece_len = seg_len // devices
        here = (position >= start) & (position < start + piece_len)
        inner = position + (own_rank * piece_len - start)
        offset = 0
        for entry_label, entry_dims, spread in segment:
            extent = math.prod(entry_dims)
            inside = here & (inner >= offset) & (inner < offset + extent)
            rates = jnp.where(inside, rate_for(spread), rates)
            decays = jnp.where(inside, decay_for(spread), decays)
            offset += extent
        start += piece_len
    return rates, decays


def mm(a, b):
    return jnp.dot(a, b, preferred_element_type=F32)


def mm_tn(a, b):
    return lax.dot_general(a, b, (((0,), (0,)), ((), ())), preferred_element_type=F32)


def mm_nt(a, b):
    return lax.dot_general(a, b, (((1,), (1,)), ((), ())), preferred_element_type=F32)


def low(v):
    return v.astype(BF16)


def split_three(v):
    hi = low(v)
    rest = v - hi.astype(F32)
    mid = low(rest)
    return hi, mid, low(rest - mid.astype(F32))


def mm_exact(a, b):
    hi, mid, lo = split_three(a)
    return mm(hi, b) + (mm(mid, b) + mm(lo, b))


LAM = (math.sqrt(2.0 / math.pi) * 0.044715) ** (-1.0 / 3.0)
ARG = math.sqrt(2.0 / math.pi) * LAM


def gelu_twice(y):
    square = y * y
    near = square + ARG
    t = jnp.tanh(y * near)
    up = 1.0 + t
    g = y * up
    return g, up + g * (1.0 - t) * (near + (square + square))


def gelu_pair(v):
    g, d = gelu_twice(low(v * (1.0 / LAM)))
    return low(g.astype(F32) * (0.5 * LAM)), d * 0.5


def patch_ones():
    i = lax.broadcasted_iota(jnp.int32, (256, 256), 0) // GROUP
    j = lax.broadcasted_iota(jnp.int32, (256, 256), 1) // GROUP
    return (i == j).astype(F32).astype(BF16)


def token_ones():
    t = lax.broadcasted_iota(jnp.int32, (TOK, TILE), 0)
    p = lax.broadcasted_iota(jnp.int32, (TOK, TILE), 1) // GROUP
    return (t == p).astype(F32).astype(BF16)


def patch_sum(rows, ones):
    return mm_exact(rows, ones)


def rank_of(peer_dp, peer_core):
    return peer_dp * NC + peer_core


def me():
    return rank_of(lax.axis_index("dp"), lax.axis_index("fsdp"))


def all_peers(dp):
    n = dp * NC
    peers = []
    for k in range(1, n):
        p = lax.rem(me() + k, n)
        peers.append((p // NC, lax.rem(p, NC)))
    return peers


def greet(peers):
    barrier = pltpu.get_barrier_semaphore()
    for peer in peers:
        pl.semaphore_signal(barrier, inc=1, device_id=peer, device_id_type=MESH)


def greeted(peers):
    pl.semaphore_wait(pltpu.get_barrier_semaphore(), len(peers))


def sum_copies(dp, src, dst_of, send, recv):
    return [
        pltpu.make_async_remote_copy(
            src_ref=src, dst_ref=dst_of(k), send_sem=send.at[k], recv_sem=recv.at[k],
            device_id=peer, device_id_type=MESH,
        )
        for k, peer in enumerate(all_peers(dp))
    ]


def send_to_all(dp, src, dst_of, send, recv):
    copies = sum_copies(dp, src, dst_of, send, recv)
    for copy in copies:
        copy.start()
    return copies


def sum_start(dp, acc, slots, send, recv):
    return send_to_all(dp, acc, lambda k: slots.at[k], send, recv)


def sum_finish(acc, slots, copies):
    for copy in copies:
        copy.wait()
    return acc[...] + jnp.sum(slots[...], axis=0)


def sum_scratch(dp):
    n = dp * NC - 1
    return [
        pltpu.VMEM((8, 128), F32), pltpu.VMEM((n, 8, 128), F32),
        pltpu.SemaphoreType.DMA((n,)), pltpu.SemaphoreType.DMA((n,)),
    ]


def as_rows(*vectors):
    return jnp.concatenate(
        [v[:, 128 * k : 128 * k + 128] for v in vectors for k in range(v.shape[1] // 128)], axis=0
    )


def as_vector(rows, first, count):
    return jnp.concatenate([rows[k : k + 1, :] for k in range(first, first + count)], axis=1)


def vmem(count):
    return [pl.BlockSpec(memory_space=pltpu.VMEM)] * count


def shaped(*items):
    return [jax.ShapeDtypeStruct(s, t) for s, t in items]


def params(**more):
    return pltpu.CompilerParams(vmem_limit_bytes=VMEM_LIMIT, **more)


def where_am_i():
    at = lax.axis_index("dp")
    return at // (NY * NX), lax.rem(at // NX, NY), lax.rem(at, NX), lax.axis_index("fsdp")


def chip(z, y, x):
    return (z * NY + y) * NX + x


def spread_tokens(values):
    t = lax.broadcasted_iota(jnp.int32, (8, 256), 0)
    p = lax.broadcasted_iota(jnp.int32, (8, 256), 1) // GROUP
    return mm(low(values.astype(F32)), low((t == p).astype(F32)))


def geometry(points_ref, tokens_ref, rel_ref, counts_s, picked_s):
    pieces = points_ref.shape[1] // 256
    lane = lax.rem(lax.broadcasted_iota(jnp.int32, (1, 256), 1), GROUP).astype(F32)
    counts_s[...] = spread_tokens(tokens_ref[...])
    for i in range(pieces):
        at = slice(256 * i, 256 * i + 256)
        pick = (lane == counts_s[pieces + i : pieces + i + 1, :]).astype(F32)
        rows = points_ref[:, at] * pick
        picked_s[8 * i : 8 * i + 8, :] = jnp.concatenate([rows, jnp.zeros((5, 256), F32)], axis=0)
    picked_s[...] = patch_sum(picked_s[...], patch_ones())
    for i in range(pieces):
        at = slice(256 * i, 256 * i + 256)
        valid = (lane < counts_s[i : i + 1, :]).astype(F32)
        relative = (points_ref[:, at] - picked_s[8 * i : 8 * i + 3, :]) * valid
        rel_ref[:, at] = low(jnp.concatenate([relative, valid, relative, valid], axis=0))
    rel = rel_ref[...]
    return mm_nt(rel, rel)


def prepare_one(moments, small):
    n = moments[3:4, 3:4]
    w = [small[k : k + 1, :] for k in range(3)]
    gain, shift = small[3:4, :], small[4:5, :]
    mean = sum(w[k] * moments[k : k + 1, 3:4] for k in range(3)) / n
    square = jnp.zeros_like(mean)
    for j in range(3):
        for k in range(3):
            square = square + w[j] * w[k] * moments[j : j + 1, k : k + 1]
    inverse = lax.rsqrt(square / n - mean * mean + EPS_NORM)
    scale = inverse * gain
    scaled = [wk * scale for wk in w]
    parts = [v * (1.0 / LAM) for v in scaled + [shift - mean * scale]]
    high = [low(v) for v in parts]
    rest = [low(v - h.astype(F32)) for v, h in zip(parts, high)]
    forward = jnp.concatenate(high + rest, axis=0)
    high = [low(v) for v in scaled]
    rest = [low(v - h.astype(F32)) for v, h in zip(scaled, high)]
    zero = jnp.zeros((1, C1), BF16)
    backward = jnp.concatenate(high + [zero] + rest + [zero], axis=0)
    stats = jnp.concatenate(
        [mean, inverse, jnp.broadcast_to(n, (1, C1)), scale, jnp.zeros((4, C1), F32)], axis=0
    )
    return forward, backward, stats


def flat_rows(pieces, length, rows):
    lane = lax.broadcasted_iota(jnp.int32, (1, 128), 1)
    out = [jnp.zeros((1, 128), F32) for _ in range(rows)]
    for r in range(pieces.shape[0]):
        row = jnp.where(lane < length, pieces[r : r + 1, :], 0.0)
        at = length * r
        row = pltpu.roll(row, at % 128, 1) if at % 128 else row
        first = at // 128
        out[first] = out[first] + jnp.where(lane >= at % 128, row, 0.0)
        if at % 128 + length > 128:
            out[first + 1] = out[first + 1] + jnp.where(lane < at % 128, row, 0.0)
    return jnp.concatenate(out, axis=0)


def piece_of(rows, at, length):
    lane = lax.broadcasted_iota(jnp.int32, (1, 128), 1)
    first, shift = at // 128, at % 128
    row = rows[first : first + 1, :]
    if shift:
        row = pltpu.roll(row, 128 - shift, 1)
        if shift + length > 128:
            other = pltpu.roll(rows[first + 1 : first + 2, :], 128 - shift, 1)
            row = jnp.where(lane < 128 - shift, row, other)
    return jnp.where(lane < length, row, 0.0)


def segments_apart(flat, small):
    lane = lax.broadcasted_iota(jnp.int32, (1, 128), 1)
    turned = pltpu.roll(flat, 128 - small, 1)
    return jnp.where(lane < 128 - small, pltpu.roll(turned, 1, 0), turned)


def segments_joined(rows, first, small):
    lane = lax.broadcasted_iota(jnp.int32, (1, 128), 1)
    turned = pltpu.roll(rows, small, 1)
    row = lax.broadcasted_iota(jnp.int32, (rows.shape[0], 1), 0)
    joined = jnp.where(lane < small, turned, pltpu.roll(turned, rows.shape[0] - 1, 0))
    return jnp.where((lane < small) & (row == 0), first, joined)


def first_tile(rel, wn, ext_ref, gp_ref, start):
    valid = rel[3:4, :].astype(F32)
    for j in range(TILE // 256):
        at = slice(256 * j, 256 * j + 256)
        to = slice(start + 256 * j, start + 256 * j + 256)
        g, d = gelu_twice(mm_tn(wn, rel[:, at]))
        ext_ref[0:C1, to] = low(g * (valid[:, at] * (0.5 * LAM)))
        gp_ref[:, to] = low(d * (valid[:, at] * 0.5))
    ext_ref[C1:, start : start + TILE] = jnp.concatenate([rel[3:4], jnp.zeros((15, TILE), BF16)], axis=0)


def first_tokens(gext, ps_ref, w2e, w3_ref, pooled_o, gm_o, fw_o):
    lower = w3_ref[C2:, :]
    count = ps_ref[:, C1 : C1 + 1]
    fs = mm_exact(ps_ref[:, 0 : C1 + 16], w2e)
    pooled = low(fs / count)
    pooled_o[...] = pooled
    g = mm(pooled, w3_ref[0:C2, :])
    gm_o[...] = g
    fw = mm_exact(fs, lower)
    fw_o[...] = fw
    gram = sum(mm_tn(w2e, part) for part in split_three(mm_exact(gext, w2e)))
    one = jnp.sum(fw + count * g, axis=0, keepdims=True)
    two = jnp.sum(mm_exact(gram, lower) * lower.astype(F32), axis=0, keepdims=True)
    two = two + jnp.sum(g * (2.0 * fw + count * g), axis=0, keepdims=True)
    return as_rows(one, two)


def third_vectors(totals, n, psmall_ref):
    mean = as_vector(totals, 0, 4) / n
    inverse = lax.rsqrt(as_vector(totals, 4, 4) / n - mean * mean + EPS_NORM)
    gain, shift = as_vector(psmall_ref, 7, 4), as_vector(psmall_ref, 11, 4)
    return jnp.concatenate([inverse * gain, shift, mean, inverse, jnp.zeros((4, C3), F32)], axis=0)


def second_tile(act, mask, w23, gm, count, sv_ref, gp_o, start, pa_o, pg_o, pc_o, first):
    scale, shift = low(sv_ref[0:1, :] * (1.0 / LAM)), low(sv_ref[1:2, :] * (1.0 / LAM))
    turned = act.T
    c = mm(jnp.concatenate([turned, turned], axis=1), w23).reshape(TOK, GROUP, C3) + gm[:, None, :]
    c = low(c)
    g, gp = gelu_twice(c * scale[None] + shift[None])
    gc = (gp * c).reshape(TILE, C3)
    gp = gp.reshape(TILE, C3)
    gp_o[start : start + TILE, :] = gp
    g = g.reshape(TILE, C3)
    means, gps, gcs = [], [], []
    for q in range(TILE // 256):
        at = slice(256 * q, 256 * q + 256)
        m = mask[8 * q : 8 * q + 8, at]
        means.append(mm(m, g[at]) * (0.5 * LAM) / count[8 * q : 8 * q + 8, :])
        gps.append(mm(m, gp[at]) * 0.5)
        gcs.append(mm(m, gc[at]) * 0.5)
    for ref, parts in ((pa_o, means), (pg_o, gps), (pc_o, gcs)):
        ref[first, :] = low(jnp.concatenate(parts, axis=0))


class Gather:
    def __init__(self, blocks, send, recv, base):
        self.blocks, self.sems, self.base = blocks, (send, recv), base
        z, y, x, core = where_am_i()
        half = blocks.shape[-1] // 2
        one, two = pl.ds(0, half), pl.ds(half, half)
        every = slice(None)
        near = [(chip(lax.rem(z + k, NZ), y, x), core) for k in range(1, NZ)]
        over_y, over_x, twin = (chip(z, 1 - y, x), core), (chip(z, y, 1 - x), core), (chip(z, y, x), 1 - core)
        self.stages = [
            [((z, y, x, core), peer) for peer in near],
            [((every, y, x, core, every, one), over_y), ((every, y, x, core, every, two), over_x)],
            [((every, every, x, core, every, one), over_x), ((every, y, every, core, every, two), over_y)],
            [],
        ]
        self.inner = [
            [],
            [((every, y, x, core), twin)],
            [((every, 1 - y, x, core, every, one), twin), ((every, y, 1 - x, core, every, two), twin)],
            [((every, every, 1 - x, core, every, one), twin), ((every, 1 - y, every, core, every, two), twin)],
        ]

    def copies(self, stage, inner):
        table = self.inner if inner else self.stages
        k = self.base + (7 if inner else 0) + sum(len(s) for s in table[:stage])
        out = []
        for i, (index, peer) in enumerate(table[stage]):
            view = self.blocks.at[index]
            out.append(
                pltpu.make_async_remote_copy(
                    src_ref=view, dst_ref=view, send_sem=self.sems[0].at[k + i], recv_sem=self.sems[1].at[k + i],
                    device_id=peer, device_id_type=MESH,
                )
            )
        return out

    def advance(self, stage):
        if stage > 0:
            for copy in self.copies(stage - 1, False):
                copy.wait()
        if stage < 4:
            for copy in self.copies(stage, False) + self.copies(stage, True):
                copy.start()
        else:
            for inner_stage in range(4):
                for copy in self.copies(inner_stage, True):
                    copy.wait()


GATHER_SEMS = 12
ATT_WIDTH, FFN_WIDTH = 4 * D, 6 * D


def attention_rows(bal, pal, stage):
    start = 1
    for at, cols in ((0, 3 * D), (3 * D, D)):
        for j in range(cols // 128):
            stage[0:12, at + 128 * j : at + 128 * j + 128] = bal[pl.ds(start + j, 12, stride=cols // 128), :]
        start += 12 * cols // 128
    for k in range(4):
        for j in range(D // 128):
            to = D * k + 128 * j
            stage[12:16, to : to + 128] = pal[pl.ds(73 + 12 * k + j, 4, stride=3), :]


def attention_flat(stage, bal, pal):
    start = 1
    for at, cols in ((0, 3 * D), (3 * D, D)):
        for j in range(cols // 128):
            bal[pl.ds(start + j, 12, stride=cols // 128), :] = stage[0:12, at + 128 * j : at + 128 * j + 128]
        start += 12 * cols // 128
    for k in range(4):
        for j in range(D // 128):
            at = D * k + 128 * j
            pal[pl.ds(73 + 12 * k + j, 4, stride=3), :] = stage[12:16, at : at + 128]


FFN_PIECES = [(0, 16, 0, FF), (16, 16, 0, FF + D)] + [(32 + 4 * k, 4, 12, D * k) for k in range(4)]
FFN_START = 1 + 12 * 4 * D // 128


def ffn_rows(bal, stage):
    for j in range(FF // 128):
        stage[0:12, 128 * j : 128 * j + 128] = bal[pl.ds(FFN_START + j, 12, stride=FF // 128), :]
    start = FFN_START + 12 * FF // 128
    for row, rows, under, at in FFN_PIECES:
        for j in range(D // 128):
            to = at + 128 * j
            stage[under : under + rows, to : to + 128] = bal[pl.ds(start + 3 * row + j, rows, stride=3), :]


def ffn_flat(stage, bal):
    for j in range(FF // 128):
        bal[pl.ds(FFN_START + j, 12, stride=FF // 128), :] = stage[0:12, 128 * j : 128 * j + 128]
    start = FFN_START + 12 * FF // 128
    for row, rows, under, at in FFN_PIECES:
        for j in range(D // 128):
            bal[pl.ds(start + 3 * row + j, rows, stride=3), :] = stage[
                under : under + rows, at + 128 * j : at + 128 * j + 128
            ]


def place(d):
    return d // 8, d // 4 % 2, d // 2 % 2, d % 2


def forward_kernel(known, dp, *refs):
    refs = list(refs)
    take = lambda count: [refs.pop(0) for _ in range(count)]
    points_ref, tokens_ref, pflat, bflat = take(4) if known else [None] * 4
    rel_o, moment_o, psmall_o, bsmall_o, w2_o, w3_o = take(6)
    w4_o, wqkv_o, wo_o, wf1_o, wf2_o = take(5) if known else [None] * 5
    ext_o, gp1_o, g_o, ps_o, gm_o, fw_o, pooled_o, sv_o, stats_o, wd_o, w23_o, gp_o, pa_o, pg_o, pc_o = take(15)
    ext_s, gm_s, fw_s, e_s, wn_s, w2_s, w23_s, acc3, sums3, ssend3, srecv3 = take(11)
    step = pl.program_id(0)
    tiles = pl.num_programs(0) // 2
    peers = all_peers(dp)
    if known:
        (
            tiny, att, ffn, three, stage, wide, flat2, pal, bal, counts_s, picked_s,
            tsend, trecv, gsend, grecv,
        ) = take(15)
        z, y, x, core = where_am_i()
        gather_w3 = Gather(three, gsend, grecv, 0)
        gather_att = Gather(att, gsend, grecv, GATHER_SEMS)
        gather_ffn = Gather(ffn, gsend, grecv, 2 * GATHER_SEMS)

    @pl.when(step == 0)
    def _():
        greet(peers)
        g_o[...] = jnp.zeros_like(g_o)
        e_s[...] = token_ones()
        if known:
            pal[...] = segments_apart(pflat[...], PSMALL)
            bal[...] = segments_apart(bflat[...], BSMALL)
            moments = geometry(points_ref, tokens_ref, rel_o, counts_s, picked_s)[0:4, :]
            moments = jnp.concatenate([moments, jnp.zeros((4, 120), F32)], axis=1)
            hi, mid, lo = [part.astype(F32) for part in split_three(moments)]
            packed = hi + pltpu.roll(mid, 8, 1) + pltpu.roll(lo, 16, 1)
            rows = [pal[1:9, :], pflat[0:1, :], bflat[0:1, :], packed, jnp.zeros((2, 128), F32)]
            own = tiny.at[me()]
            own[...] = low(jnp.concatenate(rows, axis=0))
            greeted(peers)
            copies = send_to_all(dp, own, lambda k: own, tsend, trecv)
            for j in range(C3 // 128):
                three[z, y, x, core, :, 128 * j : 128 * j + 128] = low(pal[pl.ds(9 + j, 16, stride=C3 // 128), :])
            gather_w3.advance(0)
            attention_rows(bal, pal, stage)
            att[z, y, x, core] = low(stage[:, 0:ATT_WIDTH])
            gather_att.advance(0)
            ffn_rows(bal, stage)
            ffn[z, y, x, core] = low(stage[...])
            for copy in copies:
                copy.wait()
            gather_w3.advance(1)
            gather_att.advance(1)
            gather_ffn.advance(0)
            psmall, bsmall = [], []
            packed = jnp.zeros((4, 128), F32)
            for d in range(dp * NC):
                rows = tiny[d].astype(F32)
                flat2[8 * d : 8 * d + 8, :] = rows[0:8, :]
                psmall.append(rows[8:9, :])
                bsmall.append(rows[9:10, :])
                packed = packed + rows[10:14, :]
            total = packed + pltpu.roll(packed, 120, 1) + pltpu.roll(packed, 112, 1)
            moment_o[...] = jnp.concatenate([total, jnp.zeros((4, 128), F32)], axis=0)
            psmall_o[0:18, :] = flat_rows(jnp.concatenate(psmall, axis=0), PSMALL, 18)
            bsmall_o[0:30, :] = flat_rows(jnp.concatenate(bsmall, axis=0), BSMALL, 30)
            for j in range(2):
                w2_o[:, 128 * j : 128 * j + 128] = low(flat2[pl.ds(j, C1, stride=2), :])
        else:
            greeted(peers)
        small = psmall_o[...]
        forward, backward, stats = prepare_one(moment_o[:, 0:8], small)
        wn_s[...] = forward
        wd_o[...] = backward
        stats_o[...] = stats
        w2_s[0:C1, :] = w2_o[...]
        b2 = as_vector(small, 5, 2)
        w2_s[C1:, :] = low(jnp.concatenate([b2, jnp.zeros((15, C2), F32)], axis=0))

    if known:
        for at_step, gather, number in (
            (1, gather_w3, 2), (1, gather_att, 2), (2, gather_w3, 3), (2, gather_ffn, 1), (3, gather_att, 3),
            (4, gather_w3, 4), (4, gather_ffn, 2), (5, gather_att, 4), (5, gather_ffn, 3),
        ):
            pl.when(step == at_step)(functools.partial(gather.advance, number))

    def tile_at(half):
        tile = lax.rem(step, tiles) * STEP_TILES + half
        return pl.ds(pl.multiple_of(tile * TILE, TILE), TILE), pl.ds(pl.multiple_of(tile * TOK, TOK), TOK)

    @pl.when(step < tiles)
    def _():
        for half in range(STEP_TILES):
            at, ts = tile_at(half)
            first_tile(rel_o[:, at], wn_s[...], ext_o, gp1_o, half * TILE)
            ext = ext_o[:, half * TILE : half * TILE + TILE]
            ext_s[:, at] = ext[0:C1]
            both = mm_nt(jnp.concatenate([ext, e_s[...]], axis=0), ext)
            g_o[:, 0 : C1 + 16] += both[0 : C1 + 16]
            ps_o[ts, 0 : C1 + 16] = both[C1 + 16 :]

    @pl.when(step == tiles)
    def _():
        if known:
            for d in range(dp * NC):
                w3_o[16 * d : 16 * d + 16, :] = three[place(d)]
        acc3[...] = first_tokens(g_o[:, 0 : C1 + 16], ps_o, w2_s[...], w3_o, pooled_o, gm_s, fw_s)
        copies = sum_start(dp, acc3, sums3, ssend3, srecv3)
        w23 = mm(w2_s[...], w3_o[C2:, :])
        w23_o[...] = w23
        high = low(w23[0:C1])
        w23_s[0:C1, :] = high
        w23_s[C1:, :] = low(w23[0:C1] - high.astype(F32))
        sv_o[...] = third_vectors(sum_finish(acc3, sums3, copies), stats_o[2:3, 0:1], psmall_o)
        mean = sv_o[2:3, :]
        gm = gm_s[...] - mean
        fw_o[...] = low(fw_s[...] + ps_o[:, C1 : C1 + 1] * gm)
        gm = gm + w23[C1 : C1 + 1, :]
        gm_s[...] = gm
        gm_o[...] = low(gm)

    @pl.when(step >= tiles)
    def _():
        for half in range(STEP_TILES):
            at, ts = tile_at(half)
            second_tile(
                ext_s[:, at], e_s[...] * rel_o[3:4, at], w23_s[...], gm_s[ts, :], ps_o[ts, C1 : C1 + 1], sv_o,
                gp_o, half * TILE, pa_o, pg_o, pc_o, ts,
            )

    if known:

        @pl.when(step == tiles + 1)
        def _():
            for d in range(dp * NC):
                under = att[place(d)].astype(F32)
                wide[12 * d : 12 * d + 12, :] = under[0:12, :]
                tail = [under[12:16, D * k : D * k + D] for k in range(4)]
                w4_o[16 * d : 16 * d + 16, :] = low(jnp.concatenate(tail, axis=0))
            wqkv_o[...] = low(wide[:, 0 : 3 * D])
            wo_o[...] = low(wide[:, 3 * D : 4 * D])

        @pl.when(step == 2 * tiles - 1)
        def _():
            gather_ffn.advance(4)
            for d in range(dp * NC):
                block = ffn.at[place(d)]
                under = block[:, 0:FF].astype(F32)
                wide[12 * d : 12 * d + 12, :] = under[0:12, :]
                wf2_o[48 * d : 48 * d + 16, :] = block[:, FF : FF + D]
                wf2_o[48 * d + 16 : 48 * d + 32, :] = block[:, FF + D : FF + 2 * D]
                tail = [under[12:16, D * k : D * k + D] for k in range(4)]
                wf2_o[48 * d + 32 : 48 * d + 48, :] = low(jnp.concatenate(tail, axis=0))
            wf1_o[...] = low(wide[...])


def forward_call(known, dp, count, *args):
    tokens, tiles = count // GROUP, count // WIDE
    single = dict(pipeline_mode=pl.Buffered(1))
    full = lambda *s: pl.BlockSpec(s, lambda i: (0, 0), **single)
    early = lambda r: pl.BlockSpec((r, WIDE), lambda i: (0, jnp.minimum(i, tiles - 1)))
    given = [
        ((8, count), BF16), ((8, 128), F32), ((24, 128), F32), ((32, 128), F32), ((C1, C2), BF16), ((2 * C2, C3), BF16),
    ]
    gathered = [((C3, D), BF16), ((D, 3 * D), BF16), ((D, D), BF16), ((D, FF), BF16), ((FF, D), BF16)]
    outs = [(full(*s), s, t) for s, t in given + gathered] if known else []
    outs += [(early(C1 + 16), (C1 + 16, count), BF16), (early(C1), (C1, count), BF16)]
    outs += [
        (full(*s), s, t)
        for s, t in (
            ((C1 + 16, 256), F32), ((tokens, 256), F32), ((tokens, C3), BF16), ((tokens, C3), BF16),
            ((tokens, C2), BF16), ((8, C3), F32), ((8, C1), F32), ((8, C1), BF16), ((C1 + 16, C3), F32),
        )
    ]
    outs += [(pl.BlockSpec((WIDE, C3), lambda i: (jnp.maximum(i - tiles, 0), 0)), (count, C3), BF16)]
    outs += [(full(tokens, C3), (tokens, C3), BF16)] * 3
    scratch = [
        pltpu.VMEM((C1, count), BF16), pltpu.VMEM((tokens, C3), F32), pltpu.VMEM((tokens, C3), F32),
        pltpu.VMEM((TOK, TILE), BF16), pltpu.VMEM((8, C1), BF16),
        pltpu.VMEM((C1 + 16, C2), BF16), pltpu.VMEM((2 * C1, C3), BF16),
    ] + sum_scratch(dp)
    if known:
        n = dp * NC
        scratch += [
            pltpu.VMEM((n, 16, 128), BF16),
            pltpu.VMEM((NZ, NY, NX, NC, 16, ATT_WIDTH), BF16),
            pltpu.VMEM((NZ, NY, NX, NC, 16, FFN_WIDTH), BF16),
            pltpu.VMEM((NZ, NY, NX, NC, 16, C3), BF16),
            pltpu.VMEM((16, FFN_WIDTH), F32),
            pltpu.VMEM((D, FF), F32),
            pltpu.VMEM((8 * n, 128), F32),
            pltpu.VMEM((PROWS, 128), F32), pltpu.VMEM((BROWS, 128), F32),
            pltpu.VMEM((count // 128, 256), F32), pltpu.VMEM((count // 32, 256), F32),
            pltpu.SemaphoreType.DMA((n - 1,)), pltpu.SemaphoreType.DMA((n - 1,)),
            pltpu.SemaphoreType.DMA((3 * GATHER_SEMS,)), pltpu.SemaphoreType.DMA((3 * GATHER_SEMS,)),
        ]
    return pl.pallas_call(
        functools.partial(forward_kernel, known, dp),
        grid=(2 * tiles,),
        in_specs=[full(*a.shape) for a in args],
        out_specs=[o[0] for o in outs],
        out_shape=shaped(*[o[1:] for o in outs]),
        scratch_shapes=scratch,
        compiler_params=params(collective_id=0, has_side_effects=True),
        name="forward",
    )(*args)


def wide_row(ref, first, rows):
    return jnp.concatenate([ref[k : k + 1, :] for k in range(first, first + rows)], axis=1)


def layer_norm(v, gain, shift):
    centred = v - jnp.mean(v, -1, keepdims=True)
    inverse = lax.rsqrt(jnp.mean(centred * centred, -1, keepdims=True) + EPS_NORM)
    unit = centred * inverse
    return unit, inverse, low(unit * gain + shift)


def norm_back(d_unit, unit, inverse):
    return inverse * (
        d_unit - jnp.mean(d_unit, -1, keepdims=True) - unit * jnp.mean(d_unit * unit, -1, keepdims=True)
    )


def col_sum(v):
    return jnp.sum(v, axis=0, keepdims=True)


def block_step(
    pa_ref, pg_ref, pc_ref, cnt_ref, len_ref, cot_ref, psmall_ref, bsmall_ref, sv_ref,
    w4_ref, wqkv_ref, wo_ref, wf1_ref, wf2_ref,
    out_o, small_o, tok_o, tg_o, back_o, qkv_s, mixed_s, soft_s, dmix_s, dqkv_s, dhid_s,
    ffn_grads, between, token_grads, attention_grads,
):
    count = cnt_ref[:, C1 : C1 + 1]
    scale = HEAD_DIM ** (-0.5)
    b4 = wide_row(psmall_ref, 15, 3)
    ln1_gain, ln1_shift, bo = wide_row(bsmall_ref, 0, 3), wide_row(bsmall_ref, 3, 3), wide_row(bsmall_ref, 6, 3)
    ln2_gain, ln2_shift = wide_row(bsmall_ref, 9, 3), wide_row(bsmall_ref, 12, 3)
    bf1, bf2 = wide_row(bsmall_ref, 15, 12), wide_row(bsmall_ref, 27, 3)

    act = pa_ref[...]
    x_zero = mm(act, w4_ref[...]) + b4
    unit_a, inv_a, normed_a = layer_norm(x_zero, ln1_gain, ln1_shift)
    qkv_s[...] = low(mm(normed_a, wqkv_ref[...]))

    row_cloud = lax.broadcasted_iota(jnp.int32, (PAIR, PAIR), 0) // PATCHES
    col = lax.broadcasted_iota(jnp.int32, (PAIR, PAIR), 1)
    left = lax.broadcasted_iota(jnp.int32, (1, 128), 1) < HEAD_DIM
    zero = jnp.zeros((1, 1), BF16)

    def halves(v):
        return jnp.where(left, v, zero), jnp.where(left, zero, v)

    tiles = pa_ref.shape[0] // PAIR
    for s in range(tiles):
        seen = jnp.zeros((1, PAIR), jnp.int32)
        for c in range(PAIR // PATCHES):
            seen = jnp.where(col[0:1, :] // PATCHES == c, len_ref[s * (PAIR // PATCHES) + c], seen)
        visible = (row_cloud == col // PATCHES) & (lax.rem(col, PATCHES) < seen)
        rows = slice(PAIR * s, PAIR * s + PAIR)
        for p in range(HEADS // 2):
            at = 128 * p
            q = qkv_s[rows, at : at + 128]
            k = qkv_s[rows, D + at : D + at + 128]
            v = qkv_s[rows, 2 * D + at : 2 * D + at + 128]
            mixed = []
            for a, q_half in enumerate(halves(q)):
                score = jnp.where(visible, mm_nt(q_half, k) * scale, NEG_FILL)
                raised = jnp.exp(score - jnp.max(score, -1, keepdims=True))
                soft = raised / jnp.sum(raised, -1, keepdims=True)
                soft_s[(s * (HEADS // 2) + p) * 2 + a] = soft
                mixed.append(mm(low(soft), v))
            mixed_s[rows, at : at + 128] = low(jnp.where(left, mixed[0], mixed[1]))

    mixed_low = mixed_s[...]
    x_one = x_zero + mm(mixed_low, wo_ref[...]) + bo
    unit_b, inv_b, normed_b = layer_norm(x_one, ln2_gain, ln2_shift)
    hidden, d_hidden = gelu_pair(mm(normed_b, wf1_ref[...]) + bf1)
    dhid_s[...] = d_hidden
    out_o[...] = x_one + mm(hidden, wf2_ref[...]) + bf2

    cot = cot_ref[...]
    grad = low(cot)
    d_pre = mm_nt(grad, wf2_ref[...]) * dhid_s[...].astype(F32)
    d_pre_low = low(d_pre)
    small_o[7:8, :] = col_sum(d_pre)
    ffn_grads(mm_tn(normed_b, d_pre_low), mm_tn(hidden, grad))
    d_normed_b = mm_nt(d_pre_low, wf1_ref[...])
    d_x_one = cot + norm_back(d_normed_b * ln2_gain, unit_b, inv_b)
    d_x_low = low(d_x_one)
    d_x_one_low = d_x_low
    dmix_s[...] = low(mm_nt(d_x_low, wo_ref[...]))

    for s in range(tiles):
        rows = slice(PAIR * s, PAIR * s + PAIR)
        for p in range(HEADS // 2):
            at = 128 * p
            q = qkv_s[rows, at : at + 128]
            k = qkv_s[rows, D + at : D + at + 128]
            v = qkv_s[rows, 2 * D + at : 2 * D + at + 128]
            dm = dmix_s[rows, at : at + 128]
            d_q, d_k, d_v = [], [], []
            for a, dm_half in enumerate(halves(dm)):
                soft = soft_s[(s * (HEADS // 2) + p) * 2 + a]
                d_soft = mm_nt(dm_half, v)
                d_v.append(mm_tn(low(soft), dm))
                d_score = low(soft * (d_soft - jnp.sum(soft * d_soft, -1, keepdims=True)))
                d_q.append(mm(d_score, k))
                d_k.append(mm_tn(d_score, q))
            dqkv_s[rows, at : at + 128] = low(jnp.where(left, d_q[0], d_q[1]) * scale)
            dqkv_s[rows, D + at : D + at + 128] = low(jnp.where(left, d_k[0], d_k[1]) * scale)
            dqkv_s[rows, 2 * D + at : 2 * D + at + 128] = low(jnp.where(left, d_v[0], d_v[1]))

    between()
    d_qkv = dqkv_s[...]
    d_normed_a = mm_nt(d_qkv, wqkv_ref[...])
    d_x_zero = d_x_one + norm_back(d_normed_a * ln1_gain, unit_a, inv_a)
    d_x_low = low(d_x_zero)
    token = mm_nt(d_x_low, w4_ref[...]) / count
    tok_o[...] = token
    grouped = token * pg_ref[...].astype(F32)
    tg_o[...] = grouped
    back_o[...] = as_rows(col_sum(grouped), col_sum(token * pc_ref[...].astype(F32)) * sv_ref[3:4, :])
    token_grads()
    narrow = [
        col_sum(d_normed_a * unit_a), col_sum(d_normed_a), col_sum(d_x_one),
        col_sum(d_normed_b * unit_b), col_sum(d_normed_b), col_sum(cot), col_sum(d_x_zero),
    ]
    for k, row in enumerate(narrow):
        small_o[k : k + 1, 0:D] = row
    attention_grads(mm_tn(normed_a, d_qkv), mm_tn(mixed_low, d_x_one_low), mm_tn(act, d_x_low))


def third_back_tokens(
    totals, tg_ref, sc_ref, gm_ref, ps_ref, pooled_ref, gext_ref, w2_ref, w3_ref, w23_ref, sv_ref, stats_ref,
    kap_o, k_o, wb_o, top_o, corr_o, base_o,
):
    gain = sv_ref[0:1, :]
    n = stats_ref[2:3, 0:1]
    alpha = gain * as_vector(totals, 0, 4) / n
    beta = gain * as_vector(totals, 4, 4) * sv_ref[3:4, :] / n
    count = ps_ref[:, C1 : C1 + 1]
    w23 = w23_ref[...]
    act = low(w23[0:C1])
    per_token = low(gain * tg_ref[...] - (count * alpha + beta * sc_ref[...].astype(F32)))
    pooled = low(mm_nt(per_token, w3_ref[0:C2, :]) / count)
    shifted = low(alpha + beta * gm_ref[...].astype(F32))
    kap_o[...] = low(mm_nt(pooled, w2_ref[...]) - mm_nt(shifted, act))
    k_o[:, 0:C1] = low(-mm_nt(low(w23[0:C1] * beta), act))
    wb_o[...] = low(w23[0:C1] * gain)
    top_o[...] = mm_tn(pooled_ref[...], per_token)
    sums = low(ps_ref[:, 0 : C1 + 16])
    corr_o[...] = mm_tn(sums, shifted) + beta * mm(low(gext_ref[:, 0:C1]), act)
    base_o[...] = mm_tn(sums, pooled)


def last_tile(gp, ext, gp1, rel, tok, kap, k_s, xe_s, wb_ref, wd_ref, h_o, q_o, d_at):
    dn = (gp.reshape(TOK, GROUP, C3) * tok[:, None, :]).reshape(TILE, C3)
    xe_s[0:C1, :] = ext[0:C1, :]
    k_s[:, C1 : C1 + TOK] = kap.T
    h_o[...] += mm(ext, dn)
    d_act = mm_nt(wb_ref[...], dn) + mm(k_s[...], xe_s[...])
    d_one = low(d_act * gp1.astype(F32))
    d_at(mm(wd_ref[...], d_one))
    q_o[...] += mm_nt(rel, d_one)


def last_weights(h, gain, corr, base, w2e, w3_ref):
    m = h * gain - corr
    parts = split_three(m)[0:2]
    grad_w3 = sum(mm_tn(w2e, part) for part in parts)
    return grad_w3, sum(mm_nt(part, w3_ref[C2:, :]) for part in parts) + base


def first_grads(q, moments, psmall, stats):
    mean, inverse, n, scale = stats[0:1], stats[1:2], stats[2:3], stats[3:4]
    w = [psmall[k : k + 1, :] for k in range(3)]
    one = q[3:4, :]
    two = inverse * (sum(w[k] * q[k : k + 1, :] for k in range(3)) - mean * one)
    grad_w = []
    for k in range(3):
        along = sum(w[j] * moments[k : k + 1, j : j + 1] for j in range(3)) - mean * moments[k : k + 1, 3:4]
        grad_w.append(scale * (q[k : k + 1, :] - (one * moments[k : k + 1, 3:4] + two * inverse * along) / n))
    flat = [
        jnp.sum(scale * w[k] * (one - two * inverse * mean) / n, axis=1, keepdims=True) for k in range(3)
    ]
    slope = [
        [jnp.sum(scale * w[k] * two * inverse * w[j] / n, axis=1, keepdims=True) for j in range(3)]
        for k in range(3)
    ]
    return grad_w, two, one, flat, slope


def point_gradient(d_ref, rel_ref, tokens_ref, flat, slope, out_ref, spread_s, sums_s):
    pieces = d_ref.shape[1] // 256
    lane = lax.rem(lax.broadcasted_iota(jnp.int32, (1, 256), 1), GROUP).astype(F32)
    base = jnp.concatenate(flat, axis=0)
    columns = [jnp.concatenate([slope[k][j] for k in range(3)], axis=0) for j in range(3)]
    spread_s[...] = spread_tokens(tokens_ref[pieces : 2 * pieces, :])
    for i in range(pieces):
        at = slice(256 * i, 256 * i + 256)
        rel = rel_ref[:, at].astype(F32)
        d = d_ref[:, at]
        out = d[0:3] + d[4:7] - rel[3:4] * base
        for j in range(3):
            out = out - columns[j] * rel[j : j + 1]
        out_ref[:, at] = out
        sums_s[8 * i : 8 * i + 8, :] = jnp.concatenate([out, jnp.zeros((5, 256), F32)], axis=0)
    sums_s[...] = patch_sum(sums_s[...], patch_ones())
    for i in range(pieces):
        at = slice(256 * i, 256 * i + 256)
        pick = (lane == spread_s[i : i + 1, :]).astype(F32)
        out_ref[:, at] = out_ref[:, at] - pick * sums_s[8 * i : 8 * i + 3, :]


def point_small_rows(grad_w, gain1, shift1, b2, tot, b4):
    rows = list(grad_w) + [gain1, shift1]
    rows += [b2[:, 128 * k : 128 * k + 128] for k in range(2)]
    rows += [tot[4:8, :], tot[0:4, :]]
    rows += [b4[:, 128 * k : 128 * k + 128] for k in range(3)]
    return jnp.concatenate(rows, axis=0)


def block_small_rows(small_ref):
    rows = [small_ref[k : k + 1, 128 * j : 128 * j + 128] for k in range(5) for j in range(3)]
    rows += [small_ref[7:8, 128 * j : 128 * j + 128] for j in range(12)]
    rows += [small_ref[5:6, 128 * j : 128 * j + 128] for j in range(3)]
    return jnp.concatenate(rows, axis=0)


class Scatter:
    def __init__(self, blocks, lands, send, recv, base):
        self.blocks, self.lands, self.sems, self.base = blocks, lands, (send, recv), base
        z, y, x, core = self.at = where_am_i()
        half = blocks.shape[-1] // 2
        self.one, self.two = pl.ds(0, half), pl.ds(half, half)
        every = slice(None)
        mine = blocks.at[core]
        near = [(chip(lax.rem(z + k, NZ), y, x), core) for k in range(1, NZ)]
        over_y, over_x, twin = (chip(z, 1 - y, x), core), (chip(z, y, 1 - x), core), (chip(z, y, x), 1 - core)
        land1, land2, land3, land4 = lands
        self.stages = [
            [(blocks.at[1 - core], land1, twin)],
            [
                (mine.at[:, :, 1 - x, :, self.one], land2.at[0], over_x),
                (mine.at[:, 1 - y, :, :, self.two], land2.at[1], over_y),
            ],
            [
                (mine.at[:, 1 - y, x, :, self.one], land3.at[0], over_y),
                (mine.at[:, y, 1 - x, :, self.two], land3.at[1], over_x),
            ],
            [(mine.at[lax.rem(z + k, NZ), y, x], land4.at[k - 1], near[k - 1]) for k in range(1, NZ)],
        ]

    def copies(self, stage):
        k = self.base + sum(len(s) for s in self.stages[:stage])
        return [
            pltpu.make_async_remote_copy(
                src_ref=src, dst_ref=dst, send_sem=self.sems[0].at[k + i], recv_sem=self.sems[1].at[k + i],
                device_id=peer, device_id_type=MESH,
            )
            for i, (src, dst, peer) in enumerate(self.stages[stage])
        ]

    def advance(self, stage):
        z, y, x, core = self.at
        mine = self.blocks.at[core]
        land1, land2, land3, land4 = self.lands
        if stage > 0:
            for copy in self.copies(stage - 1):
                copy.wait()
        if stage == 1:
            for cz in range(NZ):
                for cy in range(NY):
                    for cx in range(NX):
                        mine[cz, cy, cx] = mine[cz, cy, cx] + land1[cz, cy, cx]
        if stage == 2:
            for cz in range(NZ):
                for k in range(2):
                    mine[cz, k, x, :, self.one] = mine[cz, k, x, :, self.one] + land2[0, cz, k]
                    mine[cz, y, k, :, self.two] = mine[cz, y, k, :, self.two] + land2[1, cz, k]
        if stage == 3:
            for cz in range(NZ):
                mine[cz, y, x, :, self.one] = mine[cz, y, x, :, self.one] + land3[0, cz]
                mine[cz, y, x, :, self.two] = mine[cz, y, x, :, self.two] + land3[1, cz]
        if stage < 4:
            for copy in self.copies(stage):
                copy.start()
            return None
        total = mine[z, y, x].astype(F32)
        for k in range(NZ - 1):
            total = total + land4[k].astype(F32)
        return total


SCATTER_SEMS = 8
POINT_WIDTH = 768


def scatter_scratch(width):
    return [
        pltpu.VMEM((NC, NZ, NY, NX, 16, width), BF16),
        pltpu.VMEM((NZ, NY, NX, 16, width), BF16),
        pltpu.VMEM((2, NZ, 2, 16, width // 2), BF16),
        pltpu.VMEM((2, NZ, 16, width // 2), BF16),
        pltpu.VMEM((NZ - 1, 16, width), BF16),
    ]


def backward_kernel(known, dp, *refs):
    refs = list(refs)
    take = lambda count: [refs.pop(0) for _ in range(count)]
    pa_ref, pg_ref, pc_ref, ps_ref, len_ref, cot_ref, psmall_ref, bsmall_ref, sv_ref, stats_ref, moment_ref = take(11)
    w2_ref, w3_ref, w4_ref, wqkv_ref, wo_ref, wf1_ref, wf2_ref, w23_ref = take(8)
    sc_ref, gm_ref, pooled_ref, gext_ref, wd_ref, rel_ref, tokens_ref, gp_ref, ext_ref, gp1_ref = take(10)
    out_o, pg_o = take(2)
    if known:
        pflat_o, bflat_o = take(2)
    else:
        prow_o, brow_o, gw2_o, gw3_o, gw4_o, gwqkv_o, gwo_o, gwf1_o, gwf2_o = take(9)
    small_s, tok_s, tg_s, acc3, qkv_s, mixed_s, soft_s, dmix_s, dqkv_s, dhid_s = take(10)
    tot_s, kap_s, k_s, wb_s, top_s, corr_s, base_s, h_s, q_s, d_s, xe_s, spread_s, sums_s = take(13)
    acc, slots, ssend, srecv, unused, slots3, ssend3, srecv3 = take(8)
    gp_r, ext_r, gp1_r, read_sem = take(4)
    step = pl.program_id(0)
    steps = pl.num_programs(0)
    peers = all_peers(dp)
    if known:
        ffn0, ffn1, ffn2, ffn3, ffn4, att0, att1, att2, att3, att4, point0, point1, point2, point3, point4 = take(15)
        wide, tall, stage, pstage, pal, bal, gsend, grecv = take(8)
        z, y, x, core = where_am_i()
        ffn = Scatter(ffn0, (ffn1, ffn2, ffn3, ffn4), gsend, grecv, 0)
        att = Scatter(att0, (att1, att2, att3, att4), gsend, grecv, SCATTER_SEMS)
        point = Scatter(point0, (point1, point2, point3, point4), gsend, grecv, 2 * SCATTER_SEMS)

    def ffn_grads(gwf1, gwf2):
        if not known:
            gwf1_o[...], gwf2_o[...] = gwf1, gwf2
            return
        wide[...] = gwf1
        tall[...] = gwf2
        for d in range(dp * NC):
            stage[0:12, 0:FF] = wide[12 * d : 12 * d + 12, :]
            for row, rows, under, at in FFN_PIECES:
                stage[under : under + rows, at : at + D] = tall[48 * d + row : 48 * d + row + rows, :]
            cz, cy, cx, cc = place(d)
            ffn0[cc, cz, cy, cx] = low(stage[...])
        greeted(peers)
        ffn.advance(0)

    def between():
        if known:
            ffn.advance(1)

    def token_grads():
        if not known:
            greeted(peers)
        sum_start(dp, acc3, slots3, ssend3, srecv3)

    def attention_grads(gwqkv, gwo, gw4):
        if not known:
            gwqkv_o[...], gwo_o[...], gw4_o[...] = gwqkv, gwo, gw4
            return
        wide[:, 0 : 3 * D] = gwqkv
        wide[:, 3 * D :] = gwo
        tall[0:C3, :] = gw4
        for d in range(dp * NC):
            stage[0:12, 0:ATT_WIDTH] = wide[12 * d : 12 * d + 12, :]
            for k in range(4):
                stage[12:16, D * k : D * k + D] = tall[16 * d + 4 * k : 16 * d + 4 * k + 4, :]
            cz, cy, cx, cc = place(d)
            att0[cc, cz, cy, cx] = low(stage[:, 0:ATT_WIDTH])
        att.advance(0)
        ffn.advance(2)
        att.advance(1)

    def reads(tile, slot):
        at = pl.ds(pl.multiple_of(tile * TILE, TILE), TILE)
        pairs = ((gp_ref.at[at, :], gp_r), (ext_ref.at[:, at], ext_r), (gp1_ref.at[:, at], gp1_r))
        return [
            pltpu.make_async_copy(src, ring.at[slot], read_sem.at[slot, k]) for k, (src, ring) in enumerate(pairs)
        ]

    @pl.when(step == 0)
    def _():
        greet(peers)
        for tile in range(AHEAD):
            for copy in reads(tile, tile):
                copy.start()
        block_step(
            pa_ref, pg_ref, pc_ref, ps_ref, len_ref, cot_ref, psmall_ref, bsmall_ref, sv_ref,
            w4_ref, wqkv_ref, wo_ref, wf1_ref, wf2_ref,
            out_o, small_s, tok_s, tg_s, acc3, qkv_s, mixed_s, soft_s, dmix_s, dqkv_s, dhid_s,
            ffn_grads, between, token_grads, attention_grads,
        )
        for ref in (h_s, q_s):
            ref[...] = jnp.zeros_like(ref)
        xe_s[C1:, :] = token_ones()
        tot_s[...] = sum_finish(acc3, slots3, sum_copies(dp, acc3, lambda k: slots3.at[k], ssend3, srecv3))
        third_back_tokens(
            tot_s[...], tg_s, sc_ref, gm_ref, ps_ref, pooled_ref, gext_ref, w2_ref, w3_ref, w23_ref, sv_ref, stats_ref,
            kap_s, k_s, wb_s, top_s, corr_s, base_s,
        )

    if known:
        for at_step, group, number in ((3, ffn, 3), (4, att, 2), (6, att, 3)):
            pl.when(step == at_step)(functools.partial(group.advance, number))

    @pl.when(step >= 1)
    def _():
        tile = step - 1
        at = pl.ds(pl.multiple_of(tile * TILE, TILE), TILE)
        ts = pl.ds(pl.multiple_of(tile * TOK, TOK), TOK)
        slot = lax.rem(tile, AHEAD)

        def put(d):
            d_s[:, at] = d

        for copy in reads(tile, slot):
            copy.wait()
        last_tile(
            gp_r[slot], ext_r[slot], gp1_r[slot], rel_ref[:, at], low(tok_s[ts, :] * 0.5), kap_s[ts, :],
            k_s, xe_s, wb_s, wd_ref, h_s, q_s, put,
        )

        @pl.when(tile + AHEAD < steps - 1)
        def _():
            for copy in reads(tile + AHEAD, slot):
                copy.start()

    @pl.when(step == steps - 1)
    def _():
        acc[...] = q_s[...]
        b2 = as_vector(psmall_ref, 5, 2)
        w2e = jnp.concatenate([w2_ref[...], low(jnp.concatenate([b2, jnp.zeros((15, C2), F32)], axis=0))], axis=0)
        gw3, gw2 = last_weights(h_s[...], sv_ref[0:1, :], corr_s[...], base_s[...], w2e, w3_ref)
        none = jnp.zeros((1, 128), F32)
        prow = point_small_rows([none] * 3, none, none, gw2[C1 : C1 + 1, :], jnp.zeros((8, 128), F32), small_s[6:7, 0:D])
        brow = block_small_rows(small_s)
        if known:
            pstage[...] = jnp.zeros_like(pstage)
            for d in range(dp * NC):
                if d < 16:
                    pstage[:, 0:C3] = top_s[16 * d : 16 * d + 16, :]
                else:
                    pstage[:, 0:C3] = gw3[16 * (d - 16) : 16 * (d - 16) + 16, :]
                pstage[0:4, C3 : C3 + C2] = gw2[4 * d : 4 * d + 4, :]
                pstage[4:5, C3 : C3 + 128] = piece_of(prow, PSMALL * d, PSMALL)
                pstage[5:6, C3 : C3 + 128] = piece_of(brow, BSMALL * d, BSMALL)
                cz, cy, cx, cc = place(d)
                point0[cc, cz, cy, cx] = low(pstage[...])
            point.advance(0)
        copies = sum_start(dp, acc, slots, ssend, srecv)
        if known:
            point.advance(1)
        totals = sum_finish(acc, slots, copies)
        grad_w, gain1, shift1, flat, slope = first_grads(totals, moment_ref[...], psmall_ref[...], stats_ref[...])
        full_rows = point_small_rows(grad_w, gain1, shift1, jnp.zeros((1, C2), F32), tot_s[...], jnp.zeros((1, D), F32))
        if known:
            point.advance(2)
            stage[...] = ffn.advance(4)
            ffn_flat(stage, bal)
            stage[:, 0:ATT_WIDTH] = att.advance(4)
            attention_flat(stage, bal, pal)
            point.advance(3)
        point_gradient(d_s, rel_ref, tokens_ref, flat, slope, pg_o, spread_s, sums_s)
        if not known:
            prow_o[0:18, :] = prow + full_rows * (1.0 / (dp * NC))
            brow_o[0:30, :] = brow
            gw2_o[...] = gw2[0:C1]
            gw3_o[0:C2, :] = top_s[...]
            gw3_o[C2:, :] = gw3
            return
        own = jnp.zeros((1, 128), F32)
        for d in range(dp * NC):
            own = own + jnp.where(me() == d, piece_of(full_rows, PSMALL * d, PSMALL), 0.0)
        pstage[...] = point.advance(4)
        for j in range(C2 // 128):
            pal[pl.ds(1 + j, 4, stride=2), :] = pstage[0:4, C3 + 128 * j : C3 + 128 * j + 128]
        for j in range(C3 // 128):
            pal[pl.ds(9 + j, 16, stride=4), :] = pstage[:, 128 * j : 128 * j + 128]
        pflat_o[...] = segments_joined(pal[...], pstage[4:5, C3 : C3 + 128] + own, PSMALL)
        bflat_o[...] = segments_joined(bal[...], pstage[5:6, C3 : C3 + 128], BSMALL)


def backward_call(known, dp, *args):
    count = args[24].shape[1]
    tokens, tiles = count // GROUP, count // TILE
    single = dict(pipeline_mode=pl.Buffered(1))
    full = lambda *s: pl.BlockSpec(s, lambda i: (0, 0), **single)
    specs = [full(*a.shape) for a in args[:26]]
    specs[4] = pl.BlockSpec(memory_space=pltpu.SMEM)
    specs += [pl.BlockSpec(memory_space=pl.ANY)] * 3
    outs = [((tokens, D), F32), ((3, count), F32)]
    if known:
        outs += [((PROWS, 128), F32), ((BROWS, 128), F32)]
    else:
        outs += [((24, 128), F32), ((32, 128), F32), ((C1, C2), F32), ((2 * C2, C3), F32), ((C3, D), F32)]
        outs += [((D, 3 * D), F32), ((D, D), F32), ((D, FF), F32), ((FF, D), F32)]
    pieces = count // 256
    scratch = [
        pltpu.VMEM((8, FF), F32), pltpu.VMEM((tokens, C3), F32), pltpu.VMEM((tokens, C3), F32), pltpu.VMEM((8, 128), F32),
        pltpu.VMEM((tokens, 3 * D), BF16), pltpu.VMEM((tokens, D), BF16),
        pltpu.VMEM((tokens // PAIR * HEADS, PAIR, PAIR), F32), pltpu.VMEM((tokens, D), BF16),
        pltpu.VMEM((tokens, 3 * D), BF16), pltpu.VMEM((tokens, FF), BF16),
        pltpu.VMEM((8, 128), F32), pltpu.VMEM((tokens, C1), BF16), pltpu.VMEM((C1, C1 + TOK), BF16),
        pltpu.VMEM((C1, C3), BF16), pltpu.VMEM((C2, C3), F32), pltpu.VMEM((C1 + 16, C3), F32),
        pltpu.VMEM((C1 + 16, C2), F32), pltpu.VMEM((C1 + 16, C3), F32), pltpu.VMEM((8, C1), F32),
        pltpu.VMEM((8, count), F32), pltpu.VMEM((C1 + TOK, TILE), BF16),
        pltpu.VMEM((pieces, 256), F32), pltpu.VMEM((8 * pieces, 256), F32),
    ]
    scratch += sum_scratch(dp) + sum_scratch(dp)
    scratch += [
        pltpu.VMEM((AHEAD, TILE, C3), BF16), pltpu.VMEM((AHEAD, C1 + 16, TILE), BF16), pltpu.VMEM((AHEAD, C1, TILE), BF16),
        pltpu.SemaphoreType.DMA((AHEAD, 3)),
    ]
    if known:
        scratch += scatter_scratch(FFN_WIDTH) + scatter_scratch(ATT_WIDTH) + scatter_scratch(POINT_WIDTH)
        scratch += [
            pltpu.VMEM((D, FF), F32), pltpu.VMEM((FF, D), F32),
            pltpu.VMEM((16, FFN_WIDTH), F32), pltpu.VMEM((16, POINT_WIDTH), F32),
            pltpu.VMEM((PROWS, 128), F32), pltpu.VMEM((BROWS, 128), F32),
            pltpu.SemaphoreType.DMA((3 * SCATTER_SEMS,)), pltpu.SemaphoreType.DMA((3 * SCATTER_SEMS,)),
        ]
    return pl.pallas_call(
        functools.partial(backward_kernel, known, dp),
        grid=(1 + tiles,),
        in_specs=specs,
        out_specs=[full(*s) for s, t in outs],
        out_shape=shaped(*outs),
        scratch_shapes=scratch,
        compiler_params=params(collective_id=1, has_side_effects=True),
        name="backward",
    )(*args)


def geometry_kernel(points_ref, tokens_ref, rel_o, moment_o, counts_s, picked_s):
    moment_o[...] = jnp.concatenate(
        [geometry(points_ref, tokens_ref, rel_o, counts_s, picked_s), jnp.zeros((8, 120), F32)], axis=1
    )


def geometry_call(points, tokens):
    count = points.shape[1]
    return pl.pallas_call(
        geometry_kernel,
        out_shape=shaped(((8, count), BF16), ((8, 128), F32)),
        in_specs=vmem(2),
        out_specs=vmem(2),
        scratch_shapes=[pltpu.VMEM((count // 128, 256), F32), pltpu.VMEM((count // 32, 256), F32)],
        compiler_params=params(),
        name="geometry",
    )(points, tokens)


def gather_plain(points, tokens, point_master, block_master, devices):
    rel, moments = geometry_call(points, tokens)
    moments = lax.psum(moments, AXES)
    tables = []
    for master, layout in ((point_master, point_layout()), (block_master, block_layout())):
        offset = 0
        parts = []
        for seg_len in segment_lengths(layout, devices):
            piece = master[offset : offset + seg_len // devices].astype(BF16)
            offset += seg_len // devices
            parts.append(lax.all_gather(piece, AXES, axis=0, tiled=True))
        tables.append(parts)
    (ps, w2, w3, w4), (bs, wqkv, wo, wf1, wf2) = tables

    def rows_of(v, rows, used):
        v = v[:used].astype(F32).reshape(-1, 128)
        return jnp.concatenate([v, jnp.zeros((rows - v.shape[0], 128), F32)], axis=0)

    small = (rel, moments, rows_of(ps, 24, 18 * 128), rows_of(bs, 32, 30 * 128))
    point = (w2.reshape(C1, C2), w3.reshape(2 * C2, C3))
    block = (w4.reshape(C3, D), wqkv.reshape(D, 3 * D), wo.reshape(D, D), wf1.reshape(D, FF), wf2.reshape(FF, D))
    return small + point, block


def scatter_plain(devices, prow, brow, gw2, gw3, gw4, gwqkv, gwo, gwf1, gwf2):
    pieces = []
    for layout, tables in (
        (point_layout(), (prow[:18], gw2, gw3, gw4)),
        (block_layout(), (brow[:30], gwqkv, gwo, gwf1, gwf2)),
    ):
        parts = []
        for values, seg_len in zip(tables, segment_lengths(layout, devices)):
            values = values.reshape(-1)
            values = jnp.concatenate([values, jnp.zeros((seg_len - values.shape[0],), F32)])
            parts.append(lax.psum_scatter(values, AXES, scatter_dimension=0, tiled=True))
        pieces.append(parts)
    return pieces


def adam_update(master, moment_one, moment_two, gradient, step_rates, decays):
    one_new = BETA_ONE * moment_one + (1.0 - BETA_ONE) * gradient
    two_new = BETA_TWO * moment_two + (1.0 - BETA_TWO) * gradient * gradient
    fix_one = 1.0 - BETA_ONE**STEP
    fix_two = 1.0 - BETA_TWO**STEP
    direction = one_new / fix_one / (jnp.sqrt(two_new / fix_two) + ADAM_EPS)
    master_new = master - step_rates * (direction + decays * master)
    return (master_new, one_new, two_new)


def flat_of(vector, rows):
    return jnp.pad(vector, (0, rows * 128 - vector.shape[0])).reshape(rows, 128)


def on_device(
    points, point_count, centre_slot, cloud_length, cotangent, point_master, block_master,
    point_first, block_first, point_second, block_second,
):
    dp, fsdp = lax.axis_size("dp"), lax.axis_size("fsdp")
    devices = dp * fsdp
    own_rank = lax.axis_index(AXES)
    known = dp == NZ * NY * NX and fsdp == NC
    count = points.shape[1]
    tokens = jnp.concatenate([point_count, centre_slot]).reshape(-1, 8)
    if known:
        outs = forward_call(
            True, dp, count, points, tokens, flat_of(point_master, PROWS), flat_of(block_master, BROWS)
        )
        given, block, outs = outs[:6], outs[6:11], outs[11:]
    else:
        given, block = gather_plain(points, tokens, point_master, block_master, devices)
        outs = forward_call(False, dp, count, *given)
    rel, moments, psmall, bsmall, w2, w3 = given
    ext, gp1, gext, ps, gm, sc, pooled, sv, stats, wd, w23, gp, pa, pg, pc = outs
    outs = backward_call(
        known, dp, pa, pg, pc, ps, cloud_length, cotangent, psmall, bsmall, sv, stats, moments,
        w2, w3, *block, w23, sc, gm, pooled, gext, wd, rel, tokens, gp, ext, gp1,
    )
    tokens_out, point_grad = outs[:2]
    if known:
        point_gradient_vec = outs[2].reshape(-1)[: point_master.shape[0]]
        block_gradient = outs[3].reshape(-1)[: block_master.shape[0]]
        block_small = block_gradient[:BSMALL]
    else:
        point_parts, block_parts = scatter_plain(devices, *outs[2:])
        block_small = block_parts[0]
        point_gradient_vec = jnp.concatenate(point_parts)
        block_gradient = jnp.concatenate(block_parts)
    point_rates, point_decays = shard_rates(point_layout(), devices, own_rank)
    block_rates, block_decays = shard_rates(block_layout(), devices, own_rank)
    point_new, point_one, point_two = adam_update(
        point_master, point_first, point_second, point_gradient_vec, point_rates, point_decays
    )
    block_new, block_one, block_two = adam_update(
        block_master, block_first, block_second, block_gradient, block_rates, block_decays
    )
    return (
        tokens_out, point_grad, point_new, block_new, point_one, block_one, point_two, block_two,
        point_new.astype(BF16), block_new.astype(BF16), block_small,
    )


def solution(mesh):
    split = P(AXES)
    return jax.shard_map(
        on_device,
        mesh=mesh,
        in_specs=(P(None, AXES), split, split, split, P(AXES, None)) + (split,) * 6,
        out_specs=(P(AXES, None), P(None, AXES)) + (split,) * 9,
        check_vma=False,
    )
```

```python
import functools
import math

import jax
import jax.numpy as jnp
from jax import lax
from jax.experimental import pallas as pl
from jax.experimental.pallas import tpu as pltpu
from jax.sharding import PartitionSpec as P

C1 = 128
C2 = 256
C3 = 512
D = 384
HEADS = 6
HEAD_DIM = 64
FF = 1536
GROUP = 32
PATCHES = 64
STEP = 10

EPS_NORM = 1e-05
BETA_ONE = 0.9
BETA_TWO = 0.95
ADAM_EPS = 1e-08
DECAY_RATE = 0.05
NEG_FILL = -1e30

F32 = jnp.float32
BF16 = jnp.bfloat16
AXES = ("dp", "fsdp")
MESH = pl.DeviceIdType.MESH
VMEM_LIMIT = 60 * 2**20
TILE = 2048
TOK = TILE // GROUP
STEP_TILES = 2
AHEAD = 4
WIDE = TILE * STEP_TILES
PAIR = 256

NZ, NY, NX, NC = 4, 2, 2, 2
PROWS, BROWS = 128, 440
PSMALL, BSMALL = 72, 120


def point_layout():
    return [
        [
            ("w1", (3, C1), 3.0 ** (-0.5)),
            ("bn1_gain", (C1,), 0.0),
            ("bn1_shift", (C1,), -1.0),
            ("b2", (C2,), -1.0),
            ("bn3_gain", (C3,), 0.0),
            ("bn3_shift", (C3,), -1.0),
            ("b4", (D,), -1.0),
        ],
        [("w2", (C1, C2), C1 ** (-0.5))],
        [("w3", (2 * C2, C3), (2 * C2) ** (-0.5))],
        [("w4", (C3, D), C3 ** (-0.5))],
    ]


def block_layout():
    return [
        [
            ("ln1_gain", (D,), 0.0),
            ("ln1_shift", (D,), -1.0),
            ("bo", (D,), -1.0),
            ("ln2_gain", (D,), 0.0),
            ("ln2_shift", (D,), -1.0),
            ("bf1", (FF,), -1.0),
            ("bf2", (D,), -1.0),
        ],
        [("wqkv", (D, 3 * D), D ** (-0.5))],
        [("wo", (D, D), 3.0 * D ** (-0.5))],
        [("wf1", (D, FF), D ** (-0.5))],
        [("wf2", (FF, D), FF ** (-0.5))],
    ]


def rate_for(spread):
    return 2.0 * spread if spread > 0.0 else 0.5 if spread == 0.0 else 0.6


def decay_for(spread):
    return DECAY_RATE if spread > 0.0 else 0.0


def segment_lengths(layout, devices):
    lengths_out = []
    for segment in layout:
        used_len = sum((math.prod(entry[1]) for entry in segment))
        lengths_out.append(-(-used_len // devices) * devices)
    return lengths_out


def shard_rates(layout, devices, own_rank):
    lengths = segment_lengths(layout, devices)
    position = jnp.arange(sum(lengths) // devices, dtype=jnp.int32)
    rates = jnp.zeros(position.shape, F32)
    decays = jnp.zeros(position.shape, F32)
    start = 0
    for segment, seg_len in zip(layout, lengths):
        piece_len = seg_len // devices
        here = (position >= start) & (position < start + piece_len)
        inner = position + (own_rank * piece_len - start)
        offset = 0
        for entry_label, entry_dims, spread in segment:
            extent = math.prod(entry_dims)
            inside = here & (inner >= offset) & (inner < offset + extent)
            rates = jnp.where(inside, rate_for(spread), rates)
            decays = jnp.where(inside, decay_for(spread), decays)
            offset += extent
        start += piece_len
    return rates, decays


def mm(a, b):
    return jnp.dot(a, b, preferred_element_type=F32)


def mm_tn(a, b):
    return lax.dot_general(a, b, (((0,), (0,)), ((), ())), preferred_element_type=F32)


def mm_nt(a, b):
    return lax.dot_general(a, b, (((1,), (1,)), ((), ())), preferred_element_type=F32)


def low(v):
    return v.astype(BF16)


def split_three(v):
    hi = low(v)
    rest = v - hi.astype(F32)
    mid = low(rest)
    return hi, mid, low(rest - mid.astype(F32))


def mm_exact(a, b):
    hi, mid, lo = split_three(a)
    return mm(hi, b) + (mm(mid, b) + mm(lo, b))


LAM = (math.sqrt(2.0 / math.pi) * 0.044715) ** (-1.0 / 3.0)
ARG = math.sqrt(2.0 / math.pi) * LAM


def gelu_twice(y):
    square = y * y
    near = square + ARG
    t = jnp.tanh(y * near)
    up = 1.0 + t
    g = y * up
    return g, up + g * (1.0 - t) * (near + (square + square))


def gelu_pair(v):
    g, d = gelu_twice(low(v * (1.0 / LAM)))
    return low(g.astype(F32) * (0.5 * LAM)), d * 0.5


def patch_ones():
    i = lax.broadcasted_iota(jnp.int32, (256, 256), 0) // GROUP
    j = lax.broadcasted_iota(jnp.int32, (256, 256), 1) // GROUP
    return (i == j).astype(F32).astype(BF16)


def token_ones():
    t = lax.broadcasted_iota(jnp.int32, (TOK, TILE), 0)
    p = lax.broadcasted_iota(jnp.int32, (TOK, TILE), 1) // GROUP
    return (t == p).astype(F32).astype(BF16)


def patch_sum(rows, ones):
    return mm_exact(rows, ones)


def rank_of(peer_dp, peer_core):
    return peer_dp * NC + peer_core


def me():
    return rank_of(lax.axis_index("dp"), lax.axis_index("fsdp"))


def all_peers(dp):
    n = dp * NC
    peers = []
    for k in range(1, n):
        p = lax.rem(me() + k, n)
        peers.append((p // NC, lax.rem(p, NC)))
    return peers


def greet(peers):
    barrier = pltpu.get_barrier_semaphore()
    for peer in peers:
        pl.semaphore_signal(barrier, inc=1, device_id=peer, device_id_type=MESH)


def greeted(peers):
    pl.semaphore_wait(pltpu.get_barrier_semaphore(), len(peers))


def sum_copies(dp, src, dst_of, send, recv):
    return [
        pltpu.make_async_remote_copy(
            src_ref=src, dst_ref=dst_of(k), send_sem=send.at[k], recv_sem=recv.at[k],
            device_id=peer, device_id_type=MESH,
        )
        for k, peer in enumerate(all_peers(dp))
    ]


def send_to_all(dp, src, dst_of, send, recv):
    copies = sum_copies(dp, src, dst_of, send, recv)
    for copy in copies:
        copy.start()
    return copies


def sum_start(dp, acc, slots, send, recv):
    return send_to_all(dp, acc, lambda k: slots.at[k], send, recv)


def sum_finish(acc, slots, copies):
    for copy in copies:
        copy.wait()
    return acc[...] + jnp.sum(slots[...], axis=0)


def sum_scratch(dp):
    n = dp * NC - 1
    return [
        pltpu.VMEM((8, 128), F32), pltpu.VMEM((n, 8, 128), F32),
        pltpu.SemaphoreType.DMA((n,)), pltpu.SemaphoreType.DMA((n,)),
    ]


def as_rows(*vectors):
    return jnp.concatenate(
        [v[:, 128 * k : 128 * k + 128] for v in vectors for k in range(v.shape[1] // 128)], axis=0
    )


def as_vector(rows, first, count):
    return jnp.concatenate([rows[k : k + 1, :] for k in range(first, first + count)], axis=1)


def vmem(count):
    return [pl.BlockSpec(memory_space=pltpu.VMEM)] * count


def shaped(*items):
    return [jax.ShapeDtypeStruct(s, t) for s, t in items]


def params(**more):
    return pltpu.CompilerParams(vmem_limit_bytes=VMEM_LIMIT, **more)


def where_am_i():
    at = lax.axis_index("dp")
    return at // (NY * NX), lax.rem(at // NX, NY), lax.rem(at, NX), lax.axis_index("fsdp")


def chip(z, y, x):
    return (z * NY + y) * NX + x


def spread_tokens(values):
    tokens = values.shape[1]
    piece = lax.broadcasted_iota(jnp.int32, (tokens // 8, tokens), 0)
    token = lax.broadcasted_iota(jnp.int32, (tokens // 8, tokens), 1)
    apart = jnp.where(piece == token // 8, values.astype(F32), 0.0)
    token = lax.rem(lax.broadcasted_iota(jnp.int32, (tokens, 256), 0), 8)
    patch = lax.broadcasted_iota(jnp.int32, (tokens, 256), 1) // GROUP
    return mm(low(apart), low((token == patch).astype(F32)))


def geometry(points_ref, counts_ref, centres_ref, rel_ref, counts_s, picked_s):
    pieces = points_ref.shape[1] // 256
    lane = lax.rem(lax.broadcasted_iota(jnp.int32, (1, 256), 1), GROUP).astype(F32)
    counts_s[0:pieces, :] = spread_tokens(counts_ref[...])
    counts_s[pieces:, :] = spread_tokens(centres_ref[...])
    for i in range(pieces):
        at = slice(256 * i, 256 * i + 256)
        pick = (lane == counts_s[pieces + i : pieces + i + 1, :]).astype(F32)
        rows = points_ref[:, at] * pick
        picked_s[8 * i : 8 * i + 8, :] = jnp.concatenate([rows, jnp.zeros((5, 256), F32)], axis=0)
    picked_s[...] = patch_sum(picked_s[...], patch_ones())
    for i in range(pieces):
        at = slice(256 * i, 256 * i + 256)
        valid = (lane < counts_s[i : i + 1, :]).astype(F32)
        relative = (points_ref[:, at] - picked_s[8 * i : 8 * i + 3, :]) * valid
        rel_ref[:, at] = low(jnp.concatenate([relative, valid, relative, valid], axis=0))
    rel = rel_ref[...]
    return mm_nt(rel, rel)


def prepare_one(moments, small):
    n = moments[3:4, 3:4]
    w = [small[k : k + 1, :] for k in range(3)]
    gain, shift = small[3:4, :], small[4:5, :]
    mean = sum(w[k] * moments[k : k + 1, 3:4] for k in range(3)) / n
    square = jnp.zeros_like(mean)
    for j in range(3):
        for k in range(3):
            square = square + w[j] * w[k] * moments[j : j + 1, k : k + 1]
    inverse = lax.rsqrt(square / n - mean * mean + EPS_NORM)
    scale = inverse * gain
    scaled = [wk * scale for wk in w]
    parts = [v * (1.0 / LAM) for v in scaled + [shift - mean * scale]]
    high = [low(v) for v in parts]
    rest = [low(v - h.astype(F32)) for v, h in zip(parts, high)]
    forward = jnp.concatenate(high + rest, axis=0)
    high = [low(v) for v in scaled]
    rest = [low(v - h.astype(F32)) for v, h in zip(scaled, high)]
    zero = jnp.zeros((1, C1), BF16)
    backward = jnp.concatenate(high + [zero] + rest + [zero], axis=0)
    stats = jnp.concatenate(
        [mean, inverse, jnp.broadcast_to(n, (1, C1)), scale, jnp.zeros((4, C1), F32)], axis=0
    )
    return forward, backward, stats


def flat_rows(pieces, length, rows):
    lane = lax.broadcasted_iota(jnp.int32, (1, 128), 1)
    out = [jnp.zeros((1, 128), F32) for _ in range(rows)]
    for r in range(pieces.shape[0]):
        row = jnp.where(lane < length, pieces[r : r + 1, :], 0.0)
        at = length * r
        row = pltpu.roll(row, at % 128, 1) if at % 128 else row
        first = at // 128
        out[first] = out[first] + jnp.where(lane >= at % 128, row, 0.0)
        if at % 128 + length > 128:
            out[first + 1] = out[first + 1] + jnp.where(lane < at % 128, row, 0.0)
    return jnp.concatenate(out, axis=0)


def piece_of(rows, at, length):
    lane = lax.broadcasted_iota(jnp.int32, (1, 128), 1)
    first, shift = at // 128, at % 128
    row = rows[first : first + 1, :]
    if shift:
        row = pltpu.roll(row, 128 - shift, 1)
        if shift + length > 128:
            other = pltpu.roll(rows[first + 1 : first + 2, :], 128 - shift, 1)
            row = jnp.where(lane < 128 - shift, row, other)
    return jnp.where(lane < length, row, 0.0)


def segments_apart(flat, small):
    lane = lax.broadcasted_iota(jnp.int32, (1, 128), 1)
    turned = pltpu.roll(flat, 128 - small, 1)
    return jnp.where(lane < 128 - small, pltpu.roll(turned, 1, 0), turned)


def segments_joined(rows, first, small):
    lane = lax.broadcasted_iota(jnp.int32, (1, 128), 1)
    turned = pltpu.roll(rows, small, 1)
    row = lax.broadcasted_iota(jnp.int32, (rows.shape[0], 1), 0)
    joined = jnp.where(lane < small, turned, pltpu.roll(turned, rows.shape[0] - 1, 0))
    return jnp.where((lane < small) & (row == 0), first, joined)


def first_tile(rel, wn, ext_ref, gp_ref, start):
    valid = rel[3:4, :].astype(F32)
    for j in range(TILE // 256):
        at = slice(256 * j, 256 * j + 256)
        to = slice(start + 256 * j, start + 256 * j + 256)
        g, d = gelu_twice(mm_tn(wn, rel[:, at]))
        ext_ref[0:C1, to] = low(g * (valid[:, at] * (0.5 * LAM)))
        gp_ref[:, to] = low(d * (valid[:, at] * 0.5))
    ext_ref[C1:, start : start + TILE] = jnp.concatenate([rel[3:4], jnp.zeros((15, TILE), BF16)], axis=0)


def first_tokens(gext, ps_ref, w2e, w3_ref, pooled_o, gm_o, fw_o):
    lower = w3_ref[C2:, :]
    count = ps_ref[:, C1 : C1 + 1]
    fs = mm_exact(ps_ref[:, 0 : C1 + 16], w2e)
    pooled = low(fs / count)
    pooled_o[...] = pooled
    g = mm(pooled, w3_ref[0:C2, :])
    gm_o[...] = g
    fw = mm_exact(fs, lower)
    fw_o[...] = fw
    gram = sum(mm_tn(w2e, part) for part in split_three(mm_exact(gext, w2e)))
    one = jnp.sum(fw + count * g, axis=0, keepdims=True)
    two = jnp.sum(mm_exact(gram, lower) * lower.astype(F32), axis=0, keepdims=True)
    two = two + jnp.sum(g * (2.0 * fw + count * g), axis=0, keepdims=True)
    return as_rows(one, two)


def third_vectors(totals, n, psmall_ref):
    mean = as_vector(totals, 0, 4) / n
    inverse = lax.rsqrt(as_vector(totals, 4, 4) / n - mean * mean + EPS_NORM)
    gain, shift = as_vector(psmall_ref, 7, 4), as_vector(psmall_ref, 11, 4)
    return jnp.concatenate([inverse * gain, shift, mean, inverse, jnp.zeros((4, C3), F32)], axis=0)


def second_tile(act, mask, w23, gm, count, sv_ref, gp_o, start, pa_o, pg_o, pc_o, first):
    scale, shift = low(sv_ref[0:1, :] * (1.0 / LAM)), low(sv_ref[1:2, :] * (1.0 / LAM))
    turned = act.T
    c = mm(jnp.concatenate([turned, turned], axis=1), w23).reshape(TOK, GROUP, C3) + gm[:, None, :]
    c = low(c)
    g, gp = gelu_twice(c * scale[None] + shift[None])
    gc = (gp * c).reshape(TILE, C3)
    gp = gp.reshape(TILE, C3)
    gp_o[start : start + TILE, :] = gp
    g = g.reshape(TILE, C3)
    means, gps, gcs = [], [], []
    for q in range(TILE // 256):
        at = slice(256 * q, 256 * q + 256)
        m = mask[8 * q : 8 * q + 8, at]
        means.append(mm(m, g[at]) * (0.5 * LAM) / count[8 * q : 8 * q + 8, :])
        gps.append(mm(m, gp[at]) * 0.5)
        gcs.append(mm(m, gc[at]) * 0.5)
    for ref, parts in ((pa_o, means), (pg_o, gps), (pc_o, gcs)):
        ref[first, :] = low(jnp.concatenate(parts, axis=0))


class Gather:
    def __init__(self, blocks, send, recv, base):
        self.blocks, self.sems, self.base = blocks, (send, recv), base
        z, y, x, core = where_am_i()
        half = blocks.shape[-1] // 2
        one, two = pl.ds(0, half), pl.ds(half, half)
        every = slice(None)
        near = [(chip(lax.rem(z + k, NZ), y, x), core) for k in range(1, NZ)]
        over_y, over_x, twin = (chip(z, 1 - y, x), core), (chip(z, y, 1 - x), core), (chip(z, y, x), 1 - core)
        self.stages = [
            [((z, y, x, core), peer) for peer in near],
            [((every, y, x, core, every, one), over_y), ((every, y, x, core, every, two), over_x)],
            [((every, every, x, core, every, one), over_x), ((every, y, every, core, every, two), over_y)],
            [],
        ]
        self.inner = [
            [],
            [((every, y, x, core), twin)],
            [((every, 1 - y, x, core, every, one), twin), ((every, y, 1 - x, core, every, two), twin)],
            [((every, every, 1 - x, core, every, one), twin), ((every, 1 - y, every, core, every, two), twin)],
        ]

    def copies(self, stage, inner):
        table = self.inner if inner else self.stages
        k = self.base + (7 if inner else 0) + sum(len(s) for s in table[:stage])
        out = []
        for i, (index, peer) in enumerate(table[stage]):
            view = self.blocks.at[index]
            out.append(
                pltpu.make_async_remote_copy(
                    src_ref=view, dst_ref=view, send_sem=self.sems[0].at[k + i], recv_sem=self.sems[1].at[k + i],
                    device_id=peer, device_id_type=MESH,
                )
            )
        return out

    def advance(self, stage):
        if stage > 0:
            for copy in self.copies(stage - 1, False):
                copy.wait()
        if stage < 4:
            for copy in self.copies(stage, False) + self.copies(stage, True):
                copy.start()
        else:
            for inner_stage in range(4):
                for copy in self.copies(inner_stage, True):
                    copy.wait()


GATHER_SEMS = 12
ATT_WIDTH, FFN_WIDTH = 4 * D, 6 * D


def attention_rows(bal, pal, stage):
    start = 1
    for at, cols in ((0, 3 * D), (3 * D, D)):
        for j in range(cols // 128):
            stage[0:12, at + 128 * j : at + 128 * j + 128] = bal[pl.ds(start + j, 12, stride=cols // 128), :]
        start += 12 * cols // 128
    for k in range(4):
        for j in range(D // 128):
            to = D * k + 128 * j
            stage[12:16, to : to + 128] = pal[pl.ds(73 + 12 * k + j, 4, stride=3), :]


def attention_flat(stage, bal, pal):
    start = 1
    for at, cols in ((0, 3 * D), (3 * D, D)):
        for j in range(cols // 128):
            bal[pl.ds(start + j, 12, stride=cols // 128), :] = stage[0:12, at + 128 * j : at + 128 * j + 128]
        start += 12 * cols // 128
    for k in range(4):
        for j in range(D // 128):
            at = D * k + 128 * j
            pal[pl.ds(73 + 12 * k + j, 4, stride=3), :] = stage[12:16, at : at + 128]


FFN_PIECES = [(0, 16, 0, FF), (16, 16, 0, FF + D)] + [(32 + 4 * k, 4, 12, D * k) for k in range(4)]
FFN_START = 1 + 12 * 4 * D // 128


def ffn_rows(bal, stage):
    for j in range(FF // 128):
        stage[0:12, 128 * j : 128 * j + 128] = bal[pl.ds(FFN_START + j, 12, stride=FF // 128), :]
    start = FFN_START + 12 * FF // 128
    for row, rows, under, at in FFN_PIECES:
        for j in range(D // 128):
            to = at + 128 * j
            stage[under : under + rows, to : to + 128] = bal[pl.ds(start + 3 * row + j, rows, stride=3), :]


def ffn_flat(stage, bal):
    for j in range(FF // 128):
        bal[pl.ds(FFN_START + j, 12, stride=FF // 128), :] = stage[0:12, 128 * j : 128 * j + 128]
    start = FFN_START + 12 * FF // 128
    for row, rows, under, at in FFN_PIECES:
        for j in range(D // 128):
            bal[pl.ds(start + 3 * row + j, rows, stride=3), :] = stage[
                under : under + rows, at + 128 * j : at + 128 * j + 128
            ]


def place(d):
    return d // 8, d // 4 % 2, d // 2 % 2, d % 2


def forward_kernel(known, dp, *refs):
    refs = list(refs)
    take = lambda count: [refs.pop(0) for _ in range(count)]
    points_ref, counts_ref, centres_ref, pflat, bflat = take(5) if known else [None] * 5
    rel_o, moment_o, psmall_o, bsmall_o, w2_o, w3_o = take(6)
    w4_o, wqkv_o, wo_o, wf1_o, wf2_o = take(5) if known else [None] * 5
    ext_o, gp1_o, g_o, ps_o, gm_o, fw_o, pooled_o, sv_o, stats_o, wd_o, w23_o, gp_o, pa_o, pg_o, pc_o = take(15)
    ext_s, gm_s, fw_s, e_s, wn_s, w2_s, w23_s, acc3, sums3, ssend3, srecv3 = take(11)
    step = pl.program_id(0)
    tiles = pl.num_programs(0) // 2
    peers = all_peers(dp)
    if known:
        (
            tiny, att, ffn, three, stage, wide, flat2, pal, bal, counts_s, picked_s,
            tsend, trecv, gsend, grecv,
        ) = take(15)
        z, y, x, core = where_am_i()
        gather_w3 = Gather(three, gsend, grecv, 0)
        gather_att = Gather(att, gsend, grecv, GATHER_SEMS)
        gather_ffn = Gather(ffn, gsend, grecv, 2 * GATHER_SEMS)

    @pl.when(step == 0)
    def _():
        greet(peers)
        g_o[...] = jnp.zeros_like(g_o)
        e_s[...] = token_ones()
        if known:
            pal[...] = segments_apart(pflat[...], PSMALL)
            bal[...] = segments_apart(bflat[...], BSMALL)
            moments = geometry(points_ref, counts_ref, centres_ref, rel_o, counts_s, picked_s)[0:4, :]
            moments = jnp.concatenate([moments, jnp.zeros((4, 120), F32)], axis=1)
            hi, mid, lo = [part.astype(F32) for part in split_three(moments)]
            packed = hi + pltpu.roll(mid, 8, 1) + pltpu.roll(lo, 16, 1)
            rows = [pal[1:9, :], pflat[0:1, :], bflat[0:1, :], packed, jnp.zeros((2, 128), F32)]
            own = tiny.at[me()]
            own[...] = low(jnp.concatenate(rows, axis=0))
            greeted(peers)
            copies = send_to_all(dp, own, lambda k: own, tsend, trecv)
            for j in range(C3 // 128):
                three[z, y, x, core, :, 128 * j : 128 * j + 128] = low(pal[pl.ds(9 + j, 16, stride=C3 // 128), :])
            gather_w3.advance(0)
            attention_rows(bal, pal, stage)
            att[z, y, x, core] = low(stage[:, 0:ATT_WIDTH])
            gather_att.advance(0)
            ffn_rows(bal, stage)
            ffn[z, y, x, core] = low(stage[...])
            gather_w3.advance(1)
            for copy in copies:
                copy.wait()
            gather_att.advance(1)
            gather_ffn.advance(0)
            psmall, bsmall = [], []
            packed = jnp.zeros((4, 128), F32)
            for d in range(dp * NC):
                rows = tiny[d].astype(F32)
                flat2[8 * d : 8 * d + 8, :] = rows[0:8, :]
                psmall.append(rows[8:9, :])
                bsmall.append(rows[9:10, :])
                packed = packed + rows[10:14, :]
            total = packed + pltpu.roll(packed, 120, 1) + pltpu.roll(packed, 112, 1)
            moment_o[...] = jnp.concatenate([total, jnp.zeros((4, 128), F32)], axis=0)
            psmall_o[0:18, :] = flat_rows(jnp.concatenate(psmall, axis=0), PSMALL, 18)
            bsmall_o[0:30, :] = flat_rows(jnp.concatenate(bsmall, axis=0), BSMALL, 30)
            for j in range(2):
                w2_o[:, 128 * j : 128 * j + 128] = low(flat2[pl.ds(j, C1, stride=2), :])
        else:
            greeted(peers)
        small = psmall_o[...]
        forward, backward, stats = prepare_one(moment_o[:, 0:8], small)
        wn_s[...] = forward
        wd_o[...] = backward
        stats_o[...] = stats
        w2_s[0:C1, :] = w2_o[...]
        b2 = as_vector(small, 5, 2)
        w2_s[C1:, :] = low(jnp.concatenate([b2, jnp.zeros((15, C2), F32)], axis=0))

    if known:
        for at_step, gather, number in (
            (1, gather_w3, 2), (2, gather_w3, 3), (2, gather_att, 2), (3, gather_ffn, 1), (4, gather_w3, 4),
            (5, gather_att, 3), (5, gather_ffn, 2), (6, gather_att, 4), (7, gather_ffn, 3),
        ):
            pl.when(step == at_step)(functools.partial(gather.advance, number))

    def tile_at(half):
        tile = lax.rem(step, tiles) * STEP_TILES + half
        return pl.ds(pl.multiple_of(tile * TILE, TILE), TILE), pl.ds(pl.multiple_of(tile * TOK, TOK), TOK)

    @pl.when(step < tiles)
    def _():
        for half in range(STEP_TILES):
            at, ts = tile_at(half)
            first_tile(rel_o[:, at], wn_s[...], ext_o, gp1_o, half * TILE)
            ext = ext_o[:, half * TILE : half * TILE + TILE]
            ext_s[:, at] = ext[0:C1]
            both = mm_nt(jnp.concatenate([ext, e_s[...]], axis=0), ext)
            g_o[:, 0 : C1 + 16] += both[0 : C1 + 16]
            ps_o[ts, 0 : C1 + 16] = both[C1 + 16 :]

    @pl.when(step == tiles)
    def _():
        if known:
            for d in range(dp * NC):
                w3_o[16 * d : 16 * d + 16, :] = three[place(d)]
        acc3[...] = first_tokens(g_o[:, 0 : C1 + 16], ps_o, w2_s[...], w3_o, pooled_o, gm_s, fw_s)
        copies = sum_start(dp, acc3, sums3, ssend3, srecv3)
        w23 = mm(w2_s[...], w3_o[C2:, :])
        w23_o[...] = w23
        high = low(w23[0:C1])
        w23_s[0:C1, :] = high
        w23_s[C1:, :] = low(w23[0:C1] - high.astype(F32))
        sv_o[...] = third_vectors(sum_finish(acc3, sums3, copies), stats_o[2:3, 0:1], psmall_o)
        mean = sv_o[2:3, :]
        gm = gm_s[...] - mean
        fw_o[...] = low(fw_s[...] + ps_o[:, C1 : C1 + 1] * gm)
        gm = gm + w23[C1 : C1 + 1, :]
        gm_s[...] = gm
        gm_o[...] = low(gm)

    @pl.when(step >= tiles)
    def _():
        for half in range(STEP_TILES):
            at, ts = tile_at(half)
            second_tile(
                ext_s[:, at], e_s[...] * rel_o[3:4, at], w23_s[...], gm_s[ts, :], ps_o[ts, C1 : C1 + 1], sv_o,
                gp_o, half * TILE, pa_o, pg_o, pc_o, ts,
            )

    if known:

        @pl.when(step == tiles + 2)
        def _():
            for d in range(dp * NC):
                under = att[place(d)].astype(F32)
                wide[12 * d : 12 * d + 12, :] = under[0:12, :]
                tail = [under[12:16, D * k : D * k + D] for k in range(4)]
                w4_o[16 * d : 16 * d + 16, :] = low(jnp.concatenate(tail, axis=0))
            wqkv_o[...] = low(wide[:, 0 : 3 * D])
            wo_o[...] = low(wide[:, 3 * D : 4 * D])

        @pl.when(step == 2 * tiles - 1)
        def _():
            gather_ffn.advance(4)
            for d in range(dp * NC):
                block = ffn.at[place(d)]
                under = block[:, 0:FF].astype(F32)
                wide[12 * d : 12 * d + 12, :] = under[0:12, :]
                wf2_o[48 * d : 48 * d + 16, :] = block[:, FF : FF + D]
                wf2_o[48 * d + 16 : 48 * d + 32, :] = block[:, FF + D : FF + 2 * D]
                tail = [under[12:16, D * k : D * k + D] for k in range(4)]
                wf2_o[48 * d + 32 : 48 * d + 48, :] = low(jnp.concatenate(tail, axis=0))
            wf1_o[...] = low(wide[...])


def forward_call(known, dp, count, *args):
    tokens, tiles = count // GROUP, count // WIDE
    single = dict(pipeline_mode=pl.Buffered(1))
    full = lambda *s: pl.BlockSpec(s, lambda i: (0, 0), **single)
    early = lambda r: pl.BlockSpec((r, WIDE), lambda i: (0, jnp.minimum(i, tiles - 1)))
    given = [
        ((8, count), BF16), ((8, 128), F32), ((24, 128), F32), ((32, 128), F32), ((C1, C2), BF16), ((2 * C2, C3), BF16),
    ]
    gathered = [((C3, D), BF16), ((D, 3 * D), BF16), ((D, D), BF16), ((D, FF), BF16), ((FF, D), BF16)]
    outs = [(full(*s), s, t) for s, t in given + gathered] if known else []
    outs += [(early(C1 + 16), (C1 + 16, count), BF16), (early(C1), (C1, count), BF16)]
    outs += [
        (full(*s), s, t)
        for s, t in (
            ((C1 + 16, 256), F32), ((tokens, 256), F32), ((tokens, C3), BF16), ((tokens, C3), BF16),
            ((tokens, C2), BF16), ((8, C3), F32), ((8, C1), F32), ((8, C1), BF16), ((C1 + 16, C3), F32),
        )
    ]
    outs += [(pl.BlockSpec((WIDE, C3), lambda i: (jnp.maximum(i - tiles, 0), 0)), (count, C3), BF16)]
    outs += [(full(tokens, C3), (tokens, C3), BF16)] * 3
    scratch = [
        pltpu.VMEM((C1, count), BF16), pltpu.VMEM((tokens, C3), F32), pltpu.VMEM((tokens, C3), F32),
        pltpu.VMEM((TOK, TILE), BF16), pltpu.VMEM((8, C1), BF16),
        pltpu.VMEM((C1 + 16, C2), BF16), pltpu.VMEM((2 * C1, C3), BF16),
    ] + sum_scratch(dp)
    if known:
        n = dp * NC
        scratch += [
            pltpu.VMEM((n, 16, 128), BF16),
            pltpu.VMEM((NZ, NY, NX, NC, 16, ATT_WIDTH), BF16),
            pltpu.VMEM((NZ, NY, NX, NC, 16, FFN_WIDTH), BF16),
            pltpu.VMEM((NZ, NY, NX, NC, 16, C3), BF16),
            pltpu.VMEM((16, FFN_WIDTH), F32),
            pltpu.VMEM((D, FF), F32),
            pltpu.VMEM((8 * n, 128), F32),
            pltpu.VMEM((PROWS, 128), F32), pltpu.VMEM((BROWS, 128), F32),
            pltpu.VMEM((count // 128, 256), F32), pltpu.VMEM((count // 32, 256), F32),
            pltpu.SemaphoreType.DMA((n - 1,)), pltpu.SemaphoreType.DMA((n - 1,)),
            pltpu.SemaphoreType.DMA((3 * GATHER_SEMS,)), pltpu.SemaphoreType.DMA((3 * GATHER_SEMS,)),
        ]
    return pl.pallas_call(
        functools.partial(forward_kernel, known, dp),
        grid=(2 * tiles,),
        in_specs=[full(*a.shape) for a in args],
        out_specs=[o[0] for o in outs],
        out_shape=shaped(*[o[1:] for o in outs]),
        scratch_shapes=scratch,
        compiler_params=params(collective_id=0, has_side_effects=True),
        name="forward",
    )(*args)


def wide_row(ref, first, rows):
    return jnp.concatenate([ref[k : k + 1, :] for k in range(first, first + rows)], axis=1)


def layer_norm(v, gain, shift):
    centred = v - jnp.mean(v, -1, keepdims=True)
    inverse = lax.rsqrt(jnp.mean(centred * centred, -1, keepdims=True) + EPS_NORM)
    unit = centred * inverse
    return unit, inverse, low(unit * gain + shift)


def norm_back(d_unit, unit, inverse):
    return inverse * (
        d_unit - jnp.mean(d_unit, -1, keepdims=True) - unit * jnp.mean(d_unit * unit, -1, keepdims=True)
    )


def col_sum(v):
    return jnp.sum(v, axis=0, keepdims=True)


def block_step(
    pa_ref, pg_ref, pc_ref, cnt_ref, len_ref, cot_ref, psmall_ref, bsmall_ref, sv_ref,
    w4_ref, wqkv_ref, wo_ref, wf1_ref, wf2_ref,
    out_o, small_o, tok_o, tg_o, back_o, qkv_s, mixed_s, soft_s, dmix_s, dqkv_s, dhid_s,
    ffn_grads, between, token_grads, attention_grads,
):
    count = cnt_ref[:, C1 : C1 + 1]
    scale = HEAD_DIM ** (-0.5)
    b4 = wide_row(psmall_ref, 15, 3)
    ln1_gain, ln1_shift, bo = wide_row(bsmall_ref, 0, 3), wide_row(bsmall_ref, 3, 3), wide_row(bsmall_ref, 6, 3)
    ln2_gain, ln2_shift = wide_row(bsmall_ref, 9, 3), wide_row(bsmall_ref, 12, 3)
    bf1, bf2 = wide_row(bsmall_ref, 15, 12), wide_row(bsmall_ref, 27, 3)

    act = pa_ref[...]
    x_zero = mm(act, w4_ref[...]) + b4
    unit_a, inv_a, normed_a = layer_norm(x_zero, ln1_gain, ln1_shift)
    qkv_s[...] = low(mm(normed_a, wqkv_ref[...]))

    row_cloud = lax.broadcasted_iota(jnp.int32, (PAIR, PAIR), 0) // PATCHES
    col = lax.broadcasted_iota(jnp.int32, (PAIR, PAIR), 1)
    left = lax.broadcasted_iota(jnp.int32, (1, 128), 1) < HEAD_DIM
    zero = jnp.zeros((1, 1), BF16)

    def halves(v):
        return jnp.where(left, v, zero), jnp.where(left, zero, v)

    tiles = pa_ref.shape[0] // PAIR
    for s in range(tiles):
        seen = jnp.zeros((1, PAIR), jnp.int32)
        for c in range(PAIR // PATCHES):
            seen = jnp.where(col[0:1, :] // PATCHES == c, len_ref[s * (PAIR // PATCHES) + c], seen)
        visible = (row_cloud == col // PATCHES) & (lax.rem(col, PATCHES) < seen)
        rows = slice(PAIR * s, PAIR * s + PAIR)
        for p in range(HEADS // 2):
            at = 128 * p
            q = qkv_s[rows, at : at + 128]
            k = qkv_s[rows, D + at : D + at + 128]
            v = qkv_s[rows, 2 * D + at : 2 * D + at + 128]
            mixed = []
            for a, q_half in enumerate(halves(q)):
                score = jnp.where(visible, mm_nt(q_half, k) * scale, NEG_FILL)
                raised = jnp.exp(score - jnp.max(score, -1, keepdims=True))
                soft = raised / jnp.sum(raised, -1, keepdims=True)
                soft_s[(s * (HEADS // 2) + p) * 2 + a] = soft
                mixed.append(mm(low(soft), v))
            mixed_s[rows, at : at + 128] = low(jnp.where(left, mixed[0], mixed[1]))

    mixed_low = mixed_s[...]
    x_one = x_zero + mm(mixed_low, wo_ref[...]) + bo
    unit_b, inv_b, normed_b = layer_norm(x_one, ln2_gain, ln2_shift)
    hidden, d_hidden = gelu_pair(mm(normed_b, wf1_ref[...]) + bf1)
    dhid_s[...] = d_hidden
    out_o[...] = x_one + mm(hidden, wf2_ref[...]) + bf2

    cot = cot_ref[...]
    grad = low(cot)
    d_pre = mm_nt(grad, wf2_ref[...]) * dhid_s[...].astype(F32)
    d_pre_low = low(d_pre)
    small_o[7:8, :] = col_sum(d_pre)
    ffn_grads(mm_tn(normed_b, d_pre_low), mm_tn(hidden, grad))
    d_normed_b = mm_nt(d_pre_low, wf1_ref[...])
    d_x_one = cot + norm_back(d_normed_b * ln2_gain, unit_b, inv_b)
    d_x_low = low(d_x_one)
    d_x_one_low = d_x_low
    dmix_s[...] = low(mm_nt(d_x_low, wo_ref[...]))

    for s in range(tiles):
        rows = slice(PAIR * s, PAIR * s + PAIR)
        for p in range(HEADS // 2):
            at = 128 * p
            q = qkv_s[rows, at : at + 128]
            k = qkv_s[rows, D + at : D + at + 128]
            v = qkv_s[rows, 2 * D + at : 2 * D + at + 128]
            dm = dmix_s[rows, at : at + 128]
            d_q, d_k, d_v = [], [], []
            for a, dm_half in enumerate(halves(dm)):
                soft = soft_s[(s * (HEADS // 2) + p) * 2 + a]
                d_soft = mm_nt(dm_half, v)
                d_v.append(mm_tn(low(soft), dm))
                d_score = low(soft * (d_soft - jnp.sum(soft * d_soft, -1, keepdims=True)))
                d_q.append(mm(d_score, k))
                d_k.append(mm_tn(d_score, q))
            dqkv_s[rows, at : at + 128] = low(jnp.where(left, d_q[0], d_q[1]) * scale)
            dqkv_s[rows, D + at : D + at + 128] = low(jnp.where(left, d_k[0], d_k[1]) * scale)
            dqkv_s[rows, 2 * D + at : 2 * D + at + 128] = low(jnp.where(left, d_v[0], d_v[1]))

    between()
    d_qkv = dqkv_s[...]
    d_normed_a = mm_nt(d_qkv, wqkv_ref[...])
    d_x_zero = d_x_one + norm_back(d_normed_a * ln1_gain, unit_a, inv_a)
    d_x_low = low(d_x_zero)
    token = mm_nt(d_x_low, w4_ref[...]) / count
    tok_o[...] = token
    grouped = token * pg_ref[...].astype(F32)
    tg_o[...] = grouped
    back_o[...] = as_rows(col_sum(grouped), col_sum(token * pc_ref[...].astype(F32)) * sv_ref[3:4, :])
    token_grads()
    narrow = [
        col_sum(d_normed_a * unit_a), col_sum(d_normed_a), col_sum(d_x_one),
        col_sum(d_normed_b * unit_b), col_sum(d_normed_b), col_sum(cot), col_sum(d_x_zero),
    ]
    for k, row in enumerate(narrow):
        small_o[k : k + 1, 0:D] = row
    attention_grads(mm_tn(normed_a, d_qkv), mm_tn(mixed_low, d_x_one_low), mm_tn(act, d_x_low))


def third_back_tokens(
    totals, tg_ref, sc_ref, gm_ref, ps_ref, pooled_ref, gext_ref, w2_ref, w3_ref, w23_ref, sv_ref, stats_ref,
    kap_o, k_o, wb_o, top_o, corr_o, base_o,
):
    gain = sv_ref[0:1, :]
    n = stats_ref[2:3, 0:1]
    alpha = gain * as_vector(totals, 0, 4) / n
    beta = gain * as_vector(totals, 4, 4) * sv_ref[3:4, :] / n
    count = ps_ref[:, C1 : C1 + 1]
    w23 = w23_ref[...]
    act = low(w23[0:C1])
    per_token = low(gain * tg_ref[...] - (count * alpha + beta * sc_ref[...].astype(F32)))
    pooled = low(mm_nt(per_token, w3_ref[0:C2, :]) / count)
    shifted = low(alpha + beta * gm_ref[...].astype(F32))
    kap_o[...] = low(mm_nt(pooled, w2_ref[...]) - mm_nt(shifted, act))
    k_o[:, 0:C1] = low(-mm_nt(low(w23[0:C1] * beta), act))
    wb_o[...] = low(w23[0:C1] * gain)
    top_o[...] = mm_tn(pooled_ref[...], per_token)
    sums = low(ps_ref[:, 0 : C1 + 16])
    corr_o[...] = mm_tn(sums, shifted) + beta * mm(low(gext_ref[:, 0:C1]), act)
    base_o[...] = mm_tn(sums, pooled)


def last_tile(gp, ext, gp1, rel, tok, kap, k_s, xe_s, wb_ref, wd_ref, h_o, q_o, d_at):
    dn = (gp.reshape(TOK, GROUP, C3) * tok[:, None, :]).reshape(TILE, C3)
    xe_s[0:C1, :] = ext[0:C1, :]
    k_s[:, C1 : C1 + TOK] = kap.T
    h_o[...] += mm(ext, dn)
    d_act = mm_nt(wb_ref[...], dn) + mm(k_s[...], xe_s[...])
    d_one = low(d_act * gp1.astype(F32))
    d_at(mm(wd_ref[...], d_one))
    q_o[...] += mm_nt(rel, d_one)


def last_weights(h, gain, corr, base, w2e, w3_ref):
    m = h * gain - corr
    parts = split_three(m)[0:2]
    grad_w3 = sum(mm_tn(w2e, part) for part in parts)
    return grad_w3, sum(mm_nt(part, w3_ref[C2:, :]) for part in parts) + base


def first_grads(q, moments, psmall, stats):
    mean, inverse, n, scale = stats[0:1], stats[1:2], stats[2:3], stats[3:4]
    w = [psmall[k : k + 1, :] for k in range(3)]
    one = q[3:4, :]
    two = inverse * (sum(w[k] * q[k : k + 1, :] for k in range(3)) - mean * one)
    grad_w = []
    for k in range(3):
        along = sum(w[j] * moments[k : k + 1, j : j + 1] for j in range(3)) - mean * moments[k : k + 1, 3:4]
        grad_w.append(scale * (q[k : k + 1, :] - (one * moments[k : k + 1, 3:4] + two * inverse * along) / n))
    flat = [
        jnp.sum(scale * w[k] * (one - two * inverse * mean) / n, axis=1, keepdims=True) for k in range(3)
    ]
    slope = [
        [jnp.sum(scale * w[k] * two * inverse * w[j] / n, axis=1, keepdims=True) for j in range(3)]
        for k in range(3)
    ]
    return grad_w, two, one, flat, slope


def point_gradient(d_ref, rel_ref, centres_ref, flat, slope, out_ref, spread_s, sums_s):
    pieces = d_ref.shape[1] // 256
    lane = lax.rem(lax.broadcasted_iota(jnp.int32, (1, 256), 1), GROUP).astype(F32)
    base = jnp.concatenate(flat, axis=0)
    columns = [jnp.concatenate([slope[k][j] for k in range(3)], axis=0) for j in range(3)]
    spread_s[...] = spread_tokens(centres_ref[...])
    for i in range(pieces):
        at = slice(256 * i, 256 * i + 256)
        rel = rel_ref[:, at].astype(F32)
        d = d_ref[:, at]
        out = d[0:3] + d[4:7] - rel[3:4] * base
        for j in range(3):
            out = out - columns[j] * rel[j : j + 1]
        out_ref[:, at] = out
        sums_s[8 * i : 8 * i + 8, :] = jnp.concatenate([out, jnp.zeros((5, 256), F32)], axis=0)
    sums_s[...] = patch_sum(sums_s[...], patch_ones())
    for i in range(pieces):
        at = slice(256 * i, 256 * i + 256)
        pick = (lane == spread_s[i : i + 1, :]).astype(F32)
        out_ref[:, at] = out_ref[:, at] - pick * sums_s[8 * i : 8 * i + 3, :]


def point_small_rows(grad_w, gain1, shift1, b2, tot, b4):
    rows = list(grad_w) + [gain1, shift1]
    rows += [b2[:, 128 * k : 128 * k + 128] for k in range(2)]
    rows += [tot[4:8, :], tot[0:4, :]]
    rows += [b4[:, 128 * k : 128 * k + 128] for k in range(3)]
    return jnp.concatenate(rows, axis=0)


def block_small_rows(small_ref):
    rows = [small_ref[k : k + 1, 128 * j : 128 * j + 128] for k in range(5) for j in range(3)]
    rows += [small_ref[7:8, 128 * j : 128 * j + 128] for j in range(12)]
    rows += [small_ref[5:6, 128 * j : 128 * j + 128] for j in range(3)]
    return jnp.concatenate(rows, axis=0)


class Scatter:
    def __init__(self, blocks, lands, send, recv, base):
        self.blocks, self.lands, self.sems, self.base = blocks, lands, (send, recv), base
        z, y, x, core = self.at = where_am_i()
        half = blocks.shape[-1] // 2
        self.one, self.two = pl.ds(0, half), pl.ds(half, half)
        every = slice(None)
        mine = blocks.at[core]
        near = [(chip(lax.rem(z + k, NZ), y, x), core) for k in range(1, NZ)]
        over_y, over_x, twin = (chip(z, 1 - y, x), core), (chip(z, y, 1 - x), core), (chip(z, y, x), 1 - core)
        land1, land2, land3, land4 = lands
        self.stages = [
            [(blocks.at[1 - core], land1, twin)],
            [
                (mine.at[:, :, 1 - x, :, self.one], land2.at[0], over_x),
                (mine.at[:, 1 - y, :, :, self.two], land2.at[1], over_y),
            ],
            [
                (mine.at[:, 1 - y, x, :, self.one], land3.at[0], over_y),
                (mine.at[:, y, 1 - x, :, self.two], land3.at[1], over_x),
            ],
            [(mine.at[lax.rem(z + k, NZ), y, x], land4.at[k - 1], near[k - 1]) for k in range(1, NZ)],
        ]

    def copies(self, stage):
        k = self.base + sum(len(s) for s in self.stages[:stage])
        return [
            pltpu.make_async_remote_copy(
                src_ref=src, dst_ref=dst, send_sem=self.sems[0].at[k + i], recv_sem=self.sems[1].at[k + i],
                device_id=peer, device_id_type=MESH,
            )
            for i, (src, dst, peer) in enumerate(self.stages[stage])
        ]

    def advance(self, stage):
        z, y, x, core = self.at
        mine = self.blocks.at[core]
        land1, land2, land3, land4 = self.lands
        if stage > 0:
            for copy in self.copies(stage - 1):
                copy.wait()
        if stage == 1:
            for cz in range(NZ):
                for cy in range(NY):
                    for cx in range(NX):
                        mine[cz, cy, cx] = mine[cz, cy, cx] + land1[cz, cy, cx]
        if stage == 2:
            for cz in range(NZ):
                for k in range(2):
                    mine[cz, k, x, :, self.one] = mine[cz, k, x, :, self.one] + land2[0, cz, k]
                    mine[cz, y, k, :, self.two] = mine[cz, y, k, :, self.two] + land2[1, cz, k]
        if stage == 3:
            for cz in range(NZ):
                mine[cz, y, x, :, self.one] = mine[cz, y, x, :, self.one] + land3[0, cz]
                mine[cz, y, x, :, self.two] = mine[cz, y, x, :, self.two] + land3[1, cz]
        if stage < 4:
            for copy in self.copies(stage):
                copy.start()
            return None
        total = mine[z, y, x].astype(F32)
        for k in range(NZ - 1):
            total = total + land4[k].astype(F32)
        return total


SCATTER_SEMS = 8
POINT_WIDTH = 768


def scatter_scratch(width):
    return [
        pltpu.VMEM((NC, NZ, NY, NX, 16, width), BF16),
        pltpu.VMEM((NZ, NY, NX, 16, width), BF16),
        pltpu.VMEM((2, NZ, 2, 16, width // 2), BF16),
        pltpu.VMEM((2, NZ, 16, width // 2), BF16),
        pltpu.VMEM((NZ - 1, 16, width), BF16),
    ]


def backward_kernel(known, dp, *refs):
    refs = list(refs)
    take = lambda count: [refs.pop(0) for _ in range(count)]
    pa_ref, pg_ref, pc_ref, ps_ref, len_ref, cot_ref, psmall_ref, bsmall_ref, sv_ref, stats_ref, moment_ref = take(11)
    w2_ref, w3_ref, w4_ref, wqkv_ref, wo_ref, wf1_ref, wf2_ref, w23_ref = take(8)
    sc_ref, gm_ref, pooled_ref, gext_ref, wd_ref, rel_ref, centres_ref, gp_ref, ext_ref, gp1_ref = take(10)
    out_o, pg_o = take(2)
    if known:
        pflat_o, bflat_o = take(2)
    else:
        prow_o, brow_o, gw2_o, gw3_o, gw4_o, gwqkv_o, gwo_o, gwf1_o, gwf2_o = take(9)
    small_s, tok_s, tg_s, acc3, qkv_s, mixed_s, soft_s, dmix_s, dqkv_s, dhid_s = take(10)
    tot_s, kap_s, k_s, wb_s, top_s, corr_s, base_s, h_s, q_s, d_s, xe_s, spread_s, sums_s = take(13)
    acc, slots, ssend, srecv, unused, slots3, ssend3, srecv3 = take(8)
    gp_r, ext_r, gp1_r, read_sem = take(4)
    step = pl.program_id(0)
    steps = pl.num_programs(0)
    peers = all_peers(dp)
    if known:
        ffn0, ffn1, ffn2, ffn3, ffn4, att0, att1, att2, att3, att4, point0, point1, point2, point3, point4 = take(15)
        wide, tall, stage, pstage, pal, bal, gsend, grecv = take(8)
        z, y, x, core = where_am_i()
        ffn = Scatter(ffn0, (ffn1, ffn2, ffn3, ffn4), gsend, grecv, 0)
        att = Scatter(att0, (att1, att2, att3, att4), gsend, grecv, SCATTER_SEMS)
        point = Scatter(point0, (point1, point2, point3, point4), gsend, grecv, 2 * SCATTER_SEMS)

    def ffn_grads(gwf1, gwf2):
        if not known:
            gwf1_o[...], gwf2_o[...] = gwf1, gwf2
            return
        wide[...] = gwf1
        tall[...] = gwf2
        for d in range(dp * NC):
            stage[0:12, 0:FF] = wide[12 * d : 12 * d + 12, :]
            for row, rows, under, at in FFN_PIECES:
                stage[under : under + rows, at : at + D] = tall[48 * d + row : 48 * d + row + rows, :]
            cz, cy, cx, cc = place(d)
            ffn0[cc, cz, cy, cx] = low(stage[...])
        greeted(peers)
        ffn.advance(0)

    def between():
        if known:
            ffn.advance(1)

    def token_grads():
        if not known:
            greeted(peers)
        sum_start(dp, acc3, slots3, ssend3, srecv3)

    def attention_grads(gwqkv, gwo, gw4):
        if not known:
            gwqkv_o[...], gwo_o[...], gw4_o[...] = gwqkv, gwo, gw4
            return
        wide[:, 0 : 3 * D] = gwqkv
        wide[:, 3 * D :] = gwo
        tall[0:C3, :] = gw4
        for d in range(dp * NC):
            stage[0:12, 0:ATT_WIDTH] = wide[12 * d : 12 * d + 12, :]
            for k in range(4):
                stage[12:16, D * k : D * k + D] = tall[16 * d + 4 * k : 16 * d + 4 * k + 4, :]
            cz, cy, cx, cc = place(d)
            att0[cc, cz, cy, cx] = low(stage[:, 0:ATT_WIDTH])
        att.advance(0)
        ffn.advance(2)
        att.advance(1)

    def reads(tile, slot):
        at = pl.ds(pl.multiple_of(tile * TILE, TILE), TILE)
        pairs = ((gp_ref.at[at, :], gp_r), (ext_ref.at[:, at], ext_r), (gp1_ref.at[:, at], gp1_r))
        return [
            pltpu.make_async_copy(src, ring.at[slot], read_sem.at[slot, k]) for k, (src, ring) in enumerate(pairs)
        ]

    @pl.when(step == 0)
    def _():
        greet(peers)
        for tile in range(AHEAD):
            for copy in reads(tile, tile):
                copy.start()
        block_step(
            pa_ref, pg_ref, pc_ref, ps_ref, len_ref, cot_ref, psmall_ref, bsmall_ref, sv_ref,
            w4_ref, wqkv_ref, wo_ref, wf1_ref, wf2_ref,
            out_o, small_s, tok_s, tg_s, acc3, qkv_s, mixed_s, soft_s, dmix_s, dqkv_s, dhid_s,
            ffn_grads, between, token_grads, attention_grads,
        )
        for ref in (h_s, q_s):
            ref[...] = jnp.zeros_like(ref)
        xe_s[C1:, :] = token_ones()
        tot_s[...] = sum_finish(acc3, slots3, sum_copies(dp, acc3, lambda k: slots3.at[k], ssend3, srecv3))
        third_back_tokens(
            tot_s[...], tg_s, sc_ref, gm_ref, ps_ref, pooled_ref, gext_ref, w2_ref, w3_ref, w23_ref, sv_ref, stats_ref,
            kap_s, k_s, wb_s, top_s, corr_s, base_s,
        )

    if known:
        for at_step, group, number in ((4, ffn, 3), (5, att, 2), (7, att, 3)):
            pl.when(step == at_step)(functools.partial(group.advance, number))

    @pl.when(step >= 1)
    def _():
        tile = step - 1
        at = pl.ds(pl.multiple_of(tile * TILE, TILE), TILE)
        ts = pl.ds(pl.multiple_of(tile * TOK, TOK), TOK)
        slot = lax.rem(tile, AHEAD)

        def put(d):
            d_s[:, at] = d

        for copy in reads(tile, slot):
            copy.wait()
        last_tile(
            gp_r[slot], ext_r[slot], gp1_r[slot], rel_ref[:, at], low(tok_s[ts, :] * 0.5), kap_s[ts, :],
            k_s, xe_s, wb_s, wd_ref, h_s, q_s, put,
        )

        @pl.when(tile + AHEAD < steps - 1)
        def _():
            for copy in reads(tile + AHEAD, slot):
                copy.start()

    @pl.when(step == steps - 1)
    def _():
        acc[...] = q_s[...]
        b2 = as_vector(psmall_ref, 5, 2)
        w2e = jnp.concatenate([w2_ref[...], low(jnp.concatenate([b2, jnp.zeros((15, C2), F32)], axis=0))], axis=0)
        gw3, gw2 = last_weights(h_s[...], sv_ref[0:1, :], corr_s[...], base_s[...], w2e, w3_ref)
        none = jnp.zeros((1, 128), F32)
        prow = point_small_rows([none] * 3, none, none, gw2[C1 : C1 + 1, :], jnp.zeros((8, 128), F32), small_s[6:7, 0:D])
        brow = block_small_rows(small_s)
        if known:
            pstage[...] = jnp.zeros_like(pstage)
            for d in range(dp * NC):
                if d < 16:
                    pstage[:, 0:C3] = top_s[16 * d : 16 * d + 16, :]
                else:
                    pstage[:, 0:C3] = gw3[16 * (d - 16) : 16 * (d - 16) + 16, :]
                pstage[0:4, C3 : C3 + C2] = gw2[4 * d : 4 * d + 4, :]
                pstage[4:5, C3 : C3 + 128] = piece_of(prow, PSMALL * d, PSMALL)
                pstage[5:6, C3 : C3 + 128] = piece_of(brow, BSMALL * d, BSMALL)
                cz, cy, cx, cc = place(d)
                point0[cc, cz, cy, cx] = low(pstage[...])
            point.advance(0)
        copies = sum_start(dp, acc, slots, ssend, srecv)
        if known:
            point.advance(1)
        totals = sum_finish(acc, slots, copies)
        grad_w, gain1, shift1, flat, slope = first_grads(totals, moment_ref[...], psmall_ref[...], stats_ref[...])
        full_rows = point_small_rows(grad_w, gain1, shift1, jnp.zeros((1, C2), F32), tot_s[...], jnp.zeros((1, D), F32))
        if known:
            point.advance(2)
            stage[...] = ffn.advance(4)
            ffn_flat(stage, bal)
            stage[:, 0:ATT_WIDTH] = att.advance(4)
            attention_flat(stage, bal, pal)
            point.advance(3)
        point_gradient(d_s, rel_ref, centres_ref, flat, slope, pg_o, spread_s, sums_s)
        if not known:
            prow_o[0:18, :] = prow + full_rows * (1.0 / (dp * NC))
            brow_o[0:30, :] = brow
            gw2_o[...] = gw2[0:C1]
            gw3_o[0:C2, :] = top_s[...]
            gw3_o[C2:, :] = gw3
            return
        own = jnp.zeros((1, 128), F32)
        for d in range(dp * NC):
            own = own + jnp.where(me() == d, piece_of(full_rows, PSMALL * d, PSMALL), 0.0)
        pstage[...] = point.advance(4)
        for j in range(C2 // 128):
            pal[pl.ds(1 + j, 4, stride=2), :] = pstage[0:4, C3 + 128 * j : C3 + 128 * j + 128]
        for j in range(C3 // 128):
            pal[pl.ds(9 + j, 16, stride=4), :] = pstage[:, 128 * j : 128 * j + 128]
        pflat_o[...] = segments_joined(pal[...], pstage[4:5, C3 : C3 + 128] + own, PSMALL)
        bflat_o[...] = segments_joined(bal[...], pstage[5:6, C3 : C3 + 128], BSMALL)


def backward_call(known, dp, *args):
    count = args[24].shape[1]
    tokens, tiles = count // GROUP, count // TILE
    single = dict(pipeline_mode=pl.Buffered(1))
    full = lambda *s: pl.BlockSpec(s, lambda i: (0, 0), **single)
    specs = [full(*a.shape) for a in args[:26]]
    specs[4] = pl.BlockSpec(memory_space=pltpu.SMEM)
    specs += [pl.BlockSpec(memory_space=pl.ANY)] * 3
    outs = [((tokens, D), F32), ((3, count), F32)]
    if known:
        outs += [((PROWS, 128), F32), ((BROWS, 128), F32)]
    else:
        outs += [((24, 128), F32), ((32, 128), F32), ((C1, C2), F32), ((2 * C2, C3), F32), ((C3, D), F32)]
        outs += [((D, 3 * D), F32), ((D, D), F32), ((D, FF), F32), ((FF, D), F32)]
    pieces = count // 256
    scratch = [
        pltpu.VMEM((8, FF), F32), pltpu.VMEM((tokens, C3), F32), pltpu.VMEM((tokens, C3), F32), pltpu.VMEM((8, 128), F32),
        pltpu.VMEM((tokens, 3 * D), BF16), pltpu.VMEM((tokens, D), BF16),
        pltpu.VMEM((tokens // PAIR * HEADS, PAIR, PAIR), F32), pltpu.VMEM((tokens, D), BF16),
        pltpu.VMEM((tokens, 3 * D), BF16), pltpu.VMEM((tokens, FF), BF16),
        pltpu.VMEM((8, 128), F32), pltpu.VMEM((tokens, C1), BF16), pltpu.VMEM((C1, C1 + TOK), BF16),
        pltpu.VMEM((C1, C3), BF16), pltpu.VMEM((C2, C3), F32), pltpu.VMEM((C1 + 16, C3), F32),
        pltpu.VMEM((C1 + 16, C2), F32), pltpu.VMEM((C1 + 16, C3), F32), pltpu.VMEM((8, C1), F32),
        pltpu.VMEM((8, count), F32), pltpu.VMEM((C1 + TOK, TILE), BF16),
        pltpu.VMEM((pieces, 256), F32), pltpu.VMEM((8 * pieces, 256), F32),
    ]
    scratch += sum_scratch(dp) + sum_scratch(dp)
    scratch += [
        pltpu.VMEM((AHEAD, TILE, C3), BF16), pltpu.VMEM((AHEAD, C1 + 16, TILE), BF16), pltpu.VMEM((AHEAD, C1, TILE), BF16),
        pltpu.SemaphoreType.DMA((AHEAD, 3)),
    ]
    if known:
        scratch += scatter_scratch(FFN_WIDTH) + scatter_scratch(ATT_WIDTH) + scatter_scratch(POINT_WIDTH)
        scratch += [
            pltpu.VMEM((D, FF), F32), pltpu.VMEM((FF, D), F32),
            pltpu.VMEM((16, FFN_WIDTH), F32), pltpu.VMEM((16, POINT_WIDTH), F32),
            pltpu.VMEM((PROWS, 128), F32), pltpu.VMEM((BROWS, 128), F32),
            pltpu.SemaphoreType.DMA((3 * SCATTER_SEMS,)), pltpu.SemaphoreType.DMA((3 * SCATTER_SEMS,)),
        ]
    return pl.pallas_call(
        functools.partial(backward_kernel, known, dp),
        grid=(1 + tiles,),
        in_specs=specs,
        out_specs=[full(*s) for s, t in outs],
        out_shape=shaped(*outs),
        scratch_shapes=scratch,
        compiler_params=params(collective_id=1, has_side_effects=True),
        name="backward",
    )(*args)


def geometry_kernel(points_ref, counts_ref, centres_ref, rel_o, moment_o, counts_s, picked_s):
    moments = geometry(points_ref, counts_ref, centres_ref, rel_o, counts_s, picked_s)
    moment_o[...] = jnp.concatenate([moments, jnp.zeros((8, 120), F32)], axis=1)


def geometry_call(points, counts, centres):
    count = points.shape[1]
    return pl.pallas_call(
        geometry_kernel,
        out_shape=shaped(((8, count), BF16), ((8, 128), F32)),
        in_specs=vmem(3),
        out_specs=vmem(2),
        scratch_shapes=[pltpu.VMEM((count // 128, 256), F32), pltpu.VMEM((count // 32, 256), F32)],
        compiler_params=params(),
        name="geometry",
    )(points, counts, centres)


def gather_plain(points, counts, centres, point_master, block_master, devices):
    rel, moments = geometry_call(points, counts, centres)
    moments = lax.psum(moments, AXES)
    tables = []
    for master, layout in ((point_master, point_layout()), (block_master, block_layout())):
        offset = 0
        parts = []
        for seg_len in segment_lengths(layout, devices):
            piece = master[offset : offset + seg_len // devices].astype(BF16)
            offset += seg_len // devices
            parts.append(lax.all_gather(piece, AXES, axis=0, tiled=True))
        tables.append(parts)
    (ps, w2, w3, w4), (bs, wqkv, wo, wf1, wf2) = tables

    def rows_of(v, rows, used):
        v = v[:used].astype(F32).reshape(-1, 128)
        return jnp.concatenate([v, jnp.zeros((rows - v.shape[0], 128), F32)], axis=0)

    small = (rel, moments, rows_of(ps, 24, 18 * 128), rows_of(bs, 32, 30 * 128))
    point = (w2.reshape(C1, C2), w3.reshape(2 * C2, C3))
    block = (w4.reshape(C3, D), wqkv.reshape(D, 3 * D), wo.reshape(D, D), wf1.reshape(D, FF), wf2.reshape(FF, D))
    return small + point, block


def scatter_plain(devices, prow, brow, gw2, gw3, gw4, gwqkv, gwo, gwf1, gwf2):
    pieces = []
    for layout, tables in (
        (point_layout(), (prow[:18], gw2, gw3, gw4)),
        (block_layout(), (brow[:30], gwqkv, gwo, gwf1, gwf2)),
    ):
        parts = []
        for values, seg_len in zip(tables, segment_lengths(layout, devices)):
            values = values.reshape(-1)
            values = jnp.concatenate([values, jnp.zeros((seg_len - values.shape[0],), F32)])
            parts.append(lax.psum_scatter(values, AXES, scatter_dimension=0, tiled=True))
        pieces.append(parts)
    return pieces


def adam_update(master, moment_one, moment_two, gradient, step_rates, decays):
    one_new = BETA_ONE * moment_one + (1.0 - BETA_ONE) * gradient
    two_new = BETA_TWO * moment_two + (1.0 - BETA_TWO) * gradient * gradient
    fix_one = 1.0 - BETA_ONE**STEP
    fix_two = 1.0 - BETA_TWO**STEP
    direction = one_new / fix_one / (jnp.sqrt(two_new / fix_two) + ADAM_EPS)
    master_new = master - step_rates * (direction + decays * master)
    return (master_new, one_new, two_new)


def flat_of(vector, rows):
    return jnp.pad(vector, (0, rows * 128 - vector.shape[0])).reshape(rows, 128)


def on_device(
    points, point_count, centre_slot, cloud_length, cotangent, point_master, block_master,
    point_first, block_first, point_second, block_second,
):
    dp, fsdp = lax.axis_size("dp"), lax.axis_size("fsdp")
    devices = dp * fsdp
    own_rank = lax.axis_index(AXES)
    known = dp == NZ * NY * NX and fsdp == NC
    count = points.shape[1]
    counts, centres = point_count.reshape(1, -1), centre_slot.reshape(1, -1)
    if known:
        outs = forward_call(
            True, dp, count, points, counts, centres, flat_of(point_master, PROWS), flat_of(block_master, BROWS)
        )
        given, block, outs = outs[:6], outs[6:11], outs[11:]
    else:
        given, block = gather_plain(points, counts, centres, point_master, block_master, devices)
        outs = forward_call(False, dp, count, *given)
    rel, moments, psmall, bsmall, w2, w3 = given
    ext, gp1, gext, ps, gm, sc, pooled, sv, stats, wd, w23, gp, pa, pg, pc = outs
    outs = backward_call(
        known, dp, pa, pg, pc, ps, cloud_length, cotangent, psmall, bsmall, sv, stats, moments,
        w2, w3, *block, w23, sc, gm, pooled, gext, wd, rel, centres, gp, ext, gp1,
    )
    tokens_out, point_grad = outs[:2]
    if known:
        point_gradient_vec = outs[2].reshape(-1)[: point_master.shape[0]]
        block_gradient = outs[3].reshape(-1)[: block_master.shape[0]]
        block_small = block_gradient[:BSMALL]
    else:
        point_parts, block_parts = scatter_plain(devices, *outs[2:])
        block_small = block_parts[0]
        point_gradient_vec = jnp.concatenate(point_parts)
        block_gradient = jnp.concatenate(block_parts)
    point_rates, point_decays = shard_rates(point_layout(), devices, own_rank)
    block_rates, block_decays = shard_rates(block_layout(), devices, own_rank)
    point_new, point_one, point_two = adam_update(
        point_master, point_first, point_second, point_gradient_vec, point_rates, point_decays
    )
    block_new, block_one, block_two = adam_update(
        block_master, block_first, block_second, block_gradient, block_rates, block_decays
    )
    return (
        tokens_out, point_grad, point_new, block_new, point_one, block_one, point_two, block_two,
        point_new.astype(BF16), block_new.astype(BF16), block_small,
    )


def solution(mesh):
    split = P(AXES)
    return jax.shard_map(
        on_device,
        mesh=mesh,
        in_specs=(P(None, AXES), split, split, split, P(AXES, None)) + (split,) * 6,
        out_specs=(P(AXES, None), P(None, AXES)) + (split,) * 9,
        check_vma=False,
    )
```

```python
import functools
import math

import jax
import jax.numpy as jnp
from jax import lax
from jax.experimental import pallas as pl
from jax.experimental.pallas import tpu as pltpu
from jax.sharding import PartitionSpec as P

C1 = 128
C2 = 256
C3 = 512
D = 384
HEADS = 6
HEAD_DIM = 64
FF = 1536
GROUP = 32
PATCHES = 64
STEP = 10

EPS_NORM = 1e-05
BETA_ONE = 0.9
BETA_TWO = 0.95
ADAM_EPS = 1e-08
DECAY_RATE = 0.05
NEG_FILL = -1e30

F32 = jnp.float32
BF16 = jnp.bfloat16
AXES = ("dp", "fsdp")
MESH = pl.DeviceIdType.MESH
VMEM_LIMIT = 60 * 2**20
TILE = 2048
TOK = TILE // GROUP
STEP_TILES = 2
AHEAD = 4
WIDE = TILE * STEP_TILES
PAIR = 256

NZ, NY, NX, NC = 4, 2, 2, 2
PROWS, BROWS = 128, 440
PSMALL, BSMALL = 72, 120


def point_layout():
    return [
        [
            ("w1", (3, C1), 3.0 ** (-0.5)),
            ("bn1_gain", (C1,), 0.0),
            ("bn1_shift", (C1,), -1.0),
            ("b2", (C2,), -1.0),
            ("bn3_gain", (C3,), 0.0),
            ("bn3_shift", (C3,), -1.0),
            ("b4", (D,), -1.0),
        ],
        [("w2", (C1, C2), C1 ** (-0.5))],
        [("w3", (2 * C2, C3), (2 * C2) ** (-0.5))],
        [("w4", (C3, D), C3 ** (-0.5))],
    ]


def block_layout():
    return [
        [
            ("ln1_gain", (D,), 0.0),
            ("ln1_shift", (D,), -1.0),
            ("bo", (D,), -1.0),
            ("ln2_gain", (D,), 0.0),
            ("ln2_shift", (D,), -1.0),
            ("bf1", (FF,), -1.0),
            ("bf2", (D,), -1.0),
        ],
        [("wqkv", (D, 3 * D), D ** (-0.5))],
        [("wo", (D, D), 3.0 * D ** (-0.5))],
        [("wf1", (D, FF), D ** (-0.5))],
        [("wf2", (FF, D), FF ** (-0.5))],
    ]


def rate_for(spread):
    return 2.0 * spread if spread > 0.0 else 0.5 if spread == 0.0 else 0.6


def decay_for(spread):
    return DECAY_RATE if spread > 0.0 else 0.0


def segment_lengths(layout, devices):
    lengths_out = []
    for segment in layout:
        used_len = sum((math.prod(entry[1]) for entry in segment))
        lengths_out.append(-(-used_len // devices) * devices)
    return lengths_out


def shard_rates(layout, devices, own_rank):
    lengths = segment_lengths(layout, devices)
    position = jnp.arange(sum(lengths) // devices, dtype=jnp.int32)
    rates = jnp.zeros(position.shape, F32)
    decays = jnp.zeros(position.shape, F32)
    start = 0
    for segment, seg_len in zip(layout, lengths):
        piece_len = seg_len // devices
        here = (position >= start) & (position < start + piece_len)
        inner = position + (own_rank * piece_len - start)
        offset = 0
        for entry_label, entry_dims, spread in segment:
            extent = math.prod(entry_dims)
            inside = here & (inner >= offset) & (inner < offset + extent)
            rates = jnp.where(inside, rate_for(spread), rates)
            decays = jnp.where(inside, decay_for(spread), decays)
            offset += extent
        start += piece_len
    return rates, decays


def mm(a, b):
    return jnp.dot(a, b, preferred_element_type=F32)


def mm_tn(a, b):
    return lax.dot_general(a, b, (((0,), (0,)), ((), ())), preferred_element_type=F32)


def mm_nt(a, b):
    return lax.dot_general(a, b, (((1,), (1,)), ((), ())), preferred_element_type=F32)


def low(v):
    return v.astype(BF16)


def split_three(v):
    hi = low(v)
    rest = v - hi.astype(F32)
    mid = low(rest)
    return hi, mid, low(rest - mid.astype(F32))


def mm_exact(a, b):
    hi, mid, lo = split_three(a)
    return mm(hi, b) + (mm(mid, b) + mm(lo, b))


LAM = (math.sqrt(2.0 / math.pi) * 0.044715) ** (-1.0 / 3.0)
ARG = math.sqrt(2.0 / math.pi) * LAM


def gelu_twice(y):
    square = y * y
    near = square + ARG
    t = jnp.tanh(y * near)
    up = 1.0 + t
    g = y * up
    return g, up + g * (1.0 - t) * (near + (square + square))


def gelu_pair(v):
    g, d = gelu_twice(low(v * (1.0 / LAM)))
    return low(g.astype(F32) * (0.5 * LAM)), d * 0.5


def patch_ones():
    i = lax.broadcasted_iota(jnp.int32, (256, 256), 0) // GROUP
    j = lax.broadcasted_iota(jnp.int32, (256, 256), 1) // GROUP
    return (i == j).astype(F32).astype(BF16)


def token_ones():
    t = lax.broadcasted_iota(jnp.int32, (TOK, TILE), 0)
    p = lax.broadcasted_iota(jnp.int32, (TOK, TILE), 1) // GROUP
    return (t == p).astype(F32).astype(BF16)


def patch_sum(rows, ones):
    return mm_exact(rows, ones)


def rank_of(peer_dp, peer_core):
    return peer_dp * NC + peer_core


def me():
    return rank_of(lax.axis_index("dp"), lax.axis_index("fsdp"))


def all_peers(dp):
    n = dp * NC
    peers = []
    for k in range(1, n):
        p = lax.rem(me() + k, n)
        peers.append((p // NC, lax.rem(p, NC)))
    return peers


def greet(peers):
    barrier = pltpu.get_barrier_semaphore()
    for peer in peers:
        pl.semaphore_signal(barrier, inc=1, device_id=peer, device_id_type=MESH)


def greeted(peers):
    pl.semaphore_wait(pltpu.get_barrier_semaphore(), len(peers))


def sum_copies(dp, src, dst_of, send, recv):
    return [
        pltpu.make_async_remote_copy(
            src_ref=src, dst_ref=dst_of(k), send_sem=send.at[k], recv_sem=recv.at[k],
            device_id=peer, device_id_type=MESH,
        )
        for k, peer in enumerate(all_peers(dp))
    ]


def send_to_all(dp, src, dst_of, send, recv):
    copies = sum_copies(dp, src, dst_of, send, recv)
    for copy in copies:
        copy.start()
    return copies


def sum_start(dp, acc, slots, send, recv):
    return send_to_all(dp, acc, lambda k: slots.at[k], send, recv)


def sum_finish(acc, slots, copies):
    for copy in copies:
        copy.wait()
    return acc[...] + jnp.sum(slots[...], axis=0)


def sum_scratch(dp):
    n = dp * NC - 1
    return [
        pltpu.VMEM((8, 128), F32), pltpu.VMEM((n, 8, 128), F32),
        pltpu.SemaphoreType.DMA((n,)), pltpu.SemaphoreType.DMA((n,)),
    ]


def as_rows(*vectors):
    return jnp.concatenate(
        [v[:, 128 * k : 128 * k + 128] for v in vectors for k in range(v.shape[1] // 128)], axis=0
    )


def as_vector(rows, first, count):
    return jnp.concatenate([rows[k : k + 1, :] for k in range(first, first + count)], axis=1)


def vmem(count):
    return [pl.BlockSpec(memory_space=pltpu.VMEM)] * count


def shaped(*items):
    return [jax.ShapeDtypeStruct(s, t) for s, t in items]


def params(**more):
    return pltpu.CompilerParams(vmem_limit_bytes=VMEM_LIMIT, **more)


def where_am_i():
    at = lax.axis_index("dp")
    return at // (NY * NX), lax.rem(at // NX, NY), lax.rem(at, NX), lax.axis_index("fsdp")


def chip(z, y, x):
    return (z * NY + y) * NX + x


def spread_tokens(values):
    tokens = values.shape[1]
    piece = lax.broadcasted_iota(jnp.int32, (tokens // 8, tokens), 0)
    token = lax.broadcasted_iota(jnp.int32, (tokens // 8, tokens), 1)
    apart = jnp.where(piece == token // 8, values.astype(F32), 0.0)
    token = lax.rem(lax.broadcasted_iota(jnp.int32, (tokens, 256), 0), 8)
    patch = lax.broadcasted_iota(jnp.int32, (tokens, 256), 1) // GROUP
    return mm(low(apart), low((token == patch).astype(F32)))


def geometry(points_ref, counts_ref, centres_ref, rel_ref, counts_s, picked_s):
    pieces = points_ref.shape[1] // 256
    lane = lax.rem(lax.broadcasted_iota(jnp.int32, (1, 256), 1), GROUP).astype(F32)
    counts_s[0:pieces, :] = spread_tokens(counts_ref[...])
    counts_s[pieces:, :] = spread_tokens(centres_ref[...])
    for i in range(pieces):
        at = slice(256 * i, 256 * i + 256)
        pick = (lane == counts_s[pieces + i : pieces + i + 1, :]).astype(F32)
        rows = points_ref[:, at] * pick
        picked_s[8 * i : 8 * i + 8, :] = jnp.concatenate([rows, jnp.zeros((5, 256), F32)], axis=0)
    picked_s[...] = patch_sum(picked_s[...], patch_ones())
    for i in range(pieces):
        at = slice(256 * i, 256 * i + 256)
        valid = (lane < counts_s[i : i + 1, :]).astype(F32)
        relative = (points_ref[:, at] - picked_s[8 * i : 8 * i + 3, :]) * valid
        rel_ref[:, at] = low(jnp.concatenate([relative, valid, relative, valid], axis=0))
    rel = rel_ref[...]
    return mm_nt(rel, rel)


def prepare_one(moments, small):
    n = moments[3:4, 3:4]
    w = [small[k : k + 1, :] for k in range(3)]
    gain, shift = small[3:4, :], small[4:5, :]
    mean = sum(w[k] * moments[k : k + 1, 3:4] for k in range(3)) / n
    square = jnp.zeros_like(mean)
    for j in range(3):
        for k in range(3):
            square = square + w[j] * w[k] * moments[j : j + 1, k : k + 1]
    inverse = lax.rsqrt(square / n - mean * mean + EPS_NORM)
    scale = inverse * gain
    scaled = [wk * scale for wk in w]
    parts = [v * (1.0 / LAM) for v in scaled + [shift - mean * scale]]
    high = [low(v) for v in parts]
    rest = [low(v - h.astype(F32)) for v, h in zip(parts, high)]
    forward = jnp.concatenate(high + rest, axis=0)
    high = [low(v) for v in scaled]
    rest = [low(v - h.astype(F32)) for v, h in zip(scaled, high)]
    zero = jnp.zeros((1, C1), BF16)
    backward = jnp.concatenate(high + [zero] + rest + [zero], axis=0)
    stats = jnp.concatenate(
        [mean, inverse, jnp.broadcast_to(n, (1, C1)), scale, jnp.zeros((4, C1), F32)], axis=0
    )
    return forward, backward, stats


def flat_rows(pieces, length, rows):
    lane = lax.broadcasted_iota(jnp.int32, (1, 128), 1)
    out = [jnp.zeros((1, 128), F32) for _ in range(rows)]
    for r in range(pieces.shape[0]):
        row = jnp.where(lane < length, pieces[r : r + 1, :], 0.0)
        at = length * r
        row = pltpu.roll(row, at % 128, 1) if at % 128 else row
        first = at // 128
        out[first] = out[first] + jnp.where(lane >= at % 128, row, 0.0)
        if at % 128 + length > 128:
            out[first + 1] = out[first + 1] + jnp.where(lane < at % 128, row, 0.0)
    return jnp.concatenate(out, axis=0)


def piece_of(rows, at, length):
    lane = lax.broadcasted_iota(jnp.int32, (1, 128), 1)
    first, shift = at // 128, at % 128
    row = rows[first : first + 1, :]
    if shift:
        row = pltpu.roll(row, 128 - shift, 1)
        if shift + length > 128:
            other = pltpu.roll(rows[first + 1 : first + 2, :], 128 - shift, 1)
            row = jnp.where(lane < 128 - shift, row, other)
    return jnp.where(lane < length, row, 0.0)


def segments_apart(flat, small):
    lane = lax.broadcasted_iota(jnp.int32, (1, 128), 1)
    turned = pltpu.roll(flat, 128 - small, 1)
    return jnp.where(lane < 128 - small, pltpu.roll(turned, 1, 0), turned)


def segments_joined(rows, first, small):
    lane = lax.broadcasted_iota(jnp.int32, (1, 128), 1)
    turned = pltpu.roll(rows, small, 1)
    row = lax.broadcasted_iota(jnp.int32, (rows.shape[0], 1), 0)
    joined = jnp.where(lane < small, turned, pltpu.roll(turned, rows.shape[0] - 1, 0))
    return jnp.where((lane < small) & (row == 0), first, joined)


def first_tile(rel, wn, ext_ref, gp_ref, start):
    valid = rel[3:4, :].astype(F32)
    for j in range(TILE // 256):
        at = slice(256 * j, 256 * j + 256)
        to = slice(start + 256 * j, start + 256 * j + 256)
        g, d = gelu_twice(mm_tn(wn, rel[:, at]))
        ext_ref[0:C1, to] = low(g * (valid[:, at] * (0.5 * LAM)))
        gp_ref[:, to] = low(d * (valid[:, at] * 0.5))
    ext_ref[C1:, start : start + TILE] = jnp.concatenate([rel[3:4], jnp.zeros((15, TILE), BF16)], axis=0)


def first_tokens(gext, ps_ref, w2e, w3_ref, pooled_o, gm_o, fw_o):
    lower = w3_ref[C2:, :]
    count = ps_ref[:, C1 : C1 + 1]
    fs = mm_exact(ps_ref[:, 0 : C1 + 16], w2e)
    pooled = low(fs / count)
    pooled_o[...] = pooled
    g = mm(pooled, w3_ref[0:C2, :])
    gm_o[...] = g
    fw = mm_exact(fs, lower)
    fw_o[...] = fw
    gram = sum(mm_tn(w2e, part) for part in split_three(mm_exact(gext, w2e)))
    one = jnp.sum(fw + count * g, axis=0, keepdims=True)
    two = jnp.sum(mm_exact(gram, lower) * lower.astype(F32), axis=0, keepdims=True)
    two = two + jnp.sum(g * (2.0 * fw + count * g), axis=0, keepdims=True)
    return as_rows(one, two)


def third_vectors(totals, n, psmall_ref):
    mean = as_vector(totals, 0, 4) / n
    inverse = lax.rsqrt(as_vector(totals, 4, 4) / n - mean * mean + EPS_NORM)
    gain, shift = as_vector(psmall_ref, 7, 4), as_vector(psmall_ref, 11, 4)
    return jnp.concatenate([inverse * gain, shift, mean, inverse, jnp.zeros((4, C3), F32)], axis=0)


def second_tile(act, mask, w23, gm, count, sv_ref, gp_o, start, pa_o, pg_o, pc_o, first):
    scale, shift = low(sv_ref[0:1, :] * (1.0 / LAM)), low(sv_ref[1:2, :] * (1.0 / LAM))
    turned = act.T
    c = mm(jnp.concatenate([turned, turned], axis=1), w23).reshape(TOK, GROUP, C3) + gm[:, None, :]
    c = low(c)
    g, gp = gelu_twice(c * scale[None] + shift[None])
    gc = (gp * c).reshape(TILE, C3)
    gp = gp.reshape(TILE, C3)
    gp_o[start : start + TILE, :] = gp
    g = g.reshape(TILE, C3)
    means, gps, gcs = [], [], []
    for q in range(TILE // 256):
        at = slice(256 * q, 256 * q + 256)
        m = mask[8 * q : 8 * q + 8, at]
        means.append(mm(m, g[at]) * (0.5 * LAM) / count[8 * q : 8 * q + 8, :])
        gps.append(mm(m, gp[at]) * 0.5)
        gcs.append(mm(m, gc[at]) * 0.5)
    for ref, parts in ((pa_o, means), (pg_o, gps), (pc_o, gcs)):
        ref[first, :] = low(jnp.concatenate(parts, axis=0))


class Gather:
    def __init__(self, blocks, send, recv, base):
        self.blocks, self.sems, self.base = blocks, (send, recv), base
        z, y, x, core = where_am_i()
        half = blocks.shape[-1] // 2
        one, two = pl.ds(0, half), pl.ds(half, half)
        every = slice(None)
        near = [(chip(lax.rem(z + k, NZ), y, x), core) for k in range(1, NZ)]
        over_y, over_x, twin = (chip(z, 1 - y, x), core), (chip(z, y, 1 - x), core), (chip(z, y, x), 1 - core)
        self.stages = [
            [((z, y, x, core), peer) for peer in near],
            [((every, y, x, core, every, one), over_y), ((every, y, x, core, every, two), over_x)],
            [((every, every, x, core, every, one), over_x), ((every, y, every, core, every, two), over_y)],
            [],
        ]
        self.inner = [
            [],
            [((every, y, x, core), twin)],
            [((every, 1 - y, x, core, every, one), twin), ((every, y, 1 - x, core, every, two), twin)],
            [((every, every, 1 - x, core, every, one), twin), ((every, 1 - y, every, core, every, two), twin)],
        ]

    def copies(self, stage, inner):
        table = self.inner if inner else self.stages
        k = self.base + (7 if inner else 0) + sum(len(s) for s in table[:stage])
        out = []
        for i, (index, peer) in enumerate(table[stage]):
            view = self.blocks.at[index]
            out.append(
                pltpu.make_async_remote_copy(
                    src_ref=view, dst_ref=view, send_sem=self.sems[0].at[k + i], recv_sem=self.sems[1].at[k + i],
                    device_id=peer, device_id_type=MESH,
                )
            )
        return out

    def advance(self, stage):
        if stage > 0:
            for copy in self.copies(stage - 1, False):
                copy.wait()
        if stage < 4:
            for copy in self.copies(stage, False) + self.copies(stage, True):
                copy.start()
        else:
            for inner_stage in range(4):
                for copy in self.copies(inner_stage, True):
                    copy.wait()


GATHER_SEMS = 12
ATT_WIDTH, FFN_WIDTH = 4 * D, 6 * D


def attention_rows(bal, pal, stage):
    start = 1
    for at, cols in ((0, 3 * D), (3 * D, D)):
        for j in range(cols // 128):
            stage[0:12, at + 128 * j : at + 128 * j + 128] = bal[pl.ds(start + j, 12, stride=cols // 128), :]
        start += 12 * cols // 128
    for k in range(4):
        for j in range(D // 128):
            to = D * k + 128 * j
            stage[12:16, to : to + 128] = pal[pl.ds(73 + 12 * k + j, 4, stride=3), :]


def attention_flat(stage, bal, pal):
    start = 1
    for at, cols in ((0, 3 * D), (3 * D, D)):
        for j in range(cols // 128):
            bal[pl.ds(start + j, 12, stride=cols // 128), :] = stage[0:12, at + 128 * j : at + 128 * j + 128]
        start += 12 * cols // 128
    for k in range(4):
        for j in range(D // 128):
            at = D * k + 128 * j
            pal[pl.ds(73 + 12 * k + j, 4, stride=3), :] = stage[12:16, at : at + 128]


FFN_PIECES = [(0, 16, 0, FF), (16, 16, 0, FF + D)] + [(32 + 4 * k, 4, 12, D * k) for k in range(4)]
FFN_START = 1 + 12 * 4 * D // 128


def ffn_rows(bal, stage):
    for j in range(FF // 128):
        stage[0:12, 128 * j : 128 * j + 128] = bal[pl.ds(FFN_START + j, 12, stride=FF // 128), :]
    start = FFN_START + 12 * FF // 128
    for row, rows, under, at in FFN_PIECES:
        for j in range(D // 128):
            to = at + 128 * j
            stage[under : under + rows, to : to + 128] = bal[pl.ds(start + 3 * row + j, rows, stride=3), :]


def ffn_flat(stage, bal):
    for j in range(FF // 128):
        bal[pl.ds(FFN_START + j, 12, stride=FF // 128), :] = stage[0:12, 128 * j : 128 * j + 128]
    start = FFN_START + 12 * FF // 128
    for row, rows, under, at in FFN_PIECES:
        for j in range(D // 128):
            bal[pl.ds(start + 3 * row + j, rows, stride=3), :] = stage[
                under : under + rows, at + 128 * j : at + 128 * j + 128
            ]


def place(d):
    return d // 8, d // 4 % 2, d // 2 % 2, d % 2


def forward_kernel(known, dp, *refs):
    refs = list(refs)
    take = lambda count: [refs.pop(0) for _ in range(count)]
    points_ref, counts_ref, centres_ref, pflat, bflat = take(5) if known else [None] * 5
    rel_o, moment_o, psmall_o, bsmall_o, w2_o, w3_o = take(6)
    w4_o, wqkv_o, wo_o, wf1_o, wf2_o = take(5) if known else [None] * 5
    ext_o, gp1_o, g_o, ps_o, gm_o, fw_o, pooled_o, sv_o, stats_o, wd_o, w23_o, gp_o, pa_o, pg_o, pc_o = take(15)
    ext_s, gm_s, fw_s, e_s, wn_s, w2_s, w23_s, acc3, sums3, ssend3, srecv3 = take(11)
    step = pl.program_id(0)
    tiles = pl.num_programs(0) // 2
    peers = all_peers(dp)
    if known:
        (
            tiny, att, ffn, three, stage, wide, flat2, pal, bal, counts_s, picked_s,
            tsend, trecv, gsend, grecv,
        ) = take(15)
        z, y, x, core = where_am_i()
        gather_w3 = Gather(three, gsend, grecv, 0)
        gather_att = Gather(att, gsend, grecv, GATHER_SEMS)
        gather_ffn = Gather(ffn, gsend, grecv, 2 * GATHER_SEMS)

    @pl.when(step == 0)
    def _():
        greet(peers)
        g_o[...] = jnp.zeros_like(g_o)
        e_s[...] = token_ones()
        if known:
            for vector, rows, small in ((pflat, pal, PSMALL), (bflat, bal, BSMALL)):
                rows[...] = jnp.zeros_like(rows)
                length = vector.shape[0]
                for k in range(-(-length // 128)):
                    width = min(128, length - 128 * k)
                    rows[k, 0:width] = vector[128 * k : 128 * k + width]
                first = rows[0:1, :]
                rows[...] = segments_apart(rows[...], small)
                rows[0:1, :] = first
            moments = geometry(points_ref, counts_ref, centres_ref, rel_o, counts_s, picked_s)[0:4, :]
            moments = jnp.concatenate([moments, jnp.zeros((4, 120), F32)], axis=1)
            hi, mid, lo = [part.astype(F32) for part in split_three(moments)]
            packed = hi + pltpu.roll(mid, 8, 1) + pltpu.roll(lo, 16, 1)
            firsts = [pal[0:1, :], bal[0:1, :]]
            rows = [pal[1:9, :], *firsts, packed, jnp.zeros((2, 128), F32)]
            own = tiny.at[me()]
            own[...] = low(jnp.concatenate(rows, axis=0))
            greeted(peers)
            copies = send_to_all(dp, own, lambda k: own, tsend, trecv)
            for j in range(C3 // 128):
                three[z, y, x, core, :, 128 * j : 128 * j + 128] = low(pal[pl.ds(9 + j, 16, stride=C3 // 128), :])
            gather_w3.advance(0)
            attention_rows(bal, pal, stage)
            att[z, y, x, core] = low(stage[:, 0:ATT_WIDTH])
            gather_att.advance(0)
            ffn_rows(bal, stage)
            ffn[z, y, x, core] = low(stage[...])
            gather_w3.advance(1)
            for copy in copies:
                copy.wait()
            gather_att.advance(1)
            gather_ffn.advance(0)
            psmall, bsmall = [], []
            packed = jnp.zeros((4, 128), F32)
            for d in range(dp * NC):
                rows = tiny[d].astype(F32)
                flat2[8 * d : 8 * d + 8, :] = rows[0:8, :]
                psmall.append(rows[8:9, :])
                bsmall.append(rows[9:10, :])
                packed = packed + rows[10:14, :]
            total = packed + pltpu.roll(packed, 120, 1) + pltpu.roll(packed, 112, 1)
            moment_o[...] = jnp.concatenate([total, jnp.zeros((4, 128), F32)], axis=0)
            psmall_o[0:18, :] = flat_rows(jnp.concatenate(psmall, axis=0), PSMALL, 18)
            bsmall_o[0:30, :] = flat_rows(jnp.concatenate(bsmall, axis=0), BSMALL, 30)
            for j in range(2):
                w2_o[:, 128 * j : 128 * j + 128] = low(flat2[pl.ds(j, C1, stride=2), :])
        else:
            greeted(peers)
        small = psmall_o[...]
        forward, backward, stats = prepare_one(moment_o[:, 0:8], small)
        wn_s[...] = forward
        wd_o[...] = backward
        stats_o[...] = stats
        w2_s[0:C1, :] = w2_o[...]
        b2 = as_vector(small, 5, 2)
        w2_s[C1:, :] = low(jnp.concatenate([b2, jnp.zeros((15, C2), F32)], axis=0))

    if known:
        for at_step, gather, number in (
            (1, gather_w3, 2), (2, gather_w3, 3), (2, gather_att, 2), (3, gather_ffn, 1), (4, gather_w3, 4),
            (5, gather_att, 3), (5, gather_ffn, 2), (6, gather_att, 4), (7, gather_ffn, 3),
        ):
            pl.when(step == at_step)(functools.partial(gather.advance, number))

    def tile_at(half):
        tile = lax.rem(step, tiles) * STEP_TILES + half
        return pl.ds(pl.multiple_of(tile * TILE, TILE), TILE), pl.ds(pl.multiple_of(tile * TOK, TOK), TOK)

    @pl.when(step < tiles)
    def _():
        for half in range(STEP_TILES):
            at, ts = tile_at(half)
            first_tile(rel_o[:, at], wn_s[...], ext_o, gp1_o, half * TILE)
            ext = ext_o[:, half * TILE : half * TILE + TILE]
            ext_s[:, at] = ext[0:C1]
            both = mm_nt(jnp.concatenate([ext, e_s[...]], axis=0), ext)
            g_o[:, 0 : C1 + 16] += both[0 : C1 + 16]
            ps_o[ts, 0 : C1 + 16] = both[C1 + 16 :]

    @pl.when(step == tiles)
    def _():
        if known:
            for d in range(dp * NC):
                w3_o[16 * d : 16 * d + 16, :] = three[place(d)]
        acc3[...] = first_tokens(g_o[:, 0 : C1 + 16], ps_o, w2_s[...], w3_o, pooled_o, gm_s, fw_s)
        copies = sum_start(dp, acc3, sums3, ssend3, srecv3)
        w23 = mm(w2_s[...], w3_o[C2:, :])
        w23_o[...] = w23
        high = low(w23[0:C1])
        w23_s[0:C1, :] = high
        w23_s[C1:, :] = low(w23[0:C1] - high.astype(F32))
        sv_o[...] = third_vectors(sum_finish(acc3, sums3, copies), stats_o[2:3, 0:1], psmall_o)
        mean = sv_o[2:3, :]
        gm = gm_s[...] - mean
        fw_o[...] = low(fw_s[...] + ps_o[:, C1 : C1 + 1] * gm)
        gm = gm + w23[C1 : C1 + 1, :]
        gm_s[...] = gm
        gm_o[...] = low(gm)

    @pl.when(step >= tiles)
    def _():
        for half in range(STEP_TILES):
            at, ts = tile_at(half)
            second_tile(
                ext_s[:, at], e_s[...] * rel_o[3:4, at], w23_s[...], gm_s[ts, :], ps_o[ts, C1 : C1 + 1], sv_o,
                gp_o, half * TILE, pa_o, pg_o, pc_o, ts,
            )

    if known:

        @pl.when(step == tiles + 2)
        def _():
            for d in range(dp * NC):
                under = att[place(d)].astype(F32)
                wide[12 * d : 12 * d + 12, :] = under[0:12, :]
                tail = [under[12:16, D * k : D * k + D] for k in range(4)]
                w4_o[16 * d : 16 * d + 16, :] = low(jnp.concatenate(tail, axis=0))
            wqkv_o[...] = low(wide[:, 0 : 3 * D])
            wo_o[...] = low(wide[:, 3 * D : 4 * D])

        @pl.when(step == 2 * tiles - 1)
        def _():
            gather_ffn.advance(4)
            for d in range(dp * NC):
                block = ffn.at[place(d)]
                under = block[:, 0:FF].astype(F32)
                wide[12 * d : 12 * d + 12, :] = under[0:12, :]
                wf2_o[48 * d : 48 * d + 16, :] = block[:, FF : FF + D]
                wf2_o[48 * d + 16 : 48 * d + 32, :] = block[:, FF + D : FF + 2 * D]
                tail = [under[12:16, D * k : D * k + D] for k in range(4)]
                wf2_o[48 * d + 32 : 48 * d + 48, :] = low(jnp.concatenate(tail, axis=0))
            wf1_o[...] = low(wide[...])


def forward_call(known, dp, count, *args):
    tokens, tiles = count // GROUP, count // WIDE
    single = dict(pipeline_mode=pl.Buffered(1))
    full = lambda *s: pl.BlockSpec(s, lambda i: (0, 0), **single)
    early = lambda r: pl.BlockSpec((r, WIDE), lambda i: (0, jnp.minimum(i, tiles - 1)))
    given = [
        ((8, count), BF16), ((8, 128), F32), ((24, 128), F32), ((32, 128), F32), ((C1, C2), BF16), ((2 * C2, C3), BF16),
    ]
    gathered = [((C3, D), BF16), ((D, 3 * D), BF16), ((D, D), BF16), ((D, FF), BF16), ((FF, D), BF16)]
    outs = [(full(*s), s, t) for s, t in given + gathered] if known else []
    outs += [(early(C1 + 16), (C1 + 16, count), BF16), (early(C1), (C1, count), BF16)]
    outs += [
        (full(*s), s, t)
        for s, t in (
            ((C1 + 16, 256), F32), ((tokens, 256), F32), ((tokens, C3), BF16), ((tokens, C3), BF16),
            ((tokens, C2), BF16), ((8, C3), F32), ((8, C1), F32), ((8, C1), BF16), ((C1 + 16, C3), F32),
        )
    ]
    outs += [(pl.BlockSpec((WIDE, C3), lambda i: (jnp.maximum(i - tiles, 0), 0)), (count, C3), BF16)]
    outs += [(full(tokens, C3), (tokens, C3), BF16)] * 3
    scratch = [
        pltpu.VMEM((C1, count), BF16), pltpu.VMEM((tokens, C3), F32), pltpu.VMEM((tokens, C3), F32),
        pltpu.VMEM((TOK, TILE), BF16), pltpu.VMEM((8, C1), BF16),
        pltpu.VMEM((C1 + 16, C2), BF16), pltpu.VMEM((2 * C1, C3), BF16),
    ] + sum_scratch(dp)
    if known:
        n = dp * NC
        scratch += [
            pltpu.VMEM((n, 16, 128), BF16),
            pltpu.VMEM((NZ, NY, NX, NC, 16, ATT_WIDTH), BF16),
            pltpu.VMEM((NZ, NY, NX, NC, 16, FFN_WIDTH), BF16),
            pltpu.VMEM((NZ, NY, NX, NC, 16, C3), BF16),
            pltpu.VMEM((16, FFN_WIDTH), F32),
            pltpu.VMEM((D, FF), F32),
            pltpu.VMEM((8 * n, 128), F32),
            pltpu.VMEM((PROWS, 128), F32), pltpu.VMEM((BROWS, 128), F32),
            pltpu.VMEM((count // 128, 256), F32), pltpu.VMEM((count // 32, 256), F32),
            pltpu.SemaphoreType.DMA((n - 1,)), pltpu.SemaphoreType.DMA((n - 1,)),
            pltpu.SemaphoreType.DMA((3 * GATHER_SEMS,)), pltpu.SemaphoreType.DMA((3 * GATHER_SEMS,)),
        ]
    return pl.pallas_call(
        functools.partial(forward_kernel, known, dp),
        grid=(2 * tiles,),
        in_specs=[full(*a.shape) if a.ndim == 2 else pl.BlockSpec(memory_space=pltpu.VMEM) for a in args],
        out_specs=[o[0] for o in outs],
        out_shape=shaped(*[o[1:] for o in outs]),
        scratch_shapes=scratch,
        compiler_params=params(collective_id=0, has_side_effects=True),
        name="forward",
    )(*args)


def wide_row(ref, first, rows):
    return jnp.concatenate([ref[k : k + 1, :] for k in range(first, first + rows)], axis=1)


def layer_norm(v, gain, shift):
    centred = v - jnp.mean(v, -1, keepdims=True)
    inverse = lax.rsqrt(jnp.mean(centred * centred, -1, keepdims=True) + EPS_NORM)
    unit = centred * inverse
    return unit, inverse, low(unit * gain + shift)


def norm_back(d_unit, unit, inverse):
    return inverse * (
        d_unit - jnp.mean(d_unit, -1, keepdims=True) - unit * jnp.mean(d_unit * unit, -1, keepdims=True)
    )


def col_sum(v):
    return jnp.sum(v, axis=0, keepdims=True)


def block_step(
    pa_ref, pg_ref, pc_ref, cnt_ref, len_ref, cot_ref, psmall_ref, bsmall_ref, sv_ref,
    w4_ref, wqkv_ref, wo_ref, wf1_ref, wf2_ref,
    out_o, small_o, tok_o, tg_o, back_o, qkv_s, mixed_s, soft_s, dmix_s, dqkv_s, dhid_s,
    ffn_grads, between, token_grads, attention_grads,
):
    count = cnt_ref[:, C1 : C1 + 1]
    scale = HEAD_DIM ** (-0.5)
    b4 = wide_row(psmall_ref, 15, 3)
    ln1_gain, ln1_shift, bo = wide_row(bsmall_ref, 0, 3), wide_row(bsmall_ref, 3, 3), wide_row(bsmall_ref, 6, 3)
    ln2_gain, ln2_shift = wide_row(bsmall_ref, 9, 3), wide_row(bsmall_ref, 12, 3)
    bf1, bf2 = wide_row(bsmall_ref, 15, 12), wide_row(bsmall_ref, 27, 3)

    act = pa_ref[...]
    x_zero = mm(act, w4_ref[...]) + b4
    unit_a, inv_a, normed_a = layer_norm(x_zero, ln1_gain, ln1_shift)
    qkv_s[...] = low(mm(normed_a, wqkv_ref[...]))

    row_cloud = lax.broadcasted_iota(jnp.int32, (PAIR, PAIR), 0) // PATCHES
    col = lax.broadcasted_iota(jnp.int32, (PAIR, PAIR), 1)
    left = lax.broadcasted_iota(jnp.int32, (1, 128), 1) < HEAD_DIM
    zero = jnp.zeros((1, 1), BF16)

    def halves(v):
        return jnp.where(left, v, zero), jnp.where(left, zero, v)

    tiles = pa_ref.shape[0] // PAIR
    for s in range(tiles):
        seen = jnp.zeros((1, PAIR), jnp.int32)
        for c in range(PAIR // PATCHES):
            seen = jnp.where(col[0:1, :] // PATCHES == c, len_ref[s * (PAIR // PATCHES) + c], seen)
        visible = (row_cloud == col // PATCHES) & (lax.rem(col, PATCHES) < seen)
        rows = slice(PAIR * s, PAIR * s + PAIR)
        for p in range(HEADS // 2):
            at = 128 * p
            q = qkv_s[rows, at : at + 128]
            k = qkv_s[rows, D + at : D + at + 128]
            v = qkv_s[rows, 2 * D + at : 2 * D + at + 128]
            mixed = []
            for a, q_half in enumerate(halves(q)):
                score = jnp.where(visible, mm_nt(q_half, k) * scale, NEG_FILL)
                raised = jnp.exp(score - jnp.max(score, -1, keepdims=True))
                soft = raised / jnp.sum(raised, -1, keepdims=True)
                soft_s[(s * (HEADS // 2) + p) * 2 + a] = soft
                mixed.append(mm(low(soft), v))
            mixed_s[rows, at : at + 128] = low(jnp.where(left, mixed[0], mixed[1]))

    mixed_low = mixed_s[...]
    x_one = x_zero + mm(mixed_low, wo_ref[...]) + bo
    unit_b, inv_b, normed_b = layer_norm(x_one, ln2_gain, ln2_shift)
    hidden, d_hidden = gelu_pair(mm(normed_b, wf1_ref[...]) + bf1)
    dhid_s[...] = d_hidden
    out_o[...] = x_one + mm(hidden, wf2_ref[...]) + bf2

    cot = cot_ref[...]
    grad = low(cot)
    d_pre = mm_nt(grad, wf2_ref[...]) * dhid_s[...].astype(F32)
    d_pre_low = low(d_pre)
    small_o[7:8, :] = col_sum(d_pre)
    ffn_grads(mm_tn(normed_b, d_pre_low), mm_tn(hidden, grad))
    d_normed_b = mm_nt(d_pre_low, wf1_ref[...])
    d_x_one = cot + norm_back(d_normed_b * ln2_gain, unit_b, inv_b)
    d_x_low = low(d_x_one)
    d_x_one_low = d_x_low
    dmix_s[...] = low(mm_nt(d_x_low, wo_ref[...]))

    for s in range(tiles):
        rows = slice(PAIR * s, PAIR * s + PAIR)
        for p in range(HEADS // 2):
            at = 128 * p
            q = qkv_s[rows, at : at + 128]
            k = qkv_s[rows, D + at : D + at + 128]
            v = qkv_s[rows, 2 * D + at : 2 * D + at + 128]
            dm = dmix_s[rows, at : at + 128]
            d_q, d_k, d_v = [], [], []
            for a, dm_half in enumerate(halves(dm)):
                soft = soft_s[(s * (HEADS // 2) + p) * 2 + a]
                d_soft = mm_nt(dm_half, v)
                d_v.append(mm_tn(low(soft), dm))
                d_score = low(soft * (d_soft - jnp.sum(soft * d_soft, -1, keepdims=True)))
                d_q.append(mm(d_score, k))
                d_k.append(mm_tn(d_score, q))
            dqkv_s[rows, at : at + 128] = low(jnp.where(left, d_q[0], d_q[1]) * scale)
            dqkv_s[rows, D + at : D + at + 128] = low(jnp.where(left, d_k[0], d_k[1]) * scale)
            dqkv_s[rows, 2 * D + at : 2 * D + at + 128] = low(jnp.where(left, d_v[0], d_v[1]))

    between()
    d_qkv = dqkv_s[...]
    d_normed_a = mm_nt(d_qkv, wqkv_ref[...])
    d_x_zero = d_x_one + norm_back(d_normed_a * ln1_gain, unit_a, inv_a)
    d_x_low = low(d_x_zero)
    token = mm_nt(d_x_low, w4_ref[...]) / count
    tok_o[...] = token
    grouped = token * pg_ref[...].astype(F32)
    tg_o[...] = grouped
    back_o[...] = as_rows(col_sum(grouped), col_sum(token * pc_ref[...].astype(F32)) * sv_ref[3:4, :])
    token_grads()
    narrow = [
        col_sum(d_normed_a * unit_a), col_sum(d_normed_a), col_sum(d_x_one),
        col_sum(d_normed_b * unit_b), col_sum(d_normed_b), col_sum(cot), col_sum(d_x_zero),
    ]
    for k, row in enumerate(narrow):
        small_o[k : k + 1, 0:D] = row
    attention_grads(mm_tn(normed_a, d_qkv), mm_tn(mixed_low, d_x_one_low), mm_tn(act, d_x_low))


def third_back_tokens(
    totals, tg_ref, sc_ref, gm_ref, ps_ref, pooled_ref, gext_ref, w2_ref, w3_ref, w23_ref, sv_ref, stats_ref,
    kap_o, k_o, wb_o, top_o, corr_o, base_o,
):
    gain = sv_ref[0:1, :]
    n = stats_ref[2:3, 0:1]
    alpha = gain * as_vector(totals, 0, 4) / n
    beta = gain * as_vector(totals, 4, 4) * sv_ref[3:4, :] / n
    count = ps_ref[:, C1 : C1 + 1]
    w23 = w23_ref[...]
    act = low(w23[0:C1])
    per_token = low(gain * tg_ref[...] - (count * alpha + beta * sc_ref[...].astype(F32)))
    pooled = low(mm_nt(per_token, w3_ref[0:C2, :]) / count)
    shifted = low(alpha + beta * gm_ref[...].astype(F32))
    kap_o[...] = low(mm_nt(pooled, w2_ref[...]) - mm_nt(shifted, act))
    k_o[:, 0:C1] = low(-mm_nt(low(w23[0:C1] * beta), act))
    wb_o[...] = low(w23[0:C1] * gain)
    top_o[...] = mm_tn(pooled_ref[...], per_token)
    sums = low(ps_ref[:, 0 : C1 + 16])
    corr_o[...] = mm_tn(sums, shifted) + beta * mm(low(gext_ref[:, 0:C1]), act)
    base_o[...] = mm_tn(sums, pooled)


def last_tile(gp, ext, gp1, rel, tok, kap, k_s, xe_s, wb_ref, wd_ref, h_o, q_o, d_at):
    dn = (gp.reshape(TOK, GROUP, C3) * tok[:, None, :]).reshape(TILE, C3)
    xe_s[0:C1, :] = ext[0:C1, :]
    k_s[:, C1 : C1 + TOK] = kap.T
    h_o[...] += mm(ext, dn)
    d_act = mm_nt(wb_ref[...], dn) + mm(k_s[...], xe_s[...])
    d_one = low(d_act * gp1.astype(F32))
    d_at(mm(wd_ref[...], d_one))
    q_o[...] += mm_nt(rel, d_one)


def last_weights(h, gain, corr, base, w2e, w3_ref):
    m = h * gain - corr
    parts = split_three(m)[0:2]
    grad_w3 = sum(mm_tn(w2e, part) for part in parts)
    return grad_w3, sum(mm_nt(part, w3_ref[C2:, :]) for part in parts) + base


def first_grads(q, moments, psmall, stats):
    mean, inverse, n, scale = stats[0:1], stats[1:2], stats[2:3], stats[3:4]
    w = [psmall[k : k + 1, :] for k in range(3)]
    one = q[3:4, :]
    two = inverse * (sum(w[k] * q[k : k + 1, :] for k in range(3)) - mean * one)
    grad_w = []
    for k in range(3):
        along = sum(w[j] * moments[k : k + 1, j : j + 1] for j in range(3)) - mean * moments[k : k + 1, 3:4]
        grad_w.append(scale * (q[k : k + 1, :] - (one * moments[k : k + 1, 3:4] + two * inverse * along) / n))
    flat = [
        jnp.sum(scale * w[k] * (one - two * inverse * mean) / n, axis=1, keepdims=True) for k in range(3)
    ]
    slope = [
        [jnp.sum(scale * w[k] * two * inverse * w[j] / n, axis=1, keepdims=True) for j in range(3)]
        for k in range(3)
    ]
    return grad_w, two, one, flat, slope


def point_gradient(d_ref, rel_ref, centres_ref, flat, slope, out_ref, spread_s, sums_s):
    pieces = d_ref.shape[1] // 256
    lane = lax.rem(lax.broadcasted_iota(jnp.int32, (1, 256), 1), GROUP).astype(F32)
    base = jnp.concatenate(flat, axis=0)
    columns = [jnp.concatenate([slope[k][j] for k in range(3)], axis=0) for j in range(3)]
    spread_s[...] = spread_tokens(centres_ref[...])
    for i in range(pieces):
        at = slice(256 * i, 256 * i + 256)
        rel = rel_ref[:, at].astype(F32)
        d = d_ref[:, at]
        out = d[0:3] + d[4:7] - rel[3:4] * base
        for j in range(3):
            out = out - columns[j] * rel[j : j + 1]
        out_ref[:, at] = out
        sums_s[8 * i : 8 * i + 8, :] = jnp.concatenate([out, jnp.zeros((5, 256), F32)], axis=0)
    sums_s[...] = patch_sum(sums_s[...], patch_ones())
    for i in range(pieces):
        at = slice(256 * i, 256 * i + 256)
        pick = (lane == spread_s[i : i + 1, :]).astype(F32)
        out_ref[:, at] = out_ref[:, at] - pick * sums_s[8 * i : 8 * i + 3, :]


def point_small_rows(grad_w, gain1, shift1, b2, tot, b4):
    rows = list(grad_w) + [gain1, shift1]
    rows += [b2[:, 128 * k : 128 * k + 128] for k in range(2)]
    rows += [tot[4:8, :], tot[0:4, :]]
    rows += [b4[:, 128 * k : 128 * k + 128] for k in range(3)]
    return jnp.concatenate(rows, axis=0)


def block_small_rows(small_ref):
    rows = [small_ref[k : k + 1, 128 * j : 128 * j + 128] for k in range(5) for j in range(3)]
    rows += [small_ref[7:8, 128 * j : 128 * j + 128] for j in range(12)]
    rows += [small_ref[5:6, 128 * j : 128 * j + 128] for j in range(3)]
    return jnp.concatenate(rows, axis=0)


class Scatter:
    def __init__(self, blocks, lands, send, recv, base):
        self.blocks, self.lands, self.sems, self.base = blocks, lands, (send, recv), base
        z, y, x, core = self.at = where_am_i()
        half = blocks.shape[-1] // 2
        self.one, self.two = pl.ds(0, half), pl.ds(half, half)
        every = slice(None)
        mine = blocks.at[core]
        near = [(chip(lax.rem(z + k, NZ), y, x), core) for k in range(1, NZ)]
        over_y, over_x, twin = (chip(z, 1 - y, x), core), (chip(z, y, 1 - x), core), (chip(z, y, x), 1 - core)
        land1, land2, land3, land4 = lands
        self.stages = [
            [(blocks.at[1 - core], land1, twin)],
            [
                (mine.at[:, :, 1 - x, :, self.one], land2.at[0], over_x),
                (mine.at[:, 1 - y, :, :, self.two], land2.at[1], over_y),
            ],
            [
                (mine.at[:, 1 - y, x, :, self.one], land3.at[0], over_y),
                (mine.at[:, y, 1 - x, :, self.two], land3.at[1], over_x),
            ],
            [(mine.at[lax.rem(z + k, NZ), y, x], land4.at[k - 1], near[k - 1]) for k in range(1, NZ)],
        ]

    def copies(self, stage):
        k = self.base + sum(len(s) for s in self.stages[:stage])
        return [
            pltpu.make_async_remote_copy(
                src_ref=src, dst_ref=dst, send_sem=self.sems[0].at[k + i], recv_sem=self.sems[1].at[k + i],
                device_id=peer, device_id_type=MESH,
            )
            for i, (src, dst, peer) in enumerate(self.stages[stage])
        ]

    def advance(self, stage):
        z, y, x, core = self.at
        mine = self.blocks.at[core]
        land1, land2, land3, land4 = self.lands
        if stage > 0:
            for copy in self.copies(stage - 1):
                copy.wait()
        if stage == 1:
            for cz in range(NZ):
                for cy in range(NY):
                    for cx in range(NX):
                        mine[cz, cy, cx] = mine[cz, cy, cx] + land1[cz, cy, cx]
        if stage == 2:
            for cz in range(NZ):
                for k in range(2):
                    mine[cz, k, x, :, self.one] = mine[cz, k, x, :, self.one] + land2[0, cz, k]
                    mine[cz, y, k, :, self.two] = mine[cz, y, k, :, self.two] + land2[1, cz, k]
        if stage == 3:
            for cz in range(NZ):
                mine[cz, y, x, :, self.one] = mine[cz, y, x, :, self.one] + land3[0, cz]
                mine[cz, y, x, :, self.two] = mine[cz, y, x, :, self.two] + land3[1, cz]
        if stage < 4:
            for copy in self.copies(stage):
                copy.start()
            return None
        total = mine[z, y, x].astype(F32)
        for k in range(NZ - 1):
            total = total + land4[k].astype(F32)
        return total


SCATTER_SEMS = 8
POINT_WIDTH = 768


def scatter_scratch(width):
    return [
        pltpu.VMEM((NC, NZ, NY, NX, 16, width), BF16),
        pltpu.VMEM((NZ, NY, NX, 16, width), BF16),
        pltpu.VMEM((2, NZ, 2, 16, width // 2), BF16),
        pltpu.VMEM((2, NZ, 16, width // 2), BF16),
        pltpu.VMEM((NZ - 1, 16, width), BF16),
    ]


def backward_kernel(known, dp, *refs):
    refs = list(refs)
    take = lambda count: [refs.pop(0) for _ in range(count)]
    pa_ref, pg_ref, pc_ref, ps_ref, len_ref, cot_ref, psmall_ref, bsmall_ref, sv_ref, stats_ref, moment_ref = take(11)
    w2_ref, w3_ref, w4_ref, wqkv_ref, wo_ref, wf1_ref, wf2_ref, w23_ref = take(8)
    sc_ref, gm_ref, pooled_ref, gext_ref, wd_ref, rel_ref, centres_ref, gp_ref, ext_ref, gp1_ref = take(10)
    out_o, pg_o = take(2)
    if known:
        pflat_o, bflat_o = take(2)
    else:
        prow_o, brow_o, gw2_o, gw3_o, gw4_o, gwqkv_o, gwo_o, gwf1_o, gwf2_o = take(9)
    small_s, tok_s, tg_s, acc3, qkv_s, mixed_s, soft_s, dmix_s, dqkv_s, dhid_s = take(10)
    tot_s, kap_s, k_s, wb_s, top_s, corr_s, base_s, h_s, q_s, d_s, xe_s, spread_s, sums_s = take(13)
    acc, slots, ssend, srecv, unused, slots3, ssend3, srecv3 = take(8)
    gp_r, ext_r, gp1_r, read_sem = take(4)
    step = pl.program_id(0)
    steps = pl.num_programs(0)
    peers = all_peers(dp)
    if known:
        ffn0, ffn1, ffn2, ffn3, ffn4, att0, att1, att2, att3, att4, point0, point1, point2, point3, point4 = take(15)
        wide, tall, stage, pstage, pal, bal, gsend, grecv = take(8)
        z, y, x, core = where_am_i()
        ffn = Scatter(ffn0, (ffn1, ffn2, ffn3, ffn4), gsend, grecv, 0)
        att = Scatter(att0, (att1, att2, att3, att4), gsend, grecv, SCATTER_SEMS)
        point = Scatter(point0, (point1, point2, point3, point4), gsend, grecv, 2 * SCATTER_SEMS)

    def ffn_grads(gwf1, gwf2):
        if not known:
            gwf1_o[...], gwf2_o[...] = gwf1, gwf2
            return
        wide[...] = gwf1
        tall[...] = gwf2
        for d in range(dp * NC):
            stage[0:12, 0:FF] = wide[12 * d : 12 * d + 12, :]
            for row, rows, under, at in FFN_PIECES:
                stage[under : under + rows, at : at + D] = tall[48 * d + row : 48 * d + row + rows, :]
            cz, cy, cx, cc = place(d)
            ffn0[cc, cz, cy, cx] = low(stage[...])
        greeted(peers)
        ffn.advance(0)

    def between():
        if known:
            ffn.advance(1)

    def token_grads():
        if not known:
            greeted(peers)
        sum_start(dp, acc3, slots3, ssend3, srecv3)

    def attention_grads(gwqkv, gwo, gw4):
        if not known:
            gwqkv_o[...], gwo_o[...], gw4_o[...] = gwqkv, gwo, gw4
            return
        wide[:, 0 : 3 * D] = gwqkv
        wide[:, 3 * D :] = gwo
        tall[0:C3, :] = gw4
        for d in range(dp * NC):
            stage[0:12, 0:ATT_WIDTH] = wide[12 * d : 12 * d + 12, :]
            for k in range(4):
                stage[12:16, D * k : D * k + D] = tall[16 * d + 4 * k : 16 * d + 4 * k + 4, :]
            cz, cy, cx, cc = place(d)
            att0[cc, cz, cy, cx] = low(stage[:, 0:ATT_WIDTH])
        att.advance(0)
        ffn.advance(2)
        att.advance(1)

    def reads(tile, slot):
        at = pl.ds(pl.multiple_of(tile * TILE, TILE), TILE)
        pairs = ((gp_ref.at[at, :], gp_r), (ext_ref.at[:, at], ext_r), (gp1_ref.at[:, at], gp1_r))
        return [
            pltpu.make_async_copy(src, ring.at[slot], read_sem.at[slot, k]) for k, (src, ring) in enumerate(pairs)
        ]

    @pl.when(step == 0)
    def _():
        greet(peers)
        for tile in range(AHEAD):
            for copy in reads(tile, tile):
                copy.start()
        block_step(
            pa_ref, pg_ref, pc_ref, ps_ref, len_ref, cot_ref, psmall_ref, bsmall_ref, sv_ref,
            w4_ref, wqkv_ref, wo_ref, wf1_ref, wf2_ref,
            out_o, small_s, tok_s, tg_s, acc3, qkv_s, mixed_s, soft_s, dmix_s, dqkv_s, dhid_s,
            ffn_grads, between, token_grads, attention_grads,
        )
        for ref in (h_s, q_s):
            ref[...] = jnp.zeros_like(ref)
        xe_s[C1:, :] = token_ones()
        tot_s[...] = sum_finish(acc3, slots3, sum_copies(dp, acc3, lambda k: slots3.at[k], ssend3, srecv3))
        third_back_tokens(
            tot_s[...], tg_s, sc_ref, gm_ref, ps_ref, pooled_ref, gext_ref, w2_ref, w3_ref, w23_ref, sv_ref, stats_ref,
            kap_s, k_s, wb_s, top_s, corr_s, base_s,
        )

    if known:
        for at_step, group, number in ((4, ffn, 3), (5, att, 2), (7, att, 3)):
            pl.when(step == at_step)(functools.partial(group.advance, number))

    @pl.when(step >= 1)
    def _():
        tile = step - 1
        at = pl.ds(pl.multiple_of(tile * TILE, TILE), TILE)
        ts = pl.ds(pl.multiple_of(tile * TOK, TOK), TOK)
        slot = lax.rem(tile, AHEAD)

        def put(d):
            d_s[:, at] = d

        for copy in reads(tile, slot):
            copy.wait()
        last_tile(
            gp_r[slot], ext_r[slot], gp1_r[slot], rel_ref[:, at], low(tok_s[ts, :] * 0.5), kap_s[ts, :],
            k_s, xe_s, wb_s, wd_ref, h_s, q_s, put,
        )

        @pl.when(tile + AHEAD < steps - 1)
        def _():
            for copy in reads(tile + AHEAD, slot):
                copy.start()

    @pl.when(step == steps - 1)
    def _():
        acc[...] = q_s[...]
        b2 = as_vector(psmall_ref, 5, 2)
        w2e = jnp.concatenate([w2_ref[...], low(jnp.concatenate([b2, jnp.zeros((15, C2), F32)], axis=0))], axis=0)
        gw3, gw2 = last_weights(h_s[...], sv_ref[0:1, :], corr_s[...], base_s[...], w2e, w3_ref)
        none = jnp.zeros((1, 128), F32)
        prow = point_small_rows([none] * 3, none, none, gw2[C1 : C1 + 1, :], jnp.zeros((8, 128), F32), small_s[6:7, 0:D])
        brow = block_small_rows(small_s)
        if known:
            pstage[...] = jnp.zeros_like(pstage)
            for d in range(dp * NC):
                if d < 16:
                    pstage[:, 0:C3] = top_s[16 * d : 16 * d + 16, :]
                else:
                    pstage[:, 0:C3] = gw3[16 * (d - 16) : 16 * (d - 16) + 16, :]
                pstage[0:4, C3 : C3 + C2] = gw2[4 * d : 4 * d + 4, :]
                pstage[4:5, C3 : C3 + 128] = piece_of(prow, PSMALL * d, PSMALL)
                pstage[5:6, C3 : C3 + 128] = piece_of(brow, BSMALL * d, BSMALL)
                cz, cy, cx, cc = place(d)
                point0[cc, cz, cy, cx] = low(pstage[...])
            point.advance(0)
        copies = sum_start(dp, acc, slots, ssend, srecv)
        if known:
            point.advance(1)
        totals = sum_finish(acc, slots, copies)
        grad_w, gain1, shift1, flat, slope = first_grads(totals, moment_ref[...], psmall_ref[...], stats_ref[...])
        full_rows = point_small_rows(grad_w, gain1, shift1, jnp.zeros((1, C2), F32), tot_s[...], jnp.zeros((1, D), F32))
        if known:
            point.advance(2)
            stage[...] = ffn.advance(4)
            ffn_flat(stage, bal)
            stage[:, 0:ATT_WIDTH] = att.advance(4)
            attention_flat(stage, bal, pal)
            point.advance(3)
        point_gradient(d_s, rel_ref, centres_ref, flat, slope, pg_o, spread_s, sums_s)
        if not known:
            prow_o[0:18, :] = prow + full_rows * (1.0 / (dp * NC))
            brow_o[0:30, :] = brow
            gw2_o[...] = gw2[0:C1]
            gw3_o[0:C2, :] = top_s[...]
            gw3_o[C2:, :] = gw3
            return
        own = jnp.zeros((1, 128), F32)
        for d in range(dp * NC):
            own = own + jnp.where(me() == d, piece_of(full_rows, PSMALL * d, PSMALL), 0.0)
        pstage[...] = point.advance(4)
        for j in range(C2 // 128):
            pal[pl.ds(1 + j, 4, stride=2), :] = pstage[0:4, C3 + 128 * j : C3 + 128 * j + 128]
        for j in range(C3 // 128):
            pal[pl.ds(9 + j, 16, stride=4), :] = pstage[:, 128 * j : 128 * j + 128]
        pflat_o[...] = segments_joined(pal[...], pstage[4:5, C3 : C3 + 128] + own, PSMALL)
        bflat_o[...] = segments_joined(bal[...], pstage[5:6, C3 : C3 + 128], BSMALL)


def backward_call(known, dp, *args):
    count = args[24].shape[1]
    tokens, tiles = count // GROUP, count // TILE
    single = dict(pipeline_mode=pl.Buffered(1))
    full = lambda *s: pl.BlockSpec(s, lambda i: (0, 0), **single)
    specs = [full(*a.shape) for a in args[:26]]
    specs[4] = pl.BlockSpec(memory_space=pltpu.SMEM)
    specs += [pl.BlockSpec(memory_space=pl.ANY)] * 3
    outs = [((tokens, D), F32), ((3, count), F32)]
    if known:
        outs += [((PROWS, 128), F32), ((BROWS, 128), F32)]
    else:
        outs += [((24, 128), F32), ((32, 128), F32), ((C1, C2), F32), ((2 * C2, C3), F32), ((C3, D), F32)]
        outs += [((D, 3 * D), F32), ((D, D), F32), ((D, FF), F32), ((FF, D), F32)]
    pieces = count // 256
    scratch = [
        pltpu.VMEM((8, FF), F32), pltpu.VMEM((tokens, C3), F32), pltpu.VMEM((tokens, C3), F32), pltpu.VMEM((8, 128), F32),
        pltpu.VMEM((tokens, 3 * D), BF16), pltpu.VMEM((tokens, D), BF16),
        pltpu.VMEM((tokens // PAIR * HEADS, PAIR, PAIR), F32), pltpu.VMEM((tokens, D), BF16),
        pltpu.VMEM((tokens, 3 * D), BF16), pltpu.VMEM((tokens, FF), BF16),
        pltpu.VMEM((8, 128), F32), pltpu.VMEM((tokens, C1), BF16), pltpu.VMEM((C1, C1 + TOK), BF16),
        pltpu.VMEM((C1, C3), BF16), pltpu.VMEM((C2, C3), F32), pltpu.VMEM((C1 + 16, C3), F32),
        pltpu.VMEM((C1 + 16, C2), F32), pltpu.VMEM((C1 + 16, C3), F32), pltpu.VMEM((8, C1), F32),
        pltpu.VMEM((8, count), F32), pltpu.VMEM((C1 + TOK, TILE), BF16),
        pltpu.VMEM((pieces, 256), F32), pltpu.VMEM((8 * pieces, 256), F32),
    ]
    scratch += sum_scratch(dp) + sum_scratch(dp)
    scratch += [
        pltpu.VMEM((AHEAD, TILE, C3), BF16), pltpu.VMEM((AHEAD, C1 + 16, TILE), BF16), pltpu.VMEM((AHEAD, C1, TILE), BF16),
        pltpu.SemaphoreType.DMA((AHEAD, 3)),
    ]
    if known:
        scratch += scatter_scratch(FFN_WIDTH) + scatter_scratch(ATT_WIDTH) + scatter_scratch(POINT_WIDTH)
        scratch += [
            pltpu.VMEM((D, FF), F32), pltpu.VMEM((FF, D), F32),
            pltpu.VMEM((16, FFN_WIDTH), F32), pltpu.VMEM((16, POINT_WIDTH), F32),
            pltpu.VMEM((PROWS, 128), F32), pltpu.VMEM((BROWS, 128), F32),
            pltpu.SemaphoreType.DMA((3 * SCATTER_SEMS,)), pltpu.SemaphoreType.DMA((3 * SCATTER_SEMS,)),
        ]
    return pl.pallas_call(
        functools.partial(backward_kernel, known, dp),
        grid=(1 + tiles,),
        in_specs=specs,
        out_specs=[full(*s) for s, t in outs],
        out_shape=shaped(*outs),
        scratch_shapes=scratch,
        compiler_params=params(collective_id=1, has_side_effects=True),
        name="backward",
    )(*args)


def geometry_kernel(points_ref, counts_ref, centres_ref, rel_o, moment_o, counts_s, picked_s):
    moments = geometry(points_ref, counts_ref, centres_ref, rel_o, counts_s, picked_s)
    moment_o[...] = jnp.concatenate([moments, jnp.zeros((8, 120), F32)], axis=1)


def geometry_call(points, counts, centres):
    count = points.shape[1]
    return pl.pallas_call(
        geometry_kernel,
        out_shape=shaped(((8, count), BF16), ((8, 128), F32)),
        in_specs=vmem(3),
        out_specs=vmem(2),
        scratch_shapes=[pltpu.VMEM((count // 128, 256), F32), pltpu.VMEM((count // 32, 256), F32)],
        compiler_params=params(),
        name="geometry",
    )(points, counts, centres)


def gather_plain(points, counts, centres, point_master, block_master, devices):
    rel, moments = geometry_call(points, counts, centres)
    moments = lax.psum(moments, AXES)
    tables = []
    for master, layout in ((point_master, point_layout()), (block_master, block_layout())):
        offset = 0
        parts = []
        for seg_len in segment_lengths(layout, devices):
            piece = master[offset : offset + seg_len // devices].astype(BF16)
            offset += seg_len // devices
            parts.append(lax.all_gather(piece, AXES, axis=0, tiled=True))
        tables.append(parts)
    (ps, w2, w3, w4), (bs, wqkv, wo, wf1, wf2) = tables

    def rows_of(v, rows, used):
        v = v[:used].astype(F32).reshape(-1, 128)
        return jnp.concatenate([v, jnp.zeros((rows - v.shape[0], 128), F32)], axis=0)

    small = (rel, moments, rows_of(ps, 24, 18 * 128), rows_of(bs, 32, 30 * 128))
    point = (w2.reshape(C1, C2), w3.reshape(2 * C2, C3))
    block = (w4.reshape(C3, D), wqkv.reshape(D, 3 * D), wo.reshape(D, D), wf1.reshape(D, FF), wf2.reshape(FF, D))
    return small + point, block


def scatter_plain(devices, prow, brow, gw2, gw3, gw4, gwqkv, gwo, gwf1, gwf2):
    pieces = []
    for layout, tables in (
        (point_layout(), (prow[:18], gw2, gw3, gw4)),
        (block_layout(), (brow[:30], gwqkv, gwo, gwf1, gwf2)),
    ):
        parts = []
        for values, seg_len in zip(tables, segment_lengths(layout, devices)):
            values = values.reshape(-1)
            values = jnp.concatenate([values, jnp.zeros((seg_len - values.shape[0],), F32)])
            parts.append(lax.psum_scatter(values, AXES, scatter_dimension=0, tiled=True))
        pieces.append(parts)
    return pieces


def adam_update(master, moment_one, moment_two, gradient, step_rates, decays):
    one_new = BETA_ONE * moment_one + (1.0 - BETA_ONE) * gradient
    two_new = BETA_TWO * moment_two + (1.0 - BETA_TWO) * gradient * gradient
    fix_one = 1.0 - BETA_ONE**STEP
    fix_two = 1.0 - BETA_TWO**STEP
    direction = one_new / fix_one / (jnp.sqrt(two_new / fix_two) + ADAM_EPS)
    master_new = master - step_rates * (direction + decays * master)
    return (master_new, one_new, two_new)


def on_device(
    points, point_count, centre_slot, cloud_length, cotangent, point_master, block_master,
    point_first, block_first, point_second, block_second,
):
    dp, fsdp = lax.axis_size("dp"), lax.axis_size("fsdp")
    devices = dp * fsdp
    own_rank = lax.axis_index(AXES)
    known = dp == NZ * NY * NX and fsdp == NC
    count = points.shape[1]
    counts, centres = point_count.reshape(1, -1), centre_slot.reshape(1, -1)
    if known:
        outs = forward_call(
            True, dp, count, points, counts, centres, point_master, block_master
        )
        given, block, outs = outs[:6], outs[6:11], outs[11:]
    else:
        given, block = gather_plain(points, counts, centres, point_master, block_master, devices)
        outs = forward_call(False, dp, count, *given)
    rel, moments, psmall, bsmall, w2, w3 = given
    ext, gp1, gext, ps, gm, sc, pooled, sv, stats, wd, w23, gp, pa, pg, pc = outs
    outs = backward_call(
        known, dp, pa, pg, pc, ps, cloud_length, cotangent, psmall, bsmall, sv, stats, moments,
        w2, w3, *block, w23, sc, gm, pooled, gext, wd, rel, centres, gp, ext, gp1,
    )
    tokens_out, point_grad = outs[:2]
    if known:
        point_gradient_vec = outs[2].reshape(-1)[: point_master.shape[0]]
        block_gradient = outs[3].reshape(-1)[: block_master.shape[0]]
        block_small = block_gradient[:BSMALL]
    else:
        point_parts, block_parts = scatter_plain(devices, *outs[2:])
        block_small = block_parts[0]
        point_gradient_vec = jnp.concatenate(point_parts)
        block_gradient = jnp.concatenate(block_parts)
    point_rates, point_decays = shard_rates(point_layout(), devices, own_rank)
    block_rates, block_decays = shard_rates(block_layout(), devices, own_rank)
    point_new, point_one, point_two = adam_update(
        point_master, point_first, point_second, point_gradient_vec, point_rates, point_decays
    )
    block_new, block_one, block_two = adam_update(
        block_master, block_first, block_second, block_gradient, block_rates, block_decays
    )
    return (
        tokens_out, point_grad, point_new, block_new, point_one, block_one, point_two, block_two,
        point_new.astype(BF16), block_new.astype(BF16), block_small,
    )


def solution(mesh):
    split = P(AXES)
    return jax.shard_map(
        on_device,
        mesh=mesh,
        in_specs=(P(None, AXES), split, split, split, P(AXES, None)) + (split,) * 6,
        out_specs=(P(AXES, None), P(None, AXES)) + (split,) * 9,
        check_vma=False,
    )
```
